32 devices in a mesh: batch: 8 (over z, y), seq: 4 (over x, core).
Axes of the slice: x: 2, y: 2, z: 4, core: 2. Of those that a mesh axis runs over, the one named last changes fastest.
Arguments:
- tokens: bfloat16 [1024, 16, 1024], P('seq', 'batch'), may hold values from -6 to 6
- ln1_gain: bfloat16 [1024], replicated, may hold values from 0.5 to 1.5
- ln1_bias: bfloat16 [1024], replicated, may hold values from -4 to 4
- w_qkv: bfloat16 [1024, 3072], replicated, may hold values from -0.1875 to 0.1875
- q_bias: bfloat16 [1024], replicated, may hold values from -4 to 4
- v_bias: bfloat16 [1024], replicated, may hold values from -4 to 4
- w_out: bfloat16 [1024, 1024], replicated, may hold values from -1.5 to 1.5
- out_bias: bfloat16 [1024], replicated, may hold values from -4 to 4
- ln2_gain: bfloat16 [1024], replicated, may hold values from 0.5 to 1.5
- ln2_bias: bfloat16 [1024], replicated, may hold values from -4 to 4
- w_in: bfloat16 [1024, 4096], replicated, may hold values from -0.1875 to 0.1875
- in_bias: bfloat16 [4096], replicated, may hold values from -4 to 4
- w_down: bfloat16 [4096, 1024], replicated, may hold values from -0.09375 to 0.09375
- down_bias: bfloat16 [1024], replicated, may hold values from -4 to 4
- cotangent: bfloat16 [1024, 16, 1024], P('seq', 'batch'), may hold values from -6 to 6
- segment_ids: int32 [1024, 16], P(None, 'batch'), may hold values from 0 to 3, as said below
- random_blocks: int32 [16, 16, 16, 3], P(None, 'batch'), may hold values from 0 to 15, as said below
- global_blocks: int32 [2, 16], P(None, 'batch'), may hold values from 0 to 15
Outputs:
- output: bfloat16 [1024, 16, 1024], P('seq', 'batch')
- input_grad: float32 [1024, 16, 1024], P('seq', 'batch')
- ln1_gain_grad: float32 [1024], P(('batch', 'seq'))
- ln1_bias_grad: float32 [1024], P(('batch', 'seq'))
- w_qkv_grad: float32 [1024, 3072], P(('batch', 'seq'))
- q_bias_grad: float32 [1024], P(('batch', 'seq'))
- v_bias_grad: float32 [1024], P(('batch', 'seq'))
- w_out_grad: float32 [1024, 1024], P(('batch', 'seq'))
- out_bias_grad: float32 [1024], P(('batch', 'seq'))
- ln2_gain_grad: float32 [1024], P(('batch', 'seq'))
- ln2_bias_grad: float32 [1024], P(('batch', 'seq'))
- w_in_grad: float32 [1024, 4096], P(('batch', 'seq'))
- in_bias_grad: float32 [4096], P(('batch', 'seq'))
- w_down_grad: float32 [4096, 1024], P(('batch', 'seq'))
- down_bias_grad: float32 [1024], P(('batch', 'seq'))
The draws below stay inside these ranges and needn't reach their ends.
Inputs may be any that keep to these rules, and one draw needn't show every extreme that they name: `segment_ids`: along each sequence the ids never fall. In each group of 2 sequences that one index of batch holds, one sequence drawn from the seed has a segment that begins within its first 256 tokens and ends within its last 256 tokens. `random_blocks`: take the entries of query blocks k * 4 to (k + 1) * 4 - 1 of the 2 sequences of one index of batch, over all heads and slots: for every m, exactly 96 of them name a block of m * 4 to (m + 1) * 4 - 1.
All inputs are finite; a program needn't handle non-finite values.
Results may differ from the reference program's by a relative error of at most 0.012.
Values may be sent and summed in bfloat16 or wider, within the bound.
A program may use at most 576 MiB of HBM per device.

```python
import jax
import jax.numpy as jnp
from jax import lax

D = 1024
HEADS = 16
HD = 64
FF = 4096
BLK = 64
RAND = 3
GLOB = 2
BLOCKS_DEV = 4
SEQS = 2
LEN = 1024
NB = 16
SEQUENCES = 16
N_BATCH = 8
N_SEQ = 4


def document_cuts(key):
    key = jax.random.fold_in(key, 17)
    spread_key, first_key, last_key, pick_key = jax.random.split(key, 4)
    device_rows = LEN // N_SEQ
    spread = jax.random.randint(spread_key, (3, SEQUENCES), 1, LEN, dtype=jnp.int32)
    first_cut = jax.random.randint(first_key, (SEQUENCES,), 1, device_rows, dtype=jnp.int32)
    last_cut = jax.random.randint(last_key, (SEQUENCES,), LEN - device_rows + 1, LEN, dtype=jnp.int32)
    chosen = jax.random.randint(pick_key, (N_BATCH,), 0, SEQS, dtype=jnp.int32)
    places = jnp.arange(SEQUENCES, dtype=jnp.int32)
    longest = places % SEQS == chosen[places // SEQS]
    return jnp.where(longest[None, :], jnp.stack([first_cut, last_cut, last_cut]), spread)


def draw_segment_ids(key, part):
    doc_cuts = document_cuts(key)
    token_ids = jnp.arange(LEN, dtype=jnp.int32)
    return jnp.sum((doc_cuts[:, None, :] <= token_ids[None, :, None]).astype(jnp.int32), axis=0)


def draw_random_blocks(key, part):
    key = jax.random.fold_in(key, 5)
    order_key, offset_key = jax.random.split(key, 2)
    entries = BLOCKS_DEV * SEQS * HEADS * RAND
    group_keys = jax.random.split(order_key, N_SEQ * N_BATCH)
    orders = jax.vmap(lambda one_key: jax.random.permutation(one_key, entries))(group_keys)
    owners = orders.astype(jnp.int32) % N_SEQ
    offsets = jax.random.randint(offset_key, (N_SEQ * N_BATCH, entries), 0, BLOCKS_DEV, dtype=jnp.int32)
    picked = owners * BLOCKS_DEV + offsets
    picked = picked.reshape(N_SEQ, N_BATCH, BLOCKS_DEV, SEQS, HEADS, RAND).transpose(0, 2, 1, 3, 4, 5)
    return picked.reshape(NB, SEQUENCES, HEADS, RAND).astype(jnp.int32)


def plant(drawn, key, low, top_value):
    dims = drawn.shape
    spot = [jax.random.randint(jax.random.fold_in(key, axis), (), 0, dims[axis]) for axis in range(len(dims))]
    drawn = drawn.at[tuple(spot)].set(low)
    longest = dims.index(max(dims))
    spot[longest] = (spot[longest] + 1) % dims[longest]
    return drawn.at[tuple(spot)].set(top_value)


def steps_of(rng, shape, pieces, least, largest):
    gain, own = 1.0, jax.random.fold_in(rng, 6)
    for dim, blocks in pieces:
        steps = jnp.exp(jax.random.uniform(jax.random.fold_in(own, dim), (blocks,), jnp.float32, least / len(pieces), largest / len(pieces)))
        gain = gain * jnp.repeat(steps, shape[dim] // blocks).reshape([-1 if axis == dim else 1 for axis in range(len(shape))])
    return gain


def scatter_about(key, extent, scale, bound, shards=(), kind=jnp.bfloat16):
    level = steps_of(key, extent, shards, -0.22, 0.18) if shards else 1.0
    drawn = jax.random.normal(key, extent, jnp.float32) * scale * level
    return jnp.minimum(jnp.maximum(drawn, -bound), bound).astype(kind)


def setup_inputs(seed: int = 0) -> dict:
    seeds = jax.random.split(jax.random.key(seed), 19)
    tokens = scatter_about(seeds[0], (LEN, SEQUENCES, D), 1.0, 6.0, ((0, 4), (1, 8)))
    ln1_gain = jnp.clip(1.0 + 0.1 * jax.random.normal(seeds[1], (D,), jnp.float32), 0.5, 1.5).astype(jnp.bfloat16)
    ln1_bias = scatter_about(seeds[2], (D,), 0.3, 4.0)
    w_qkv = scatter_about(seeds[3], (D, 3 * D), D ** -0.5, 0.1875)
    q_bias = scatter_about(seeds[4], (D,), 0.3, 4.0)
    v_bias = scatter_about(seeds[5], (D,), 0.3, 4.0)
    w_out = scatter_about(seeds[6], (D, D), (D // 64) ** -0.5, 1.5)
    out_bias = scatter_about(seeds[7], (D,), 0.3, 4.0)
    ln2_gain = jnp.clip(1.0 + 0.1 * jax.random.normal(seeds[8], (D,), jnp.float32), 0.5, 1.5).astype(jnp.bfloat16)
    ln2_bias = scatter_about(seeds[9], (D,), 0.3, 4.0)
    w_in = scatter_about(seeds[10], (D, FF), D ** -0.5, 0.1875)
    in_bias = scatter_about(seeds[11], (FF,), 0.3, 4.0)
    w_down = scatter_about(seeds[12], (FF, D), FF ** -0.5, 0.09375)
    down_bias = scatter_about(seeds[13], (D,), 0.3, 4.0)
    cotangent = scatter_about(seeds[14], (LEN, SEQUENCES, D), 1.0, 6.0, ((0, 4), (1, 8)))
    segment_ids = draw_segment_ids(jax.random.fold_in(seeds[18], 71), 0)
    random_blocks = draw_random_blocks(jax.random.fold_in(seeds[18], 71), 0)
    global_blocks = plant(jax.random.randint(seeds[17], (GLOB, SEQUENCES), 0, NB), jax.random.fold_in(seeds[17], 1), 0, NB - 1).astype(jnp.int32)
    return {"tokens": tokens, "ln1_gain": ln1_gain, "ln1_bias": ln1_bias, "w_qkv": w_qkv, "q_bias": q_bias, "v_bias": v_bias, "w_out": w_out, "out_bias": out_bias, "ln2_gain": ln2_gain, "ln2_bias": ln2_bias, "w_in": w_in, "in_bias": in_bias, "w_down": w_down, "down_bias": down_bias, "cotangent": cotangent, "segment_ids": segment_ids, "random_blocks": random_blocks, "global_blocks": global_blocks}


@jax.custom_vjp
def low(v):
    return lax.optimization_barrier(v.astype(jnp.bfloat16)).astype(jnp.float32)

@jax.custom_vjp
def low_back(v):
    return v

def low_keep(v):
    return (low(v), None)

def low_pass(kept, grad):
    return (grad,)

def back_keep(v):
    return (v, None)

def back_low(kept, grad):
    return (low(grad),)
low.defvjp(low_keep, low_pass)
low_back.defvjp(back_keep, back_low)
eps = 1e-05
highest = lax.Precision.HIGHEST

def layer_norm(values, gain_vec, shift_vec):
    row_mean = lax.optimization_barrier(jnp.mean(values, axis=-1, keepdims=True))
    centred = values - row_mean
    spread = lax.optimization_barrier(jnp.mean(centred * centred, axis=-1, keepdims=True))
    return centred * lax.rsqrt(spread + eps) * gain_vec + shift_vec

def matmul(left_side, right_side):
    return jnp.dot(left_side, right_side, precision=highest, preferred_element_type=jnp.float32)

def attend_group(query_group, index_group, key_segment, query_segment, keyval_heads):
    group_size = query_group.shape[0]
    key_blocks = index_group.shape[-1]
    head_ids = jnp.arange(HEADS, dtype=jnp.int32)[None, :, None]
    chosen = keyval_heads[head_ids, index_group]
    key_rows = chosen[:, :, :, :, 0].reshape(group_size, HEADS, key_blocks * BLK, HD)
    value_rows = chosen[:, :, :, :, 1].reshape(group_size, HEADS, key_blocks * BLK, HD)
    raw_scores = low_back(jnp.einsum('gthd,ghkd->ghtk', query_group, key_rows, precision=highest) * HD ** (-0.5))
    allowed = key_segment[:, :, None, :] == query_segment[:, None, :, None]
    masked = jnp.where(allowed, raw_scores, -1e+30)
    row_max = lax.optimization_barrier(jnp.max(masked, axis=-1, keepdims=True))
    weights = jnp.exp(masked - row_max)
    attn_probs = low(weights / lax.optimization_barrier(jnp.sum(weights, axis=-1, keepdims=True)))
    return jnp.einsum('ghtk,ghkd->gthd', attn_probs, value_rows, precision=highest)

def sequence_forward(params, seq_tokens, segment, random_ids, global_ids):
    ln1_gain, ln1_bias, w_qkv, q_bias, v_bias, w_out, out_bias, ln2_gain, ln2_bias, w_in, in_bias, w_down, down_bias = params
    key_blocks = 3 + RAND + GLOB
    normed = low(layer_norm(seq_tokens, ln1_gain, ln1_bias))
    projected = matmul(normed, w_qkv)
    queries = low(low_back(projected[:, :D] + q_bias))
    keyval = low(low_back(projected[:, D:] + jnp.concatenate([jnp.zeros((D,), jnp.float32), v_bias])))
    keyval_heads = keyval.reshape(NB, BLK, 2, HEADS, HD).transpose(3, 0, 1, 2, 4)
    block_ids = jnp.arange(NB, dtype=jnp.int32)
    window_raw = block_ids[:, None] + jnp.arange(-1, 2, dtype=jnp.int32)[None, :]
    inside_seq = (window_raw >= 0) & (window_raw < NB)
    window_ids = jnp.clip(window_raw, 0, NB - 1)
    block_index = jnp.concatenate([jnp.broadcast_to(window_ids[:, None, :], (NB, HEADS, 3)), random_ids, jnp.broadcast_to(global_ids[None, None, :], (NB, HEADS, GLOB))], axis=-1)
    present = jnp.concatenate([jnp.broadcast_to(inside_seq[:, None, :], (NB, HEADS, 3)), block_index[:, :, 3:] >= 0], axis=-1)
    positions = block_index[..., None] * BLK + jnp.arange(BLK, dtype=jnp.int32)
    key_segment = jnp.where(present[..., None], segment[positions], -1).reshape(NB, HEADS, key_blocks * BLK)
    query_segment = segment.reshape(NB, BLK)
    groups = NB // 8
    packed = (queries.reshape(groups, 8, BLK, HEADS, HD), block_index.reshape(groups, 8, HEADS, key_blocks), key_segment.reshape(groups, 8, HEADS, key_blocks * BLK), query_segment.reshape(groups, 8, BLK))

    def attend_items(group_items):
        return attend_group(group_items[0], group_items[1], group_items[2], group_items[3], keyval_heads)
    context = lax.map(jax.checkpoint(attend_items), packed)
    context = low(low_back(context.reshape(LEN, D)))
    mid_stream = seq_tokens + low_back(matmul(context, w_out) + out_bias)
    normed2 = low(layer_norm(mid_stream, ln2_gain, ln2_bias))
    hidden = low(jax.nn.gelu(low_back(matmul(normed2, w_in) + in_bias), approximate=True))
    return mid_stream + low_back(matmul(hidden, w_down) + down_bias)

def reference(tokens, ln1_gain, ln1_bias, w_qkv, q_bias, v_bias, w_out, out_bias, ln2_gain, ln2_bias, w_in, in_bias, w_down, down_bias, cotangent, segment_ids, random_blocks, global_blocks):
    params = (ln1_gain.astype(jnp.float32), ln1_bias.astype(jnp.float32), w_qkv.astype(jnp.float32), q_bias.astype(jnp.float32), v_bias.astype(jnp.float32), w_out.astype(jnp.float32), out_bias.astype(jnp.float32), ln2_gain.astype(jnp.float32), ln2_bias.astype(jnp.float32), w_in.astype(jnp.float32), in_bias.astype(jnp.float32), w_down.astype(jnp.float32), down_bias.astype(jnp.float32))

    def one_sequence(totals, scanned):
        seq_tokens, seq_cot, segment, random_ids, global_ids = scanned

        def forward(weights_now, tokens_now):
            return sequence_forward(weights_now, tokens_now, segment, random_ids, global_ids)
        seq_out, pullback = jax.vjp(forward, params, seq_tokens.astype(jnp.float32))
        grad_params, grad_tokens = pullback(seq_cot.astype(jnp.float32))
        totals = jax.tree.map(lambda first_sum, second_sum: first_sum + second_sum, totals, grad_params)
        return (totals, (seq_out.astype(jnp.bfloat16), grad_tokens))
    zero_grads = jax.tree.map(jnp.zeros_like, params)
    scanned = (jnp.moveaxis(tokens, 1, 0), jnp.moveaxis(cotangent, 1, 0), segment_ids.T, jnp.moveaxis(random_blocks, 1, 0), global_blocks.T)
    totals, (seq_outputs, seq_grads) = lax.scan(one_sequence, zero_grads, scanned)
    output = jnp.moveaxis(seq_outputs, 0, 1)
    input_grad = jnp.moveaxis(seq_grads, 0, 1)
    return (output, input_grad, totals[0], totals[1], totals[2], totals[3], totals[4], totals[5], totals[6], totals[7], totals[8], totals[9], totals[10], totals[11], totals[12])
```

```python
import jax
import jax.numpy as jnp
import numpy as np
from jax import lax
from jax.experimental import pallas as pl
from jax.experimental.pallas import tpu as pltpu
from jax.sharding import PartitionSpec as P

D = 1024
HEADS = 16
HD = 64
BLK = 64
RAND = 3
GLOB = 2


eps = 1e-05


def padded(x, sides, width):
    for axis, dim in sides:
        size, length = (lax.axis_size(axis), x.shape[dim])
        up = [(i, (i + 1) % size) for i in range(size - 1)]
        down = [(j, i) for i, j in up]
        last = lax.slice_in_dim(x, length - width, length, axis=dim)
        initial = lax.slice_in_dim(x, 0, width, axis=dim)
        before = lax.ppermute(last, axis, up)
        after = lax.ppermute(initial, axis, down)
        x = jnp.concatenate([before, x, after], axis=dim)
    return x


def layer_norm(values, gain_vec, shift_vec):
    row_mean = jnp.mean(values, axis=-1, keepdims=True)
    centred = values - row_mean
    spread = jnp.mean(centred * centred, axis=-1, keepdims=True)
    return centred * lax.rsqrt(spread + eps) * gain_vec + shift_vec


def gelu_tanh(values):
    return jax.nn.gelu(values, approximate=True)


def window_stack(extended, query_blocks):
    return jnp.stack(
        [extended[0:query_blocks], extended[1 : query_blocks + 1], extended[2 : query_blocks + 2]],
        axis=1,
    )


def pick_blocks(shard_rows, random_local, global_blocks):
    block_total = shard_rows.shape[0] // BLK
    seq_count = shard_rows.shape[1]
    numbers = jnp.arange(block_total, dtype=jnp.int32)
    random_hits = (random_local[..., None] == numbers).astype(jnp.bfloat16)
    global_hits = (global_blocks[..., None] == numbers).astype(jnp.bfloat16)
    blocks = shard_rows.reshape(block_total, BLK, seq_count, 2, HEADS, HD)
    picked_random = jnp.einsum(
        "ishjb,busxhd->ishjuxd", random_hits, blocks, preferred_element_type=jnp.float32
    )
    picked_global = jnp.einsum(
        "gsb,busc->gusc",
        global_hits,
        shard_rows.reshape(block_total, BLK, seq_count, 2 * D),
        preferred_element_type=jnp.float32,
    )
    return (picked_random, picked_global)


def key_products(left_side, window_kv, far_random, far_global, which_half):
    near_part = jnp.einsum(
        "itshd,iwushd->ishtwu",
        left_side,
        window_kv[:, :, :, :, which_half],
        preferred_element_type=jnp.float32,
    )
    far_part = jnp.einsum(
        "itshd,ishjud->ishtju",
        left_side,
        far_random[:, :, :, :, :, which_half],
        preferred_element_type=jnp.float32,
    )
    global_part = jnp.einsum(
        "itshd,gushd->ishtgu",
        left_side,
        far_global[:, :, :, which_half],
        preferred_element_type=jnp.float32,
    )
    lead_shape = near_part.shape[:4]
    return jnp.concatenate(
        [
            near_part.reshape(lead_shape + (-1,)),
            far_part.reshape(lead_shape + (-1,)),
            global_part.reshape(lead_shape + (-1,)),
        ],
        axis=-1,
    )


def split_slots(weights):
    lead_shape = weights.shape[:4]
    near_cut = 3 * BLK
    far_cut = (3 + RAND) * BLK
    near_part = weights[..., :near_cut].reshape(lead_shape + (3, BLK))
    far_part = weights[..., near_cut:far_cut].reshape(lead_shape + (RAND, BLK))
    global_part = weights[..., far_cut:].reshape(lead_shape + (GLOB, BLK))
    return (near_part, far_part, global_part)


def key_mix(weights, window_kv, far_random, far_global, which_half):
    near_part, far_part, global_part = split_slots(weights)
    mixed = jnp.einsum(
        "ishtwu,iwushd->itshd",
        near_part,
        window_kv[:, :, :, :, which_half],
        preferred_element_type=jnp.float32,
    )
    mixed = mixed + jnp.einsum(
        "ishtju,ishjud->itshd",
        far_part,
        far_random[:, :, :, :, :, which_half],
        preferred_element_type=jnp.float32,
    )
    mixed = mixed + jnp.einsum(
        "ishtgu,gushd->itshd",
        global_part,
        far_global[:, :, :, which_half],
        preferred_element_type=jnp.float32,
    )
    return mixed


def key_grads(weights, left_side):
    near_part, far_part, global_part = split_slots(weights)
    near_grad = jnp.einsum(
        "ishtwu,itshd->iwushd", near_part, left_side, preferred_element_type=jnp.float32
    )
    far_grad = jnp.einsum(
        "ishtju,itshd->ishjud", far_part, left_side, preferred_element_type=jnp.float32
    )
    global_grad = jnp.einsum(
        "ishtgu,itshd->gushd", global_part, left_side, preferred_element_type=jnp.float32
    )
    return (near_grad, far_grad, global_grad)


def per_device(
    tokens,
    ln1_gain,
    ln1_bias,
    w_qkv,
    q_bias,
    v_bias,
    w_out,
    out_bias,
    ln2_gain,
    ln2_bias,
    w_in,
    in_bias,
    w_down,
    down_bias,
    cotangent,
    segment_ids,
    random_blocks,
    global_blocks,
):
    row_count = tokens.shape[0]
    seq_count = tokens.shape[1]
    query_blocks = row_count // BLK
    seq_length = segment_ids.shape[0]
    device_now = lax.axis_index("seq")
    first_row = device_now * row_count
    score_scale = HD ** (-0.5)
    random_local = lax.dynamic_slice_in_dim(
        random_blocks, device_now * query_blocks, query_blocks, 0
    )
    inputs = tokens.astype(jnp.float32)
    normed_full, first_norm_back = jax.vjp(
        layer_norm, inputs, ln1_gain.astype(jnp.float32), ln1_bias.astype(jnp.float32)
    )
    normed = normed_full.astype(jnp.bfloat16)
    projected = jnp.einsum("rsd,de->rse", normed, w_qkv, preferred_element_type=jnp.float32)
    queries = (projected[:, :, :D] + q_bias.astype(jnp.float32)).astype(jnp.bfloat16)
    value_shift = jnp.concatenate([jnp.zeros((D,), jnp.float32), v_bias.astype(jnp.float32)])
    keyval = (projected[:, :, D:] + value_shift).astype(jnp.bfloat16)
    extended = padded(keyval, (("seq", 0),), BLK)
    window_kv = window_stack(
        extended.reshape(query_blocks + 2, BLK, seq_count, 2, HEADS, HD), query_blocks
    )
    picked = pick_blocks(
        lax.all_gather(keyval, "seq", axis=0, tiled=True), random_local, global_blocks
    )
    far_random = picked[0].astype(jnp.bfloat16)
    far_global = picked[1].astype(jnp.bfloat16).reshape(GLOB, BLK, seq_count, 2, HEADS, HD)
    query_segment = lax.dynamic_slice_in_dim(segment_ids, first_row, row_count, 0)
    query_segment = query_segment.reshape(query_blocks, BLK, seq_count).transpose(0, 2, 1)
    window_spots = first_row - BLK + jnp.arange(row_count + 2 * BLK, dtype=jnp.int32)
    inside_seq = (window_spots >= 0) & (window_spots < seq_length)
    near_segment = jnp.take(segment_ids, jnp.clip(window_spots, 0, seq_length - 1), axis=0)
    near_segment = jnp.where(inside_seq[:, None], near_segment, -1)
    near_segment = window_stack(
        near_segment.reshape(query_blocks + 2, BLK, seq_count), query_blocks
    )
    near_segment = near_segment.transpose(0, 3, 1, 2).reshape(query_blocks, seq_count, 1, 3 * BLK)
    segment_rows = segment_ids.T
    sequence_pick = jnp.arange(seq_count, dtype=jnp.int32)
    offsets = jnp.arange(BLK, dtype=jnp.int32)
    far_segment = segment_rows[
        sequence_pick[None, :, None, None, None], random_local[..., None] * BLK + offsets
    ]
    far_segment = far_segment.reshape(query_blocks, seq_count, HEADS, RAND * BLK)
    global_segment = segment_rows[
        sequence_pick[None, :, None], global_blocks[..., None] * BLK + offsets
    ]
    global_segment = global_segment.transpose(1, 0, 2).reshape(1, seq_count, 1, GLOB * BLK)
    key_segment = jnp.concatenate(
        [
            jnp.broadcast_to(near_segment, (query_blocks, seq_count, HEADS, 3 * BLK)),
            far_segment,
            jnp.broadcast_to(global_segment, (query_blocks, seq_count, HEADS, GLOB * BLK)),
        ],
        axis=-1,
    )
    allowed = key_segment[:, :, :, None, :] == query_segment[:, :, None, :, None]
    query_rows = queries.reshape(query_blocks, BLK, seq_count, HEADS, HD)
    scores = jnp.where(
        allowed, key_products(query_rows, window_kv, far_random, far_global, 0) * score_scale, -1e30
    )
    row_max = jnp.max(scores, axis=-1, keepdims=True)
    log_total = row_max + jnp.log(jnp.sum(jnp.exp(scores - row_max), axis=-1, keepdims=True))
    soft_full = jnp.exp(scores - log_total)
    attn_probs = soft_full.astype(jnp.bfloat16)
    context = (
        key_mix(attn_probs, window_kv, far_random, far_global, 1)
        .reshape(row_count, seq_count, D)
        .astype(jnp.bfloat16)
    )
    mid_stream = (
        inputs
        + jnp.einsum("rsd,de->rse", context, w_out, preferred_element_type=jnp.float32)
        + out_bias.astype(jnp.float32)
    )
    normed2_full, second_norm_back = jax.vjp(
        layer_norm, mid_stream, ln2_gain.astype(jnp.float32), ln2_bias.astype(jnp.float32)
    )
    normed2 = normed2_full.astype(jnp.bfloat16)
    pre_act = jnp.einsum(
        "rsd,df->rsf", normed2, w_in, preferred_element_type=jnp.float32
    ) + in_bias.astype(jnp.float32)
    hidden_full, gelu_back = jax.vjp(gelu_tanh, pre_act)
    hidden = hidden_full.astype(jnp.bfloat16)
    output = (
        mid_stream
        + jnp.einsum("rsf,fd->rsd", hidden, w_down, preferred_element_type=jnp.float32)
        + down_bias.astype(jnp.float32)
    ).astype(jnp.bfloat16)
    grad_out = cotangent.astype(jnp.float32)
    w_down_grad = jnp.einsum("rsf,rsd->fd", hidden, cotangent, preferred_element_type=jnp.float32)
    down_bias_grad = jnp.sum(grad_out, axis=(0, 1))
    pre_grad = gelu_back(
        jnp.einsum("rsd,fd->rsf", cotangent, w_down, preferred_element_type=jnp.float32)
    )[0].astype(jnp.bfloat16)
    w_in_grad = jnp.einsum("rsd,rsf->df", normed2, pre_grad, preferred_element_type=jnp.float32)
    in_bias_grad = jnp.sum(pre_grad.astype(jnp.float32), axis=(0, 1))
    mid_part, ln2_gain_grad, ln2_bias_grad = second_norm_back(
        jnp.einsum("rsf,df->rsd", pre_grad, w_in, preferred_element_type=jnp.float32)
    )
    mid_grad = grad_out + mid_part
    branch_grad = mid_grad.astype(jnp.bfloat16)
    w_out_grad = jnp.einsum("rsd,rse->de", context, branch_grad, preferred_element_type=jnp.float32)
    out_bias_grad = jnp.sum(branch_grad.astype(jnp.float32), axis=(0, 1))
    context_grad = jnp.einsum(
        "rse,de->rsd", branch_grad, w_out, preferred_element_type=jnp.float32
    ).astype(jnp.bfloat16)
    grad_rows = context_grad.reshape(query_blocks, BLK, seq_count, HEADS, HD)
    probs_grad = key_products(grad_rows, window_kv, far_random, far_global, 1)
    score_grad = (
        soft_full * (probs_grad - jnp.sum(soft_full * probs_grad, axis=-1, keepdims=True))
    ).astype(jnp.bfloat16)
    query_grad = (
        (key_mix(score_grad, window_kv, far_random, far_global, 0) * score_scale)
        .reshape(row_count, seq_count, D)
        .astype(jnp.bfloat16)
    )
    near_key, far_key, global_key = key_grads(score_grad, query_rows)
    near_value, far_value, global_value = key_grads(attn_probs, grad_rows)
    near_kv = jnp.stack([near_key * score_scale, near_value], axis=4)
    far_kv = jnp.stack([far_key * score_scale, far_value], axis=5)
    global_kv = jnp.stack([global_key * score_scale, global_value], axis=3).reshape(
        GLOB, BLK, seq_count, 2 * D
    )
    rest_pad = ((0, 0),) * 5
    extended_grad = (
        jnp.pad(near_kv[:, 0], ((0, 2),) + rest_pad)
        + jnp.pad(near_kv[:, 1], ((1, 1),) + rest_pad)
        + jnp.pad(near_kv[:, 2], ((2, 0),) + rest_pad)
    )
    extended_grad = extended_grad.reshape(row_count + 2 * BLK, seq_count, 2 * D)
    rim_grads = jnp.concatenate([extended_grad[:BLK], extended_grad[row_count + BLK :]], axis=0)
    returned = padded(rim_grads.astype(jnp.bfloat16), (("seq", 0),), BLK).astype(rim_grads.dtype)
    near_total = extended_grad[BLK : row_count + BLK]
    near_total = (
        near_total.at[:BLK].add(returned[:BLK]).at[row_count - BLK :].add(returned[3 * BLK :])
    )
    block_total = row_count * lax.axis_size("seq") // BLK
    numbers = jnp.arange(block_total, dtype=jnp.int32)
    random_hits = (random_local[..., None] == numbers).astype(jnp.float32)
    global_rows_hit = (global_blocks[..., None] == numbers).astype(jnp.float32)

    def far_sum(one_sequence):
        hits, kv, global_rows, global_sum = one_sequence
        random_term = jnp.einsum(
            "ihjb,ihjuxd->buxhd", hits, kv, precision=lax.Precision.HIGHEST
        )
        global_term = jnp.einsum(
            "gb,guc->buc", global_rows, global_sum, precision=lax.Precision.HIGHEST
        )
        flat = (block_total * BLK, 2 * D)
        return (random_term.reshape(flat) + global_term.reshape(flat)).astype(jnp.bfloat16)

    far_parts = lax.map(
        far_sum,
        (
            jnp.moveaxis(random_hits, 1, 0),
            jnp.moveaxis(far_kv, 1, 0),
            jnp.moveaxis(global_rows_hit, 1, 0),
            jnp.moveaxis(global_kv, 2, 0),
        ),
    )
    far_total = lax.psum_scatter(far_parts, "seq", scatter_dimension=1, tiled=True)
    far_total = jnp.moveaxis(far_total, 0, 1).astype(jnp.float32)
    keyval_grad = (near_total + far_total).astype(jnp.bfloat16)
    qkv_grad = jnp.concatenate([query_grad, keyval_grad], axis=-1)
    q_bias_grad = jnp.sum(query_grad.astype(jnp.float32), axis=(0, 1))
    v_bias_grad = jnp.sum(keyval_grad[:, :, D:].astype(jnp.float32), axis=(0, 1))
    w_qkv_grad = jnp.einsum("rsd,rse->de", normed, qkv_grad, preferred_element_type=jnp.float32)
    input_part, ln1_gain_grad, ln1_bias_grad = first_norm_back(
        jnp.einsum("rse,de->rsd", qkv_grad, w_qkv, preferred_element_type=jnp.float32)
    )
    input_grad = mid_grad + input_part
    summed = (
        lax.psum_scatter(ln1_gain_grad, ("batch", "seq"), scatter_dimension=0, tiled=True),
        lax.psum_scatter(ln1_bias_grad, ("batch", "seq"), scatter_dimension=0, tiled=True),
        lax.psum_scatter(w_qkv_grad, ("batch", "seq"), scatter_dimension=0, tiled=True),
        lax.psum_scatter(q_bias_grad, ("batch", "seq"), scatter_dimension=0, tiled=True),
        lax.psum_scatter(v_bias_grad, ("batch", "seq"), scatter_dimension=0, tiled=True),
        lax.psum_scatter(w_out_grad, ("batch", "seq"), scatter_dimension=0, tiled=True),
        lax.psum_scatter(out_bias_grad, ("batch", "seq"), scatter_dimension=0, tiled=True),
        lax.psum_scatter(ln2_gain_grad, ("batch", "seq"), scatter_dimension=0, tiled=True),
        lax.psum_scatter(ln2_bias_grad, ("batch", "seq"), scatter_dimension=0, tiled=True),
        lax.psum_scatter(w_in_grad, ("batch", "seq"), scatter_dimension=0, tiled=True),
        lax.psum_scatter(in_bias_grad, ("batch", "seq"), scatter_dimension=0, tiled=True),
        lax.psum_scatter(w_down_grad, ("batch", "seq"), scatter_dimension=0, tiled=True),
        lax.psum_scatter(down_bias_grad, ("batch", "seq"), scatter_dimension=0, tiled=True),
    )
    return (
        output,
        input_grad,
        summed[0],
        summed[1],
        summed[2],
        summed[3],
        summed[4],
        summed[5],
        summed[6],
        summed[7],
        summed[8],
        summed[9],
        summed[10],
        summed[11],
        summed[12],
    )


NEG = -1e30
LANES = 128
MESH_IDS = pl.DeviceIdType.MESH
VMEM_BYTES = 60 * 1024 * 1024
F32 = jnp.float32
BF16 = jnp.bfloat16
SEG_VALUES = 4


def flip(axis, x):
    return lax.ppermute(x, axis, [(0, 1), (1, 0)])


def three_parts(x):
    hi = x.astype(BF16)
    rest = x - hi.astype(F32)
    mid = rest.astype(BF16)
    low = (rest - mid.astype(F32)).astype(BF16)
    return hi, mid, low


def dot_nt(a, b):
    return lax.dot_general(a, b, (((1,), (1,)), ((), ())), preferred_element_type=F32)


def dot_nn(a, b):
    return lax.dot_general(a, b, (((1,), (0,)), ((), ())), preferred_element_type=F32)


def dot_tn(a, b):
    return lax.dot_general(a, b, (((0,), (0,)), ((), ())), preferred_element_type=F32)


def attend_forward(q, k, v, feat_q, feat_k, lse_lane, tile=256):
    length, width = q.shape
    pairs = width // LANES
    tiles = length // tile

    def body(q_ref, k_ref, v_ref, fq_ref, fk_ref, ctx_ref, qa_ref, ka_ref):
        @pl.when(pl.program_id(1) == 0)
        def _():
            low_half = lax.broadcasted_iota(jnp.int32, (length, LANES), 1) < HD
            keys = k_ref[...]
            feats = fk_ref[0]
            ka_ref[0] = jnp.where(low_half, keys, feats)
            ka_ref[1] = jnp.where(low_half, feats, keys)

        lane = lax.broadcasted_iota(jnp.int32, (tile, LANES), 1)
        low_half = lane < HD
        scaled = q_ref[...] * jnp.asarray(HD ** (-0.5), BF16)
        feats = fq_ref[...]
        results = []
        for parity in range(2):
            if parity == 0:
                rows = jnp.where(low_half, scaled, feats)
                first = HD + lse_lane
            else:
                rows = jnp.where(low_half, feats, scaled)
                first = lse_lane
            scores = dot_nt(rows, ka_ref[parity])
            top = jnp.max(scores, axis=-1, keepdims=True)
            weights = jnp.exp(scores - top)
            total = jnp.sum(weights, axis=-1, keepdims=True)
            mixed = dot_nn(weights.astype(BF16), v_ref[...])
            results.append(mixed / total)
            hi, mid, low = three_parts(-(top + jnp.log(total)))
            rows = jnp.where(lane == first, hi, rows)
            rows = jnp.where(lane == first + 1, mid, rows)
            rows = jnp.where(lane == first + 2, low, rows)
            qa_ref[parity] = rows
        ctx_ref[...] = jnp.where(low_half, results[0], results[1]).astype(BF16)

    return pl.pallas_call(
        body,
        grid=(pairs, tiles),
        out_shape=(
            jax.ShapeDtypeStruct((length, width), BF16),
            jax.ShapeDtypeStruct((2 * pairs, length, LANES), BF16),
        ),
        in_specs=[
            pl.BlockSpec((tile, LANES), lambda p, t: (t, p)),
            pl.BlockSpec((length, LANES), lambda p, t: (0, p)),
            pl.BlockSpec((length, LANES), lambda p, t: (0, p)),
            pl.BlockSpec((tile, LANES), lambda p, t: (t, 0)),
            pl.BlockSpec((1, length, LANES), lambda p, t: (p, 0, 0)),
        ],
        out_specs=(
            pl.BlockSpec((tile, LANES), lambda p, t: (t, p)),
            pl.BlockSpec((2, tile, LANES), lambda p, t: (p, t, 0)),
        ),
        scratch_shapes=[pltpu.VMEM((2, length, LANES), BF16)],
        compiler_params=pltpu.CompilerParams(vmem_limit_bytes=VMEM_BYTES),
        name="attend_forward",
    )(q, k, v, feat_q, feat_k)


def attend_backward(rows_aug, k, v, feat_k, ctx, ctx_grad, lse_lane, tile=256):
    length, width = k.shape
    pairs = width // LANES
    tiles = length // tile

    def body(qa_ref, k_ref, v_ref, fk_ref, ctx_ref, g_ref, dq_ref, dk_ref, dv_ref, ga_ref, acc_ref):
        step = pl.program_id(1)

        @pl.when(step == 0)
        def _():
            lane = lax.broadcasted_iota(jnp.int32, (length, LANES), 1)
            low_half = lane < HD
            grads = g_ref[...]
            prod = grads.astype(F32) * ctx_ref[...].astype(F32)
            for parity in range(2):
                mine = low_half if parity == 0 else jnp.logical_not(low_half)
                first = HD if parity == 0 else 0
                delta = -jnp.sum(jnp.where(mine, prod, 0.0), axis=-1, keepdims=True)
                hi, mid, low = three_parts(delta)
                rows = jnp.where(mine, grads, jnp.zeros_like(grads))
                rows = jnp.where(lane == first, hi, rows)
                rows = jnp.where(lane == first + 1, mid, rows)
                ga_ref[parity] = jnp.where(lane == first + 2, low, rows)
            acc_ref[...] = jnp.zeros_like(acc_ref)

        lane = lax.broadcasted_iota(jnp.int32, (tile, LANES), 1)
        low_half = lane < HD
        keys = k_ref[...]
        values = v_ref[...]
        feats = fk_ref[0]
        keys_t = keys.astype(F32).T.astype(BF16)
        dks, dvs = [], []
        for parity in range(2):
            first = HD if parity == 0 else 0
            mine = low_half if parity == 0 else jnp.logical_not(low_half)
            key_rows = jnp.where(mine, keys, feats)
            ones = jnp.where((lane >= first) & (lane < first + 3), 1.0, 0.0).astype(BF16)
            value_rows = jnp.where(mine, values, ones)
            probs = jnp.exp(dot_nt(key_rows, qa_ref[parity]))
            diff = dot_nt(value_rows, ga_ref[parity])
            score_grad = (probs * diff).astype(BF16)
            dvs.append(dot_nn(probs.astype(BF16), g_ref[...]))
            dks.append(dot_nn(score_grad, qa_ref[parity]))
            half = keys_t[parity * HD : (parity + 1) * HD]
            acc_ref[parity * HD : (parity + 1) * HD] += dot_nn(half, score_grad)
        dk_ref[...] = jnp.where(low_half, dks[0], dks[1]).astype(BF16)
        dv_ref[...] = jnp.where(low_half, dvs[0], dvs[1]).astype(BF16)

        @pl.when(step == tiles - 1)
        def _():
            dq_ref[...] = (acc_ref[...].T * HD ** (-0.5)).astype(BF16)

    slab = pl.BlockSpec((length, LANES), lambda p, t: (0, p))
    part = pl.BlockSpec((tile, LANES), lambda p, t: (t, p))
    shape = jax.ShapeDtypeStruct((length, width), BF16)
    return pl.pallas_call(
        body,
        grid=(pairs, tiles),
        out_shape=(shape, shape, shape),
        in_specs=[
            pl.BlockSpec((2, length, LANES), lambda p, t: (p, 0, 0)),
            part,
            part,
            pl.BlockSpec((1, tile, LANES), lambda p, t: (p, t, 0)),
            slab,
            slab,
        ],
        out_specs=(slab, part, part),
        scratch_shapes=[pltpu.VMEM((2, length, LANES), BF16), pltpu.VMEM((LANES, length), F32)],
        compiler_params=pltpu.CompilerParams(vmem_limit_bytes=VMEM_BYTES),
        name="attend_backward",
    )(rows_aug, k, v, feat_k, ctx, ctx_grad)


def feed_forward(n2, n2_t, cot, w_in, in_bias, w_down, chunk=256):
    rows = n2.shape[0]
    hidden_units = w_in.shape[1]
    steps = hidden_units // chunk
    root = (2.0 / np.pi) ** 0.5
    cube = 0.044715

    def body(n_ref, nt_ref, c_ref, wi_ref, b_ref, wd_ref, out_ref, dn_ref, gi_ref, gd_ref, gb_ref):
        step = pl.program_id(0)
        wi = wi_ref[...]
        wd = wd_ref[...]
        pre = dot_nn(n_ref[...], wi) + b_ref[...]
        square = pre * pre
        th = jnp.tanh(root * pre * (1.0 + cube * square))
        half_up = 0.5 * (1.0 + th)
        hidden = (pre * half_up).astype(BF16)
        slope = half_up + 0.5 * pre * (1.0 - th * th) * (root * (1.0 + 3.0 * cube * square))
        pre_grad_full = dot_nt(c_ref[...], wd) * slope
        pre_grad = pre_grad_full.astype(BF16)
        gb_ref[...] = jnp.sum(pre_grad.astype(F32), axis=0, keepdims=True)
        gd_ref[...] = dot_tn(hidden, c_ref[...]).astype(BF16)
        gi_ref[...] = dot_nn(nt_ref[...], pre_grad).astype(BF16)

        @pl.when(step == 0)
        def _():
            out_ref[...] = dot_nn(hidden, wd)
            dn_ref[...] = dot_nt(pre_grad, wi)

        @pl.when(step > 0)
        def _():
            out_ref[...] += dot_nn(hidden, wd)
            dn_ref[...] += dot_nt(pre_grad, wi)

    whole = pl.BlockSpec((rows, D), lambda j: (0, 0))
    return pl.pallas_call(
        body,
        grid=(steps,),
        out_shape=(
            jax.ShapeDtypeStruct((rows, D), F32),
            jax.ShapeDtypeStruct((rows, D), F32),
            jax.ShapeDtypeStruct((D, hidden_units), BF16),
            jax.ShapeDtypeStruct((hidden_units, D), BF16),
            jax.ShapeDtypeStruct((1, hidden_units), F32),
        ),
        in_specs=[
            whole,
            pl.BlockSpec((D, rows), lambda j: (0, 0)),
            whole,
            pl.BlockSpec((D, chunk), lambda j: (0, j)),
            pl.BlockSpec((1, chunk), lambda j: (0, j)),
            pl.BlockSpec((chunk, D), lambda j: (j, 0)),
        ],
        out_specs=(
            whole,
            whole,
            pl.BlockSpec((D, chunk), lambda j: (0, j)),
            pl.BlockSpec((chunk, D), lambda j: (j, 0)),
            pl.BlockSpec((1, chunk), lambda j: (0, j)),
        ),
        compiler_params=pltpu.CompilerParams(vmem_limit_bytes=VMEM_BYTES),
        name="feed_forward",
    )(n2, n2_t, cot, w_in, in_bias, w_down)


ORDERS = ((3, 2, 1, 0), (2, 3, 1, 0), (1, 3, 2, 0))


def my_bits():
    batch = lax.axis_index("batch")
    return (
        lax.div(batch, 4),
        lax.rem(lax.div(batch, 2), 2),
        lax.rem(batch, 2),
        lax.axis_index("half"),
    )


def device_across(bit):
    batch = lax.axis_index("batch")
    half = lax.axis_index("half")
    member = lax.axis_index("member")
    bits = my_bits()
    if bit == 3:
        return (batch, 1 - half, member)
    stride = (4, 2, 1)[bit]
    return (batch + stride * (1 - 2 * bits[bit]), half, member)


def pick(order, depth, first):
    left = sorted(order[depth:])
    at = left.index(order[depth])
    return tuple(slice(None) for _ in range(at)) + (first,)


def sum_over_chips(arrays, splits, collective):
    pieces = []
    for index, split in enumerate(splits):
        start = 0
        for order, size in zip(ORDERS, split):
            if size:
                pieces.append((index, start, size, order))
            start += size
    count = len(arrays)

    def body(*refs):
        ins, outs, scratch = refs[:count], refs[count : 2 * count], refs[2 * count :]
        send_sem, recv_sem = scratch[-2:]
        slots = scratch[:-2]
        bits = my_bits()
        barrier = pltpu.get_barrier_semaphore()
        for bit in range(4):
            pl.semaphore_signal(barrier, inc=1, device_id=device_across(bit), device_id_type=MESH_IDS)
        pl.semaphore_wait(barrier, 4)

        def source(piece, depth):
            index, start, size, _ = pieces[piece]
            if depth == 0:
                return ins[index].at[:, :, :, :, :, pl.ds(start, size)]
            return slots[piece * 4 + depth - 1]

        def copy(piece, depth):
            order = pieces[piece][3]
            bit = order[depth]
            return pltpu.make_async_remote_copy(
                src_ref=source(piece, depth).at[pick(order, depth, 1 - bits[bit])],
                dst_ref=slots[piece * 4 + depth],
                send_sem=send_sem.at[piece, depth],
                recv_sem=recv_sem.at[piece, depth],
                device_id=device_across(bit),
                device_id_type=MESH_IDS,
            )

        for piece in range(len(pieces)):
            copy(piece, 0).start()
        for depth in range(4):
            for piece in range(len(pieces)):
                index, start, size, order = pieces[piece]
                copy(piece, depth).wait_recv()
                mine = source(piece, depth).at[pick(order, depth, bits[order[depth]])]
                slot = slots[piece * 4 + depth]
                total = mine[...].astype(F32) + slot[...].astype(F32)
                if depth < 3:
                    slot[...] = total.astype(BF16)
                    copy(piece, depth + 1).start()
                else:
                    outs[index][:, pl.ds(start, size)] = total
        for depth in range(4):
            for piece in range(len(pieces)):
                copy(piece, depth).wait_send()

    slots = []
    for index, _, size, _ in pieces:
        rows = arrays[index].shape[1]
        for depth in range(4):
            slots.append(pltpu.VMEM((2,) * (3 - depth) + (rows, size), BF16))
    shaped = [a.reshape((2, 2, 2, 2) + a.shape[1:]) for a in arrays]
    return pl.pallas_call(
        body,
        out_shape=tuple(jax.ShapeDtypeStruct(a.shape[1:], F32) for a in arrays),
        in_specs=[pl.BlockSpec(memory_space=pltpu.VMEM)] * count,
        out_specs=tuple(pl.BlockSpec(memory_space=pltpu.VMEM) for _ in arrays),
        scratch_shapes=slots
        + [pltpu.SemaphoreType.DMA((len(pieces), 4)), pltpu.SemaphoreType.DMA((len(pieces), 4))],
        compiler_params=pltpu.CompilerParams(
            collective_id=collective, has_side_effects=True, vmem_limit_bytes=VMEM_BYTES
        ),
        name="sum_over_chips",
    )(*shaped)


def normalise(values):
    mean = jnp.mean(values, axis=-1, keepdims=True)
    centred = values - mean
    scale = lax.rsqrt(jnp.mean(centred * centred, axis=-1, keepdims=True) + eps)
    return centred * scale, scale


def normalise_back(unit, scale, grad):
    first = jnp.mean(grad, axis=-1, keepdims=True)
    second = jnp.mean(grad * unit, axis=-1, keepdims=True)
    return (grad - first - unit * second) * scale


def per_device_pair(
    tokens,
    ln1_gain,
    ln1_bias,
    w_qkv,
    q_bias,
    v_bias,
    w_out,
    out_bias,
    ln2_gain,
    ln2_bias,
    w_in,
    in_bias,
    w_down,
    down_bias,
    cotangent,
    segment_ids,
    random_blocks,
    global_blocks,
):
    rows = tokens.shape[0]
    own = 2 * rows
    length = segment_ids.shape[0]
    blocks = length // BLK
    half = lax.axis_index("half")
    member = lax.axis_index("member")
    mine_d = D // 2
    heads = HEADS // 2
    ff_half = w_in.shape[1] // 2
    chips = lax.axis_size("batch") * 2

    def gather_rows(x):
        kept = lax.dynamic_index_in_dim(x, half, 1, keepdims=False)
        sent = lax.dynamic_index_in_dim(x, 1 - half, 1, keepdims=False)
        held = jnp.concatenate([kept, flip("half", sent)], axis=0)
        return jnp.concatenate([held, flip("member", held)], axis=0)

    def return_rows(x):
        kept, other = x[:rows], flip("half", x[rows:])
        return jnp.where(
            half == 0, jnp.stack([kept, other], axis=1), jnp.stack([other, kept], axis=1)
        )

    seq_tokens = gather_rows(tokens)
    cot = gather_rows(cotangent)

    per_row = rows // BLK
    order = jnp.concatenate(
        [
            ((half + t) % 2 * 2 + (member + j) % 2) * per_row + jnp.arange(per_row, dtype=jnp.int32)
            for j in range(2)
            for t in range(2)
        ]
    )
    numbers = jnp.arange(blocks, dtype=jnp.int32)
    seq_random = lax.dynamic_index_in_dim(random_blocks, half, 1, keepdims=False)
    seq_random = lax.dynamic_slice_in_dim(seq_random, member * heads, heads, 1)
    seq_global = lax.dynamic_index_in_dim(global_blocks, half, 1, keepdims=False)
    seq_segment = lax.dynamic_index_in_dim(segment_ids, half, 1, keepdims=False).reshape(blocks, BLK)
    move = (order[:, None] == numbers).astype(F32)
    segment = jnp.sum(move[:, :, None] * seq_segment.astype(F32)[None], axis=1).reshape(length, 1)
    hits = jnp.sum((seq_random[..., None] == order).astype(F32), axis=2)
    near = (jnp.abs(numbers[:, None] - order) <= 1).astype(F32)
    far = jnp.sum((seq_global[:, None] == order).astype(F32), axis=0)
    times = hits + (near + far)[:, None, :]
    bias = jnp.where(times > 0, jnp.log(jnp.maximum(times, 1.0)), NEG).transpose(1, 2, 0)
    bias_hi = bias.astype(BF16)
    bias_lo = (bias - bias_hi.astype(F32)).astype(BF16)
    lse_lane = SEG_VALUES + 2 * blocks
    spare = HD - lse_lane - 3
    same = (segment == jnp.arange(SEG_VALUES, dtype=F32)).astype(BF16)
    spot = jnp.repeat(move, BLK, axis=0).astype(BF16)
    feat_q = jnp.concatenate(
        [(same - 1) * jnp.asarray(-NEG, BF16), spot, spot, jnp.zeros((length, 3 + spare), BF16)], axis=1
    )
    feat_q = jnp.concatenate([feat_q, feat_q], axis=1)
    by_block = jnp.concatenate(
        [bias_hi, bias_lo, jnp.ones((heads, blocks, 3), BF16), jnp.zeros((heads, blocks, spare), BF16)],
        axis=2,
    )
    feat_k = jnp.concatenate(
        [
            jnp.broadcast_to(same, (heads, length, SEG_VALUES)),
            jnp.broadcast_to(by_block[:, :, None], (heads, blocks, BLK, HD - SEG_VALUES)).reshape(
                heads, length, HD - SEG_VALUES
            ),
        ],
        axis=2,
    ).reshape(heads // 2, 2, length, HD)
    feat_k = jnp.concatenate([feat_k[:, 1], feat_k[:, 0]], axis=-1)

    def columns(w, part):
        return lax.dynamic_slice_in_dim(w, part * D + member * mine_d, mine_d, 1)

    w_q, w_k, w_v = (columns(w_qkv, part) for part in range(3))
    w_in_mine = lax.dynamic_index_in_dim(
        w_in.reshape(D, chips, 2, LANES), member, 2, keepdims=False
    ).reshape(D, ff_half)
    w_down_mine = lax.dynamic_index_in_dim(
        w_down.reshape(chips, 2, LANES, D), member, 1, keepdims=False
    ).reshape(ff_half, D)
    in_bias_mine = lax.dynamic_index_in_dim(
        in_bias.reshape(chips, 2, LANES), member, 1, keepdims=False
    ).reshape(1, ff_half)
    q_bias_mine = lax.dynamic_slice_in_dim(q_bias, member * mine_d, mine_d, 0)
    v_bias_mine = lax.dynamic_slice_in_dim(v_bias, member * mine_d, mine_d, 0)
    w_out_mine = lax.dynamic_slice_in_dim(w_out, member * mine_d, mine_d, 0)
    w_out_other = lax.dynamic_slice_in_dim(w_out, (1 - member) * mine_d, mine_d, 0)

    inputs = seq_tokens.astype(F32)
    unit1, scale1 = normalise(inputs)
    normed = (unit1 * ln1_gain.astype(F32) + ln1_bias.astype(F32)).astype(BF16)
    queries = (dot_nn(normed, w_q) + q_bias_mine.astype(F32)).astype(BF16)
    keys = dot_nn(normed, w_k).astype(BF16)
    values = (dot_nn(normed, w_v) + v_bias_mine.astype(F32)).astype(BF16)

    context, rows_aug = attend_forward(queries, keys, values, feat_q, feat_k, lse_lane)
    context_other = flip("member", context)
    context_other = jnp.concatenate([context_other[own:], context_other[:own]], axis=0)

    mid_stream = (
        inputs[:own]
        + dot_nn(context[:own], w_out_mine)
        + dot_nn(context_other[:own], w_out_other)
        + out_bias.astype(F32)
    )
    unit2, scale2 = normalise(mid_stream)
    n2_own = (unit2 * ln2_gain.astype(F32) + ln2_bias.astype(F32)).astype(BF16)
    n2 = jnp.concatenate([n2_own, flip("member", n2_own)], axis=0)

    out_part, n2_grad_part, g_in, g_down, in_bias_grad = feed_forward(
        n2, n2.T, cot, w_in_mine, in_bias_mine.astype(F32), w_down_mine
    )
    summed_in, summed_down = sum_over_chips(
        [g_in.reshape(chips, D // chips, ff_half), g_down.reshape(chips, LANES, D)],
        ((640, 640, 768), (384, 384, 256)),
        1,
    )
    output_own = (
        mid_stream
        + out_part[:own]
        + flip("member", out_part[own:].astype(BF16)).astype(F32)
        + down_bias.astype(F32)
    ).astype(BF16)
    output = return_rows(output_own)

    n2_grad = n2_grad_part[:own] + flip("member", n2_grad_part[own:].astype(BF16)).astype(F32)
    cot_own = cot[:own].astype(F32)
    ln2_gain_grad = jnp.sum(n2_grad * unit2, axis=0)
    ln2_bias_grad = jnp.sum(n2_grad, axis=0)
    mid_grad = cot_own + normalise_back(unit2, scale2, n2_grad * ln2_gain.astype(F32))
    branch_own = mid_grad.astype(BF16)
    branch = jnp.concatenate([branch_own, flip("member", branch_own)], axis=0)
    context_grad = dot_nt(branch, w_out_mine).astype(BF16)
    branch_columns = lax.dynamic_slice_in_dim(branch, member * mine_d, mine_d, 1)
    g_out_mine = dot_tn(context, branch_columns).astype(BF16)
    g_out_other = dot_tn(context_other, branch_columns).astype(BF16)
    g_out = jnp.where(
        member == 0,
        jnp.concatenate([g_out_mine, g_out_other], axis=0),
        jnp.concatenate([g_out_other, g_out_mine], axis=0),
    )

    dq, dk, dv = attend_backward(rows_aug, keys, values, feat_k, context, context_grad, lse_lane)

    normed_grad_part = dot_nt(dq, w_q) + dot_nt(dk, w_k) + dot_nt(dv, w_v)
    g_qkv = [dot_tn(normed, x).astype(BF16) for x in (dq, dk, dv)]
    normed_grad = normed_grad_part[:own] + flip("member", normed_grad_part[own:].astype(BF16)).astype(F32)
    unit1_own, scale1_own = unit1[:own], scale1[:own]
    ln1_gain_grad = jnp.sum(normed_grad * unit1_own, axis=0)
    ln1_bias_grad = jnp.sum(normed_grad, axis=0)
    input_grad_own = mid_grad + normalise_back(unit1_own, scale1_own, normed_grad * ln1_gain.astype(F32))
    input_grad = return_rows(input_grad_own)

    def placed(x):
        full = jnp.zeros((D,), F32)
        return lax.dynamic_update_slice_in_dim(full, x, member * mine_d, 0)

    in_bias_rows = in_bias_grad.reshape(chips, 2, LANES // 2).transpose(1, 0, 2).reshape(2, D)
    gone = jnp.zeros_like(in_bias_rows)
    vectors = jnp.stack(
        [
            ln1_gain_grad,
            ln1_bias_grad,
            jnp.sum(branch_own.astype(F32), axis=0),
            ln2_gain_grad,
            ln2_bias_grad,
            jnp.sum(cot_own, axis=0),
            placed(jnp.sum(dq.astype(F32), axis=0)),
            placed(jnp.sum(dv.astype(F32), axis=0)),
        ]
    )
    vectors = jnp.concatenate(
        [
            vectors,
            jnp.where(member == 0, in_bias_rows, gone),
            jnp.where(member == 1, in_bias_rows, gone),
            jnp.zeros((LANES - 12, D), F32),
        ]
    ).T.astype(BF16)
    g_tail = jnp.concatenate(g_qkv + [g_out, vectors], axis=1)
    (summed_tail,) = sum_over_chips(
        [g_tail.reshape(chips, D // chips, g_tail.shape[1])], ((768, 768, 640),), 2
    )

    chip_rows = jnp.concatenate([summed_tail, summed_in], axis=1)
    per = chip_rows.shape[0] // 2
    mine_rows = lax.dynamic_slice_in_dim(chip_rows, member * per, per, 0)
    other_rows = lax.dynamic_slice_in_dim(chip_rows, (1 - member) * per, per, 0)
    got_rows = flip("member", other_rows)
    left = jnp.where(member == 0, mine_rows, got_rows)
    right = jnp.where(member == 0, got_rows, mine_rows)

    def both(start, size):
        return jnp.concatenate([left[:, start : start + size], right[:, start : start + size]], axis=1)

    w_qkv_grad = jnp.concatenate([both(part * mine_d, mine_d) for part in range(3)], axis=1)
    w_out_grad = both(3 * mine_d, mine_d)
    start = 4 * mine_d
    vector_sums = left[:, start : start + LANES] + right[:, start : start + LANES]
    start += LANES
    w_in_grad = jnp.concatenate(
        [
            x[:, start + j * LANES : start + (j + 1) * LANES]
            for j in range(chips)
            for x in (left, right)
        ],
        axis=1,
    )
    in_mine = lax.dynamic_slice_in_dim(summed_tail, 4 * mine_d + 8 + 2 * member, 2, 1)
    in_bias_out = in_mine.T.reshape(LANES)
    vec = [vector_sums[:, i] for i in range(8)]
    return (
        output,
        input_grad,
        vec[0],
        vec[1],
        w_qkv_grad,
        vec[6],
        vec[7],
        w_out_grad,
        vec[2],
        vec[3],
        vec[4],
        w_in_grad,
        in_bias_out,
        summed_down,
        vec[5],
    )


def solution(mesh):
    def program(*args):
        sequences = args[0].shape[1] // mesh.shape["batch"]
        seq = mesh.shape["seq"]
        fast = sequences == 2 and seq == 4 and mesh.shape["batch"] == 8
        if fast:
            use = jax.sharding.Mesh(
                mesh.devices.reshape(mesh.shape["batch"], 2, 2), ("batch", "half", "member")
            )
            seq_axes, all_axes, run = ("half", "member"), ("batch", "half", "member"), per_device_pair
        else:
            use, seq_axes, all_axes, run = mesh, "seq", ("batch", "seq"), per_device
        rows = P(seq_axes, "batch", None)
        in_specs = (rows,) + (P(),) * 13 + (
            rows,
            P(None, "batch"),
            P(None, "batch", None, None),
            P(None, "batch"),
        )
        vector, matrix = P(all_axes), P(all_axes, None)
        out_specs = (
            rows,
            rows,
            vector,
            vector,
            matrix,
            vector,
            vector,
            matrix,
            vector,
            vector,
            vector,
            matrix,
            vector,
            matrix,
            vector,
        )
        return jax.shard_map(
            run, mesh=use, in_specs=in_specs, out_specs=out_specs, check_vma=False
        )(*args)

    return program
```

```python
import jax
import jax.numpy as jnp
import numpy as np
from jax import lax
from jax.experimental import pallas as pl
from jax.experimental.pallas import tpu as pltpu
from jax.sharding import PartitionSpec as P

D = 1024
HEADS = 16
HD = 64
BLK = 64
RAND = 3
GLOB = 2


eps = 1e-05


def padded(x, sides, width):
    for axis, dim in sides:
        size, length = (lax.axis_size(axis), x.shape[dim])
        up = [(i, (i + 1) % size) for i in range(size - 1)]
        down = [(j, i) for i, j in up]
        last = lax.slice_in_dim(x, length - width, length, axis=dim)
        initial = lax.slice_in_dim(x, 0, width, axis=dim)
        before = lax.ppermute(last, axis, up)
        after = lax.ppermute(initial, axis, down)
        x = jnp.concatenate([before, x, after], axis=dim)
    return x


def layer_norm(values, gain_vec, shift_vec):
    row_mean = jnp.mean(values, axis=-1, keepdims=True)
    centred = values - row_mean
    spread = jnp.mean(centred * centred, axis=-1, keepdims=True)
    return centred * lax.rsqrt(spread + eps) * gain_vec + shift_vec


def gelu_tanh(values):
    return jax.nn.gelu(values, approximate=True)


def window_stack(extended, query_blocks):
    return jnp.stack(
        [extended[0:query_blocks], extended[1 : query_blocks + 1], extended[2 : query_blocks + 2]],
        axis=1,
    )


def pick_blocks(shard_rows, random_local, global_blocks):
    block_total = shard_rows.shape[0] // BLK
    seq_count = shard_rows.shape[1]
    numbers = jnp.arange(block_total, dtype=jnp.int32)
    random_hits = (random_local[..., None] == numbers).astype(jnp.bfloat16)
    global_hits = (global_blocks[..., None] == numbers).astype(jnp.bfloat16)
    blocks = shard_rows.reshape(block_total, BLK, seq_count, 2, HEADS, HD)
    picked_random = jnp.einsum(
        "ishjb,busxhd->ishjuxd", random_hits, blocks, preferred_element_type=jnp.float32
    )
    picked_global = jnp.einsum(
        "gsb,busc->gusc",
        global_hits,
        shard_rows.reshape(block_total, BLK, seq_count, 2 * D),
        preferred_element_type=jnp.float32,
    )
    return (picked_random, picked_global)


def key_products(left_side, window_kv, far_random, far_global, which_half):
    near_part = jnp.einsum(
        "itshd,iwushd->ishtwu",
        left_side,
        window_kv[:, :, :, :, which_half],
        preferred_element_type=jnp.float32,
    )
    far_part = jnp.einsum(
        "itshd,ishjud->ishtju",
        left_side,
        far_random[:, :, :, :, :, which_half],
        preferred_element_type=jnp.float32,
    )
    global_part = jnp.einsum(
        "itshd,gushd->ishtgu",
        left_side,
        far_global[:, :, :, which_half],
        preferred_element_type=jnp.float32,
    )
    lead_shape = near_part.shape[:4]
    return jnp.concatenate(
        [
            near_part.reshape(lead_shape + (-1,)),
            far_part.reshape(lead_shape + (-1,)),
            global_part.reshape(lead_shape + (-1,)),
        ],
        axis=-1,
    )


def split_slots(weights):
    lead_shape = weights.shape[:4]
    near_cut = 3 * BLK
    far_cut = (3 + RAND) * BLK
    near_part = weights[..., :near_cut].reshape(lead_shape + (3, BLK))
    far_part = weights[..., near_cut:far_cut].reshape(lead_shape + (RAND, BLK))
    global_part = weights[..., far_cut:].reshape(lead_shape + (GLOB, BLK))
    return (near_part, far_part, global_part)


def key_mix(weights, window_kv, far_random, far_global, which_half):
    near_part, far_part, global_part = split_slots(weights)
    mixed = jnp.einsum(
        "ishtwu,iwushd->itshd",
        near_part,
        window_kv[:, :, :, :, which_half],
        preferred_element_type=jnp.float32,
    )
    mixed = mixed + jnp.einsum(
        "ishtju,ishjud->itshd",
        far_part,
        far_random[:, :, :, :, :, which_half],
        preferred_element_type=jnp.float32,
    )
    mixed = mixed + jnp.einsum(
        "ishtgu,gushd->itshd",
        global_part,
        far_global[:, :, :, which_half],
        preferred_element_type=jnp.float32,
    )
    return mixed


def key_grads(weights, left_side):
    near_part, far_part, global_part = split_slots(weights)
    near_grad = jnp.einsum(
        "ishtwu,itshd->iwushd", near_part, left_side, preferred_element_type=jnp.float32
    )
    far_grad = jnp.einsum(
        "ishtju,itshd->ishjud", far_part, left_side, preferred_element_type=jnp.float32
    )
    global_grad = jnp.einsum(
        "ishtgu,itshd->gushd", global_part, left_side, preferred_element_type=jnp.float32
    )
    return (near_grad, far_grad, global_grad)


def per_device(
    tokens,
    ln1_gain,
    ln1_bias,
    w_qkv,
    q_bias,
    v_bias,
    w_out,
    out_bias,
    ln2_gain,
    ln2_bias,
    w_in,
    in_bias,
    w_down,
    down_bias,
    cotangent,
    segment_ids,
    random_blocks,
    global_blocks,
):
    row_count = tokens.shape[0]
    seq_count = tokens.shape[1]
    query_blocks = row_count // BLK
    seq_length = segment_ids.shape[0]
    device_now = lax.axis_index("seq")
    first_row = device_now * row_count
    score_scale = HD ** (-0.5)
    random_local = lax.dynamic_slice_in_dim(
        random_blocks, device_now * query_blocks, query_blocks, 0
    )
    inputs = tokens.astype(jnp.float32)
    normed_full, first_norm_back = jax.vjp(
        layer_norm, inputs, ln1_gain.astype(jnp.float32), ln1_bias.astype(jnp.float32)
    )
    normed = normed_full.astype(jnp.bfloat16)
    projected = jnp.einsum("rsd,de->rse", normed, w_qkv, preferred_element_type=jnp.float32)
    queries = (projected[:, :, :D] + q_bias.astype(jnp.float32)).astype(jnp.bfloat16)
    value_shift = jnp.concatenate([jnp.zeros((D,), jnp.float32), v_bias.astype(jnp.float32)])
    keyval = (projected[:, :, D:] + value_shift).astype(jnp.bfloat16)
    extended = padded(keyval, (("seq", 0),), BLK)
    window_kv = window_stack(
        extended.reshape(query_blocks + 2, BLK, seq_count, 2, HEADS, HD), query_blocks
    )
    picked = pick_blocks(
        lax.all_gather(keyval, "seq", axis=0, tiled=True), random_local, global_blocks
    )
    far_random = picked[0].astype(jnp.bfloat16)
    far_global = picked[1].astype(jnp.bfloat16).reshape(GLOB, BLK, seq_count, 2, HEADS, HD)
    query_segment = lax.dynamic_slice_in_dim(segment_ids, first_row, row_count, 0)
    query_segment = query_segment.reshape(query_blocks, BLK, seq_count).transpose(0, 2, 1)
    window_spots = first_row - BLK + jnp.arange(row_count + 2 * BLK, dtype=jnp.int32)
    inside_seq = (window_spots >= 0) & (window_spots < seq_length)
    near_segment = jnp.take(segment_ids, jnp.clip(window_spots, 0, seq_length - 1), axis=0)
    near_segment = jnp.where(inside_seq[:, None], near_segment, -1)
    near_segment = window_stack(
        near_segment.reshape(query_blocks + 2, BLK, seq_count), query_blocks
    )
    near_segment = near_segment.transpose(0, 3, 1, 2).reshape(query_blocks, seq_count, 1, 3 * BLK)
    segment_rows = segment_ids.T
    sequence_pick = jnp.arange(seq_count, dtype=jnp.int32)
    offsets = jnp.arange(BLK, dtype=jnp.int32)
    far_segment = segment_rows[
        sequence_pick[None, :, None, None, None], random_local[..., None] * BLK + offsets
    ]
    far_segment = far_segment.reshape(query_blocks, seq_count, HEADS, RAND * BLK)
    global_segment = segment_rows[
        sequence_pick[None, :, None], global_blocks[..., None] * BLK + offsets
    ]
    global_segment = global_segment.transpose(1, 0, 2).reshape(1, seq_count, 1, GLOB * BLK)
    key_segment = jnp.concatenate(
        [
            jnp.broadcast_to(near_segment, (query_blocks, seq_count, HEADS, 3 * BLK)),
            far_segment,
            jnp.broadcast_to(global_segment, (query_blocks, seq_count, HEADS, GLOB * BLK)),
        ],
        axis=-1,
    )
    allowed = key_segment[:, :, :, None, :] == query_segment[:, :, None, :, None]
    query_rows = queries.reshape(query_blocks, BLK, seq_count, HEADS, HD)
    scores = jnp.where(
        allowed, key_products(query_rows, window_kv, far_random, far_global, 0) * score_scale, -1e30
    )
    row_max = jnp.max(scores, axis=-1, keepdims=True)
    log_total = row_max + jnp.log(jnp.sum(jnp.exp(scores - row_max), axis=-1, keepdims=True))
    soft_full = jnp.exp(scores - log_total)
    attn_probs = soft_full.astype(jnp.bfloat16)
    context = (
        key_mix(attn_probs, window_kv, far_random, far_global, 1)
        .reshape(row_count, seq_count, D)
        .astype(jnp.bfloat16)
    )
    mid_stream = (
        inputs
        + jnp.einsum("rsd,de->rse", context, w_out, preferred_element_type=jnp.float32)
        + out_bias.astype(jnp.float32)
    )
    normed2_full, second_norm_back = jax.vjp(
        layer_norm, mid_stream, ln2_gain.astype(jnp.float32), ln2_bias.astype(jnp.float32)
    )
    normed2 = normed2_full.astype(jnp.bfloat16)
    pre_act = jnp.einsum(
        "rsd,df->rsf", normed2, w_in, preferred_element_type=jnp.float32
    ) + in_bias.astype(jnp.float32)
    hidden_full, gelu_back = jax.vjp(gelu_tanh, pre_act)
    hidden = hidden_full.astype(jnp.bfloat16)
    output = (
        mid_stream
        + jnp.einsum("rsf,fd->rsd", hidden, w_down, preferred_element_type=jnp.float32)
        + down_bias.astype(jnp.float32)
    ).astype(jnp.bfloat16)
    grad_out = cotangent.astype(jnp.float32)
    w_down_grad = jnp.einsum("rsf,rsd->fd", hidden, cotangent, preferred_element_type=jnp.float32)
    down_bias_grad = jnp.sum(grad_out, axis=(0, 1))
    pre_grad = gelu_back(
        jnp.einsum("rsd,fd->rsf", cotangent, w_down, preferred_element_type=jnp.float32)
    )[0].astype(jnp.bfloat16)
    w_in_grad = jnp.einsum("rsd,rsf->df", normed2, pre_grad, preferred_element_type=jnp.float32)
    in_bias_grad = jnp.sum(pre_grad.astype(jnp.float32), axis=(0, 1))
    mid_part, ln2_gain_grad, ln2_bias_grad = second_norm_back(
        jnp.einsum("rsf,df->rsd", pre_grad, w_in, preferred_element_type=jnp.float32)
    )
    mid_grad = grad_out + mid_part
    branch_grad = mid_grad.astype(jnp.bfloat16)
    w_out_grad = jnp.einsum("rsd,rse->de", context, branch_grad, preferred_element_type=jnp.float32)
    out_bias_grad = jnp.sum(branch_grad.astype(jnp.float32), axis=(0, 1))
    context_grad = jnp.einsum(
        "rse,de->rsd", branch_grad, w_out, preferred_element_type=jnp.float32
    ).astype(jnp.bfloat16)
    grad_rows = context_grad.reshape(query_blocks, BLK, seq_count, HEADS, HD)
    probs_grad = key_products(grad_rows, window_kv, far_random, far_global, 1)
    score_grad = (
        soft_full * (probs_grad - jnp.sum(soft_full * probs_grad, axis=-1, keepdims=True))
    ).astype(jnp.bfloat16)
    query_grad = (
        (key_mix(score_grad, window_kv, far_random, far_global, 0) * score_scale)
        .reshape(row_count, seq_count, D)
        .astype(jnp.bfloat16)
    )
    near_key, far_key, global_key = key_grads(score_grad, query_rows)
    near_value, far_value, global_value = key_grads(attn_probs, grad_rows)
    near_kv = jnp.stack([near_key * score_scale, near_value], axis=4)
    far_kv = jnp.stack([far_key * score_scale, far_value], axis=5)
    global_kv = jnp.stack([global_key * score_scale, global_value], axis=3).reshape(
        GLOB, BLK, seq_count, 2 * D
    )
    rest_pad = ((0, 0),) * 5
    extended_grad = (
        jnp.pad(near_kv[:, 0], ((0, 2),) + rest_pad)
        + jnp.pad(near_kv[:, 1], ((1, 1),) + rest_pad)
        + jnp.pad(near_kv[:, 2], ((2, 0),) + rest_pad)
    )
    extended_grad = extended_grad.reshape(row_count + 2 * BLK, seq_count, 2 * D)
    rim_grads = jnp.concatenate([extended_grad[:BLK], extended_grad[row_count + BLK :]], axis=0)
    returned = padded(rim_grads.astype(jnp.bfloat16), (("seq", 0),), BLK).astype(rim_grads.dtype)
    near_total = extended_grad[BLK : row_count + BLK]
    near_total = (
        near_total.at[:BLK].add(returned[:BLK]).at[row_count - BLK :].add(returned[3 * BLK :])
    )
    block_total = row_count * lax.axis_size("seq") // BLK
    numbers = jnp.arange(block_total, dtype=jnp.int32)
    random_hits = (random_local[..., None] == numbers).astype(jnp.float32)
    global_rows_hit = (global_blocks[..., None] == numbers).astype(jnp.float32)

    def far_sum(one_sequence):
        hits, kv, global_rows, global_sum = one_sequence
        random_term = jnp.einsum(
            "ihjb,ihjuxd->buxhd", hits, kv, precision=lax.Precision.HIGHEST
        )
        global_term = jnp.einsum(
            "gb,guc->buc", global_rows, global_sum, precision=lax.Precision.HIGHEST
        )
        flat = (block_total * BLK, 2 * D)
        return (random_term.reshape(flat) + global_term.reshape(flat)).astype(jnp.bfloat16)

    far_parts = lax.map(
        far_sum,
        (
            jnp.moveaxis(random_hits, 1, 0),
            jnp.moveaxis(far_kv, 1, 0),
            jnp.moveaxis(global_rows_hit, 1, 0),
            jnp.moveaxis(global_kv, 2, 0),
        ),
    )
    far_total = lax.psum_scatter(far_parts, "seq", scatter_dimension=1, tiled=True)
    far_total = jnp.moveaxis(far_total, 0, 1).astype(jnp.float32)
    keyval_grad = (near_total + far_total).astype(jnp.bfloat16)
    qkv_grad = jnp.concatenate([query_grad, keyval_grad], axis=-1)
    q_bias_grad = jnp.sum(query_grad.astype(jnp.float32), axis=(0, 1))
    v_bias_grad = jnp.sum(keyval_grad[:, :, D:].astype(jnp.float32), axis=(0, 1))
    w_qkv_grad = jnp.einsum("rsd,rse->de", normed, qkv_grad, preferred_element_type=jnp.float32)
    input_part, ln1_gain_grad, ln1_bias_grad = first_norm_back(
        jnp.einsum("rse,de->rsd", qkv_grad, w_qkv, preferred_element_type=jnp.float32)
    )
    input_grad = mid_grad + input_part
    summed = (
        lax.psum_scatter(ln1_gain_grad, ("batch", "seq"), scatter_dimension=0, tiled=True),
        lax.psum_scatter(ln1_bias_grad, ("batch", "seq"), scatter_dimension=0, tiled=True),
        lax.psum_scatter(w_qkv_grad, ("batch", "seq"), scatter_dimension=0, tiled=True),
        lax.psum_scatter(q_bias_grad, ("batch", "seq"), scatter_dimension=0, tiled=True),
        lax.psum_scatter(v_bias_grad, ("batch", "seq"), scatter_dimension=0, tiled=True),
        lax.psum_scatter(w_out_grad, ("batch", "seq"), scatter_dimension=0, tiled=True),
        lax.psum_scatter(out_bias_grad, ("batch", "seq"), scatter_dimension=0, tiled=True),
        lax.psum_scatter(ln2_gain_grad, ("batch", "seq"), scatter_dimension=0, tiled=True),
        lax.psum_scatter(ln2_bias_grad, ("batch", "seq"), scatter_dimension=0, tiled=True),
        lax.psum_scatter(w_in_grad, ("batch", "seq"), scatter_dimension=0, tiled=True),
        lax.psum_scatter(in_bias_grad, ("batch", "seq"), scatter_dimension=0, tiled=True),
        lax.psum_scatter(w_down_grad, ("batch", "seq"), scatter_dimension=0, tiled=True),
        lax.psum_scatter(down_bias_grad, ("batch", "seq"), scatter_dimension=0, tiled=True),
    )
    return (
        output,
        input_grad,
        summed[0],
        summed[1],
        summed[2],
        summed[3],
        summed[4],
        summed[5],
        summed[6],
        summed[7],
        summed[8],
        summed[9],
        summed[10],
        summed[11],
        summed[12],
    )


NEG = -1e30
LANES = 128
MESH_IDS = pl.DeviceIdType.MESH
VMEM_BYTES = 60 * 1024 * 1024
F32 = jnp.float32
BF16 = jnp.bfloat16
SEG_VALUES = 4


def flip(axis, x):
    return lax.ppermute(x, axis, [(0, 1), (1, 0)])


def three_parts(x):
    hi = x.astype(BF16)
    rest = x - hi.astype(F32)
    mid = rest.astype(BF16)
    low = (rest - mid.astype(F32)).astype(BF16)
    return hi, mid, low


def dot_nt(a, b):
    return lax.dot_general(a, b, (((1,), (1,)), ((), ())), preferred_element_type=F32)


def dot_nn(a, b):
    return lax.dot_general(a, b, (((1,), (0,)), ((), ())), preferred_element_type=F32)


def dot_tn(a, b):
    return lax.dot_general(a, b, (((0,), (0,)), ((), ())), preferred_element_type=F32)


def attend_forward(q, k, v, segment, block_of, bias, tile=256):
    length, width = q.shape
    pairs = width // LANES
    tiles = length // tile
    blocks = bias.shape[1]

    def body(q_ref, k_ref, v_ref, seg_ref, blk_ref, bias_ref, ctx_ref, qa_ref, fk_ref, fq_ref, ka_ref):
        first_tile = pl.program_id(1) == 0
        numbers = lax.broadcasted_iota(jnp.int32, (8, length), 0).astype(F32)
        same = seg_ref[...] == numbers

        @pl.when(first_tile & (pl.program_id(0) == 0))
        def _():
            count = lax.broadcasted_iota(jnp.int32, (blocks, length), 0).astype(F32)
            here = jnp.where(blk_ref[...] == count, 1.0, 0.0)
            rest = jnp.zeros((HD - 8 - 2 * blocks, length), F32)
            apart = jnp.where(same | (numbers >= SEG_VALUES), 0.0, NEG)
            feats = jnp.concatenate([apart, here, here, rest], axis=0)
            fq_ref[...] = jnp.concatenate([feats, feats], axis=0).T.astype(BF16)

        @pl.when(first_tile)
        def _():
            rest = jnp.zeros((HD - 16 - 2 * blocks, length), F32)
            ones = jnp.where(numbers < 3, 1.0, 0.0)
            sides = []
            for parity in (1, 0):
                full = bias_ref[parity]
                high = full.astype(BF16).astype(F32)
                sides += [jnp.where(same, 1.0, 0.0), high, full - high, ones, rest]
            feats = jnp.concatenate(sides, axis=0).T.astype(BF16)
            fk_ref[0] = feats
            low_half = lax.broadcasted_iota(jnp.int32, (length, LANES), 1) < HD
            keys = k_ref[...]
            ka_ref[0] = jnp.where(low_half, keys, feats)
            ka_ref[1] = jnp.where(low_half, feats, keys)

        lane = lax.broadcasted_iota(jnp.int32, (tile, LANES), 1)
        low_half = lane < HD
        scaled = q_ref[...] * jnp.asarray(HD ** (-0.5), BF16)
        start = pl.multiple_of(pl.program_id(1) * tile, tile)
        feats = fq_ref[pl.ds(start, tile), :]
        results = []
        for parity in range(2):
            if parity == 0:
                rows = jnp.where(low_half, scaled, feats)
                first = HD + 8 + 2 * blocks
            else:
                rows = jnp.where(low_half, feats, scaled)
                first = 8 + 2 * blocks
            scores = dot_nt(rows, ka_ref[parity])
            top = jnp.max(scores, axis=-1, keepdims=True)
            weights = jnp.exp(scores - top)
            total = jnp.sum(weights, axis=-1, keepdims=True)
            mixed = dot_nn(weights.astype(BF16), v_ref[...])
            results.append(mixed / total)
            hi, mid, low = three_parts(-(top + jnp.log(total)))
            rows = jnp.where(lane == first, hi, rows)
            rows = jnp.where(lane == first + 1, mid, rows)
            rows = jnp.where(lane == first + 2, low, rows)
            qa_ref[parity] = rows
        ctx_ref[...] = jnp.where(low_half, results[0], results[1]).astype(BF16)

    return pl.pallas_call(
        body,
        grid=(pairs, tiles),
        out_shape=(
            jax.ShapeDtypeStruct((length, width), BF16),
            jax.ShapeDtypeStruct((2 * pairs, length, LANES), BF16),
            jax.ShapeDtypeStruct((pairs, length, LANES), BF16),
        ),
        in_specs=[
            pl.BlockSpec((tile, LANES), lambda p, t: (t, p)),
            pl.BlockSpec((length, LANES), lambda p, t: (0, p)),
            pl.BlockSpec((length, LANES), lambda p, t: (0, p)),
            pl.BlockSpec((1, length), lambda p, t: (0, 0)),
            pl.BlockSpec((1, length), lambda p, t: (0, 0)),
            pl.BlockSpec((2, blocks, length), lambda p, t: (p, 0, 0)),
        ],
        out_specs=(
            pl.BlockSpec((tile, LANES), lambda p, t: (t, p)),
            pl.BlockSpec((2, tile, LANES), lambda p, t: (p, t, 0)),
            pl.BlockSpec((1, length, LANES), lambda p, t: (p, 0, 0)),
        ),
        scratch_shapes=[pltpu.VMEM((length, LANES), BF16), pltpu.VMEM((2, length, LANES), BF16)],
        compiler_params=pltpu.CompilerParams(vmem_limit_bytes=VMEM_BYTES),
        name="attend_forward",
    )(q, k, v, segment, block_of, bias)


def attend_backward(rows_aug, k, v, feat_k, ctx, ctx_grad, tile=256):
    length, width = k.shape
    pairs = width // LANES
    tiles = length // tile

    def body(qa_ref, k_ref, v_ref, fk_ref, ctx_ref, g_ref, dq_ref, dk_ref, dv_ref, ga_ref, acc_ref):
        step = pl.program_id(1)

        @pl.when(step == 0)
        def _():
            lane = lax.broadcasted_iota(jnp.int32, (length, LANES), 1)
            low_half = lane < HD
            grads = g_ref[...]
            prod = grads.astype(F32) * ctx_ref[...].astype(F32)
            for parity in range(2):
                mine = low_half if parity == 0 else jnp.logical_not(low_half)
                first = HD if parity == 0 else 0
                delta = -jnp.sum(jnp.where(mine, prod, 0.0), axis=-1, keepdims=True)
                hi, mid, low = three_parts(delta)
                rows = jnp.where(mine, grads, jnp.zeros_like(grads))
                rows = jnp.where(lane == first, hi, rows)
                rows = jnp.where(lane == first + 1, mid, rows)
                ga_ref[parity] = jnp.where(lane == first + 2, low, rows)
            acc_ref[...] = jnp.zeros_like(acc_ref)

        lane = lax.broadcasted_iota(jnp.int32, (tile, LANES), 1)
        low_half = lane < HD
        keys = k_ref[...]
        values = v_ref[...]
        feats = fk_ref[0]
        keys_t = keys.astype(F32).T.astype(BF16)
        dks, dvs = [], []
        for parity in range(2):
            first = HD if parity == 0 else 0
            mine = low_half if parity == 0 else jnp.logical_not(low_half)
            key_rows = jnp.where(mine, keys, feats)
            ones = jnp.where((lane >= first) & (lane < first + 3), 1.0, 0.0).astype(BF16)
            value_rows = jnp.where(mine, values, ones)
            probs = jnp.exp(dot_nt(key_rows, qa_ref[parity]))
            diff = dot_nt(value_rows, ga_ref[parity])
            score_grad = (probs * diff).astype(BF16)
            dvs.append(dot_nn(probs.astype(BF16), g_ref[...]))
            dks.append(dot_nn(score_grad, qa_ref[parity]))
            half = keys_t[parity * HD : (parity + 1) * HD]
            acc_ref[parity * HD : (parity + 1) * HD] += dot_nn(half, score_grad)
        dk_ref[...] = jnp.where(low_half, dks[0], dks[1]).astype(BF16)
        dv_ref[...] = jnp.where(low_half, dvs[0], dvs[1]).astype(BF16)

        @pl.when(step == tiles - 1)
        def _():
            dq_ref[...] = (acc_ref[...].T * HD ** (-0.5)).astype(BF16)

    slab = pl.BlockSpec((length, LANES), lambda p, t: (0, p))
    part = pl.BlockSpec((tile, LANES), lambda p, t: (t, p))
    shape = jax.ShapeDtypeStruct((length, width), BF16)
    return pl.pallas_call(
        body,
        grid=(pairs, tiles),
        out_shape=(shape, shape, shape),
        in_specs=[
            pl.BlockSpec((2, length, LANES), lambda p, t: (p, 0, 0)),
            part,
            part,
            pl.BlockSpec((1, tile, LANES), lambda p, t: (p, t, 0)),
            slab,
            slab,
        ],
        out_specs=(slab, part, part),
        scratch_shapes=[pltpu.VMEM((2, length, LANES), BF16), pltpu.VMEM((LANES, length), F32)],
        compiler_params=pltpu.CompilerParams(vmem_limit_bytes=VMEM_BYTES),
        name="attend_backward",
    )(rows_aug, k, v, feat_k, ctx, ctx_grad)


ORDERS = ((3, 2, 1, 0), (2, 3, 1, 0), (1, 3, 2, 0))


def my_bits():
    batch = lax.axis_index("batch")
    return (
        lax.div(batch, 4),
        lax.rem(lax.div(batch, 2), 2),
        lax.rem(batch, 2),
        lax.axis_index("half"),
    )


def device_across(bit):
    batch = lax.axis_index("batch")
    half = lax.axis_index("half")
    member = lax.axis_index("member")
    bits = my_bits()
    if bit == 3:
        return (batch, 1 - half, member)
    stride = (4, 2, 1)[bit]
    return (batch + stride * (1 - 2 * bits[bit]), half, member)


def pick(order, depth, first):
    left = sorted(order[depth:])
    at = left.index(order[depth])
    return tuple(slice(None) for _ in range(at)) + (first,)


def sum_over_chips(arrays, splits, collective):
    pieces = []
    for index, split in enumerate(splits):
        start = 0
        for order, size in zip(ORDERS, split):
            if size:
                pieces.append((index, start, size, order))
            start += size
    count = len(arrays)

    def body(*refs):
        ins, outs, scratch = refs[:count], refs[count : 2 * count], refs[2 * count :]
        send_sem, recv_sem = scratch[-2:]
        slots = scratch[:-2]
        bits = my_bits()
        barrier = pltpu.get_barrier_semaphore()
        for bit in range(4):
            pl.semaphore_signal(barrier, inc=1, device_id=device_across(bit), device_id_type=MESH_IDS)
        pl.semaphore_wait(barrier, 4)

        def source(piece, depth):
            index, start, size, _ = pieces[piece]
            if depth == 0:
                return ins[index].at[:, :, :, :, :, pl.ds(start, size)]
            return slots[piece * 4 + depth - 1]

        def copy(piece, depth):
            order = pieces[piece][3]
            bit = order[depth]
            return pltpu.make_async_remote_copy(
                src_ref=source(piece, depth).at[pick(order, depth, 1 - bits[bit])],
                dst_ref=slots[piece * 4 + depth],
                send_sem=send_sem.at[piece, depth],
                recv_sem=recv_sem.at[piece, depth],
                device_id=device_across(bit),
                device_id_type=MESH_IDS,
            )

        for piece in range(len(pieces)):
            copy(piece, 0).start()
        for depth in range(4):
            for piece in range(len(pieces)):
                index, start, size, order = pieces[piece]
                copy(piece, depth).wait_recv()
                mine = source(piece, depth).at[pick(order, depth, bits[order[depth]])]
                slot = slots[piece * 4 + depth]
                total = mine[...].astype(F32) + slot[...].astype(F32)
                if depth < 3:
                    slot[...] = total.astype(BF16)
                    copy(piece, depth + 1).start()
                else:
                    outs[index][:, pl.ds(start, size)] = total
        for depth in range(4):
            for piece in range(len(pieces)):
                copy(piece, depth).wait_send()

    slots = []
    for index, _, size, _ in pieces:
        rows = arrays[index].shape[1]
        for depth in range(4):
            slots.append(pltpu.VMEM((2,) * (3 - depth) + (rows, size), BF16))
    shaped = [a.reshape((2, 2, 2, 2) + a.shape[1:]) for a in arrays]
    return pl.pallas_call(
        body,
        out_shape=tuple(jax.ShapeDtypeStruct(a.shape[1:], F32) for a in arrays),
        in_specs=[pl.BlockSpec(memory_space=pltpu.VMEM)] * count,
        out_specs=tuple(pl.BlockSpec(memory_space=pltpu.VMEM) for _ in arrays),
        scratch_shapes=slots
        + [pltpu.SemaphoreType.DMA((len(pieces), 4)), pltpu.SemaphoreType.DMA((len(pieces), 4))],
        compiler_params=pltpu.CompilerParams(
            collective_id=collective, has_side_effects=True, vmem_limit_bytes=VMEM_BYTES
        ),
        name="sum_over_chips",
    )(*shaped)


IN_CUTS = ((0, 16), (16, 16), (32, 32))
DOWN_CUTS = ((0, 384), (384, 384), (768, 256))


def remote(src, dst, send, recv, bit):
    return pltpu.make_async_remote_copy(
        src_ref=src,
        dst_ref=dst,
        send_sem=send,
        recv_sem=recv,
        device_id=device_across(bit),
        device_id_type=MESH_IDS,
    )


def greet(bits):
    barrier = pltpu.get_barrier_semaphore()
    for bit in bits:
        pl.semaphore_signal(barrier, inc=1, device_id=device_across(bit), device_id_type=MESH_IDS)
    pl.semaphore_wait(barrier, len(bits))


def feed_forward(n2, cot, w_in, in_bias, w_down):
    rows = n2.shape[0]
    chunk = 2 * LANES
    hidden_units = w_in.shape[1] // 2
    steps = hidden_units // chunk
    root = (2.0 / np.pi) ** 0.5
    cube = 0.044715

    def body(*refs):
        n_ref, c_ref, wi0_ref, wi1_ref, b0_ref, b1_ref, wd0_ref, wd1_ref = refs[:8]
        out_ref, dn_ref, gb_ref = refs[8:11]
        keep, got = refs[11:17], refs[17:23]
        nt_ref, gi_ref, gd_ref, send_sem, recv_sem, keep_sem = refs[23:]
        step = pl.program_id(0)
        bits = my_bits()

        @pl.when(step == 0)
        def _():
            greet((1, 2, 3))
            nt_ref[...] = n_ref[...].astype(F32).T.astype(BF16)

        wi = jnp.concatenate([wi0_ref[...], wi1_ref[...]], axis=1)
        wd = jnp.concatenate([wd0_ref[...], wd1_ref[...]], axis=0)
        pre = dot_nn(n_ref[...], wi) + jnp.concatenate([b0_ref[...], b1_ref[...]], axis=1)
        square = pre * pre
        th = jnp.tanh(root * pre * (1.0 + cube * square))
        half_up = 0.5 * (1.0 + th)
        hidden = (pre * half_up).astype(BF16)
        slope = half_up + 0.5 * pre * (1.0 - th * th) * (root * (1.0 + 3.0 * cube * square))
        pre_grad = (dot_nt(c_ref[...], wd) * slope).astype(BF16)
        gb_ref[...] = jnp.sum(pre_grad.astype(F32), axis=0, keepdims=True)
        gd_ref[step] = dot_tn(hidden, c_ref[...]).astype(BF16).reshape(2, LANES, D)
        gi_ref[step] = dot_nn(nt_ref[...], pre_grad).astype(BF16).reshape(2, 2, 2, 2, D // 16, chunk)

        def moves(kind, at):
            if kind < 3:
                first, size = IN_CUTS[kind]
                bit = (3, 2, 1)[kind]
                lead = {3: (slice(None),) * 3, 2: (slice(None),) * 2, 1: (slice(None),)}[bit]
                return lambda side: gi_ref.at[(at,) + lead + (side,)].at[
                    (slice(None),) * 3 + (pl.ds(first, size),)
                ], at, bit
            first, size = DOWN_CUTS[kind - 3]
            cols = pl.ds(first, size)
            if kind == 3:
                return lambda side: gd_ref.at[at, side, :, cols], at, 3
            if kind == 4:
                return lambda side: gd_ref.at[2 * at + side, :, :, cols], at, 2
            return lambda side: gd_ref.at[pl.ds(4 * at + 2 * side, 2), :, :, cols], at, 1

        def go(kind, at):
            where, slot, bit = moves(kind, at)
            pltpu.make_async_copy(where(bits[bit]), keep[kind].at[slot], keep_sem.at[kind, slot]).start()
            remote(
                where(1 - bits[bit]),
                got[kind].at[slot],
                send_sem.at[kind, slot],
                recv_sem.at[kind, slot],
                bit,
            ).start()

        for kind in range(4):
            go(kind, step)

        @pl.when(lax.rem(step, 2) == 1)
        def _():
            go(4, lax.div(step, 2))

        @pl.when(lax.rem(step, 4) == 3)
        def _():
            go(5, lax.div(step, 4))

        @pl.when(step == 0)
        def _():
            out_ref[...] = dot_nn(hidden, wd)
            dn_ref[...] = dot_nt(pre_grad, wi)

        @pl.when(step > 0)
        def _():
            out_ref[...] += dot_nn(hidden, wd)
            dn_ref[...] += dot_nt(pre_grad, wi)

        @pl.when(step == steps - 1)
        def _():
            for kind in range(6):
                for at in range((steps, steps, steps, steps, steps // 2, steps // 4)[kind]):
                    where, slot, bit = moves(kind, at)
                    pltpu.make_async_copy(
                        where(bits[bit]), keep[kind].at[slot], keep_sem.at[kind, slot]
                    ).wait()
                    remote(
                        where(1 - bits[bit]),
                        got[kind].at[slot],
                        send_sem.at[kind, slot],
                        recv_sem.at[kind, slot],
                        bit,
                    ).wait()

    def unit(which):
        return lambda j: (0, 4 * j + 2 * which + lax.axis_index("member"))

    def unit_rows(which):
        return lambda j: (4 * j + 2 * which + lax.axis_index("member"), 0)

    whole = pl.BlockSpec((rows, D), lambda j: (0, 0))
    anywhere = pl.BlockSpec(memory_space=pl.ANY)
    parts = [jax.ShapeDtypeStruct((steps, 2, 2, 2, size, chunk), BF16) for _, size in IN_CUTS] + [
        jax.ShapeDtypeStruct((steps, LANES, DOWN_CUTS[0][1]), BF16),
        jax.ShapeDtypeStruct((steps // 2, 2, LANES, DOWN_CUTS[1][1]), BF16),
        jax.ShapeDtypeStruct((steps // 4, 2, 2, LANES, DOWN_CUTS[2][1]), BF16),
    ]
    results = pl.pallas_call(
        body,
        grid=(steps,),
        out_shape=[
            jax.ShapeDtypeStruct((rows, D), F32),
            jax.ShapeDtypeStruct((rows, D), F32),
            jax.ShapeDtypeStruct((1, hidden_units), F32),
        ]
        + parts
        + parts,
        in_specs=[
            whole,
            whole,
            pl.BlockSpec((D, LANES), unit(0)),
            pl.BlockSpec((D, LANES), unit(1)),
            pl.BlockSpec((1, LANES), unit(0)),
            pl.BlockSpec((1, LANES), unit(1)),
            pl.BlockSpec((LANES, D), unit_rows(0)),
            pl.BlockSpec((LANES, D), unit_rows(1)),
        ],
        out_specs=[whole, whole, pl.BlockSpec((1, chunk), lambda j: (0, j))] + [anywhere] * 12,
        scratch_shapes=[
            pltpu.VMEM((D, rows), BF16),
            pltpu.VMEM((steps, 2, 2, 2, 2, D // 16, chunk), BF16),
            pltpu.VMEM((steps, 2, LANES, D), BF16),
            pltpu.SemaphoreType.DMA((6, steps)),
            pltpu.SemaphoreType.DMA((6, steps)),
            pltpu.SemaphoreType.DMA((6, steps)),
        ],
        compiler_params=pltpu.CompilerParams(
            collective_id=1, has_side_effects=True, vmem_limit_bytes=VMEM_BYTES
        ),
        name="feed_forward",
    )(n2, cot, w_in, w_in, in_bias, in_bias, w_down, w_down)
    return results[:3], results[3:9], results[9:]


LATER = ((2, 1, 0), (1, 3, 0), (3, 2, 0))


def finish_sums(kept, got):
    steps = kept[0].shape[0]
    chunk = kept[0].shape[-1]
    shapes = [a.shape for a in kept[:3]] + [
        (1, 2, 2, 2, LANES, a.shape[-1]) for a in kept[3:]
    ]
    kept = [a.reshape(shape) for a, shape in zip(kept, shapes)]
    got = [a.reshape(shape) for a, shape in zip(got, shapes)]

    def body(*refs):
        keep, first, outs = refs[:6], refs[6:12], refs[12:14]
        begin, slots = refs[14:20], refs[20:-2]
        send_sem, recv_sem = refs[-2:]
        bits = my_bits()
        greet((0, 1, 2, 3))

        def held(kind, depth):
            return begin[kind] if depth == 0 else slots[kind * 3 + depth - 1]

        def side(kind, depth, value):
            order = LATER[kind % 3]
            return held(kind, depth).at[(slice(None),) + pick(order, depth, value)]

        def copy(kind, depth):
            bit = LATER[kind % 3][depth]
            return remote(
                side(kind, depth, 1 - bits[bit]),
                slots[kind * 3 + depth],
                send_sem.at[kind, depth],
                recv_sem.at[kind, depth],
                bit,
            )

        for kind in range(6):
            begin[kind][...] = (keep[kind][...].astype(F32) + first[kind][...].astype(F32)).astype(BF16)
            copy(kind, 0).start()
        for depth in range(3):
            for kind in range(6):
                copy(kind, depth).wait_recv()
                slot = slots[kind * 3 + depth]
                mine = side(kind, depth, bits[LATER[kind % 3][depth]])
                total = mine[...].astype(F32) + slot[...].astype(F32)
                if depth < 2:
                    slot[...] = total.astype(BF16)
                    copy(kind, depth + 1).start()
                elif kind < 3:
                    row, size = IN_CUTS[kind]
                    for j in range(steps):
                        outs[0][pl.ds(row, size), pl.ds(j * chunk, chunk)] = total[j]
                else:
                    col, size = DOWN_CUTS[kind - 3]
                    outs[1][:, pl.ds(col, size)] = total[0]
        for depth in range(3):
            for kind in range(6):
                copy(kind, depth).wait_send()

    slots = [pltpu.VMEM(shape, BF16) for shape in shapes]
    for shape in shapes:
        for depth in range(3):
            slots.append(pltpu.VMEM((shape[0],) + (2,) * (2 - depth) + shape[4:], BF16))
    in_vmem = pl.BlockSpec(memory_space=pltpu.VMEM)
    return pl.pallas_call(
        body,
        out_shape=(
            jax.ShapeDtypeStruct((D // 16, steps * chunk), F32),
            jax.ShapeDtypeStruct((LANES, D), F32),
        ),
        in_specs=[in_vmem] * 12,
        out_specs=(in_vmem, in_vmem),
        scratch_shapes=slots + [pltpu.SemaphoreType.DMA((6, 3)), pltpu.SemaphoreType.DMA((6, 3))],
        compiler_params=pltpu.CompilerParams(
            collective_id=3, has_side_effects=True, vmem_limit_bytes=VMEM_BYTES
        ),
        name="finish_sums",
    )(*kept, *got)


def normalise(values):
    mean = jnp.mean(values, axis=-1, keepdims=True)
    centred = values - mean
    scale = lax.rsqrt(jnp.mean(centred * centred, axis=-1, keepdims=True) + eps)
    return centred * scale, scale


def normalise_back(unit, scale, grad):
    first = jnp.mean(grad, axis=-1, keepdims=True)
    second = jnp.mean(grad * unit, axis=-1, keepdims=True)
    return (grad - first - unit * second) * scale


def per_device_pair(
    tokens,
    ln1_gain,
    ln1_bias,
    w_qkv,
    q_bias,
    v_bias,
    w_out,
    out_bias,
    ln2_gain,
    ln2_bias,
    w_in,
    in_bias,
    w_down,
    down_bias,
    cotangent,
    segment_ids,
    random_blocks,
    global_blocks,
):
    rows = tokens.shape[0]
    own = 2 * rows
    length = segment_ids.shape[0]
    blocks = length // BLK
    half = lax.axis_index("half")
    member = lax.axis_index("member")
    mine_d = D // 2
    heads = HEADS // 2
    chips = lax.axis_size("batch") * 2

    def gather_rows(x):
        kept = lax.dynamic_index_in_dim(x, half, 1, keepdims=False)
        sent = lax.dynamic_index_in_dim(x, 1 - half, 1, keepdims=False)
        held = jnp.concatenate([kept, flip("half", sent)], axis=0)
        return jnp.concatenate([held, flip("member", held)], axis=0)

    def return_rows(x):
        kept, other = x[:rows], flip("half", x[rows:].astype(BF16)).astype(x.dtype)
        return jnp.where(
            half == 0, jnp.stack([kept, other], axis=1), jnp.stack([other, kept], axis=1)
        )

    seq_tokens = gather_rows(tokens)
    later, _ = lax.optimization_barrier((cotangent, seq_tokens))
    cot = gather_rows(later)

    per_row = rows // BLK
    order = jnp.concatenate(
        [
            ((half + t) % 2 * 2 + (member + j) % 2) * per_row + jnp.arange(per_row, dtype=jnp.int32)
            for j in range(2)
            for t in range(2)
        ]
    )
    numbers = jnp.arange(blocks, dtype=jnp.int32)
    seq_random = lax.dynamic_index_in_dim(random_blocks, half, 1, keepdims=False)
    seq_random = lax.dynamic_slice_in_dim(seq_random, member * heads, heads, 1)
    seq_global = lax.dynamic_index_in_dim(global_blocks, half, 1, keepdims=False)
    seq_segment = lax.dynamic_index_in_dim(segment_ids, half, 1, keepdims=False).reshape(blocks, BLK)
    move = (order[:, None] == numbers).astype(F32)
    segment = jnp.sum(move[:, :, None] * seq_segment.astype(F32)[None], axis=1).reshape(1, length)
    block_of = jnp.broadcast_to(order.astype(F32)[:, None], (blocks, BLK)).reshape(1, length)
    hits = jnp.sum((seq_random[..., None] == order).astype(F32), axis=2)
    near = (jnp.abs(numbers[:, None] - order) <= 1).astype(F32)
    far = jnp.sum((seq_global[:, None] == order).astype(F32), axis=0)
    times = hits + (near + far)[:, None, :]
    bias = jnp.where(times > 0, jnp.log(jnp.maximum(times, 1.0)), NEG).transpose(1, 0, 2)
    bias = jnp.broadcast_to(bias[..., None], (heads, blocks, blocks, BLK)).reshape(heads, blocks, length)

    def columns(w, part):
        return lax.dynamic_slice_in_dim(w, part * D + member * mine_d, mine_d, 1)

    w_q, w_k, w_v = (columns(w_qkv, part) for part in range(3))
    q_bias_mine = lax.dynamic_slice_in_dim(q_bias, member * mine_d, mine_d, 0)
    v_bias_mine = lax.dynamic_slice_in_dim(v_bias, member * mine_d, mine_d, 0)
    w_out_mine = lax.dynamic_slice_in_dim(w_out, member * mine_d, mine_d, 0)
    w_out_other = lax.dynamic_slice_in_dim(w_out, (1 - member) * mine_d, mine_d, 0)

    inputs = seq_tokens.astype(F32)
    unit1, scale1 = normalise(inputs)
    normed = (unit1 * ln1_gain.astype(F32) + ln1_bias.astype(F32)).astype(BF16)
    queries = (dot_nn(normed, w_q) + q_bias_mine.astype(F32)).astype(BF16)
    keys = dot_nn(normed, w_k).astype(BF16)
    values = (dot_nn(normed, w_v) + v_bias_mine.astype(F32)).astype(BF16)

    context, rows_aug, feat_k = attend_forward(queries, keys, values, segment, block_of, bias)
    context_other = flip("member", context)
    context_other = jnp.concatenate([context_other[own:], context_other[:own]], axis=0)

    mid_stream = (
        inputs[:own]
        + dot_nn(context[:own], w_out_mine)
        + dot_nn(context_other[:own], w_out_other)
        + out_bias.astype(F32)
    )
    unit2, scale2 = normalise(mid_stream)
    n2_own = (unit2 * ln2_gain.astype(F32) + ln2_bias.astype(F32)).astype(BF16)
    n2 = jnp.concatenate([n2_own, flip("member", n2_own)], axis=0)

    (out_part, n2_grad_part, in_bias_grad), kept_parts, got_parts = feed_forward(
        n2, cot, w_in, in_bias.astype(F32).reshape(1, -1), w_down
    )
    summed_in, summed_down = finish_sums(kept_parts, got_parts)
    output_own = (
        mid_stream
        + out_part[:own]
        + flip("member", out_part[own:].astype(BF16)).astype(F32)
        + down_bias.astype(F32)
    ).astype(BF16)
    output = return_rows(output_own)

    n2_grad = n2_grad_part[:own] + flip("member", n2_grad_part[own:].astype(BF16)).astype(F32)
    cot_own = cot[:own].astype(F32)
    ln2_gain_grad = jnp.sum(n2_grad * unit2, axis=0)
    ln2_bias_grad = jnp.sum(n2_grad, axis=0)
    mid_grad = cot_own + normalise_back(unit2, scale2, n2_grad * ln2_gain.astype(F32))
    branch_own = mid_grad.astype(BF16)
    branch = jnp.concatenate([branch_own, flip("member", branch_own)], axis=0)
    context_grad = dot_nt(branch, w_out_mine).astype(BF16)
    branch_columns = lax.dynamic_slice_in_dim(branch, member * mine_d, mine_d, 1)
    g_out_mine = dot_tn(context, branch_columns).astype(BF16)
    g_out_other = dot_tn(context_other, branch_columns).astype(BF16)
    g_out = jnp.where(
        member == 0,
        jnp.concatenate([g_out_mine, g_out_other], axis=0),
        jnp.concatenate([g_out_other, g_out_mine], axis=0),
    )

    dq, dk, dv = attend_backward(rows_aug, keys, values, feat_k, context, context_grad)

    normed_grad_part = dot_nt(dq, w_q) + dot_nt(dk, w_k) + dot_nt(dv, w_v)
    g_qkv = [dot_tn(normed, x).astype(BF16) for x in (dq, dk, dv)]
    normed_grad = normed_grad_part[:own] + flip("member", normed_grad_part[own:].astype(BF16)).astype(F32)
    unit1_own, scale1_own = unit1[:own], scale1[:own]
    ln1_gain_grad = jnp.sum(normed_grad * unit1_own, axis=0)
    ln1_bias_grad = jnp.sum(normed_grad, axis=0)
    input_grad_own = mid_grad + normalise_back(unit1_own, scale1_own, normed_grad * ln1_gain.astype(F32))
    input_grad = return_rows(input_grad_own)

    def placed(x):
        full = jnp.zeros((D,), F32)
        return lax.dynamic_update_slice_in_dim(full, x, member * mine_d, 0)

    in_bias_rows = in_bias_grad.reshape(chips, 2, LANES // 2).transpose(1, 0, 2).reshape(2, D)
    gone = jnp.zeros_like(in_bias_rows)
    vectors = jnp.stack(
        [
            ln1_gain_grad,
            ln1_bias_grad,
            jnp.sum(branch_own.astype(F32), axis=0),
            ln2_gain_grad,
            ln2_bias_grad,
            jnp.sum(cot_own, axis=0),
            placed(jnp.sum(dq.astype(F32), axis=0)),
            placed(jnp.sum(dv.astype(F32), axis=0)),
        ]
    )
    vectors = jnp.concatenate(
        [
            vectors,
            jnp.where(member == 0, in_bias_rows, gone),
            jnp.where(member == 1, in_bias_rows, gone),
            jnp.zeros((LANES - 12, D), F32),
        ]
    ).T.astype(BF16)
    g_tail = jnp.concatenate(g_qkv + [g_out, vectors], axis=1)
    (summed_tail,) = sum_over_chips(
        [g_tail.reshape(chips, D // chips, g_tail.shape[1])], ((768, 768, 640),), 2
    )

    chip_rows = jnp.concatenate([summed_tail, summed_in], axis=1)
    per = chip_rows.shape[0] // 2
    mine_rows = lax.dynamic_slice_in_dim(chip_rows, member * per, per, 0)
    other_rows = lax.dynamic_slice_in_dim(chip_rows, (1 - member) * per, per, 0)
    got_rows = flip("member", other_rows)
    left = jnp.where(member == 0, mine_rows, got_rows)
    right = jnp.where(member == 0, got_rows, mine_rows)

    def both(start, size):
        return jnp.concatenate([left[:, start : start + size], right[:, start : start + size]], axis=1)

    w_qkv_grad = jnp.concatenate([both(part * mine_d, mine_d) for part in range(3)], axis=1)
    w_out_grad = both(3 * mine_d, mine_d)
    start = 4 * mine_d
    vector_sums = left[:, start : start + LANES] + right[:, start : start + LANES]
    start += LANES
    w_in_grad = jnp.concatenate(
        [
            x[:, start + j * LANES : start + (j + 1) * LANES]
            for j in range(chips)
            for x in (left, right)
        ],
        axis=1,
    )
    in_mine = lax.dynamic_slice_in_dim(summed_tail, 4 * mine_d + 8 + 2 * member, 2, 1)
    in_bias_out = in_mine.T.reshape(LANES)
    vec = [vector_sums[:, i] for i in range(8)]
    return (
        output,
        input_grad,
        vec[0],
        vec[1],
        w_qkv_grad,
        vec[6],
        vec[7],
        w_out_grad,
        vec[2],
        vec[3],
        vec[4],
        w_in_grad,
        in_bias_out,
        summed_down,
        vec[5],
    )


def solution(mesh):
    def program(*args):
        sequences = args[0].shape[1] // mesh.shape["batch"]
        seq = mesh.shape["seq"]
        fast = sequences == 2 and seq == 4 and mesh.shape["batch"] == 8
        if fast:
            use = jax.sharding.Mesh(
                mesh.devices.reshape(mesh.shape["batch"], 2, 2), ("batch", "half", "member")
            )
            seq_axes, all_axes, run = ("half", "member"), ("batch", "half", "member"), per_device_pair
        else:
            use, seq_axes, all_axes, run = mesh, "seq", ("batch", "seq"), per_device
        rows = P(seq_axes, "batch", None)
        in_specs = (rows,) + (P(),) * 13 + (
            rows,
            P(None, "batch"),
            P(None, "batch", None, None),
            P(None, "batch"),
        )
        vector, matrix = P(all_axes), P(all_axes, None)
        out_specs = (
            rows,
            rows,
            vector,
            vector,
            matrix,
            vector,
            vector,
            matrix,
            vector,
            vector,
            vector,
            matrix,
            vector,
            matrix,
            vector,
        )
        return jax.shard_map(
            run, mesh=use, in_specs=in_specs, out_specs=out_specs, check_vma=False
        )(*args)

    return program
```

```python
import jax
import jax.numpy as jnp
import numpy as np
from jax import lax
from jax.experimental import pallas as pl
from jax.experimental.pallas import tpu as pltpu
from jax.sharding import PartitionSpec as P

D = 1024
HEADS = 16
HD = 64
BLK = 64
RAND = 3
GLOB = 2


eps = 1e-05


def padded(x, sides, width):
    for axis, dim in sides:
        size, length = (lax.axis_size(axis), x.shape[dim])
        up = [(i, (i + 1) % size) for i in range(size - 1)]
        down = [(j, i) for i, j in up]
        last = lax.slice_in_dim(x, length - width, length, axis=dim)
        initial = lax.slice_in_dim(x, 0, width, axis=dim)
        before = lax.ppermute(last, axis, up)
        after = lax.ppermute(initial, axis, down)
        x = jnp.concatenate([before, x, after], axis=dim)
    return x


def layer_norm(values, gain_vec, shift_vec):
    row_mean = jnp.mean(values, axis=-1, keepdims=True)
    centred = values - row_mean
    spread = jnp.mean(centred * centred, axis=-1, keepdims=True)
    return centred * lax.rsqrt(spread + eps) * gain_vec + shift_vec


def gelu_tanh(values):
    return jax.nn.gelu(values, approximate=True)


def window_stack(extended, query_blocks):
    return jnp.stack(
        [extended[0:query_blocks], extended[1 : query_blocks + 1], extended[2 : query_blocks + 2]],
        axis=1,
    )


def pick_blocks(shard_rows, random_local, global_blocks):
    block_total = shard_rows.shape[0] // BLK
    seq_count = shard_rows.shape[1]
    numbers = jnp.arange(block_total, dtype=jnp.int32)
    random_hits = (random_local[..., None] == numbers).astype(jnp.bfloat16)
    global_hits = (global_blocks[..., None] == numbers).astype(jnp.bfloat16)
    blocks = shard_rows.reshape(block_total, BLK, seq_count, 2, HEADS, HD)
    picked_random = jnp.einsum(
        "ishjb,busxhd->ishjuxd", random_hits, blocks, preferred_element_type=jnp.float32
    )
    picked_global = jnp.einsum(
        "gsb,busc->gusc",
        global_hits,
        shard_rows.reshape(block_total, BLK, seq_count, 2 * D),
        preferred_element_type=jnp.float32,
    )
    return (picked_random, picked_global)


def key_products(left_side, window_kv, far_random, far_global, which_half):
    near_part = jnp.einsum(
        "itshd,iwushd->ishtwu",
        left_side,
        window_kv[:, :, :, :, which_half],
        preferred_element_type=jnp.float32,
    )
    far_part = jnp.einsum(
        "itshd,ishjud->ishtju",
        left_side,
        far_random[:, :, :, :, :, which_half],
        preferred_element_type=jnp.float32,
    )
    global_part = jnp.einsum(
        "itshd,gushd->ishtgu",
        left_side,
        far_global[:, :, :, which_half],
        preferred_element_type=jnp.float32,
    )
    lead_shape = near_part.shape[:4]
    return jnp.concatenate(
        [
            near_part.reshape(lead_shape + (-1,)),
            far_part.reshape(lead_shape + (-1,)),
            global_part.reshape(lead_shape + (-1,)),
        ],
        axis=-1,
    )


def split_slots(weights):
    lead_shape = weights.shape[:4]
    near_cut = 3 * BLK
    far_cut = (3 + RAND) * BLK
    near_part = weights[..., :near_cut].reshape(lead_shape + (3, BLK))
    far_part = weights[..., near_cut:far_cut].reshape(lead_shape + (RAND, BLK))
    global_part = weights[..., far_cut:].reshape(lead_shape + (GLOB, BLK))
    return (near_part, far_part, global_part)


def key_mix(weights, window_kv, far_random, far_global, which_half):
    near_part, far_part, global_part = split_slots(weights)
    mixed = jnp.einsum(
        "ishtwu,iwushd->itshd",
        near_part,
        window_kv[:, :, :, :, which_half],
        preferred_element_type=jnp.float32,
    )
    mixed = mixed + jnp.einsum(
        "ishtju,ishjud->itshd",
        far_part,
        far_random[:, :, :, :, :, which_half],
        preferred_element_type=jnp.float32,
    )
    mixed = mixed + jnp.einsum(
        "ishtgu,gushd->itshd",
        global_part,
        far_global[:, :, :, which_half],
        preferred_element_type=jnp.float32,
    )
    return mixed


def key_grads(weights, left_side):
    near_part, far_part, global_part = split_slots(weights)
    near_grad = jnp.einsum(
        "ishtwu,itshd->iwushd", near_part, left_side, preferred_element_type=jnp.float32
    )
    far_grad = jnp.einsum(
        "ishtju,itshd->ishjud", far_part, left_side, preferred_element_type=jnp.float32
    )
    global_grad = jnp.einsum(
        "ishtgu,itshd->gushd", global_part, left_side, preferred_element_type=jnp.float32
    )
    return (near_grad, far_grad, global_grad)


def per_device(
    tokens,
    ln1_gain,
    ln1_bias,
    w_qkv,
    q_bias,
    v_bias,
    w_out,
    out_bias,
    ln2_gain,
    ln2_bias,
    w_in,
    in_bias,
    w_down,
    down_bias,
    cotangent,
    segment_ids,
    random_blocks,
    global_blocks,
):
    row_count = tokens.shape[0]
    seq_count = tokens.shape[1]
    query_blocks = row_count // BLK
    seq_length = segment_ids.shape[0]
    device_now = lax.axis_index("seq")
    first_row = device_now * row_count
    score_scale = HD ** (-0.5)
    random_local = lax.dynamic_slice_in_dim(
        random_blocks, device_now * query_blocks, query_blocks, 0
    )
    inputs = tokens.astype(jnp.float32)
    normed_full, first_norm_back = jax.vjp(
        layer_norm, inputs, ln1_gain.astype(jnp.float32), ln1_bias.astype(jnp.float32)
    )
    normed = normed_full.astype(jnp.bfloat16)
    projected = jnp.einsum("rsd,de->rse", normed, w_qkv, preferred_element_type=jnp.float32)
    queries = (projected[:, :, :D] + q_bias.astype(jnp.float32)).astype(jnp.bfloat16)
    value_shift = jnp.concatenate([jnp.zeros((D,), jnp.float32), v_bias.astype(jnp.float32)])
    keyval = (projected[:, :, D:] + value_shift).astype(jnp.bfloat16)
    extended = padded(keyval, (("seq", 0),), BLK)
    window_kv = window_stack(
        extended.reshape(query_blocks + 2, BLK, seq_count, 2, HEADS, HD), query_blocks
    )
    picked = pick_blocks(
        lax.all_gather(keyval, "seq", axis=0, tiled=True), random_local, global_blocks
    )
    far_random = picked[0].astype(jnp.bfloat16)
    far_global = picked[1].astype(jnp.bfloat16).reshape(GLOB, BLK, seq_count, 2, HEADS, HD)
    query_segment = lax.dynamic_slice_in_dim(segment_ids, first_row, row_count, 0)
    query_segment = query_segment.reshape(query_blocks, BLK, seq_count).transpose(0, 2, 1)
    window_spots = first_row - BLK + jnp.arange(row_count + 2 * BLK, dtype=jnp.int32)
    inside_seq = (window_spots >= 0) & (window_spots < seq_length)
    near_segment = jnp.take(segment_ids, jnp.clip(window_spots, 0, seq_length - 1), axis=0)
    near_segment = jnp.where(inside_seq[:, None], near_segment, -1)
    near_segment = window_stack(
        near_segment.reshape(query_blocks + 2, BLK, seq_count), query_blocks
    )
    near_segment = near_segment.transpose(0, 3, 1, 2).reshape(query_blocks, seq_count, 1, 3 * BLK)
    segment_rows = segment_ids.T
    sequence_pick = jnp.arange(seq_count, dtype=jnp.int32)
    offsets = jnp.arange(BLK, dtype=jnp.int32)
    far_segment = segment_rows[
        sequence_pick[None, :, None, None, None], random_local[..., None] * BLK + offsets
    ]
    far_segment = far_segment.reshape(query_blocks, seq_count, HEADS, RAND * BLK)
    global_segment = segment_rows[
        sequence_pick[None, :, None], global_blocks[..., None] * BLK + offsets
    ]
    global_segment = global_segment.transpose(1, 0, 2).reshape(1, seq_count, 1, GLOB * BLK)
    key_segment = jnp.concatenate(
        [
            jnp.broadcast_to(near_segment, (query_blocks, seq_count, HEADS, 3 * BLK)),
            far_segment,
            jnp.broadcast_to(global_segment, (query_blocks, seq_count, HEADS, GLOB * BLK)),
        ],
        axis=-1,
    )
    allowed = key_segment[:, :, :, None, :] == query_segment[:, :, None, :, None]
    query_rows = queries.reshape(query_blocks, BLK, seq_count, HEADS, HD)
    scores = jnp.where(
        allowed, key_products(query_rows, window_kv, far_random, far_global, 0) * score_scale, -1e30
    )
    row_max = jnp.max(scores, axis=-1, keepdims=True)
    log_total = row_max + jnp.log(jnp.sum(jnp.exp(scores - row_max), axis=-1, keepdims=True))
    soft_full = jnp.exp(scores - log_total)
    attn_probs = soft_full.astype(jnp.bfloat16)
    context = (
        key_mix(attn_probs, window_kv, far_random, far_global, 1)
        .reshape(row_count, seq_count, D)
        .astype(jnp.bfloat16)
    )
    mid_stream = (
        inputs
        + jnp.einsum("rsd,de->rse", context, w_out, preferred_element_type=jnp.float32)
        + out_bias.astype(jnp.float32)
    )
    normed2_full, second_norm_back = jax.vjp(
        layer_norm, mid_stream, ln2_gain.astype(jnp.float32), ln2_bias.astype(jnp.float32)
    )
    normed2 = normed2_full.astype(jnp.bfloat16)
    pre_act = jnp.einsum(
        "rsd,df->rsf", normed2, w_in, preferred_element_type=jnp.float32
    ) + in_bias.astype(jnp.float32)
    hidden_full, gelu_back = jax.vjp(gelu_tanh, pre_act)
    hidden = hidden_full.astype(jnp.bfloat16)
    output = (
        mid_stream
        + jnp.einsum("rsf,fd->rsd", hidden, w_down, preferred_element_type=jnp.float32)
        + down_bias.astype(jnp.float32)
    ).astype(jnp.bfloat16)
    grad_out = cotangent.astype(jnp.float32)
    w_down_grad = jnp.einsum("rsf,rsd->fd", hidden, cotangent, preferred_element_type=jnp.float32)
    down_bias_grad = jnp.sum(grad_out, axis=(0, 1))
    pre_grad = gelu_back(
        jnp.einsum("rsd,fd->rsf", cotangent, w_down, preferred_element_type=jnp.float32)
    )[0].astype(jnp.bfloat16)
    w_in_grad = jnp.einsum("rsd,rsf->df", normed2, pre_grad, preferred_element_type=jnp.float32)
    in_bias_grad = jnp.sum(pre_grad.astype(jnp.float32), axis=(0, 1))
    mid_part, ln2_gain_grad, ln2_bias_grad = second_norm_back(
        jnp.einsum("rsf,df->rsd", pre_grad, w_in, preferred_element_type=jnp.float32)
    )
    mid_grad = grad_out + mid_part
    branch_grad = mid_grad.astype(jnp.bfloat16)
    w_out_grad = jnp.einsum("rsd,rse->de", context, branch_grad, preferred_element_type=jnp.float32)
    out_bias_grad = jnp.sum(branch_grad.astype(jnp.float32), axis=(0, 1))
    context_grad = jnp.einsum(
        "rse,de->rsd", branch_grad, w_out, preferred_element_type=jnp.float32
    ).astype(jnp.bfloat16)
    grad_rows = context_grad.reshape(query_blocks, BLK, seq_count, HEADS, HD)
    probs_grad = key_products(grad_rows, window_kv, far_random, far_global, 1)
    score_grad = (
        soft_full * (probs_grad - jnp.sum(soft_full * probs_grad, axis=-1, keepdims=True))
    ).astype(jnp.bfloat16)
    query_grad = (
        (key_mix(score_grad, window_kv, far_random, far_global, 0) * score_scale)
        .reshape(row_count, seq_count, D)
        .astype(jnp.bfloat16)
    )
    near_key, far_key, global_key = key_grads(score_grad, query_rows)
    near_value, far_value, global_value = key_grads(attn_probs, grad_rows)
    near_kv = jnp.stack([near_key * score_scale, near_value], axis=4)
    far_kv = jnp.stack([far_key * score_scale, far_value], axis=5)
    global_kv = jnp.stack([global_key * score_scale, global_value], axis=3).reshape(
        GLOB, BLK, seq_count, 2 * D
    )
    rest_pad = ((0, 0),) * 5
    extended_grad = (
        jnp.pad(near_kv[:, 0], ((0, 2),) + rest_pad)
        + jnp.pad(near_kv[:, 1], ((1, 1),) + rest_pad)
        + jnp.pad(near_kv[:, 2], ((2, 0),) + rest_pad)
    )
    extended_grad = extended_grad.reshape(row_count + 2 * BLK, seq_count, 2 * D)
    rim_grads = jnp.concatenate([extended_grad[:BLK], extended_grad[row_count + BLK :]], axis=0)
    returned = padded(rim_grads.astype(jnp.bfloat16), (("seq", 0),), BLK).astype(rim_grads.dtype)
    near_total = extended_grad[BLK : row_count + BLK]
    near_total = (
        near_total.at[:BLK].add(returned[:BLK]).at[row_count - BLK :].add(returned[3 * BLK :])
    )
    block_total = row_count * lax.axis_size("seq") // BLK
    numbers = jnp.arange(block_total, dtype=jnp.int32)
    random_hits = (random_local[..., None] == numbers).astype(jnp.float32)
    global_rows_hit = (global_blocks[..., None] == numbers).astype(jnp.float32)

    def far_sum(one_sequence):
        hits, kv, global_rows, global_sum = one_sequence
        random_term = jnp.einsum(
            "ihjb,ihjuxd->buxhd", hits, kv, precision=lax.Precision.HIGHEST
        )
        global_term = jnp.einsum(
            "gb,guc->buc", global_rows, global_sum, precision=lax.Precision.HIGHEST
        )
        flat = (block_total * BLK, 2 * D)
        return (random_term.reshape(flat) + global_term.reshape(flat)).astype(jnp.bfloat16)

    far_parts = lax.map(
        far_sum,
        (
            jnp.moveaxis(random_hits, 1, 0),
            jnp.moveaxis(far_kv, 1, 0),
            jnp.moveaxis(global_rows_hit, 1, 0),
            jnp.moveaxis(global_kv, 2, 0),
        ),
    )
    far_total = lax.psum_scatter(far_parts, "seq", scatter_dimension=1, tiled=True)
    far_total = jnp.moveaxis(far_total, 0, 1).astype(jnp.float32)
    keyval_grad = (near_total + far_total).astype(jnp.bfloat16)
    qkv_grad = jnp.concatenate([query_grad, keyval_grad], axis=-1)
    q_bias_grad = jnp.sum(query_grad.astype(jnp.float32), axis=(0, 1))
    v_bias_grad = jnp.sum(keyval_grad[:, :, D:].astype(jnp.float32), axis=(0, 1))
    w_qkv_grad = jnp.einsum("rsd,rse->de", normed, qkv_grad, preferred_element_type=jnp.float32)
    input_part, ln1_gain_grad, ln1_bias_grad = first_norm_back(
        jnp.einsum("rse,de->rsd", qkv_grad, w_qkv, preferred_element_type=jnp.float32)
    )
    input_grad = mid_grad + input_part
    summed = (
        lax.psum_scatter(ln1_gain_grad, ("batch", "seq"), scatter_dimension=0, tiled=True),
        lax.psum_scatter(ln1_bias_grad, ("batch", "seq"), scatter_dimension=0, tiled=True),
        lax.psum_scatter(w_qkv_grad, ("batch", "seq"), scatter_dimension=0, tiled=True),
        lax.psum_scatter(q_bias_grad, ("batch", "seq"), scatter_dimension=0, tiled=True),
        lax.psum_scatter(v_bias_grad, ("batch", "seq"), scatter_dimension=0, tiled=True),
        lax.psum_scatter(w_out_grad, ("batch", "seq"), scatter_dimension=0, tiled=True),
        lax.psum_scatter(out_bias_grad, ("batch", "seq"), scatter_dimension=0, tiled=True),
        lax.psum_scatter(ln2_gain_grad, ("batch", "seq"), scatter_dimension=0, tiled=True),
        lax.psum_scatter(ln2_bias_grad, ("batch", "seq"), scatter_dimension=0, tiled=True),
        lax.psum_scatter(w_in_grad, ("batch", "seq"), scatter_dimension=0, tiled=True),
        lax.psum_scatter(in_bias_grad, ("batch", "seq"), scatter_dimension=0, tiled=True),
        lax.psum_scatter(w_down_grad, ("batch", "seq"), scatter_dimension=0, tiled=True),
        lax.psum_scatter(down_bias_grad, ("batch", "seq"), scatter_dimension=0, tiled=True),
    )
    return (
        output,
        input_grad,
        summed[0],
        summed[1],
        summed[2],
        summed[3],
        summed[4],
        summed[5],
        summed[6],
        summed[7],
        summed[8],
        summed[9],
        summed[10],
        summed[11],
        summed[12],
    )


NEG = -1e30
LANES = 128
MESH_IDS = pl.DeviceIdType.MESH
VMEM_BYTES = 60 * 1024 * 1024
F32 = jnp.float32
BF16 = jnp.bfloat16
SEG_VALUES = 4


def flip(axis, x):
    return lax.ppermute(x, axis, [(0, 1), (1, 0)])


def three_parts(x):
    hi = x.astype(BF16)
    rest = x - hi.astype(F32)
    mid = rest.astype(BF16)
    low = (rest - mid.astype(F32)).astype(BF16)
    return hi, mid, low


def dot_nt(a, b):
    return lax.dot_general(a, b, (((1,), (1,)), ((), ())), preferred_element_type=F32)


def dot_nn(a, b):
    return lax.dot_general(a, b, (((1,), (0,)), ((), ())), preferred_element_type=F32)


def dot_tn(a, b):
    return lax.dot_general(a, b, (((0,), (0,)), ((), ())), preferred_element_type=F32)


def attend_forward(q, k, v, segment, block_of, bias, tile=256):
    length, width = q.shape
    pairs = width // LANES
    tiles = length // tile
    blocks = bias.shape[1]

    def body(q_ref, k_ref, v_ref, seg_ref, blk_ref, bias_ref, ctx_ref, qa_ref, fk_ref, fq_ref, ka_ref):
        first_tile = pl.program_id(1) == 0
        numbers = lax.broadcasted_iota(jnp.int32, (8, length), 0).astype(F32)
        same = seg_ref[...] == numbers

        @pl.when(first_tile & (pl.program_id(0) == 0))
        def _():
            count = lax.broadcasted_iota(jnp.int32, (blocks, length), 0).astype(F32)
            here = jnp.where(blk_ref[...] == count, 1.0, 0.0)
            rest = jnp.zeros((HD - 8 - 2 * blocks, length), F32)
            apart = jnp.where(same | (numbers >= SEG_VALUES), 0.0, NEG)
            feats = jnp.concatenate([apart, here, here, rest], axis=0)
            fq_ref[...] = jnp.concatenate([feats, feats], axis=0).T.astype(BF16)

        @pl.when(first_tile)
        def _():
            rest = jnp.zeros((HD - 16 - 2 * blocks, length), F32)
            ones = jnp.where(numbers < 3, 1.0, 0.0)
            sides = []
            for parity in (1, 0):
                full = bias_ref[parity]
                high = full.astype(BF16).astype(F32)
                sides += [jnp.where(same, 1.0, 0.0), high, full - high, ones, rest]
            feats = jnp.concatenate(sides, axis=0).T.astype(BF16)
            fk_ref[0] = feats
            low_half = lax.broadcasted_iota(jnp.int32, (length, LANES), 1) < HD
            keys = k_ref[...]
            ka_ref[0] = jnp.where(low_half, keys, feats)
            ka_ref[1] = jnp.where(low_half, feats, keys)

        lane = lax.broadcasted_iota(jnp.int32, (tile, LANES), 1)
        low_half = lane < HD
        scaled = q_ref[...] * jnp.asarray(HD ** (-0.5), BF16)
        start = pl.multiple_of(pl.program_id(1) * tile, tile)
        feats = fq_ref[pl.ds(start, tile), :]
        results = []
        for parity in range(2):
            if parity == 0:
                rows = jnp.where(low_half, scaled, feats)
                first = HD + 8 + 2 * blocks
            else:
                rows = jnp.where(low_half, feats, scaled)
                first = 8 + 2 * blocks
            scores = dot_nt(rows, ka_ref[parity])
            top = jnp.max(scores, axis=-1, keepdims=True)
            weights = jnp.exp(scores - top)
            total = jnp.sum(weights, axis=-1, keepdims=True)
            mixed = dot_nn(weights.astype(BF16), v_ref[...])
            results.append(mixed / total)
            hi, mid, low = three_parts(-(top + jnp.log(total)))
            rows = jnp.where(lane == first, hi, rows)
            rows = jnp.where(lane == first + 1, mid, rows)
            rows = jnp.where(lane == first + 2, low, rows)
            qa_ref[parity] = rows
        ctx_ref[...] = jnp.where(low_half, results[0], results[1]).astype(BF16)

    return pl.pallas_call(
        body,
        grid=(pairs, tiles),
        out_shape=(
            jax.ShapeDtypeStruct((length, width), BF16),
            jax.ShapeDtypeStruct((2 * pairs, length, LANES), BF16),
            jax.ShapeDtypeStruct((pairs, length, LANES), BF16),
        ),
        in_specs=[
            pl.BlockSpec((tile, LANES), lambda p, t: (t, p)),
            pl.BlockSpec((length, LANES), lambda p, t: (0, p)),
            pl.BlockSpec((length, LANES), lambda p, t: (0, p)),
            pl.BlockSpec((1, length), lambda p, t: (0, 0)),
            pl.BlockSpec((1, length), lambda p, t: (0, 0)),
            pl.BlockSpec((2, blocks, length), lambda p, t: (p, 0, 0)),
        ],
        out_specs=(
            pl.BlockSpec((tile, LANES), lambda p, t: (t, p)),
            pl.BlockSpec((2, tile, LANES), lambda p, t: (p, t, 0)),
            pl.BlockSpec((1, length, LANES), lambda p, t: (p, 0, 0)),
        ),
        scratch_shapes=[pltpu.VMEM((length, LANES), BF16), pltpu.VMEM((2, length, LANES), BF16)],
        compiler_params=pltpu.CompilerParams(vmem_limit_bytes=VMEM_BYTES),
        name="attend_forward",
    )(q, k, v, segment, block_of, bias)


def my_bits():
    batch = lax.axis_index("batch")
    return (
        lax.div(batch, 4),
        lax.rem(lax.div(batch, 2), 2),
        lax.rem(batch, 2),
        lax.axis_index("half"),
    )


def device_across(bit):
    batch = lax.axis_index("batch")
    half = lax.axis_index("half")
    member = lax.axis_index("member")
    bits = my_bits()
    if bit == 4:
        return (batch, half, 1 - member)
    if bit == 3:
        return (batch, 1 - half, member)
    stride = (4, 2, 1)[bit]
    return (batch + stride * (1 - 2 * bits[bit]), half, member)


def pick(order, depth, first):
    left = sorted(order[depth:])
    at = left.index(order[depth])
    return tuple(slice(None) for _ in range(at)) + (first,)


IN_CUTS = ((0, 16), (16, 16), (32, 32))
DOWN_CUTS = ((0, 384), (384, 384), (768, 256))


def remote(src, dst, send, recv, bit):
    return pltpu.make_async_remote_copy(
        src_ref=src,
        dst_ref=dst,
        send_sem=send,
        recv_sem=recv,
        device_id=device_across(bit),
        device_id_type=MESH_IDS,
    )


def greet(bits):
    barrier = pltpu.get_barrier_semaphore()
    for bit in bits:
        pl.semaphore_signal(barrier, inc=1, device_id=device_across(bit), device_id_type=MESH_IDS)
    pl.semaphore_wait(barrier, len(bits))


def feed_forward(n2, cot, w_in, in_bias, w_down):
    rows = n2.shape[0]
    chunk = 2 * LANES
    hidden_units = w_in.shape[1] // 2
    steps = hidden_units // chunk
    root = (2.0 / np.pi) ** 0.5
    cube = 0.044715

    def body(*refs):
        n_ref, c_ref, wi0_ref, wi1_ref, b0_ref, b1_ref, wd0_ref, wd1_ref = refs[:8]
        out_ref, dn_ref, gb_ref = refs[8:11]
        keep, got = refs[11:17], refs[17:23]
        nt_ref, gi_ref, gd_ref, send_sem, recv_sem, keep_sem = refs[23:]
        step = pl.program_id(0)
        bits = my_bits()

        @pl.when(step == 0)
        def _():
            greet((1, 2, 3))
            nt_ref[...] = n_ref[...].astype(F32).T.astype(BF16)

        wi = jnp.concatenate([wi0_ref[...], wi1_ref[...]], axis=1)
        wd = jnp.concatenate([wd0_ref[...], wd1_ref[...]], axis=0)
        pre = dot_nn(n_ref[...], wi) + jnp.concatenate([b0_ref[...], b1_ref[...]], axis=1)
        square = pre * pre
        th = jnp.tanh(root * pre * (1.0 + cube * square))
        half_up = 0.5 * (1.0 + th)
        hidden = (pre * half_up).astype(BF16)
        slope = half_up + 0.5 * pre * (1.0 - th * th) * (root * (1.0 + 3.0 * cube * square))
        pre_grad = (dot_nt(c_ref[...], wd) * slope).astype(BF16)
        gb_ref[...] = jnp.sum(pre_grad.astype(F32), axis=0, keepdims=True)
        gd_ref[step] = dot_tn(hidden, c_ref[...]).astype(BF16).reshape(2, LANES, D)
        gi_ref[step] = dot_nn(nt_ref[...], pre_grad).astype(BF16).reshape(2, 2, 2, 2, D // 16, chunk)

        def moves(kind, at):
            if kind < 3:
                first, size = IN_CUTS[kind]
                bit = (3, 2, 1)[kind]
                lead = {3: (slice(None),) * 3, 2: (slice(None),) * 2, 1: (slice(None),)}[bit]
                return lambda side: gi_ref.at[(at,) + lead + (side,)].at[
                    (slice(None),) * 3 + (pl.ds(first, size),)
                ], at, bit
            first, size = DOWN_CUTS[kind - 3]
            cols = pl.ds(first, size)
            if kind == 3:
                return lambda side: gd_ref.at[at, side, :, cols], at, 3
            if kind == 4:
                return lambda side: gd_ref.at[2 * at + side, :, :, cols], at, 2
            return lambda side: gd_ref.at[pl.ds(4 * at + 2 * side, 2), :, :, cols], at, 1

        def go(kind, at):
            where, slot, bit = moves(kind, at)
            pltpu.make_async_copy(where(bits[bit]), keep[kind].at[slot], keep_sem.at[kind, slot]).start()
            remote(
                where(1 - bits[bit]),
                got[kind].at[slot],
                send_sem.at[kind, slot],
                recv_sem.at[kind, slot],
                bit,
            ).start()

        for kind in range(4):
            go(kind, step)

        @pl.when(lax.rem(step, 2) == 1)
        def _():
            go(4, lax.div(step, 2))

        @pl.when(lax.rem(step, 4) == 3)
        def _():
            go(5, lax.div(step, 4))

        @pl.when(step == 0)
        def _():
            out_ref[...] = dot_nn(hidden, wd)
            dn_ref[...] = dot_nt(pre_grad, wi)

        @pl.when(step > 0)
        def _():
            out_ref[...] += dot_nn(hidden, wd)
            dn_ref[...] += dot_nt(pre_grad, wi)

        @pl.when(step == steps - 1)
        def _():
            for kind in range(6):
                for at in range((steps, steps, steps, steps, steps // 2, steps // 4)[kind]):
                    where, slot, bit = moves(kind, at)
                    pltpu.make_async_copy(
                        where(bits[bit]), keep[kind].at[slot], keep_sem.at[kind, slot]
                    ).wait()
                    remote(
                        where(1 - bits[bit]),
                        got[kind].at[slot],
                        send_sem.at[kind, slot],
                        recv_sem.at[kind, slot],
                        bit,
                    ).wait()

    def unit(which):
        return lambda j: (0, 4 * j + 2 * which + lax.axis_index("member"))

    def unit_rows(which):
        return lambda j: (4 * j + 2 * which + lax.axis_index("member"), 0)

    whole = pl.BlockSpec((rows, D), lambda j: (0, 0))
    anywhere = pl.BlockSpec(memory_space=pl.ANY)
    parts = [jax.ShapeDtypeStruct((steps, 2, 2, 2, size, chunk), BF16) for _, size in IN_CUTS] + [
        jax.ShapeDtypeStruct((steps, LANES, DOWN_CUTS[0][1]), BF16),
        jax.ShapeDtypeStruct((steps // 2, 2, LANES, DOWN_CUTS[1][1]), BF16),
        jax.ShapeDtypeStruct((steps // 4, 2, 2, LANES, DOWN_CUTS[2][1]), BF16),
    ]
    results = pl.pallas_call(
        body,
        grid=(steps,),
        out_shape=[
            jax.ShapeDtypeStruct((rows, D), F32),
            jax.ShapeDtypeStruct((rows, D), F32),
            jax.ShapeDtypeStruct((1, hidden_units), F32),
        ]
        + parts
        + parts,
        in_specs=[
            whole,
            whole,
            pl.BlockSpec((D, LANES), unit(0)),
            pl.BlockSpec((D, LANES), unit(1)),
            pl.BlockSpec((1, LANES), unit(0)),
            pl.BlockSpec((1, LANES), unit(1)),
            pl.BlockSpec((LANES, D), unit_rows(0)),
            pl.BlockSpec((LANES, D), unit_rows(1)),
        ],
        out_specs=[whole, whole, pl.BlockSpec((1, chunk), lambda j: (0, j))] + [anywhere] * 12,
        scratch_shapes=[
            pltpu.VMEM((D, rows), BF16),
            pltpu.VMEM((steps, 2, 2, 2, 2, D // 16, chunk), BF16),
            pltpu.VMEM((steps, 2, LANES, D), BF16),
            pltpu.SemaphoreType.DMA((6, steps)),
            pltpu.SemaphoreType.DMA((6, steps)),
            pltpu.SemaphoreType.DMA((6, steps)),
        ],
        compiler_params=pltpu.CompilerParams(
            collective_id=1, has_side_effects=True, vmem_limit_bytes=VMEM_BYTES
        ),
        name="feed_forward",
    )(n2, cot, w_in, w_in, in_bias, in_bias, w_down, w_down)
    return results[:3], results[3:9], results[9:]


LATER = ((2, 1, 0), (1, 3, 0), (3, 2, 0))


WHOLE_ORDERS = ((3, 2, 1, 0), (2, 1, 3, 0), (1, 3, 2, 0))
OUT_CUTS = ((0, 128), (128, 128), (256, 256))


class Sums:
    def __init__(self, send_sem, recv_sem):
        self.bits = my_bits()
        self.send_sem, self.recv_sem = send_sem, recv_sem
        self.pieces = {}

    def add(self, name, order, number, source, slots, cut=()):
        self.pieces[name] = (order, number, source, slots, cut)

    def side(self, name, depth, across):
        order, _, source, slots, cut = self.pieces[name]
        bit = order[depth]
        value = 1 - self.bits[bit] if across else self.bits[bit]
        if depth:
            return slots[depth - 1].at[(slice(None),) + pick(order, depth, value)]
        left = len(order)
        index = (slice(None),) + pick(order, 0, value) + (slice(None),) * (left - 1 - sorted(order).index(bit))
        return source.at[index + cut] if cut else source.at[index]

    def copy(self, name, depth):
        order, number, _, slots, _ = self.pieces[name]
        return remote(
            self.side(name, depth, True),
            slots[depth],
            self.send_sem.at[number, depth],
            self.recv_sem.at[number, depth],
            order[depth],
        )

    def send(self, name, depth):
        self.copy(name, depth).start()

    def take(self, name, depth):
        order, _, _, slots, _ = self.pieces[name]
        self.copy(name, depth).wait_recv()
        total = self.side(name, depth, False)[...].astype(F32) + slots[depth][...].astype(F32)
        if depth == len(order) - 1:
            return total
        slots[depth][...] = total.astype(BF16)
        self.send(name, depth + 1)
        return None

    def finish(self):
        for name, (order, _, _, _, _) in self.pieces.items():
            for depth in range(len(order)):
                self.copy(name, depth).wait_send()


def slot_shapes(lead, bits, tail):
    return [pltpu.VMEM((lead,) + (2,) * (bits - 1 - depth) + tail, BF16) for depth in range(bits)]


def attend_backward(rows_aug, k, v, feat_k, ctx, ctx_grad, normed, w_qkv, g_out, kept, got, tile=256):
    length, width = k.shape
    pairs = width // LANES
    tiles = length // tile
    own = length // 2
    in_steps, chunk = kept[0].shape[0], kept[0].shape[-1]
    shapes = [a.shape for a in kept[:3]] + [(1, 2, 2, 2, LANES, a.shape[-1]) for a in kept[3:]]
    kept = [a.reshape(shape) for a, shape in zip(kept, shapes)]
    got = [a.reshape(shape) for a, shape in zip(got, shapes)]
    out_rows = D // 16

    def body(*refs):
        qa_ref, k_ref, v_ref, fk_ref, ctx_ref, g_ref, n_ref, wq_ref, wk_ref, wv_ref, go_ref = refs[:11]
        keep_in, got_in = refs[11:17], refs[17:23]
        dn_ref, qb_ref, vb_ref, sum_in, sum_down, sum_out, dn_got = refs[23:30]
        keep_new, got_new = refs[30:33], refs[33:36]
        ga_ref, acc_ref, nt_ref, slab_ref, dn_acc, dn_send, gq_ref = refs[36:43]
        begin, first = refs[43:49], refs[49:55]
        slots = refs[55:85]
        send_sem, recv_sem, load_sem, new_send, new_recv, new_keep, dn_sem = refs[85:]
        pair, step = pl.program_id(0), pl.program_id(1)
        now = pair * tiles + step

        sums = Sums(send_sem, recv_sem)
        for kind in range(6):
            sums.add(kind, LATER[kind % 3], kind, begin[kind], slots[3 * kind : 3 * kind + 3])
        for kind in range(3):
            cols = pl.ds(*OUT_CUTS[kind])
            sums.add(
                6 + kind,
                WHOLE_ORDERS[kind],
                6 + kind,
                go_ref,
                slots[18 + 4 * kind : 22 + 4 * kind],
                (slice(None), cols),
            )

        def loads(kind):
            return (
                pltpu.make_async_copy(keep_in[kind], begin[kind], load_sem.at[0, kind]),
                pltpu.make_async_copy(got_in[kind], first[kind], load_sem.at[1, kind]),
            )

        def begin_sum(kind):
            for one in loads(kind):
                one.wait()
            begin[kind][...] = (begin[kind][...].astype(F32) + first[kind][...].astype(F32)).astype(BF16)
            sums.send(kind, 0)

        def end_sum(kind):
            if kind >= 6:
                sum_out[:, pl.ds(*OUT_CUTS[kind - 6])] = sums.take(kind, 3)[0]
                return
            total = sums.take(kind, 2)
            if kind < 3:
                for j in range(in_steps):
                    sum_in[pl.ds(*IN_CUTS[kind]), pl.ds(j * chunk, chunk)] = total[j]
            else:
                sum_down[:, pl.ds(*DOWN_CUTS[kind - 3])] = total[0]

        def at(when, act, *work):
            @pl.when(now == when)
            def _():
                for item in work:
                    act(*item) if isinstance(item, tuple) else act(item)

        @pl.when(now == 0)
        def _():
            greet((0, 1, 2, 3, 4))
            for kind in range(6):
                for one in loads(kind):
                    one.start()
            for kind in range(6, 9):
                sums.send(kind, 0)
            nt_ref[...] = n_ref[...].astype(F32).T.astype(BF16)

        at(1, begin_sum, 0, 1, 2)
        at(2, begin_sum, 3, 4, 5)
        at(4, sums.take, (0, 0), (1, 0), (2, 0), (6, 0), (7, 0), (8, 0))
        at(7, sums.take, (3, 0), (4, 0), (5, 0), (6, 1), (7, 1), (8, 1))
        at(8, sums.take, (0, 1), (1, 1), (2, 1))
        at(10, sums.take, (3, 1), (4, 1), (5, 1), (6, 2), (7, 2), (8, 2))
        at(13, end_sum, 0, 1, 2)
        at(15, end_sum, 6, 7, 8, 3, 4, 5)

        @pl.when(step == 0)
        def _():
            lane = lax.broadcasted_iota(jnp.int32, (length, LANES), 1)
            low_half = lane < HD
            grads = g_ref[...]
            prod = grads.astype(F32) * ctx_ref[...].astype(F32)
            for parity in range(2):
                mine = low_half if parity == 0 else jnp.logical_not(low_half)
                lead = HD if parity == 0 else 0
                delta = -jnp.sum(jnp.where(mine, prod, 0.0), axis=-1, keepdims=True)
                hi, mid, low = three_parts(delta)
                rows = jnp.where(mine, grads, jnp.zeros_like(grads))
                rows = jnp.where(lane == lead, hi, rows)
                rows = jnp.where(lane == lead + 1, mid, rows)
                ga_ref[parity] = jnp.where(lane == lead + 2, low, rows)
            acc_ref[...] = jnp.zeros_like(acc_ref)

        lane = lax.broadcasted_iota(jnp.int32, (tile, LANES), 1)
        low_half = lane < HD
        keys = k_ref[...]
        values = v_ref[...]
        feats = fk_ref[0]
        keys_t = keys.astype(F32).T.astype(BF16)
        dks, dvs = [], []
        for parity in range(2):
            lead = HD if parity == 0 else 0
            mine = low_half if parity == 0 else jnp.logical_not(low_half)
            key_rows = jnp.where(mine, keys, feats)
            ones = jnp.where((lane >= lead) & (lane < lead + 3), 1.0, 0.0).astype(BF16)
            value_rows = jnp.where(mine, values, ones)
            probs = jnp.exp(dot_nt(key_rows, qa_ref[parity]))
            diff = dot_nt(value_rows, ga_ref[parity])
            score_grad = (probs * diff).astype(BF16)
            dvs.append(dot_nn(probs.astype(BF16), g_ref[...]))
            dks.append(dot_nn(score_grad, qa_ref[parity]))
            side = keys_t[parity * HD : (parity + 1) * HD]
            acc_ref[parity * HD : (parity + 1) * HD] += dot_nn(side, score_grad)
        place = pl.ds(pl.multiple_of(step * tile, tile), tile)
        slab_ref[place, LANES : 2 * LANES] = jnp.where(low_half, dks[0], dks[1]).astype(BF16)
        slab_ref[place, 2 * LANES :] = jnp.where(low_half, dvs[0], dvs[1]).astype(BF16)

        def new_copies(which, one_pair):
            bit = (3, 2, 1)[which]
            lead = {3: (slice(None),) * 3, 2: (slice(None),) * 2, 1: (slice(None),)}[bit]
            whole = gq_ref.at[one_pair, which]
            return (
                pltpu.make_async_copy(
                    whole.at[lead + (sums.bits[bit],)],
                    keep_new[which].at[one_pair],
                    new_keep.at[which, one_pair],
                ),
                remote(
                    whole.at[lead + (1 - sums.bits[bit],)],
                    got_new[which].at[one_pair],
                    new_send.at[which, one_pair],
                    new_recv.at[which, one_pair],
                    bit,
                ),
            )

        @pl.when(step == tiles - 1)
        def _():
            slab_ref[:, :LANES] = (acc_ref[...].T * HD ** (-0.5)).astype(BF16)
            slabs = slab_ref[...]
            made = dot_nn(nt_ref[...], slabs).astype(BF16)
            for which in range(3):
                gq_ref[pair, which] = made[:, which * LANES : (which + 1) * LANES].reshape(
                    2, 2, 2, 2, out_rows, LANES
                )
                for one in new_copies(which, pair):
                    one.start()
            qb_ref[...] = jnp.sum(slabs[:, :LANES].astype(F32), axis=0, keepdims=True)
            vb_ref[...] = jnp.sum(slabs[:, 2 * LANES :].astype(F32), axis=0, keepdims=True)
            weights = jnp.concatenate([wq_ref[...], wk_ref[...], wv_ref[...]], axis=1)
            grown = dot_nt(slabs, weights)

            @pl.when(pair == 0)
            def _():
                dn_acc[...] = grown

            @pl.when(pair > 0)
            def _():
                dn_acc[...] += grown

        @pl.when(now == pairs * tiles - 1)
        def _():
            dn_send[...] = dn_acc[own:, :].astype(BF16)
            swap = remote(dn_send, dn_got, dn_sem.at[0], dn_sem.at[1], 4)
            swap.start()
            dn_ref[...] = dn_acc[:own, :]
            for one_pair in range(pairs):
                for which in range(3):
                    for one in new_copies(which, one_pair):
                        one.wait()
            sums.finish()
            swap.wait()

    in_vmem = pl.BlockSpec(memory_space=pltpu.VMEM)
    anywhere = pl.BlockSpec(memory_space=pl.ANY)
    slab = pl.BlockSpec((length, LANES), lambda p, t: (0, p))
    part = pl.BlockSpec((tile, LANES), lambda p, t: (t, p))
    bias_part = pl.BlockSpec((1, LANES), lambda p, t: (0, p))

    def columns(which):
        return pl.BlockSpec(
            (D, LANES), lambda p, t: (0, (2 * which + lax.axis_index("member")) * pairs + p)
        )

    slots = []
    for shape in shapes:
        slots += slot_shapes(shape[0], 3, shape[4:])
    for _, size in OUT_CUTS:
        slots += slot_shapes(1, 4, (out_rows, size))
    new = [jax.ShapeDtypeStruct((pairs, 2, 2, 2, out_rows, LANES), BF16)] * 3
    results = pl.pallas_call(
        body,
        grid=(pairs, tiles),
        out_shape=[
            jax.ShapeDtypeStruct((own, D), F32),
            jax.ShapeDtypeStruct((1, width), F32),
            jax.ShapeDtypeStruct((1, width), F32),
            jax.ShapeDtypeStruct((out_rows, in_steps * chunk), F32),
            jax.ShapeDtypeStruct((LANES, D), F32),
            jax.ShapeDtypeStruct((out_rows, width), F32),
            jax.ShapeDtypeStruct((own, D), BF16),
        ]
        + new
        + new,
        in_specs=[
            pl.BlockSpec((2, length, LANES), lambda p, t: (p, 0, 0)),
            part,
            part,
            pl.BlockSpec((1, tile, LANES), lambda p, t: (p, t, 0)),
            slab,
            slab,
            in_vmem,
            columns(0),
            columns(1),
            columns(2),
            in_vmem,
        ]
        + [anywhere] * 12,
        out_specs=[in_vmem, bias_part, bias_part, in_vmem, in_vmem, in_vmem, anywhere] + [anywhere] * 6,
        scratch_shapes=[
            pltpu.VMEM((2, length, LANES), BF16),
            pltpu.VMEM((LANES, length), F32),
            pltpu.VMEM((D, length), BF16),
            pltpu.VMEM((length, 3 * LANES), BF16),
            pltpu.VMEM((length, D), F32),
            pltpu.VMEM((own, D), BF16),
            pltpu.VMEM((pairs, 3, 2, 2, 2, 2, out_rows, LANES), BF16),
        ]
        + [pltpu.VMEM(shape, BF16) for shape in shapes]
        + [pltpu.VMEM(shape, BF16) for shape in shapes]
        + slots
        + [
            pltpu.SemaphoreType.DMA((9, 4)),
            pltpu.SemaphoreType.DMA((9, 4)),
            pltpu.SemaphoreType.DMA((2, 6)),
            pltpu.SemaphoreType.DMA((3, pairs)),
            pltpu.SemaphoreType.DMA((3, pairs)),
            pltpu.SemaphoreType.DMA((3, pairs)),
            pltpu.SemaphoreType.DMA((2,)),
        ],
        compiler_params=pltpu.CompilerParams(
            collective_id=3, has_side_effects=True, vmem_limit_bytes=VMEM_BYTES
        ),
        name="attend_backward",
    )(
        rows_aug,
        k,
        v,
        feat_k,
        ctx,
        ctx_grad,
        normed,
        w_qkv,
        w_qkv,
        w_qkv,
        g_out.reshape(1, 2, 2, 2, 2, out_rows, width),
        *kept,
        *got,
    )
    return results[:7], results[7:10], results[10:]


def tail_sums(kept, got, vectors):
    pairs, rows = kept[0].shape[0], kept[0].shape[-2]

    def body(*refs):
        keep, first, vec_ref, qkv_ref, vec_sum = refs[:3], refs[3:6], refs[6], refs[7], refs[8]
        begin, slots = refs[9:12], refs[12:25]
        send_sem, recv_sem = refs[25:]
        greet((0, 1, 2, 3))
        sums = Sums(send_sem, recv_sem)
        sums.add(3, WHOLE_ORDERS[0], 3, vec_ref, slots[9:13])
        for kind in range(3):
            sums.add(kind, LATER[kind], kind, begin[kind], slots[3 * kind : 3 * kind + 3])
            begin[kind][...] = (keep[kind][...].astype(F32) + first[kind][...].astype(F32)).astype(BF16)
            sums.send(kind, 0)
        sums.send(3, 0)
        for depth in range(3):
            for kind in range(3):
                total = sums.take(kind, depth)
                if depth == 2:
                    for pair in range(pairs):
                        place = kind * pairs + pair
                        qkv_ref[:, place * LANES : (place + 1) * LANES] = total[pair]
            sums.take(3, depth)
        vec_sum[...] = sums.take(3, 3)[0]
        sums.finish()

    in_vmem = pl.BlockSpec(memory_space=pltpu.VMEM)
    slots = []
    for _ in range(3):
        slots += slot_shapes(pairs, 3, (rows, LANES))
    slots += slot_shapes(1, 4, (rows, LANES))
    return pl.pallas_call(
        body,
        out_shape=(
            jax.ShapeDtypeStruct((rows, 3 * pairs * LANES), F32),
            jax.ShapeDtypeStruct((rows, LANES), F32),
        ),
        in_specs=[in_vmem] * 7,
        out_specs=(in_vmem, in_vmem),
        scratch_shapes=[pltpu.VMEM(kept[0].shape, BF16)] * 3
        + slots
        + [pltpu.SemaphoreType.DMA((4, 4)), pltpu.SemaphoreType.DMA((4, 4))],
        compiler_params=pltpu.CompilerParams(
            collective_id=2, has_side_effects=True, vmem_limit_bytes=VMEM_BYTES
        ),
        name="tail_sums",
    )(*kept, *got, vectors.reshape(1, 2, 2, 2, 2, rows, LANES))


def normalise(values):
    mean = jnp.mean(values, axis=-1, keepdims=True)
    centred = values - mean
    scale = lax.rsqrt(jnp.mean(centred * centred, axis=-1, keepdims=True) + eps)
    return centred * scale, scale


def normalise_back(unit, scale, grad):
    first = jnp.mean(grad, axis=-1, keepdims=True)
    second = jnp.mean(grad * unit, axis=-1, keepdims=True)
    return (grad - first - unit * second) * scale


def per_device_pair(
    tokens,
    ln1_gain,
    ln1_bias,
    w_qkv,
    q_bias,
    v_bias,
    w_out,
    out_bias,
    ln2_gain,
    ln2_bias,
    w_in,
    in_bias,
    w_down,
    down_bias,
    cotangent,
    segment_ids,
    random_blocks,
    global_blocks,
):
    rows = tokens.shape[0]
    own = 2 * rows
    length = segment_ids.shape[0]
    blocks = length // BLK
    half = lax.axis_index("half")
    member = lax.axis_index("member")
    mine_d = D // 2
    heads = HEADS // 2
    chips = lax.axis_size("batch") * 2

    def gather_rows(x):
        kept = lax.dynamic_index_in_dim(x, half, 1, keepdims=False)
        sent = lax.dynamic_index_in_dim(x, 1 - half, 1, keepdims=False)
        held = jnp.concatenate([kept, flip("half", sent)], axis=0)
        return jnp.concatenate([held, flip("member", held)], axis=0)

    def return_rows(x):
        kept, other = x[:rows], flip("half", x[rows:].astype(BF16)).astype(x.dtype)
        return jnp.where(
            half == 0, jnp.stack([kept, other], axis=1), jnp.stack([other, kept], axis=1)
        )

    seq_tokens = gather_rows(tokens)
    later, _ = lax.optimization_barrier((cotangent, seq_tokens))
    cot = gather_rows(later)

    per_row = rows // BLK
    order = jnp.concatenate(
        [
            ((half + t) % 2 * 2 + (member + j) % 2) * per_row + jnp.arange(per_row, dtype=jnp.int32)
            for j in range(2)
            for t in range(2)
        ]
    )
    numbers = jnp.arange(blocks, dtype=jnp.int32)
    seq_random = lax.dynamic_index_in_dim(random_blocks, half, 1, keepdims=False)
    seq_random = lax.dynamic_slice_in_dim(seq_random, member * heads, heads, 1)
    seq_global = lax.dynamic_index_in_dim(global_blocks, half, 1, keepdims=False)
    seq_segment = lax.dynamic_index_in_dim(segment_ids, half, 1, keepdims=False).reshape(blocks, BLK)
    move = (order[:, None] == numbers).astype(F32)
    segment = jnp.sum(move[:, :, None] * seq_segment.astype(F32)[None], axis=1).reshape(1, length)
    block_of = jnp.broadcast_to(order.astype(F32)[:, None], (blocks, BLK)).reshape(1, length)
    hits = jnp.sum((seq_random[..., None] == order).astype(F32), axis=2)
    near = (jnp.abs(numbers[:, None] - order) <= 1).astype(F32)
    far = jnp.sum((seq_global[:, None] == order).astype(F32), axis=0)
    times = hits + (near + far)[:, None, :]
    bias = jnp.where(times > 0, jnp.log(jnp.maximum(times, 1.0)), NEG).transpose(1, 0, 2)
    bias = jnp.broadcast_to(bias[..., None], (heads, blocks, blocks, BLK)).reshape(heads, blocks, length)

    def columns(w, part):
        return lax.dynamic_slice_in_dim(w, part * D + member * mine_d, mine_d, 1)

    w_q, w_k, w_v = (columns(w_qkv, part) for part in range(3))
    q_bias_mine = lax.dynamic_slice_in_dim(q_bias, member * mine_d, mine_d, 0)
    v_bias_mine = lax.dynamic_slice_in_dim(v_bias, member * mine_d, mine_d, 0)
    w_out_mine = lax.dynamic_slice_in_dim(w_out, member * mine_d, mine_d, 0)
    w_out_other = lax.dynamic_slice_in_dim(w_out, (1 - member) * mine_d, mine_d, 0)

    inputs = seq_tokens.astype(F32)
    unit1, scale1 = normalise(inputs)
    normed = (unit1 * ln1_gain.astype(F32) + ln1_bias.astype(F32)).astype(BF16)
    queries = (dot_nn(normed, w_q) + q_bias_mine.astype(F32)).astype(BF16)
    keys = dot_nn(normed, w_k).astype(BF16)
    values = (dot_nn(normed, w_v) + v_bias_mine.astype(F32)).astype(BF16)

    context, rows_aug, feat_k = attend_forward(queries, keys, values, segment, block_of, bias)
    context_other = flip("member", context)
    context_other = jnp.concatenate([context_other[own:], context_other[:own]], axis=0)

    mid_stream = (
        inputs[:own]
        + dot_nn(context[:own], w_out_mine)
        + dot_nn(context_other[:own], w_out_other)
        + out_bias.astype(F32)
    )
    unit2, scale2 = normalise(mid_stream)
    n2_own = (unit2 * ln2_gain.astype(F32) + ln2_bias.astype(F32)).astype(BF16)
    n2 = jnp.concatenate([n2_own, flip("member", n2_own)], axis=0)

    (out_part, n2_grad_part, in_bias_grad), kept_parts, got_parts = feed_forward(
        n2, cot, w_in, in_bias.astype(F32).reshape(1, -1), w_down
    )
    output_own = (
        mid_stream
        + out_part[:own]
        + flip("member", out_part[own:].astype(BF16)).astype(F32)
        + down_bias.astype(F32)
    ).astype(BF16)
    output = return_rows(output_own)

    n2_grad = n2_grad_part[:own] + flip("member", n2_grad_part[own:].astype(BF16)).astype(F32)
    cot_own = cot[:own].astype(F32)
    ln2_gain_grad = jnp.sum(n2_grad * unit2, axis=0)
    ln2_bias_grad = jnp.sum(n2_grad, axis=0)
    mid_grad = cot_own + normalise_back(unit2, scale2, n2_grad * ln2_gain.astype(F32))
    branch_own = mid_grad.astype(BF16)
    branch = jnp.concatenate([branch_own, flip("member", branch_own)], axis=0)
    context_grad = dot_nt(branch, w_out_mine).astype(BF16)
    branch_columns = lax.dynamic_slice_in_dim(branch, member * mine_d, mine_d, 1)
    g_out_mine = dot_tn(context, branch_columns).astype(BF16)
    g_out_other = dot_tn(context_other, branch_columns).astype(BF16)
    g_out = jnp.where(
        member == 0,
        jnp.concatenate([g_out_mine, g_out_other], axis=0),
        jnp.concatenate([g_out_other, g_out_mine], axis=0),
    )

    (normed_grad_part, q_sum, v_sum, summed_in, summed_down, summed_out, normed_grad_got), kept_qkv, got_qkv = (
        attend_backward(
            rows_aug, keys, values, feat_k, context, context_grad, normed, w_qkv, g_out, kept_parts, got_parts
        )
    )
    normed_grad = normed_grad_part + normed_grad_got.astype(F32)
    unit1_own, scale1_own = unit1[:own], scale1[:own]
    ln1_gain_grad = jnp.sum(normed_grad * unit1_own, axis=0)
    ln1_bias_grad = jnp.sum(normed_grad, axis=0)
    input_grad_own = mid_grad + normalise_back(unit1_own, scale1_own, normed_grad * ln1_gain.astype(F32))
    input_grad = return_rows(input_grad_own)

    def placed(x):
        full = jnp.zeros((D,), F32)
        return lax.dynamic_update_slice_in_dim(full, x, member * mine_d, 0)

    in_bias_rows = in_bias_grad.reshape(chips, 2, LANES // 2).transpose(1, 0, 2).reshape(2, D)
    gone = jnp.zeros_like(in_bias_rows)
    vectors = jnp.stack(
        [
            ln1_gain_grad,
            ln1_bias_grad,
            jnp.sum(branch_own.astype(F32), axis=0),
            ln2_gain_grad,
            ln2_bias_grad,
            jnp.sum(cot_own, axis=0),
            placed(q_sum[0]),
            placed(v_sum[0]),
        ]
    )
    vectors = jnp.concatenate(
        [
            vectors,
            jnp.where(member == 0, in_bias_rows, gone),
            jnp.where(member == 1, in_bias_rows, gone),
            jnp.zeros((LANES - 12, D), F32),
        ]
    ).T.astype(BF16)
    summed_qkv, summed_vectors = tail_sums(kept_qkv, got_qkv, vectors)

    chip_rows = jnp.concatenate([summed_qkv, summed_out, summed_vectors, summed_in], axis=1)
    per = chip_rows.shape[0] // 2
    mine_rows = lax.dynamic_slice_in_dim(chip_rows, member * per, per, 0)
    other_rows = lax.dynamic_slice_in_dim(chip_rows, (1 - member) * per, per, 0)
    got_rows = flip("member", other_rows)
    left = jnp.where(member == 0, mine_rows, got_rows)
    right = jnp.where(member == 0, got_rows, mine_rows)

    def both(start, size):
        return jnp.concatenate([left[:, start : start + size], right[:, start : start + size]], axis=1)

    w_qkv_grad = jnp.concatenate([both(part * mine_d, mine_d) for part in range(3)], axis=1)
    w_out_grad = both(3 * mine_d, mine_d)
    start = 4 * mine_d
    vector_sums = left[:, start : start + LANES] + right[:, start : start + LANES]
    start += LANES
    w_in_grad = jnp.concatenate(
        [
            x[:, start + j * LANES : start + (j + 1) * LANES]
            for j in range(chips)
            for x in (left, right)
        ],
        axis=1,
    )
    in_mine = lax.dynamic_slice_in_dim(summed_vectors, 8 + 2 * member, 2, 1)
    in_bias_out = in_mine.T.reshape(LANES)
    vec = [vector_sums[:, i] for i in range(8)]
    return (
        output,
        input_grad,
        vec[0],
        vec[1],
        w_qkv_grad,
        vec[6],
        vec[7],
        w_out_grad,
        vec[2],
        vec[3],
        vec[4],
        w_in_grad,
        in_bias_out,
        summed_down,
        vec[5],
    )


def solution(mesh):
    def program(*args):
        sequences = args[0].shape[1] // mesh.shape["batch"]
        seq = mesh.shape["seq"]
        fast = sequences == 2 and seq == 4 and mesh.shape["batch"] == 8
        if fast:
            use = jax.sharding.Mesh(
                mesh.devices.reshape(mesh.shape["batch"], 2, 2), ("batch", "half", "member")
            )
            seq_axes, all_axes, run = ("half", "member"), ("batch", "half", "member"), per_device_pair
        else:
            use, seq_axes, all_axes, run = mesh, "seq", ("batch", "seq"), per_device
        rows = P(seq_axes, "batch", None)
        in_specs = (rows,) + (P(),) * 13 + (
            rows,
            P(None, "batch"),
            P(None, "batch", None, None),
            P(None, "batch"),
        )
        vector, matrix = P(all_axes), P(all_axes, None)
        out_specs = (
            rows,
            rows,
            vector,
            vector,
            matrix,
            vector,
            vector,
            matrix,
            vector,
            vector,
            vector,
            matrix,
            vector,
            matrix,
            vector,
        )
        return jax.shard_map(
            run, mesh=use, in_specs=in_specs, out_specs=out_specs, check_vma=False
        )(*args)

    return program
```

```python
import jax
import jax.numpy as jnp
import numpy as np
from jax import lax
from jax.experimental import pallas as pl
from jax.experimental.pallas import tpu as pltpu
from jax.sharding import PartitionSpec as P

D = 1024
HEADS = 16
HD = 64
BLK = 64
RAND = 3
GLOB = 2


eps = 1e-05


def padded(x, sides, width):
    for axis, dim in sides:
        size, length = (lax.axis_size(axis), x.shape[dim])
        up = [(i, (i + 1) % size) for i in range(size - 1)]
        down = [(j, i) for i, j in up]
        last = lax.slice_in_dim(x, length - width, length, axis=dim)
        initial = lax.slice_in_dim(x, 0, width, axis=dim)
        before = lax.ppermute(last, axis, up)
        after = lax.ppermute(initial, axis, down)
        x = jnp.concatenate([before, x, after], axis=dim)
    return x


def layer_norm(values, gain_vec, shift_vec):
    row_mean = jnp.mean(values, axis=-1, keepdims=True)
    centred = values - row_mean
    spread = jnp.mean(centred * centred, axis=-1, keepdims=True)
    return centred * lax.rsqrt(spread + eps) * gain_vec + shift_vec


def gelu_tanh(values):
    return jax.nn.gelu(values, approximate=True)


def window_stack(extended, query_blocks):
    return jnp.stack(
        [extended[0:query_blocks], extended[1 : query_blocks + 1], extended[2 : query_blocks + 2]],
        axis=1,
    )


def pick_blocks(shard_rows, random_local, global_blocks):
    block_total = shard_rows.shape[0] // BLK
    seq_count = shard_rows.shape[1]
    numbers = jnp.arange(block_total, dtype=jnp.int32)
    random_hits = (random_local[..., None] == numbers).astype(jnp.bfloat16)
    global_hits = (global_blocks[..., None] == numbers).astype(jnp.bfloat16)
    blocks = shard_rows.reshape(block_total, BLK, seq_count, 2, HEADS, HD)
    picked_random = jnp.einsum(
        "ishjb,busxhd->ishjuxd", random_hits, blocks, preferred_element_type=jnp.float32
    )
    picked_global = jnp.einsum(
        "gsb,busc->gusc",
        global_hits,
        shard_rows.reshape(block_total, BLK, seq_count, 2 * D),
        preferred_element_type=jnp.float32,
    )
    return (picked_random, picked_global)


def key_products(left_side, window_kv, far_random, far_global, which_half):
    near_part = jnp.einsum(
        "itshd,iwushd->ishtwu",
        left_side,
        window_kv[:, :, :, :, which_half],
        preferred_element_type=jnp.float32,
    )
    far_part = jnp.einsum(
        "itshd,ishjud->ishtju",
        left_side,
        far_random[:, :, :, :, :, which_half],
        preferred_element_type=jnp.float32,
    )
    global_part = jnp.einsum(
        "itshd,gushd->ishtgu",
        left_side,
        far_global[:, :, :, which_half],
        preferred_element_type=jnp.float32,
    )
    lead_shape = near_part.shape[:4]
    return jnp.concatenate(
        [
            near_part.reshape(lead_shape + (-1,)),
            far_part.reshape(lead_shape + (-1,)),
            global_part.reshape(lead_shape + (-1,)),
        ],
        axis=-1,
    )


def split_slots(weights):
    lead_shape = weights.shape[:4]
    near_cut = 3 * BLK
    far_cut = (3 + RAND) * BLK
    near_part = weights[..., :near_cut].reshape(lead_shape + (3, BLK))
    far_part = weights[..., near_cut:far_cut].reshape(lead_shape + (RAND, BLK))
    global_part = weights[..., far_cut:].reshape(lead_shape + (GLOB, BLK))
    return (near_part, far_part, global_part)


def key_mix(weights, window_kv, far_random, far_global, which_half):
    near_part, far_part, global_part = split_slots(weights)
    mixed = jnp.einsum(
        "ishtwu,iwushd->itshd",
        near_part,
        window_kv[:, :, :, :, which_half],
        preferred_element_type=jnp.float32,
    )
    mixed = mixed + jnp.einsum(
        "ishtju,ishjud->itshd",
        far_part,
        far_random[:, :, :, :, :, which_half],
        preferred_element_type=jnp.float32,
    )
    mixed = mixed + jnp.einsum(
        "ishtgu,gushd->itshd",
        global_part,
        far_global[:, :, :, which_half],
        preferred_element_type=jnp.float32,
    )
    return mixed


def key_grads(weights, left_side):
    near_part, far_part, global_part = split_slots(weights)
    near_grad = jnp.einsum(
        "ishtwu,itshd->iwushd", near_part, left_side, preferred_element_type=jnp.float32
    )
    far_grad = jnp.einsum(
        "ishtju,itshd->ishjud", far_part, left_side, preferred_element_type=jnp.float32
    )
    global_grad = jnp.einsum(
        "ishtgu,itshd->gushd", global_part, left_side, preferred_element_type=jnp.float32
    )
    return (near_grad, far_grad, global_grad)


def per_device(
    tokens,
    ln1_gain,
    ln1_bias,
    w_qkv,
    q_bias,
    v_bias,
    w_out,
    out_bias,
    ln2_gain,
    ln2_bias,
    w_in,
    in_bias,
    w_down,
    down_bias,
    cotangent,
    segment_ids,
    random_blocks,
    global_blocks,
):
    row_count = tokens.shape[0]
    seq_count = tokens.shape[1]
    query_blocks = row_count // BLK
    seq_length = segment_ids.shape[0]
    device_now = lax.axis_index("seq")
    first_row = device_now * row_count
    score_scale = HD ** (-0.5)
    random_local = lax.dynamic_slice_in_dim(
        random_blocks, device_now * query_blocks, query_blocks, 0
    )
    inputs = tokens.astype(jnp.float32)
    normed_full, first_norm_back = jax.vjp(
        layer_norm, inputs, ln1_gain.astype(jnp.float32), ln1_bias.astype(jnp.float32)
    )
    normed = normed_full.astype(jnp.bfloat16)
    projected = jnp.einsum("rsd,de->rse", normed, w_qkv, preferred_element_type=jnp.float32)
    queries = (projected[:, :, :D] + q_bias.astype(jnp.float32)).astype(jnp.bfloat16)
    value_shift = jnp.concatenate([jnp.zeros((D,), jnp.float32), v_bias.astype(jnp.float32)])
    keyval = (projected[:, :, D:] + value_shift).astype(jnp.bfloat16)
    extended = padded(keyval, (("seq", 0),), BLK)
    window_kv = window_stack(
        extended.reshape(query_blocks + 2, BLK, seq_count, 2, HEADS, HD), query_blocks
    )
    picked = pick_blocks(
        lax.all_gather(keyval, "seq", axis=0, tiled=True), random_local, global_blocks
    )
    far_random = picked[0].astype(jnp.bfloat16)
    far_global = picked[1].astype(jnp.bfloat16).reshape(GLOB, BLK, seq_count, 2, HEADS, HD)
    query_segment = lax.dynamic_slice_in_dim(segment_ids, first_row, row_count, 0)
    query_segment = query_segment.reshape(query_blocks, BLK, seq_count).transpose(0, 2, 1)
    window_spots = first_row - BLK + jnp.arange(row_count + 2 * BLK, dtype=jnp.int32)
    inside_seq = (window_spots >= 0) & (window_spots < seq_length)
    near_segment = jnp.take(segment_ids, jnp.clip(window_spots, 0, seq_length - 1), axis=0)
    near_segment = jnp.where(inside_seq[:, None], near_segment, -1)
    near_segment = window_stack(
        near_segment.reshape(query_blocks + 2, BLK, seq_count), query_blocks
    )
    near_segment = near_segment.transpose(0, 3, 1, 2).reshape(query_blocks, seq_count, 1, 3 * BLK)
    segment_rows = segment_ids.T
    sequence_pick = jnp.arange(seq_count, dtype=jnp.int32)
    offsets = jnp.arange(BLK, dtype=jnp.int32)
    far_segment = segment_rows[
        sequence_pick[None, :, None, None, None], random_local[..., None] * BLK + offsets
    ]
    far_segment = far_segment.reshape(query_blocks, seq_count, HEADS, RAND * BLK)
    global_segment = segment_rows[
        sequence_pick[None, :, None], global_blocks[..., None] * BLK + offsets
    ]
    global_segment = global_segment.transpose(1, 0, 2).reshape(1, seq_count, 1, GLOB * BLK)
    key_segment = jnp.concatenate(
        [
            jnp.broadcast_to(near_segment, (query_blocks, seq_count, HEADS, 3 * BLK)),
            far_segment,
            jnp.broadcast_to(global_segment, (query_blocks, seq_count, HEADS, GLOB * BLK)),
        ],
        axis=-1,
    )
    allowed = key_segment[:, :, :, None, :] == query_segment[:, :, None, :, None]
    query_rows = queries.reshape(query_blocks, BLK, seq_count, HEADS, HD)
    scores = jnp.where(
        allowed, key_products(query_rows, window_kv, far_random, far_global, 0) * score_scale, -1e30
    )
    row_max = jnp.max(scores, axis=-1, keepdims=True)
    log_total = row_max + jnp.log(jnp.sum(jnp.exp(scores - row_max), axis=-1, keepdims=True))
    soft_full = jnp.exp(scores - log_total)
    attn_probs = soft_full.astype(jnp.bfloat16)
    context = (
        key_mix(attn_probs, window_kv, far_random, far_global, 1)
        .reshape(row_count, seq_count, D)
        .astype(jnp.bfloat16)
    )
    mid_stream = (
        inputs
        + jnp.einsum("rsd,de->rse", context, w_out, preferred_element_type=jnp.float32)
        + out_bias.astype(jnp.float32)
    )
    normed2_full, second_norm_back = jax.vjp(
        layer_norm, mid_stream, ln2_gain.astype(jnp.float32), ln2_bias.astype(jnp.float32)
    )
    normed2 = normed2_full.astype(jnp.bfloat16)
    pre_act = jnp.einsum(
        "rsd,df->rsf", normed2, w_in, preferred_element_type=jnp.float32
    ) + in_bias.astype(jnp.float32)
    hidden_full, gelu_back = jax.vjp(gelu_tanh, pre_act)
    hidden = hidden_full.astype(jnp.bfloat16)
    output = (
        mid_stream
        + jnp.einsum("rsf,fd->rsd", hidden, w_down, preferred_element_type=jnp.float32)
        + down_bias.astype(jnp.float32)
    ).astype(jnp.bfloat16)
    grad_out = cotangent.astype(jnp.float32)
    w_down_grad = jnp.einsum("rsf,rsd->fd", hidden, cotangent, preferred_element_type=jnp.float32)
    down_bias_grad = jnp.sum(grad_out, axis=(0, 1))
    pre_grad = gelu_back(
        jnp.einsum("rsd,fd->rsf", cotangent, w_down, preferred_element_type=jnp.float32)
    )[0].astype(jnp.bfloat16)
    w_in_grad = jnp.einsum("rsd,rsf->df", normed2, pre_grad, preferred_element_type=jnp.float32)
    in_bias_grad = jnp.sum(pre_grad.astype(jnp.float32), axis=(0, 1))
    mid_part, ln2_gain_grad, ln2_bias_grad = second_norm_back(
        jnp.einsum("rsf,df->rsd", pre_grad, w_in, preferred_element_type=jnp.float32)
    )
    mid_grad = grad_out + mid_part
    branch_grad = mid_grad.astype(jnp.bfloat16)
    w_out_grad = jnp.einsum("rsd,rse->de", context, branch_grad, preferred_element_type=jnp.float32)
    out_bias_grad = jnp.sum(branch_grad.astype(jnp.float32), axis=(0, 1))
    context_grad = jnp.einsum(
        "rse,de->rsd", branch_grad, w_out, preferred_element_type=jnp.float32
    ).astype(jnp.bfloat16)
    grad_rows = context_grad.reshape(query_blocks, BLK, seq_count, HEADS, HD)
    probs_grad = key_products(grad_rows, window_kv, far_random, far_global, 1)
    score_grad = (
        soft_full * (probs_grad - jnp.sum(soft_full * probs_grad, axis=-1, keepdims=True))
    ).astype(jnp.bfloat16)
    query_grad = (
        (key_mix(score_grad, window_kv, far_random, far_global, 0) * score_scale)
        .reshape(row_count, seq_count, D)
        .astype(jnp.bfloat16)
    )
    near_key, far_key, global_key = key_grads(score_grad, query_rows)
    near_value, far_value, global_value = key_grads(attn_probs, grad_rows)
    near_kv = jnp.stack([near_key * score_scale, near_value], axis=4)
    far_kv = jnp.stack([far_key * score_scale, far_value], axis=5)
    global_kv = jnp.stack([global_key * score_scale, global_value], axis=3).reshape(
        GLOB, BLK, seq_count, 2 * D
    )
    rest_pad = ((0, 0),) * 5
    extended_grad = (
        jnp.pad(near_kv[:, 0], ((0, 2),) + rest_pad)
        + jnp.pad(near_kv[:, 1], ((1, 1),) + rest_pad)
        + jnp.pad(near_kv[:, 2], ((2, 0),) + rest_pad)
    )
    extended_grad = extended_grad.reshape(row_count + 2 * BLK, seq_count, 2 * D)
    rim_grads = jnp.concatenate([extended_grad[:BLK], extended_grad[row_count + BLK :]], axis=0)
    returned = padded(rim_grads.astype(jnp.bfloat16), (("seq", 0),), BLK).astype(rim_grads.dtype)
    near_total = extended_grad[BLK : row_count + BLK]
    near_total = (
        near_total.at[:BLK].add(returned[:BLK]).at[row_count - BLK :].add(returned[3 * BLK :])
    )
    block_total = row_count * lax.axis_size("seq") // BLK
    numbers = jnp.arange(block_total, dtype=jnp.int32)
    random_hits = (random_local[..., None] == numbers).astype(jnp.float32)
    global_rows_hit = (global_blocks[..., None] == numbers).astype(jnp.float32)

    def far_sum(one_sequence):
        hits, kv, global_rows, global_sum = one_sequence
        random_term = jnp.einsum(
            "ihjb,ihjuxd->buxhd", hits, kv, precision=lax.Precision.HIGHEST
        )
        global_term = jnp.einsum(
            "gb,guc->buc", global_rows, global_sum, precision=lax.Precision.HIGHEST
        )
        flat = (block_total * BLK, 2 * D)
        return (random_term.reshape(flat) + global_term.reshape(flat)).astype(jnp.bfloat16)

    far_parts = lax.map(
        far_sum,
        (
            jnp.moveaxis(random_hits, 1, 0),
            jnp.moveaxis(far_kv, 1, 0),
            jnp.moveaxis(global_rows_hit, 1, 0),
            jnp.moveaxis(global_kv, 2, 0),
        ),
    )
    far_total = lax.psum_scatter(far_parts, "seq", scatter_dimension=1, tiled=True)
    far_total = jnp.moveaxis(far_total, 0, 1).astype(jnp.float32)
    keyval_grad = (near_total + far_total).astype(jnp.bfloat16)
    qkv_grad = jnp.concatenate([query_grad, keyval_grad], axis=-1)
    q_bias_grad = jnp.sum(query_grad.astype(jnp.float32), axis=(0, 1))
    v_bias_grad = jnp.sum(keyval_grad[:, :, D:].astype(jnp.float32), axis=(0, 1))
    w_qkv_grad = jnp.einsum("rsd,rse->de", normed, qkv_grad, preferred_element_type=jnp.float32)
    input_part, ln1_gain_grad, ln1_bias_grad = first_norm_back(
        jnp.einsum("rse,de->rsd", qkv_grad, w_qkv, preferred_element_type=jnp.float32)
    )
    input_grad = mid_grad + input_part
    summed = (
        lax.psum_scatter(ln1_gain_grad, ("batch", "seq"), scatter_dimension=0, tiled=True),
        lax.psum_scatter(ln1_bias_grad, ("batch", "seq"), scatter_dimension=0, tiled=True),
        lax.psum_scatter(w_qkv_grad, ("batch", "seq"), scatter_dimension=0, tiled=True),
        lax.psum_scatter(q_bias_grad, ("batch", "seq"), scatter_dimension=0, tiled=True),
        lax.psum_scatter(v_bias_grad, ("batch", "seq"), scatter_dimension=0, tiled=True),
        lax.psum_scatter(w_out_grad, ("batch", "seq"), scatter_dimension=0, tiled=True),
        lax.psum_scatter(out_bias_grad, ("batch", "seq"), scatter_dimension=0, tiled=True),
        lax.psum_scatter(ln2_gain_grad, ("batch", "seq"), scatter_dimension=0, tiled=True),
        lax.psum_scatter(ln2_bias_grad, ("batch", "seq"), scatter_dimension=0, tiled=True),
        lax.psum_scatter(w_in_grad, ("batch", "seq"), scatter_dimension=0, tiled=True),
        lax.psum_scatter(in_bias_grad, ("batch", "seq"), scatter_dimension=0, tiled=True),
        lax.psum_scatter(w_down_grad, ("batch", "seq"), scatter_dimension=0, tiled=True),
        lax.psum_scatter(down_bias_grad, ("batch", "seq"), scatter_dimension=0, tiled=True),
    )
    return (
        output,
        input_grad,
        summed[0],
        summed[1],
        summed[2],
        summed[3],
        summed[4],
        summed[5],
        summed[6],
        summed[7],
        summed[8],
        summed[9],
        summed[10],
        summed[11],
        summed[12],
    )


NEG = -1e30
LANES = 128
SEG_VALUES = 4
MESH_IDS = pl.DeviceIdType.MESH
VMEM_BYTES = 60 * 1024 * 1024
F32 = jnp.float32
BF16 = jnp.bfloat16
ALL = slice(None)
Z_HIGH, Z_LOW, Y, X, MEMBER = range(5)
CHIP = (Z_HIGH, Z_LOW, Y, X)


def flip(axis, x):
    return lax.ppermute(x, axis, [(0, 1), (1, 0)])


def three_parts(x):
    hi = x.astype(BF16)
    rest = x - hi.astype(F32)
    mid = rest.astype(BF16)
    low = (rest - mid.astype(F32)).astype(BF16)
    return hi, mid, low


def dot_nt(a, b):
    return lax.dot_general(a, b, (((1,), (1,)), ((), ())), preferred_element_type=F32)


def dot_nn(a, b):
    return lax.dot_general(a, b, (((1,), (0,)), ((), ())), preferred_element_type=F32)


def dot_tn(a, b):
    return lax.dot_general(a, b, (((0,), (0,)), ((), ())), preferred_element_type=F32)


def turned(x):
    return x.astype(F32).T.astype(BF16)


def normalise(values):
    mean = jnp.mean(values, axis=-1, keepdims=True)
    centred = values - mean
    scale = lax.rsqrt(jnp.mean(centred * centred, axis=-1, keepdims=True) + eps)
    return centred * scale, scale


def normalise_back(unit, scale, grad):
    first = jnp.mean(grad, axis=-1, keepdims=True)
    second = jnp.mean(grad * unit, axis=-1, keepdims=True)
    return (grad - first - unit * second) * scale


def my_bits():
    batch = lax.axis_index("batch")
    return (
        lax.div(batch, 4),
        lax.rem(lax.div(batch, 2), 2),
        lax.rem(batch, 2),
        lax.axis_index("half"),
        lax.axis_index("member"),
    )


def device_across(bit):
    batch = lax.axis_index("batch")
    half = lax.axis_index("half")
    member = lax.axis_index("member")
    if bit == MEMBER:
        return (batch, half, 1 - member)
    if bit == X:
        return (batch, 1 - half, member)
    stride = (4, 2, 1)[bit]
    return (batch + stride * (1 - 2 * my_bits()[bit]), half, member)


def remote(src, dst, send, recv, bit):
    return pltpu.make_async_remote_copy(
        src_ref=src,
        dst_ref=dst,
        send_sem=send,
        recv_sem=recv,
        device_id=device_across(bit),
        device_id_type=MESH_IDS,
    )


def greet(bits):
    barrier = pltpu.get_barrier_semaphore()
    for bit in bits:
        pl.semaphore_signal(barrier, inc=1, device_id=device_across(bit), device_id_type=MESH_IDS)
    pl.semaphore_wait(barrier, len(bits))


class Sums:
    def __init__(self, send_sem, recv_sem):
        self.bits = my_bits()
        self.send_sem, self.recv_sem = send_sem, recv_sem
        self.pieces = {}

    def add(self, number, source, dims, order, slots, cut=()):
        self.pieces[number] = (source, dims, order, slots, cut)

    def side(self, number, depth, across):
        source, dims, order, slots, cut = self.pieces[number]
        bit = order[depth]
        value = 1 - self.bits[bit] if across else self.bits[bit]
        left = [b for b in dims if b not in order[:depth]]
        spot = left.index(bit)
        index = (ALL,) * (1 + spot) + (value,)
        if depth:
            return slots[depth - 1].at[index]
        return source.at[index + (ALL,) * (len(left) - 1 - spot) + cut]

    def copy(self, number, depth):
        _, _, order, slots, _ = self.pieces[number]
        return remote(
            self.side(number, depth, True),
            slots[depth],
            self.send_sem.at[number, depth],
            self.recv_sem.at[number, depth],
            order[depth],
        )

    def send(self, number, depth):
        self.copy(number, depth).start()

    def take(self, number, depth):
        _, _, order, slots, _ = self.pieces[number]
        self.copy(number, depth).wait_recv()
        mine = self.side(number, depth, False)[...]
        if depth == len(order) - 1:
            return mine.astype(F32) + slots[depth][...].astype(F32)
        slots[depth][...] = mine + slots[depth][...]
        self.send(number, depth + 1)
        return None

    def finish(self):
        for number, (_, _, order, _, _) in self.pieces.items():
            for depth in range(len(order)):
                self.copy(number, depth).wait_send()


def slot_shapes(lead, count, tail):
    return [pltpu.VMEM((lead,) + (2,) * (count - 1 - depth) + tail, BF16) for depth in range(count)]


ORDERS = ((X, Y, Z_LOW, Z_HIGH), (Y, Z_LOW, X, Z_HIGH), (Z_LOW, X, Y, Z_HIGH))
IN_CUTS = ((0, 16), (16, 16), (32, 32))
DOWN_CUTS = ((0, 384), (384, 384), (768, 256))
OUT_CUTS = ((0, 128), (128, 128), (256, 256))
LATER_DIMS = (
    (Z_HIGH, Z_LOW, Y),
    (Z_HIGH, Z_LOW, X),
    (Z_HIGH, Y, X),
    (Z_LOW, Y, Z_HIGH),
    (Z_LOW, Z_HIGH, X),
    (Y, Z_HIGH, X),
)


def in_vmem():
    return pl.BlockSpec(memory_space=pltpu.VMEM)


def anywhere():
    return pl.BlockSpec(memory_space=pl.ANY)


def params(collective):
    return pltpu.CompilerParams(
        collective_id=collective, has_side_effects=True, vmem_limit_bytes=VMEM_BYTES
    )


def attend_forward(q, k, v, segment, block_of, bias, tile=512):
    length, width = q.shape
    pairs = width // LANES
    tiles = length // tile
    blocks = bias.shape[1]
    own = length // 2

    def body(*refs):
        q_ref, k_ref, v_ref, seg_ref, blk_ref, bias_ref = refs[:6]
        ctx_ref, qa_ref, fk_ref, other_ref = refs[6:10]
        fq_ref, ka_ref, made_ref, send_sem, recv_sem = refs[10:]
        pair, step = pl.program_id(0), pl.program_id(1)
        numbers = lax.broadcasted_iota(jnp.int32, (8, length), 0).astype(F32)
        same = seg_ref[...] == numbers

        @pl.when((pair == 0) & (step == 0))
        def _():
            greet((MEMBER,))
            count = lax.broadcasted_iota(jnp.int32, (blocks, length), 0).astype(F32)
            here = jnp.where(blk_ref[...] == count, 1.0, 0.0)
            rest = jnp.zeros((HD - 8 - 2 * blocks, length), F32)
            apart = jnp.where(same | (numbers >= SEG_VALUES), 0.0, NEG)
            feats = jnp.concatenate([apart, here, here, rest], axis=0)
            fq_ref[...] = jnp.concatenate([feats, feats], axis=0).T.astype(BF16)

        @pl.when(step == 0)
        def _():
            rest = jnp.zeros((HD - 16 - 2 * blocks, length), F32)
            ones = jnp.where(numbers < 3, 1.0, 0.0)
            sides = []
            for parity in (1, 0):
                full = bias_ref[parity]
                high = full.astype(BF16).astype(F32)
                sides += [jnp.where(same, 1.0, 0.0), high, full - high, ones, rest]
            feats = jnp.concatenate(sides, axis=0).T.astype(BF16)
            fk_ref[0] = feats
            low_half = lax.broadcasted_iota(jnp.int32, (length, LANES), 1) < HD
            keys = k_ref[...]
            ka_ref[0] = jnp.where(low_half, keys, feats)
            ka_ref[1] = jnp.where(low_half, feats, keys)

        lane = lax.broadcasted_iota(jnp.int32, (tile, LANES), 1)
        low_half = lane < HD
        scaled = q_ref[...] * jnp.asarray(HD ** (-0.5), BF16)
        place = pl.ds(pl.multiple_of(step * tile, tile), tile)
        feats = fq_ref[place, :]
        results = []
        for parity in range(2):
            if parity == 0:
                rows = jnp.where(low_half, scaled, feats)
                first = HD + 8 + 2 * blocks
            else:
                rows = jnp.where(low_half, feats, scaled)
                first = 8 + 2 * blocks
            scores = dot_nt(rows, ka_ref[parity])
            top = jnp.max(scores, axis=-1, keepdims=True)
            weights = jnp.exp(scores - top)
            total = jnp.sum(weights, axis=-1, keepdims=True)
            mixed = dot_nn(weights.astype(BF16), v_ref[...])
            results.append(mixed / total)
            hi, mid, low = three_parts(-(top + jnp.log(total)))
            rows = jnp.where(lane == first, hi, rows)
            rows = jnp.where(lane == first + 1, mid, rows)
            rows = jnp.where(lane == first + 2, low, rows)
            qa_ref[parity] = rows
        context = jnp.where(low_half, results[0], results[1]).astype(BF16)
        ctx_ref[...] = context
        made_ref[pair, place, :] = context

        def swaps(one_pair):
            cols = pl.ds(pl.multiple_of(one_pair * LANES, LANES), LANES)
            return [
                remote(
                    made_ref.at[one_pair, pl.ds(from_row, own)],
                    other_ref.at[pl.ds(own - from_row, own), cols],
                    send_sem.at[side, one_pair],
                    recv_sem.at[side, one_pair],
                    MEMBER,
                )
                for side, from_row in enumerate((0, own))
            ]

        @pl.when(step == tiles - 1)
        def _():
            for one in swaps(pair):
                one.start()

        @pl.when((pair == pairs - 1) & (step == tiles - 1))
        def _():
            for one_pair in range(pairs):
                for one in swaps(one_pair):
                    one.wait()

    return pl.pallas_call(
        body,
        grid=(pairs, tiles),
        out_shape=(
            jax.ShapeDtypeStruct((length, width), BF16),
            jax.ShapeDtypeStruct((2 * pairs, length, LANES), BF16),
            jax.ShapeDtypeStruct((pairs, length, LANES), BF16),
            jax.ShapeDtypeStruct((length, width), BF16),
        ),
        in_specs=[
            pl.BlockSpec((tile, LANES), lambda p, t: (t, p)),
            pl.BlockSpec((length, LANES), lambda p, t: (0, p)),
            pl.BlockSpec((length, LANES), lambda p, t: (0, p)),
            pl.BlockSpec((1, length), lambda p, t: (0, 0)),
            pl.BlockSpec((1, length), lambda p, t: (0, 0)),
            pl.BlockSpec((2, blocks, length), lambda p, t: (p, 0, 0)),
        ],
        out_specs=(
            pl.BlockSpec((tile, LANES), lambda p, t: (t, p)),
            pl.BlockSpec((2, tile, LANES), lambda p, t: (p, t, 0)),
            pl.BlockSpec((1, length, LANES), lambda p, t: (p, 0, 0)),
            anywhere(),
        ),
        scratch_shapes=[
            pltpu.VMEM((length, LANES), BF16),
            pltpu.VMEM((2, length, LANES), BF16),
            pltpu.VMEM((pairs, length, LANES), BF16),
            pltpu.SemaphoreType.DMA((2, pairs)),
            pltpu.SemaphoreType.DMA((2, pairs)),
        ],
        compiler_params=params(4),
        name="attend_forward",
    )(q, k, v, segment, block_of, bias)


def feed_forward(context, context_other, tokens, w_out, vectors, cot, w_in, in_bias, w_down):
    rows = cot.shape[0]
    own = rows // 2
    width = context.shape[1]
    chunk = 4 * LANES
    steps = 4
    share = D // 16
    root = (2.0 / np.pi) ** 0.5
    cube = 0.044715

    def group(j):
        bits = my_bits()
        z_low = jnp.where(j < 2, 1 - bits[Z_LOW], bits[Z_LOW])
        return z_low, jnp.where(lax.rem(j, 2) == 0, 1 - bits[Y], bits[Y])

    def body(*refs):
        ctx_ref, other_ref, tok_ref, wo_ref, wo2_ref, vec_ref, c_ref = refs[:7]
        wi_refs, b_refs, wd_refs = refs[7:11], refs[11:15], refs[15:19]
        out_ref, out_got, dn_ref, dn_got, mid_ref, gb_ref = refs[19:25]
        keep, got = refs[25:31], refs[31:37]
        n_ref, nt_ref, out_acc, dn_acc, out_send, dn_send, gi_ref, gd_ref = refs[37:45]
        send_sem, recv_sem, keep_sem, swap_sem = refs[45:]
        step = pl.program_id(0)
        bits = my_bits()
        z_low, y = group(step)
        slot = 2 * z_low + y

        @pl.when(step == 0)
        def _():
            greet((Z_LOW, Y, X, MEMBER))
            mid = (
                tok_ref[...].astype(F32)
                + dot_nn(ctx_ref[...], wo_ref[...])
                + dot_nn(other_ref[...], wo2_ref[...])
                + vec_ref[0:1]
            )
            mid_ref[...] = mid
            unit, _ = normalise(mid)
            n2 = (unit * vec_ref[1:2] + vec_ref[2:3]).astype(BF16)
            n_ref[:own] = n2
            swap = remote(
                n_ref.at[pl.ds(0, own)], n_ref.at[pl.ds(own, own)], swap_sem.at[0, 0], swap_sem.at[1, 0], MEMBER
            )
            swap.start()
            nt_ref[:, :own] = turned(n2)
            swap.wait()
            nt_ref[:, own:] = turned(n_ref[own:])

        wi = jnp.concatenate([ref[...] for ref in wi_refs], axis=1)
        wd = jnp.concatenate([ref[...] for ref in wd_refs], axis=0)
        pre = dot_nn(n_ref[...], wi) + jnp.concatenate([ref[...] for ref in b_refs], axis=1)
        square = pre * pre
        th = jnp.tanh(root * pre * (1.0 + cube * square))
        half_up = 0.5 * (1.0 + th)
        hidden = (pre * half_up).astype(BF16)
        slope = half_up + 0.5 * pre * (1.0 - th * th) * (root * (1.0 + 3.0 * cube * square))

        def in_part(kind, at):
            bit = (X, Y, Z_LOW)[kind]
            rest = (ALL,) * (3 - bit) + (pl.ds(*IN_CUTS[kind]),)
            return lambda side: gi_ref.at[(at,) + (ALL,) * bit + (side,) + rest]

        def copies(kind, at, where, bit):
            return (
                lambda: remote(
                    where(1 - bits[bit]), got[kind].at[at], send_sem.at[kind, at], recv_sem.at[kind, at], bit
                ),
                lambda: pltpu.make_async_copy(where(bits[bit]), keep[kind].at[at], keep_sem.at[kind, at]),
            )

        def in_copies(kind, at):
            return copies(kind, at, in_part(kind, at), (X, Y, Z_LOW)[kind])

        def x_copies(at):
            return copies(3, at, lambda side: gd_ref.at[at, :, side, :, pl.ds(*DOWN_CUTS[0])], X)

        def y_copies(z):
            return copies(4, z, lambda side: gd_ref.at[2 * z + side, :, :, :, pl.ds(*DOWN_CUTS[1])], Y)

        def z_copies(at_y):
            return copies(
                5, at_y, lambda side: gd_ref.at[2 * side + at_y, :, :, :, pl.ds(*DOWN_CUTS[2])], Z_LOW
            )

        gd_ref[slot] = dot_tn(hidden, c_ref[...]).astype(BF16).reshape(2, 2, LANES, D)
        for one in x_copies(slot):
            one().start()

        @pl.when(lax.rem(step, 2) == 0)
        def _():
            y_copies(z_low)[0]().start()

        @pl.when(lax.rem(step, 2) == 1)
        def _():
            y_copies(z_low)[1]().start()

        @pl.when(step < 2)
        def _():
            z_copies(y)[0]().start()

        @pl.when(step >= 2)
        def _():
            z_copies(y)[1]().start()

        pre_grad = (dot_nt(c_ref[...], wd) * slope).astype(BF16)
        gb_ref[...] = jnp.sum(pre_grad.astype(F32), axis=0, keepdims=True)
        gi_ref[slot] = dot_nn(nt_ref[...], pre_grad).astype(BF16).reshape(2, 2, 2, 2, share, chunk)
        for kind in range(3):
            for one in in_copies(kind, slot):
                one().start()

        @pl.when(step == 0)
        def _():
            dn_acc[...] = dot_nt(pre_grad, wi)
            out_acc[...] = dot_nn(hidden, wd)

        @pl.when(step > 0)
        def _():
            dn_acc[...] += dot_nt(pre_grad, wi)
            out_acc[...] += dot_nn(hidden, wd)

        @pl.when(step == steps - 1)
        def _():
            dn_send[...] = dn_acc[own:].astype(BF16)
            out_send[...] = out_acc[own:].astype(BF16)
            swaps = [
                remote(dn_send, dn_got, swap_sem.at[0, 1], swap_sem.at[1, 1], MEMBER),
                remote(out_send, out_got, swap_sem.at[0, 2], swap_sem.at[1, 2], MEMBER),
            ]
            for one in swaps:
                one.start()
            dn_ref[...] = dn_acc[:own]
            out_ref[...] = mid_ref[...] + out_acc[:own] + vec_ref[3:4]
            for at in range(4):
                for kind in range(3):
                    for one in in_copies(kind, at):
                        one().wait()
                for one in x_copies(at):
                    one().wait()
            for at in range(2):
                for one in y_copies(at) + z_copies(at):
                    one().wait()
            for one in swaps:
                one.wait()

    def unit(z_high, x):
        def at(j):
            z_low, y = group(j)
            return 2 * (((2 * z_high + z_low) * 2 + y) * 2 + x) + lax.axis_index("member")

        return at

    units = [unit(z_high, x) for z_high in range(2) for x in range(2)]

    def column(u):
        return lambda j: (0, u(j))

    def row(u):
        return lambda j: (u(j), 0)

    def slot_of(j):
        z_low, y = group(j)
        return (0, 2 * z_low + y)

    whole = pl.BlockSpec((rows, D), lambda j: (0, 0))
    half = pl.BlockSpec((own, D), lambda j: (0, 0))
    half_ctx = pl.BlockSpec((own, width), lambda j: (0, 0))
    parts = [jax.ShapeDtypeStruct((4, 2, 2, 2, size, chunk), BF16) for _, size in IN_CUTS] + [
        jax.ShapeDtypeStruct((4, 2, LANES, DOWN_CUTS[0][1]), BF16),
        jax.ShapeDtypeStruct((2, 2, 2, LANES, DOWN_CUTS[1][1]), BF16),
        jax.ShapeDtypeStruct((2, 2, 2, LANES, DOWN_CUTS[2][1]), BF16),
    ]
    own_f32 = jax.ShapeDtypeStruct((own, D), F32)
    own_bf16 = jax.ShapeDtypeStruct((own, D), BF16)
    results = pl.pallas_call(
        body,
        grid=(steps,),
        out_shape=[
            own_f32,
            own_bf16,
            own_f32,
            own_bf16,
            own_f32,
            jax.ShapeDtypeStruct((1, steps * chunk), F32),
        ]
        + parts
        + parts,
        in_specs=[
            half_ctx,
            half_ctx,
            half,
            pl.BlockSpec((width, D), lambda j: (lax.axis_index("member"), 0)),
            pl.BlockSpec((width, D), lambda j: (1 - lax.axis_index("member"), 0)),
            pl.BlockSpec((8, D), lambda j: (0, 0)),
            whole,
        ]
        + [pl.BlockSpec((D, LANES), column(u)) for u in units]
        + [pl.BlockSpec((1, LANES), column(u)) for u in units]
        + [pl.BlockSpec((LANES, D), row(u)) for u in units],
        out_specs=[half, anywhere(), half, anywhere(), half, pl.BlockSpec((1, chunk), slot_of)]
        + [anywhere()] * 12,
        scratch_shapes=[
            pltpu.VMEM((rows, D), BF16),
            pltpu.VMEM((D, rows), BF16),
            pltpu.VMEM((rows, D), F32),
            pltpu.VMEM((rows, D), F32),
            pltpu.VMEM((own, D), BF16),
            pltpu.VMEM((own, D), BF16),
            pltpu.VMEM((4, 2, 2, 2, 2, share, chunk), BF16),
            pltpu.VMEM((4, 2, 2, LANES, D), BF16),
            pltpu.SemaphoreType.DMA((6, 4)),
            pltpu.SemaphoreType.DMA((6, 4)),
            pltpu.SemaphoreType.DMA((6, 4)),
            pltpu.SemaphoreType.DMA((2, 3)),
        ],
        compiler_params=params(1),
        name="feed_forward",
    )(context, context_other, tokens, w_out, w_out, vectors, cot, *[w_in] * 4, *[in_bias] * 4, *[w_down] * 4)
    return results[:6], results[6:12], results[12:]


def attend_backward(
    rows_aug, k, v, feat_k, ctx, ctx_other, mid, n2_grad, n2_grad_got, cot, vectors, w_out, normed, w_qkv, kept, got,
    tile=256,
):
    length, width = k.shape
    pairs = width // LANES
    early = pairs // 2
    tiles = length // tile
    own = length // 2
    chunk = kept[0].shape[-1]
    shapes = [a.shape for a in kept[:3]] + [(1, 2, 2, 2, LANES, a.shape[-1]) for a in kept[3:]]
    kept = [a.reshape(shape) for a, shape in zip(kept, shapes)]
    got = [a.reshape(shape) for a, shape in zip(got, shapes)]
    share = D // 16
    count = 9 + 3 * early

    def body(*refs):
        qa_ref, k_ref, v_ref, fk_ref, ctx_ref, other_ref, mid_ref, dn2_ref, dn2_got, c_ref, vec_ref, wo_ref = refs[:12]
        n_ref, wq_ref, wk_ref, wv_ref = refs[12:16]
        keep_in, got_in = refs[16:22], refs[22:28]
        dn_ref, mg_ref, sum_ref, qb_ref, vb_ref, sum_in, sum_down, sum_out, sum_qkv, dn_got = refs[28:38]
        keep_new, got_new = refs[38:41], refs[41:44]
        ga_ref, acc_ref, nt_ref, slab_ref, dn_acc, dn_send, gq_ref, br_ref, g_ref, go_ref = refs[44:54]
        begin, first = refs[54:60], refs[60:66]
        slots = refs[66 : 66 + 18 + 12 + 12 * early]
        send_sem, recv_sem, load_sem, new_send, new_recv, new_keep, swap_sem = refs[66 + 30 + 12 * early :]
        pair, step = pl.program_id(0), pl.program_id(1)
        now = pair * tiles + step
        member = lax.axis_index("member")

        sums = Sums(send_sem, recv_sem)
        for kind in range(6):
            sums.add(kind, begin[kind], LATER_DIMS[kind], ORDERS[kind % 3][1:], slots[3 * kind : 3 * kind + 3])
        for kind in range(3):
            sums.add(
                6 + kind,
                go_ref,
                CHIP,
                ORDERS[kind],
                slots[18 + 4 * kind : 22 + 4 * kind],
                (ALL, pl.ds(*OUT_CUTS[kind])),
            )
        for one_pair in range(early):
            for kind in range(3):
                number = 9 + 3 * one_pair + kind
                sums.add(
                    number,
                    gq_ref.at[one_pair, pl.ds(kind, 1)],
                    CHIP,
                    ORDERS[kind],
                    slots[30 + 4 * (number - 9) : 34 + 4 * (number - 9)],
                )

        def loads(kind):
            return (
                pltpu.make_async_copy(keep_in[kind], begin[kind], load_sem.at[0, kind]),
                pltpu.make_async_copy(got_in[kind], first[kind], load_sem.at[1, kind]),
            )

        def end_sum(number):
            total = sums.take(number, len(sums.pieces[number][2]) - 1)
            if number < 3:
                for z_low in range(2):
                    for y in range(2):
                        for z_high in range(2):
                            for x in range(2):
                                unit = ((2 * z_high + z_low) * 2 + y) * 2 + x
                                local = (2 * z_high + x) * LANES
                                sum_in[pl.ds(*IN_CUTS[number]), unit * LANES : (unit + 1) * LANES] = total[
                                    2 * z_low + y, :, local : local + LANES
                                ]
            elif number < 6:
                sum_down[:, pl.ds(*DOWN_CUTS[number - 3])] = total[0]
            elif number < 9:
                sum_out[:, pl.ds(*OUT_CUTS[number - 6])] = total[0]
            else:
                one_pair, kind = (number - 9) // 3, (number - 9) % 3
                place = (kind * early + one_pair) * LANES
                sum_qkv[:, place : place + LANES] = total[0]

        def at(when, depth, *numbers):
            @pl.when(now == when)
            def _():
                for number in numbers:
                    if depth == len(sums.pieces[number][2]) - 1:
                        end_sum(number)
                    else:
                        sums.take(number, depth)

        @pl.when(now == 0)
        def _():
            greet((Z_HIGH, Z_LOW, Y, X, MEMBER))
            for kind in range(6):
                for one in loads(kind):
                    one.start()
            unit, scale = normalise(mid_ref[...])
            grad = dn2_ref[...] + dn2_got[...].astype(F32)
            cot_own = c_ref[...].astype(F32)
            mid_grad = cot_own + normalise_back(unit, scale, grad * vec_ref[1:2])
            mg_ref[...] = mid_grad
            branch = mid_grad.astype(BF16)
            br_ref[:own] = branch
            swap = remote(
                br_ref.at[pl.ds(0, own)], br_ref.at[pl.ds(own, own)], swap_sem.at[0, 0], swap_sem.at[1, 0], MEMBER
            )
            swap.start()
            for kind in range(6):
                for one in loads(kind):
                    one.wait()
                begin[kind][...] = begin[kind][...] + first[kind][...]
                sums.send(kind, 0)
            sum_ref[0:1] = jnp.sum(branch.astype(F32), axis=0, keepdims=True)
            sum_ref[1:2] = jnp.sum(grad * unit, axis=0, keepdims=True)
            sum_ref[2:3] = jnp.sum(grad, axis=0, keepdims=True)
            sum_ref[3:4] = jnp.sum(cot_own, axis=0, keepdims=True)
            sum_ref[4:8] = jnp.zeros((4, D), F32)
            nt_ref[...] = turned(n_ref[...])
            swap.wait()
            g_ref[...] = dot_nt(br_ref[...], wo_ref[...]).astype(BF16)
            columns = br_ref[:, pl.ds(pl.multiple_of(member * width, width), width)]
            go_ref[0, member] = dot_tn(ctx_ref[...], columns).astype(BF16).reshape(2, 2, 2, share, width)
            go_ref[0, 1 - member] = dot_tn(other_ref[...], columns).astype(BF16).reshape(2, 2, 2, share, width)
            for kind in range(6, 9):
                sums.send(kind, 0)

        at(1, 0, 0, 1, 2)
        at(2, 0, 3, 4, 5)
        at(4, 0, 6, 7, 8)
        at(5, 1, 0, 1, 2)
        at(6, 1, 3, 4, 5)
        at(6, 0, 9, 10, 11)
        at(7, 1, 6, 7, 8)
        at(8, 1, 9, 10, 11)
        at(9, 2, 0, 1, 2)
        at(9, 2, 6, 7, 8)
        at(10, 0, 12, 13, 14)
        at(11, 2, 3, 4, 5)
        at(11, 2, 9, 10, 11)
        at(12, 1, 12, 13, 14)
        at(13, 3, 6, 7, 8)
        at(14, 2, 12, 13, 14)
        at(14, 3, 9, 10, 11)

        slab_cols = pl.ds(pl.multiple_of(pair * LANES, LANES), LANES)

        @pl.when(step == 0)
        def _():
            lane = lax.broadcasted_iota(jnp.int32, (length, LANES), 1)
            low_half = lane < HD
            grads = g_ref[:, slab_cols]
            prod = grads.astype(F32) * ctx_ref[:, slab_cols].astype(F32)
            for parity in range(2):
                mine = low_half if parity == 0 else jnp.logical_not(low_half)
                lead = HD if parity == 0 else 0
                delta = -jnp.sum(jnp.where(mine, prod, 0.0), axis=-1, keepdims=True)
                hi, mid, low = three_parts(delta)
                rows = jnp.where(mine, grads, jnp.zeros_like(grads))
                rows = jnp.where(lane == lead, hi, rows)
                rows = jnp.where(lane == lead + 1, mid, rows)
                ga_ref[parity] = jnp.where(lane == lead + 2, low, rows)
            ga_ref[2] = grads
            acc_ref[...] = jnp.zeros_like(acc_ref)

        lane = lax.broadcasted_iota(jnp.int32, (tile, LANES), 1)
        low_half = lane < HD
        keys = k_ref[...]
        values = v_ref[...]
        feats = fk_ref[0]
        keys_t = turned(keys)
        dks, dvs = [], []
        for parity in range(2):
            lead = HD if parity == 0 else 0
            mine = low_half if parity == 0 else jnp.logical_not(low_half)
            key_rows = jnp.where(mine, keys, feats)
            ones = jnp.where((lane >= lead) & (lane < lead + 3), 1.0, 0.0).astype(BF16)
            value_rows = jnp.where(mine, values, ones)
            probs = jnp.exp(dot_nt(key_rows, qa_ref[parity]))
            diff = dot_nt(value_rows, ga_ref[parity])
            score_grad = (probs * diff).astype(BF16)
            dvs.append(dot_nn(probs.astype(BF16), ga_ref[2]))
            dks.append(dot_nn(score_grad, qa_ref[parity]))
            side = keys_t[parity * HD : (parity + 1) * HD]
            acc_ref[parity * HD : (parity + 1) * HD] += dot_nn(side, score_grad)
        place = pl.ds(pl.multiple_of(step * tile, tile), tile)
        slab_ref[place, LANES : 2 * LANES] = jnp.where(low_half, dks[0], dks[1]).astype(BF16)
        slab_ref[place, 2 * LANES :] = jnp.where(low_half, dvs[0], dvs[1]).astype(BF16)

        def new_copies(kind, late):
            bit = (X, Y, Z_LOW)[kind]
            whole = gq_ref.at[early + late, kind]
            return (
                pltpu.make_async_copy(
                    whole.at[(ALL,) * bit + (sums.bits[bit],)], keep_new[kind].at[late], new_keep.at[kind, late]
                ),
                remote(
                    whole.at[(ALL,) * bit + (1 - sums.bits[bit],)],
                    got_new[kind].at[late],
                    new_send.at[kind, late],
                    new_recv.at[kind, late],
                    bit,
                ),
            )

        @pl.when(step == tiles - 1)
        def _():
            slab_ref[:, :LANES] = (acc_ref[...].T * HD ** (-0.5)).astype(BF16)
            slabs = slab_ref[...]
            made = dot_nn(nt_ref[...], slabs).astype(BF16)
            for kind in range(3):
                gq_ref[pair, kind] = made[:, kind * LANES : (kind + 1) * LANES].reshape(
                    2, 2, 2, 2, share, LANES
                )
            for one_pair in range(pairs):

                @pl.when(pair == one_pair)
                def _(one_pair=one_pair):
                    for kind in range(3):
                        if one_pair < early:
                            sums.send(9 + 3 * one_pair + kind, 0)
                        else:
                            for one in new_copies(kind, one_pair - early):
                                one.start()

            qb_ref[...] = jnp.sum(slabs[:, :LANES].astype(F32), axis=0, keepdims=True)
            vb_ref[...] = jnp.sum(slabs[:, 2 * LANES :].astype(F32), axis=0, keepdims=True)
            weights = jnp.concatenate([wq_ref[...], wk_ref[...], wv_ref[...]], axis=1)
            grown = dot_nt(slabs, weights)

            @pl.when(pair == 0)
            def _():
                dn_acc[...] = grown

            @pl.when(pair > 0)
            def _():
                dn_acc[...] += grown

        @pl.when(now == pairs * tiles - 1)
        def _():
            dn_send[...] = dn_acc[own:, :].astype(BF16)
            swap = remote(dn_send, dn_got, swap_sem.at[0, 1], swap_sem.at[1, 1], MEMBER)
            swap.start()
            dn_ref[...] = dn_acc[:own, :]
            for number in range(12, 15):
                end_sum(number)
            for late in range(pairs - early):
                for kind in range(3):
                    for one in new_copies(kind, late):
                        one.wait()
            sums.finish()
            swap.wait()

    part = pl.BlockSpec((tile, LANES), lambda p, t: (t, p))
    bias_part = pl.BlockSpec((1, LANES), lambda p, t: (0, p))

    def columns(which):
        return pl.BlockSpec(
            (D, LANES), lambda p, t: (0, (2 * which + lax.axis_index("member")) * pairs + p)
        )

    slots = []
    for shape in shapes:
        slots += slot_shapes(shape[0], 3, shape[4:])
    for _, size in OUT_CUTS:
        slots += slot_shapes(1, 4, (share, size))
    for _ in range(3 * early):
        slots += slot_shapes(1, 4, (share, LANES))
    new = [jax.ShapeDtypeStruct((pairs - early, 2, 2, 2, share, LANES), BF16)] * 3
    own_f32 = jax.ShapeDtypeStruct((own, D), F32)
    results = pl.pallas_call(
        body,
        grid=(pairs, tiles),
        out_shape=[
            own_f32,
            own_f32,
            jax.ShapeDtypeStruct((8, D), F32),
            jax.ShapeDtypeStruct((1, width), F32),
            jax.ShapeDtypeStruct((1, width), F32),
            jax.ShapeDtypeStruct((share, 4 * chunk), F32),
            jax.ShapeDtypeStruct((LANES, D), F32),
            jax.ShapeDtypeStruct((share, width), F32),
            jax.ShapeDtypeStruct((share, 3 * early * LANES), F32),
            jax.ShapeDtypeStruct((own, D), BF16),
        ]
        + new
        + new,
        in_specs=[
            pl.BlockSpec((2, length, LANES), lambda p, t: (p, 0, 0)),
            part,
            part,
            pl.BlockSpec((1, tile, LANES), lambda p, t: (p, t, 0)),
            in_vmem(),
            in_vmem(),
            in_vmem(),
            in_vmem(),
            in_vmem(),
            pl.BlockSpec((own, D), lambda p, t: (0, 0)),
            in_vmem(),
            pl.BlockSpec((width, D), lambda p, t: (lax.axis_index("member"), 0)),
            in_vmem(),
            columns(0),
            columns(1),
            columns(2),
        ]
        + [anywhere()] * 12,
        out_specs=[in_vmem(), in_vmem(), in_vmem(), bias_part, bias_part]
        + [in_vmem()] * 4
        + [anywhere()] * 7,
        scratch_shapes=[
            pltpu.VMEM((3, length, LANES), BF16),
            pltpu.VMEM((LANES, length), F32),
            pltpu.VMEM((D, length), BF16),
            pltpu.VMEM((length, 3 * LANES), BF16),
            pltpu.VMEM((length, D), F32),
            pltpu.VMEM((own, D), BF16),
            pltpu.VMEM((pairs, 3, 2, 2, 2, 2, share, LANES), BF16),
            pltpu.VMEM((length, D), BF16),
            pltpu.VMEM((length, width), BF16),
            pltpu.VMEM((1, 2, 2, 2, 2, share, width), BF16),
        ]
        + [pltpu.VMEM(shape, BF16) for shape in shapes]
        + [pltpu.VMEM(shape, BF16) for shape in shapes]
        + slots
        + [
            pltpu.SemaphoreType.DMA((count, 4)),
            pltpu.SemaphoreType.DMA((count, 4)),
            pltpu.SemaphoreType.DMA((2, 6)),
            pltpu.SemaphoreType.DMA((3, pairs - early)),
            pltpu.SemaphoreType.DMA((3, pairs - early)),
            pltpu.SemaphoreType.DMA((3, pairs - early)),
            pltpu.SemaphoreType.DMA((2, 2)),
        ],
        compiler_params=params(3),
        name="attend_backward",
    )(
        rows_aug, k, v, feat_k, ctx, ctx_other, mid, n2_grad, n2_grad_got, cot, vectors, w_out, normed,
        w_qkv, w_qkv, w_qkv, *kept, *got,
    )
    return results[:10], results[10:13], results[13:]


def finish(tokens, mid_grad, normed_grad, normed_grad_got, vectors, sums_in, in_bias_rows, q_sum, v_sum, ready, kept, got):
    own = mid_grad.shape[0]
    rows = own // 2
    width = q_sum.shape[1]
    late, share = kept[0].shape[0], kept[0].shape[-2]
    per = share // 2
    last = 3 * late * LANES + LANES

    def body(*refs):
        tok_ref, mg_ref, dn_ref, dn_got, vec_ref, sum_ref, inb_ref, qb_ref, vb_ref, ready_ref = refs[:10]
        keep, first = refs[10:13], refs[13:16]
        ig_ref, ig_got, ready_got, last_ref, last_got = refs[16:21]
        ig_send, source, last_all, flat = refs[21:25]
        begin, slots = refs[25:28], refs[28:41]
        send_sem, recv_sem, swap_sem = refs[41:]
        member = lax.axis_index("member")
        greet((Z_HIGH, Z_LOW, Y, X, MEMBER))
        sums = Sums(send_sem, recv_sem)
        for kind in range(3):
            dims = tuple(b for b in CHIP if b != ORDERS[kind][0])
            sums.add(kind, begin[kind], dims, ORDERS[kind][1:], slots[3 * kind : 3 * kind + 3])
            begin[kind][...] = keep[kind][...] + first[kind][...]
            sums.send(kind, 0)
        sums.add(3, source, CHIP, ORDERS[1], slots[9:13])
        theirs = pl.ds(pl.multiple_of((1 - member) * per, per), per)
        swaps = [
            remote(ready_ref.at[theirs], ready_got, swap_sem.at[0, 0], swap_sem.at[1, 0], MEMBER)
        ]
        swaps[0].start()

        unit, scale = normalise(tok_ref[...].astype(F32))
        grad = dn_ref[...] + dn_got[...].astype(F32)
        flat[0:1] = jnp.sum(grad * unit, axis=0, keepdims=True)
        flat[1:2] = jnp.sum(grad, axis=0, keepdims=True)
        flat[2:6] = sum_ref[0:4]
        blank = jnp.zeros((1, width), F32)
        for row, ref in ((6, qb_ref), (7, vb_ref)):
            value = ref[...]
            flat[row : row + 1, :width] = jnp.where(member == 0, value, blank)
            flat[row : row + 1, width:] = jnp.where(member == 1, value, blank)
        flat[8:16] = inb_ref[...]
        flat[16:] = jnp.zeros((LANES - 16, D), F32)
        source[...] = flat[...].T.astype(BF16).reshape(source.shape)
        sums.send(3, 0)
        input_grad = mg_ref[...] + normalise_back(unit, scale, grad * vec_ref[4:5])
        ig_send[...] = input_grad[rows:].astype(BF16)
        swaps.append(remote(ig_send, ig_got, swap_sem.at[0, 1], swap_sem.at[1, 1], X))
        swaps[1].start()
        ig_ref[...] = input_grad[:rows]

        for depth in range(3):
            for kind in range(3):
                total = sums.take(kind, depth)
                if depth == 2:
                    for pair in range(late):
                        place = (kind * late + pair) * LANES
                        last_all[:, place : place + LANES] = total[pair]
            sums.take(3, depth)
        last_all[:, last - LANES :] = sums.take(3, 3)[0]
        swaps.append(remote(last_all.at[theirs], last_got, swap_sem.at[0, 2], swap_sem.at[1, 2], MEMBER))
        swaps[2].start()
        last_ref[...] = last_all[...]
        sums.finish()
        for one in swaps:
            one.wait()

    slots = []
    for _ in range(3):
        slots += slot_shapes(late, 3, (share, LANES))
    slots += slot_shapes(1, 4, (share, LANES))
    return pl.pallas_call(
        body,
        out_shape=(
            jax.ShapeDtypeStruct((rows, D), F32),
            jax.ShapeDtypeStruct((rows, D), BF16),
            jax.ShapeDtypeStruct((per, ready.shape[1]), F32),
            jax.ShapeDtypeStruct((share, last), F32),
            jax.ShapeDtypeStruct((per, last), F32),
        ),
        in_specs=[in_vmem()] * 16,
        out_specs=(in_vmem(), anywhere(), anywhere(), in_vmem(), anywhere()),
        scratch_shapes=[
            pltpu.VMEM((rows, D), BF16),
            pltpu.VMEM((1, 2, 2, 2, 2, share, LANES), BF16),
            pltpu.VMEM((share, last), F32),
            pltpu.VMEM((LANES, D), F32),
        ]
        + [pltpu.VMEM(kept[0].shape, BF16)] * 3
        + slots
        + [
            pltpu.SemaphoreType.DMA((4, 4)),
            pltpu.SemaphoreType.DMA((4, 4)),
            pltpu.SemaphoreType.DMA((2, 3)),
        ],
        compiler_params=params(2),
        name="finish",
    )(
        tokens, mid_grad, normed_grad, normed_grad_got, vectors, sums_in, in_bias_rows, q_sum, v_sum, ready, *kept, *got
    )


def per_device_pair(
    tokens,
    ln1_gain,
    ln1_bias,
    w_qkv,
    q_bias,
    v_bias,
    w_out,
    out_bias,
    ln2_gain,
    ln2_bias,
    w_in,
    in_bias,
    w_down,
    down_bias,
    cotangent,
    segment_ids,
    random_blocks,
    global_blocks,
):
    rows = tokens.shape[0]
    own = 2 * rows
    length = segment_ids.shape[0]
    blocks = length // BLK
    half = lax.axis_index("half")
    member = lax.axis_index("member")
    mine_d = D // 2
    heads = HEADS // 2
    chips = lax.axis_size("batch") * 2

    def gather_rows(x):
        kept = lax.dynamic_index_in_dim(x, half, 1, keepdims=False)
        sent = lax.dynamic_index_in_dim(x, 1 - half, 1, keepdims=False)
        held = jnp.concatenate([kept, flip("half", sent)], axis=0)
        return jnp.concatenate([held, flip("member", held)], axis=0)

    def both_sequences(kept, other):
        return jnp.where(
            half == 0, jnp.stack([kept, other], axis=1), jnp.stack([other, kept], axis=1)
        )

    seq_tokens = gather_rows(tokens)
    later, _ = lax.optimization_barrier((cotangent, seq_tokens))
    cot = gather_rows(later)

    per_row = rows // BLK
    order = jnp.concatenate(
        [
            ((half + t) % 2 * 2 + (member + j) % 2) * per_row + jnp.arange(per_row, dtype=jnp.int32)
            for j in range(2)
            for t in range(2)
        ]
    )
    numbers = jnp.arange(blocks, dtype=jnp.int32)
    seq_random = lax.dynamic_index_in_dim(random_blocks, half, 1, keepdims=False)
    seq_random = lax.dynamic_slice_in_dim(seq_random, member * heads, heads, 1)
    seq_global = lax.dynamic_index_in_dim(global_blocks, half, 1, keepdims=False)
    seq_segment = lax.dynamic_index_in_dim(segment_ids, half, 1, keepdims=False).reshape(blocks, BLK)
    move = (order[:, None] == numbers).astype(F32)
    segment = jnp.sum(move[:, :, None] * seq_segment.astype(F32)[None], axis=1).reshape(1, length)
    block_of = jnp.broadcast_to(order.astype(F32)[:, None], (blocks, BLK)).reshape(1, length)
    hits = jnp.sum((seq_random[..., None] == order).astype(F32), axis=2)
    near = (jnp.abs(numbers[:, None] - order) <= 1).astype(F32)
    far = jnp.sum((seq_global[:, None] == order).astype(F32), axis=0)
    times = hits + (near + far)[:, None, :]
    bias = jnp.where(times > 0, jnp.log(jnp.maximum(times, 1.0)), NEG).transpose(1, 0, 2)
    bias = jnp.broadcast_to(bias[..., None], (heads, blocks, blocks, BLK)).reshape(heads, blocks, length)

    def columns(w, part):
        return lax.dynamic_slice_in_dim(w, part * D + member * mine_d, mine_d, 1)

    q_bias_mine = lax.dynamic_slice_in_dim(q_bias, member * mine_d, mine_d, 0)
    v_bias_mine = lax.dynamic_slice_in_dim(v_bias, member * mine_d, mine_d, 0)
    blank = jnp.zeros((D,), BF16)
    vectors = jnp.stack(
        [out_bias, ln2_gain, ln2_bias, down_bias, ln1_gain, blank, blank, blank]
    ).astype(F32)

    unit1, _ = normalise(seq_tokens.astype(F32))
    normed = (unit1 * ln1_gain.astype(F32) + ln1_bias.astype(F32)).astype(BF16)
    queries = (dot_nn(normed, columns(w_qkv, 0)) + q_bias_mine.astype(F32)).astype(BF16)
    keys = dot_nn(normed, columns(w_qkv, 1)).astype(BF16)
    values = (dot_nn(normed, columns(w_qkv, 2)) + v_bias_mine.astype(F32)).astype(BF16)

    context, rows_aug, feat_k, context_other = attend_forward(queries, keys, values, segment, block_of, bias)
    (out_part, out_got, n2_grad, n2_grad_got, mid_stream, in_bias_grad), kept_parts, got_parts = feed_forward(
        context,
        context_other,
        seq_tokens,
        w_out,
        vectors,
        cot,
        w_in,
        in_bias.astype(F32).reshape(1, -1),
        w_down,
    )
    output_own = (out_part + out_got.astype(F32)).astype(BF16)
    output = both_sequences(output_own[:rows], flip("half", output_own[rows:]))

    in_bias_rows = in_bias_grad.reshape(2, 2, 2, 2, 2, LANES // 2).transpose(4, 2, 0, 1, 3, 5).reshape(2, D)
    gone = jnp.zeros_like(in_bias_rows)
    in_bias_rows = jnp.concatenate(
        [
            jnp.where(member == 0, in_bias_rows, gone),
            jnp.where(member == 1, in_bias_rows, gone),
            jnp.zeros((4, D), F32),
        ]
    )

    (
        (
            normed_grad,
            mid_grad,
            sums_in,
            q_sum,
            v_sum,
            summed_in,
            summed_down,
            summed_out,
            summed_early,
            normed_grad_got,
        ),
        kept_qkv,
        got_qkv,
    ) = attend_backward(
        rows_aug,
        keys,
        values,
        feat_k,
        context,
        context_other,
        mid_stream,
        n2_grad,
        n2_grad_got,
        cot,
        vectors,
        w_out,
        normed,
        w_qkv,
        kept_parts,
        got_parts,
    )
    ready = jnp.concatenate([summed_in, summed_out, summed_early], axis=1)
    input_kept, input_other, ready_got, last_all, last_got = finish(
        seq_tokens[:own],
        mid_grad,
        normed_grad,
        normed_grad_got,
        vectors,
        sums_in,
        in_bias_rows,
        q_sum,
        v_sum,
        ready,
        kept_qkv,
        got_qkv,
    )
    input_grad = both_sequences(input_kept, input_other.astype(F32))

    per = ready.shape[0] // 2
    chip_rows = jnp.concatenate([ready, last_all], axis=1)
    mine_rows = lax.dynamic_slice_in_dim(chip_rows, member * per, per, 0)
    got_rows = jnp.concatenate([ready_got, last_got], axis=1)
    left = jnp.where(member == 0, mine_rows, got_rows)
    right = jnp.where(member == 0, got_rows, mine_rows)

    start_out = summed_in.shape[1]
    start_early = start_out + mine_d
    start_late = ready.shape[1]
    early = summed_early.shape[1] // 3
    late = mine_d - early
    pieces = []
    for part in range(3):
        for x in (left, right):
            pieces.append(x[:, start_early + part * early : start_early + (part + 1) * early])
            pieces.append(x[:, start_late + part * late : start_late + (part + 1) * late])
    w_qkv_grad = jnp.concatenate(pieces, axis=1)
    w_out_grad = jnp.concatenate([x[:, start_out : start_out + mine_d] for x in (left, right)], axis=1)
    w_in_grad = jnp.concatenate(
        [x[:, j * LANES : (j + 1) * LANES] for j in range(chips) for x in (left, right)], axis=1
    )
    start = start_late + 3 * late
    vector_sums = left[:, start : start + 8] + right[:, start : start + 8]
    in_mine = lax.dynamic_slice_in_dim(last_all, 3 * late + 8 + 2 * member, 2, 1)
    in_bias_out = in_mine.T.reshape(LANES)
    vec = [vector_sums[:, i] for i in range(8)]
    return (
        output,
        input_grad,
        vec[0],
        vec[1],
        w_qkv_grad,
        vec[6],
        vec[7],
        w_out_grad,
        vec[2],
        vec[3],
        vec[4],
        w_in_grad,
        in_bias_out,
        summed_down,
        vec[5],
    )


def solution(mesh):
    def program(*args):
        sequences = args[0].shape[1] // mesh.shape["batch"]
        seq = mesh.shape["seq"]
        fast = sequences == 2 and seq == 4 and mesh.shape["batch"] == 8
        if fast:
            use = jax.sharding.Mesh(
                mesh.devices.reshape(mesh.shape["batch"], 2, 2), ("batch", "half", "member")
            )
            seq_axes, all_axes, run = ("half", "member"), ("batch", "half", "member"), per_device_pair
        else:
            use, seq_axes, all_axes, run = mesh, "seq", ("batch", "seq"), per_device
        rows = P(seq_axes, "batch", None)
        in_specs = (rows,) + (P(),) * 13 + (
            rows,
            P(None, "batch"),
            P(None, "batch", None, None),
            P(None, "batch"),
        )
        vector, matrix = P(all_axes), P(all_axes, None)
        out_specs = (
            rows,
            rows,
            vector,
            vector,
            matrix,
            vector,
            vector,
            matrix,
            vector,
            vector,
            vector,
            matrix,
            vector,
            matrix,
            vector,
        )
        return jax.shard_map(
            run, mesh=use, in_specs=in_specs, out_specs=out_specs, check_vma=False
        )(*args)

    return program
```

```python
import jax
import jax.numpy as jnp
import numpy as np
from jax import lax
from jax.experimental import pallas as pl
from jax.experimental.pallas import tpu as pltpu
from jax.sharding import PartitionSpec as P

D = 1024
HEADS = 16
HD = 64
BLK = 64
RAND = 3
GLOB = 2


eps = 1e-05


def padded(x, sides, width):
    for axis, dim in sides:
        size, length = (lax.axis_size(axis), x.shape[dim])
        up = [(i, (i + 1) % size) for i in range(size - 1)]
        down = [(j, i) for i, j in up]
        last = lax.slice_in_dim(x, length - width, length, axis=dim)
        initial = lax.slice_in_dim(x, 0, width, axis=dim)
        before = lax.ppermute(last, axis, up)
        after = lax.ppermute(initial, axis, down)
        x = jnp.concatenate([before, x, after], axis=dim)
    return x


def layer_norm(values, gain_vec, shift_vec):
    row_mean = jnp.mean(values, axis=-1, keepdims=True)
    centred = values - row_mean
    spread = jnp.mean(centred * centred, axis=-1, keepdims=True)
    return centred * lax.rsqrt(spread + eps) * gain_vec + shift_vec


def gelu_tanh(values):
    return jax.nn.gelu(values, approximate=True)


def window_stack(extended, query_blocks):
    return jnp.stack(
        [extended[0:query_blocks], extended[1 : query_blocks + 1], extended[2 : query_blocks + 2]],
        axis=1,
    )


def pick_blocks(shard_rows, random_local, global_blocks):
    block_total = shard_rows.shape[0] // BLK
    seq_count = shard_rows.shape[1]
    numbers = jnp.arange(block_total, dtype=jnp.int32)
    random_hits = (random_local[..., None] == numbers).astype(jnp.bfloat16)
    global_hits = (global_blocks[..., None] == numbers).astype(jnp.bfloat16)
    blocks = shard_rows.reshape(block_total, BLK, seq_count, 2, HEADS, HD)
    picked_random = jnp.einsum(
        "ishjb,busxhd->ishjuxd", random_hits, blocks, preferred_element_type=jnp.float32
    )
    picked_global = jnp.einsum(
        "gsb,busc->gusc",
        global_hits,
        shard_rows.reshape(block_total, BLK, seq_count, 2 * D),
        preferred_element_type=jnp.float32,
    )
    return (picked_random, picked_global)


def key_products(left_side, window_kv, far_random, far_global, which_half):
    near_part = jnp.einsum(
        "itshd,iwushd->ishtwu",
        left_side,
        window_kv[:, :, :, :, which_half],
        preferred_element_type=jnp.float32,
    )
    far_part = jnp.einsum(
        "itshd,ishjud->ishtju",
        left_side,
        far_random[:, :, :, :, :, which_half],
        preferred_element_type=jnp.float32,
    )
    global_part = jnp.einsum(
        "itshd,gushd->ishtgu",
        left_side,
        far_global[:, :, :, which_half],
        preferred_element_type=jnp.float32,
    )
    lead_shape = near_part.shape[:4]
    return jnp.concatenate(
        [
            near_part.reshape(lead_shape + (-1,)),
            far_part.reshape(lead_shape + (-1,)),
            global_part.reshape(lead_shape + (-1,)),
        ],
        axis=-1,
    )


def split_slots(weights):
    lead_shape = weights.shape[:4]
    near_cut = 3 * BLK
    far_cut = (3 + RAND) * BLK
    near_part = weights[..., :near_cut].reshape(lead_shape + (3, BLK))
    far_part = weights[..., near_cut:far_cut].reshape(lead_shape + (RAND, BLK))
    global_part = weights[..., far_cut:].reshape(lead_shape + (GLOB, BLK))
    return (near_part, far_part, global_part)


def key_mix(weights, window_kv, far_random, far_global, which_half):
    near_part, far_part, global_part = split_slots(weights)
    mixed = jnp.einsum(
        "ishtwu,iwushd->itshd",
        near_part,
        window_kv[:, :, :, :, which_half],
        preferred_element_type=jnp.float32,
    )
    mixed = mixed + jnp.einsum(
        "ishtju,ishjud->itshd",
        far_part,
        far_random[:, :, :, :, :, which_half],
        preferred_element_type=jnp.float32,
    )
    mixed = mixed + jnp.einsum(
        "ishtgu,gushd->itshd",
        global_part,
        far_global[:, :, :, which_half],
        preferred_element_type=jnp.float32,
    )
    return mixed


def key_grads(weights, left_side):
    near_part, far_part, global_part = split_slots(weights)
    near_grad = jnp.einsum(
        "ishtwu,itshd->iwushd", near_part, left_side, preferred_element_type=jnp.float32
    )
    far_grad = jnp.einsum(
        "ishtju,itshd->ishjud", far_part, left_side, preferred_element_type=jnp.float32
    )
    global_grad = jnp.einsum(
        "ishtgu,itshd->gushd", global_part, left_side, preferred_element_type=jnp.float32
    )
    return (near_grad, far_grad, global_grad)


def per_device(
    tokens,
    ln1_gain,
    ln1_bias,
    w_qkv,
    q_bias,
    v_bias,
    w_out,
    out_bias,
    ln2_gain,
    ln2_bias,
    w_in,
    in_bias,
    w_down,
    down_bias,
    cotangent,
    segment_ids,
    random_blocks,
    global_blocks,
):
    row_count = tokens.shape[0]
    seq_count = tokens.shape[1]
    query_blocks = row_count // BLK
    seq_length = segment_ids.shape[0]
    device_now = lax.axis_index("seq")
    first_row = device_now * row_count
    score_scale = HD ** (-0.5)
    random_local = lax.dynamic_slice_in_dim(
        random_blocks, device_now * query_blocks, query_blocks, 0
    )
    inputs = tokens.astype(jnp.float32)
    normed_full, first_norm_back = jax.vjp(
        layer_norm, inputs, ln1_gain.astype(jnp.float32), ln1_bias.astype(jnp.float32)
    )
    normed = normed_full.astype(jnp.bfloat16)
    projected = jnp.einsum("rsd,de->rse", normed, w_qkv, preferred_element_type=jnp.float32)
    queries = (projected[:, :, :D] + q_bias.astype(jnp.float32)).astype(jnp.bfloat16)
    value_shift = jnp.concatenate([jnp.zeros((D,), jnp.float32), v_bias.astype(jnp.float32)])
    keyval = (projected[:, :, D:] + value_shift).astype(jnp.bfloat16)
    extended = padded(keyval, (("seq", 0),), BLK)
    window_kv = window_stack(
        extended.reshape(query_blocks + 2, BLK, seq_count, 2, HEADS, HD), query_blocks
    )
    picked = pick_blocks(
        lax.all_gather(keyval, "seq", axis=0, tiled=True), random_local, global_blocks
    )
    far_random = picked[0].astype(jnp.bfloat16)
    far_global = picked[1].astype(jnp.bfloat16).reshape(GLOB, BLK, seq_count, 2, HEADS, HD)
    query_segment = lax.dynamic_slice_in_dim(segment_ids, first_row, row_count, 0)
    query_segment = query_segment.reshape(query_blocks, BLK, seq_count).transpose(0, 2, 1)
    window_spots = first_row - BLK + jnp.arange(row_count + 2 * BLK, dtype=jnp.int32)
    inside_seq = (window_spots >= 0) & (window_spots < seq_length)
    near_segment = jnp.take(segment_ids, jnp.clip(window_spots, 0, seq_length - 1), axis=0)
    near_segment = jnp.where(inside_seq[:, None], near_segment, -1)
    near_segment = window_stack(
        near_segment.reshape(query_blocks + 2, BLK, seq_count), query_blocks
    )
    near_segment = near_segment.transpose(0, 3, 1, 2).reshape(query_blocks, seq_count, 1, 3 * BLK)
    segment_rows = segment_ids.T
    sequence_pick = jnp.arange(seq_count, dtype=jnp.int32)
    offsets = jnp.arange(BLK, dtype=jnp.int32)
    far_segment = segment_rows[
        sequence_pick[None, :, None, None, None], random_local[..., None] * BLK + offsets
    ]
    far_segment = far_segment.reshape(query_blocks, seq_count, HEADS, RAND * BLK)
    global_segment = segment_rows[
        sequence_pick[None, :, None], global_blocks[..., None] * BLK + offsets
    ]
    global_segment = global_segment.transpose(1, 0, 2).reshape(1, seq_count, 1, GLOB * BLK)
    key_segment = jnp.concatenate(
        [
            jnp.broadcast_to(near_segment, (query_blocks, seq_count, HEADS, 3 * BLK)),
            far_segment,
            jnp.broadcast_to(global_segment, (query_blocks, seq_count, HEADS, GLOB * BLK)),
        ],
        axis=-1,
    )
    allowed = key_segment[:, :, :, None, :] == query_segment[:, :, None, :, None]
    query_rows = queries.reshape(query_blocks, BLK, seq_count, HEADS, HD)
    scores = jnp.where(
        allowed, key_products(query_rows, window_kv, far_random, far_global, 0) * score_scale, -1e30
    )
    row_max = jnp.max(scores, axis=-1, keepdims=True)
    log_total = row_max + jnp.log(jnp.sum(jnp.exp(scores - row_max), axis=-1, keepdims=True))
    soft_full = jnp.exp(scores - log_total)
    attn_probs = soft_full.astype(jnp.bfloat16)
    context = (
        key_mix(attn_probs, window_kv, far_random, far_global, 1)
        .reshape(row_count, seq_count, D)
        .astype(jnp.bfloat16)
    )
    mid_stream = (
        inputs
        + jnp.einsum("rsd,de->rse", context, w_out, preferred_element_type=jnp.float32)
        + out_bias.astype(jnp.float32)
    )
    normed2_full, second_norm_back = jax.vjp(
        layer_norm, mid_stream, ln2_gain.astype(jnp.float32), ln2_bias.astype(jnp.float32)
    )
    normed2 = normed2_full.astype(jnp.bfloat16)
    pre_act = jnp.einsum(
        "rsd,df->rsf", normed2, w_in, preferred_element_type=jnp.float32
    ) + in_bias.astype(jnp.float32)
    hidden_full, gelu_back = jax.vjp(gelu_tanh, pre_act)
    hidden = hidden_full.astype(jnp.bfloat16)
    output = (
        mid_stream
        + jnp.einsum("rsf,fd->rsd", hidden, w_down, preferred_element_type=jnp.float32)
        + down_bias.astype(jnp.float32)
    ).astype(jnp.bfloat16)
    grad_out = cotangent.astype(jnp.float32)
    w_down_grad = jnp.einsum("rsf,rsd->fd", hidden, cotangent, preferred_element_type=jnp.float32)
    down_bias_grad = jnp.sum(grad_out, axis=(0, 1))
    pre_grad = gelu_back(
        jnp.einsum("rsd,fd->rsf", cotangent, w_down, preferred_element_type=jnp.float32)
    )[0].astype(jnp.bfloat16)
    w_in_grad = jnp.einsum("rsd,rsf->df", normed2, pre_grad, preferred_element_type=jnp.float32)
    in_bias_grad = jnp.sum(pre_grad.astype(jnp.float32), axis=(0, 1))
    mid_part, ln2_gain_grad, ln2_bias_grad = second_norm_back(
        jnp.einsum("rsf,df->rsd", pre_grad, w_in, preferred_element_type=jnp.float32)
    )
    mid_grad = grad_out + mid_part
    branch_grad = mid_grad.astype(jnp.bfloat16)
    w_out_grad = jnp.einsum("rsd,rse->de", context, branch_grad, preferred_element_type=jnp.float32)
    out_bias_grad = jnp.sum(branch_grad.astype(jnp.float32), axis=(0, 1))
    context_grad = jnp.einsum(
        "rse,de->rsd", branch_grad, w_out, preferred_element_type=jnp.float32
    ).astype(jnp.bfloat16)
    grad_rows = context_grad.reshape(query_blocks, BLK, seq_count, HEADS, HD)
    probs_grad = key_products(grad_rows, window_kv, far_random, far_global, 1)
    score_grad = (
        soft_full * (probs_grad - jnp.sum(soft_full * probs_grad, axis=-1, keepdims=True))
    ).astype(jnp.bfloat16)
    query_grad = (
        (key_mix(score_grad, window_kv, far_random, far_global, 0) * score_scale)
        .reshape(row_count, seq_count, D)
        .astype(jnp.bfloat16)
    )
    near_key, far_key, global_key = key_grads(score_grad, query_rows)
    near_value, far_value, global_value = key_grads(attn_probs, grad_rows)
    near_kv = jnp.stack([near_key * score_scale, near_value], axis=4)
    far_kv = jnp.stack([far_key * score_scale, far_value], axis=5)
    global_kv = jnp.stack([global_key * score_scale, global_value], axis=3).reshape(
        GLOB, BLK, seq_count, 2 * D
    )
    rest_pad = ((0, 0),) * 5
    extended_grad = (
        jnp.pad(near_kv[:, 0], ((0, 2),) + rest_pad)
        + jnp.pad(near_kv[:, 1], ((1, 1),) + rest_pad)
        + jnp.pad(near_kv[:, 2], ((2, 0),) + rest_pad)
    )
    extended_grad = extended_grad.reshape(row_count + 2 * BLK, seq_count, 2 * D)
    rim_grads = jnp.concatenate([extended_grad[:BLK], extended_grad[row_count + BLK :]], axis=0)
    returned = padded(rim_grads.astype(jnp.bfloat16), (("seq", 0),), BLK).astype(rim_grads.dtype)
    near_total = extended_grad[BLK : row_count + BLK]
    near_total = (
        near_total.at[:BLK].add(returned[:BLK]).at[row_count - BLK :].add(returned[3 * BLK :])
    )
    block_total = row_count * lax.axis_size("seq") // BLK
    numbers = jnp.arange(block_total, dtype=jnp.int32)
    random_hits = (random_local[..., None] == numbers).astype(jnp.float32)
    global_rows_hit = (global_blocks[..., None] == numbers).astype(jnp.float32)

    def far_sum(one_sequence):
        hits, kv, global_rows, global_sum = one_sequence
        random_term = jnp.einsum(
            "ihjb,ihjuxd->buxhd", hits, kv, precision=lax.Precision.HIGHEST
        )
        global_term = jnp.einsum(
            "gb,guc->buc", global_rows, global_sum, precision=lax.Precision.HIGHEST
        )
        flat = (block_total * BLK, 2 * D)
        return (random_term.reshape(flat) + global_term.reshape(flat)).astype(jnp.bfloat16)

    far_parts = lax.map(
        far_sum,
        (
            jnp.moveaxis(random_hits, 1, 0),
            jnp.moveaxis(far_kv, 1, 0),
            jnp.moveaxis(global_rows_hit, 1, 0),
            jnp.moveaxis(global_kv, 2, 0),
        ),
    )
    far_total = lax.psum_scatter(far_parts, "seq", scatter_dimension=1, tiled=True)
    far_total = jnp.moveaxis(far_total, 0, 1).astype(jnp.float32)
    keyval_grad = (near_total + far_total).astype(jnp.bfloat16)
    qkv_grad = jnp.concatenate([query_grad, keyval_grad], axis=-1)
    q_bias_grad = jnp.sum(query_grad.astype(jnp.float32), axis=(0, 1))
    v_bias_grad = jnp.sum(keyval_grad[:, :, D:].astype(jnp.float32), axis=(0, 1))
    w_qkv_grad = jnp.einsum("rsd,rse->de", normed, qkv_grad, preferred_element_type=jnp.float32)
    input_part, ln1_gain_grad, ln1_bias_grad = first_norm_back(
        jnp.einsum("rse,de->rsd", qkv_grad, w_qkv, preferred_element_type=jnp.float32)
    )
    input_grad = mid_grad + input_part
    summed = (
        lax.psum_scatter(ln1_gain_grad, ("batch", "seq"), scatter_dimension=0, tiled=True),
        lax.psum_scatter(ln1_bias_grad, ("batch", "seq"), scatter_dimension=0, tiled=True),
        lax.psum_scatter(w_qkv_grad, ("batch", "seq"), scatter_dimension=0, tiled=True),
        lax.psum_scatter(q_bias_grad, ("batch", "seq"), scatter_dimension=0, tiled=True),
        lax.psum_scatter(v_bias_grad, ("batch", "seq"), scatter_dimension=0, tiled=True),
        lax.psum_scatter(w_out_grad, ("batch", "seq"), scatter_dimension=0, tiled=True),
        lax.psum_scatter(out_bias_grad, ("batch", "seq"), scatter_dimension=0, tiled=True),
        lax.psum_scatter(ln2_gain_grad, ("batch", "seq"), scatter_dimension=0, tiled=True),
        lax.psum_scatter(ln2_bias_grad, ("batch", "seq"), scatter_dimension=0, tiled=True),
        lax.psum_scatter(w_in_grad, ("batch", "seq"), scatter_dimension=0, tiled=True),
        lax.psum_scatter(in_bias_grad, ("batch", "seq"), scatter_dimension=0, tiled=True),
        lax.psum_scatter(w_down_grad, ("batch", "seq"), scatter_dimension=0, tiled=True),
        lax.psum_scatter(down_bias_grad, ("batch", "seq"), scatter_dimension=0, tiled=True),
    )
    return (
        output,
        input_grad,
        summed[0],
        summed[1],
        summed[2],
        summed[3],
        summed[4],
        summed[5],
        summed[6],
        summed[7],
        summed[8],
        summed[9],
        summed[10],
        summed[11],
        summed[12],
    )


NEG = -1e30
LANES = 128
SEG_VALUES = 4
MESH_IDS = pl.DeviceIdType.MESH
VMEM_BYTES = 60 * 1024 * 1024
F32 = jnp.float32
BF16 = jnp.bfloat16
ALL = slice(None)
Z_HIGH, Z_LOW, Y, X, MEMBER = range(5)
CHIP = (Z_HIGH, Z_LOW, Y, X)


def three_parts(x):
    hi = x.astype(BF16)
    rest = x - hi.astype(F32)
    mid = rest.astype(BF16)
    low = (rest - mid.astype(F32)).astype(BF16)
    return hi, mid, low


def dot_nt(a, b):
    return lax.dot_general(a, b, (((1,), (1,)), ((), ())), preferred_element_type=F32)


def dot_nn(a, b):
    return lax.dot_general(a, b, (((1,), (0,)), ((), ())), preferred_element_type=F32)


def dot_tn(a, b):
    return lax.dot_general(a, b, (((0,), (0,)), ((), ())), preferred_element_type=F32)


def turned(x):
    return x.astype(F32).T.astype(BF16)


def normalise(values):
    mean = jnp.mean(values, axis=-1, keepdims=True)
    centred = values - mean
    scale = lax.rsqrt(jnp.mean(centred * centred, axis=-1, keepdims=True) + eps)
    return centred * scale, scale


def normalise_back(unit, scale, grad):
    first = jnp.mean(grad, axis=-1, keepdims=True)
    second = jnp.mean(grad * unit, axis=-1, keepdims=True)
    return (grad - first - unit * second) * scale


def my_bits():
    batch = lax.axis_index("batch")
    return (
        lax.div(batch, 4),
        lax.rem(lax.div(batch, 2), 2),
        lax.rem(batch, 2),
        lax.axis_index("half"),
        lax.axis_index("member"),
    )


def device_across(bit):
    batch = lax.axis_index("batch")
    half = lax.axis_index("half")
    member = lax.axis_index("member")
    if bit == MEMBER:
        return (batch, half, 1 - member)
    if bit == X:
        return (batch, 1 - half, member)
    stride = (4, 2, 1)[bit]
    return (batch + stride * (1 - 2 * my_bits()[bit]), half, member)


def chip_across(mask):
    z_high, z_low, y, x, member = my_bits()
    flipped = [1 - b if mask & flag else b for b, flag in zip((z_high, z_low, y, x), (8, 4, 2, 1))]
    return (4 * flipped[0] + 2 * flipped[1] + flipped[2], flipped[3], member)


def remote(src, dst, send, recv, bit):
    return pltpu.make_async_remote_copy(
        src_ref=src,
        dst_ref=dst,
        send_sem=send,
        recv_sem=recv,
        device_id=device_across(bit),
        device_id_type=MESH_IDS,
    )


def greet(bits):
    barrier = pltpu.get_barrier_semaphore()
    for bit in bits:
        pl.semaphore_signal(barrier, inc=1, device_id=device_across(bit), device_id_type=MESH_IDS)
    pl.semaphore_wait(barrier, len(bits))


class Sums:
    def __init__(self, send_sem, recv_sem):
        self.bits = my_bits()
        self.send_sem, self.recv_sem = send_sem, recv_sem
        self.pieces = {}

    def add(self, number, source, dims, order, slots, cut=()):
        self.pieces[number] = (source, dims, order, slots, cut)

    def side(self, number, depth, across):
        source, dims, order, slots, cut = self.pieces[number]
        bit = order[depth]
        value = 1 - self.bits[bit] if across else self.bits[bit]
        left = [b for b in dims if b not in order[:depth]]
        spot = left.index(bit)
        index = (ALL,) * (1 + spot) + (value,)
        if depth:
            return slots[depth - 1].at[index]
        return source.at[index + (ALL,) * (len(left) - 1 - spot) + cut]

    def copy(self, number, depth):
        _, _, order, slots, _ = self.pieces[number]
        return remote(
            self.side(number, depth, True),
            slots[depth],
            self.send_sem.at[number, depth],
            self.recv_sem.at[number, depth],
            order[depth],
        )

    def send(self, number, depth):
        self.copy(number, depth).start()

    def take(self, number, depth):
        _, _, order, slots, _ = self.pieces[number]
        self.copy(number, depth).wait_recv()
        mine = self.side(number, depth, False)[...]
        if depth == len(order) - 1:
            return mine.astype(F32) + slots[depth][...].astype(F32)
        slots[depth][...] = mine + slots[depth][...]
        self.send(number, depth + 1)
        return None

    def finish(self):
        for number, (_, _, order, _, _) in self.pieces.items():
            for depth in range(len(order)):
                self.copy(number, depth).wait_send()


def slot_shapes(lead, count, tail):
    return [pltpu.VMEM((lead,) + (2,) * (count - 1 - depth) + tail, BF16) for depth in range(count)]


ORDERS = ((X, Y, Z_LOW, Z_HIGH), (Y, Z_LOW, X, Z_HIGH), (Z_LOW, X, Y, Z_HIGH))
IN_CUTS = ((0, 16), (16, 16), (32, 32))
DOWN_CUTS = ((0, 384), (384, 384), (768, 256))
OUT_CUTS = ((0, 128), (128, 128), (256, 256))
LATER_DIMS = (
    (Z_HIGH, Z_LOW, Y),
    (Z_HIGH, Z_LOW, X),
    (Z_HIGH, Y, X),
    (Z_LOW, Y, Z_HIGH),
    (Z_LOW, Z_HIGH, X),
    (Y, Z_HIGH, X),
)


def in_vmem():
    return pl.BlockSpec(memory_space=pltpu.VMEM)


def anywhere():
    return pl.BlockSpec(memory_space=pl.ANY)


def params(collective):
    return pltpu.CompilerParams(
        collective_id=collective, has_side_effects=True, vmem_limit_bytes=VMEM_BYTES
    )


def begin(kept, sent, vectors, w_qkv, q_bias, v_bias):
    rows = kept.shape[0]
    length = 4 * rows
    width = D // 2
    cuts = 2
    size = rows // cuts

    def body(*refs):
        kept_ref, sent_ref, vec_ref, wq_ref, wk_ref, wv_ref, qb_ref, vb_ref = refs[:8]
        tok_ref, nt_ref, q_ref, k_ref, v_ref = refs[8:13]
        all_ref, send_sem, recv_sem = refs[13:]
        greet((X, MEMBER))

        def over_x(c):
            return remote(
                sent_ref.at[pl.ds(c * size, size)],
                all_ref.at[pl.ds(rows + c * size, size)],
                send_sem.at[c],
                recv_sem.at[c],
                X,
            )

        def on(c):
            return remote(
                all_ref.at[pl.ds(rows + c * size, size)],
                all_ref.at[pl.ds(3 * rows + c * size, size)],
                send_sem.at[cuts + c],
                recv_sem.at[cuts + c],
                MEMBER,
            )

        near = remote(
            kept_ref, all_ref.at[pl.ds(2 * rows, rows)], send_sem.at[2 * cuts], recv_sem.at[2 * cuts], MEMBER
        )
        for c in range(cuts):
            over_x(c).start()
        near.start()

        def project(first, count):
            place = pl.ds(first, count)
            x = kept_ref[...] if first == 0 else all_ref[place, :]
            if first < 2 * rows:
                tok_ref[place, :] = x
            unit, _ = normalise(x.astype(F32))
            normed = (unit * vec_ref[4:5] + vec_ref[5:6]).astype(BF16)
            nt_ref[:, place] = turned(normed)
            q_ref[place, :] = (dot_nn(normed, wq_ref[...]) + qb_ref[...]).astype(BF16)
            k_ref[place, :] = dot_nn(normed, wk_ref[...]).astype(BF16)
            v_ref[place, :] = (dot_nn(normed, wv_ref[...]) + vb_ref[...]).astype(BF16)

        project(0, rows)
        near.wait_recv()
        project(2 * rows, rows)
        for c in range(cuts):
            over_x(c).wait_recv()
            on(c).start()
            project(rows + c * size, size)
        for c in range(cuts):
            on(c).wait_recv()
            project(3 * rows + c * size, size)
        near.wait_send()
        for c in range(cuts):
            over_x(c).wait_send()
            on(c).wait_send()

    def weight(which):
        return pl.BlockSpec((D, width), lambda i: (0, 2 * which + lax.axis_index("member")))

    def bias():
        return pl.BlockSpec((1, width), lambda i: (0, lax.axis_index("member")))

    def shape(count, columns):
        return jax.ShapeDtypeStruct((count, columns), BF16)

    return pl.pallas_call(
        body,
        grid=(1,),
        out_shape=(shape(2 * rows, D), shape(D, length)) + (shape(length, width),) * 3,
        in_specs=[in_vmem(), in_vmem(), in_vmem(), weight(0), weight(1), weight(2), bias(), bias()],
        out_specs=(in_vmem(),) * 5,
        scratch_shapes=[
            pltpu.VMEM((length, D), BF16),
            pltpu.SemaphoreType.DMA((2 * cuts + 1,)),
            pltpu.SemaphoreType.DMA((2 * cuts + 1,)),
        ],
        compiler_params=params(5),
        name="begin",
    )(kept, sent, vectors, w_qkv, w_qkv, w_qkv, q_bias, v_bias)


def attend_forward(q, k, v, segments, random_blocks, global_blocks, cot_kept, cot_sent, tile=512):
    length, width = q.shape
    pairs = width // LANES
    tiles = length // tile
    blocks = length // BLK
    own = length // 2
    rows = own // 2

    def body(*refs):
        q_ref, k_ref, v_ref, seg_ref, rand_ref, glob_ref, kept_ref, sent_ref = refs[:8]
        ctx_ref, qa_ref, fk_ref, other_ref, cot_ref = refs[8:13]
        fq_ref, ka_ref, made_ref, seg_row, blk_row, send_sem, recv_sem, cot_send, cot_recv = refs[13:]
        pair, step = pl.program_id(0), pl.program_id(1)
        half, member = lax.axis_index("half"), lax.axis_index("member")
        numbers = lax.broadcasted_iota(jnp.int32, (8, length), 0).astype(F32)

        def stay():
            return pltpu.make_async_copy(kept_ref, cot_ref.at[pl.ds(0, rows)], cot_send.at[3])

        def cot_copy(which):
            across = pl.ds(rows, rows)
            src, to, bit = (
                (sent_ref, across, X),
                (kept_ref, pl.ds(own, rows), MEMBER),
                (cot_ref.at[across], pl.ds(own + rows, rows), MEMBER),
            )[which]
            return remote(src, cot_ref.at[to], cot_send.at[which], cot_recv.at[which], bit)

        @pl.when((pair == 0) & (step == 0))
        def _():
            greet((X, MEMBER))
            cot_copy(0).start()
            cot_copy(1).start()
            stay().start()
            both = seg_ref[...].astype(F32)
            ids = jnp.where(half == 0, both[0:1], both[1:2])
            slots = []
            for j in range(2):
                for t in range(2):
                    want = lax.rem(half + t, 2) * 2 + lax.rem(member + j, 2)
                    piece = jnp.zeros((1, rows), F32)
                    for b in range(4):
                        piece = jnp.where(want == b, ids[:, b * rows : (b + 1) * rows], piece)
                    slots.append(piece)
            seg_row[...] = jnp.concatenate(slots, axis=1)
            spot = lax.broadcasted_iota(jnp.int32, (1, length), 1)
            side = lax.rem(half + lax.rem(spot // rows, 2), 2) * 2 + lax.rem(member + spot // own, 2)
            blk_row[...] = (side * (rows // BLK) + lax.rem(spot // BLK, rows // BLK)).astype(F32)
            count = lax.broadcasted_iota(jnp.int32, (blocks, length), 0).astype(F32)
            here = jnp.where(blk_row[...] == count, 1.0, 0.0)
            rest = jnp.zeros((HD - 8 - 2 * blocks, length), F32)
            apart = jnp.where((seg_row[...] == numbers) | (numbers >= SEG_VALUES), 0.0, NEG)
            feats = jnp.concatenate([apart, here, here, rest], axis=0)
            fq_ref[...] = jnp.concatenate([feats, feats], axis=0).T.astype(BF16)

        @pl.when(step == 0)
        def _():
            same = jnp.where(seg_row[...] == numbers, 1.0, 0.0)
            rest = jnp.zeros((HD - 16 - 2 * blocks, length), F32)
            ones = jnp.where(numbers < 3, 1.0, 0.0)
            here = blk_row[...]
            count = lax.broadcasted_iota(jnp.int32, (blocks, length), 0).astype(F32)
            common = jnp.where(jnp.abs(count - here) <= 1.0, 1.0, 0.0)
            for g in range(GLOB):
                named = jnp.where(half == 0, glob_ref[g : g + 1, 0:1], glob_ref[g : g + 1, 1:2])
                common = common + jnp.where(here == named.astype(F32), 1.0, 0.0)
            drawn = rand_ref[0]
            sides = []
            for parity in (1, 0):
                times = common
                for j in range(RAND):
                    column = parity * RAND + j
                    times = times + jnp.where(drawn[:, column : column + 1] == here, 1.0, 0.0)
                full = jnp.where(times > 0, jnp.log(jnp.maximum(times, 1.0)), NEG)
                high = full.astype(BF16).astype(F32)
                sides += [same, high, full - high, ones, rest]
            feats = jnp.concatenate(sides, axis=0).T.astype(BF16)
            fk_ref[0] = feats
            low_half = lax.broadcasted_iota(jnp.int32, (length, LANES), 1) < HD
            keys = k_ref[...]
            ka_ref[0] = jnp.where(low_half, keys, feats)
            ka_ref[1] = jnp.where(low_half, feats, keys)

        lane = lax.broadcasted_iota(jnp.int32, (tile, LANES), 1)
        low_half = lane < HD
        scaled = q_ref[...] * jnp.asarray(HD ** (-0.5), BF16)
        place = pl.ds(pl.multiple_of(step * tile, tile), tile)
        feats = fq_ref[place, :]
        results = []
        for parity in range(2):
            if parity == 0:
                aug = jnp.where(low_half, scaled, feats)
                first = HD + 8 + 2 * blocks
            else:
                aug = jnp.where(low_half, feats, scaled)
                first = 8 + 2 * blocks
            scores = dot_nt(aug, ka_ref[parity])
            top = jnp.max(scores, axis=-1, keepdims=True)
            weights = jnp.exp(scores - top)
            total = jnp.sum(weights, axis=-1, keepdims=True)
            mixed = dot_nn(weights.astype(BF16), v_ref[...])
            results.append(mixed / total)
            hi, mid, low = three_parts(-(top + jnp.log(total)))
            aug = jnp.where(lane == first, hi, aug)
            aug = jnp.where(lane == first + 1, mid, aug)
            aug = jnp.where(lane == first + 2, low, aug)
            qa_ref[parity] = aug
        context = jnp.where(low_half, results[0], results[1]).astype(BF16)
        ctx_ref[...] = context
        made_ref[pair, place, :] = context

        def swaps(one_pair):
            cols = pl.ds(pl.multiple_of(one_pair * LANES, LANES), LANES)
            return [
                remote(
                    made_ref.at[one_pair, pl.ds(from_row, own)],
                    other_ref.at[pl.ds(own - from_row, own), cols],
                    send_sem.at[side, one_pair],
                    recv_sem.at[side, one_pair],
                    MEMBER,
                )
                for side, from_row in enumerate((0, own))
            ]

        @pl.when(step == tiles - 1)
        def _():
            for one in swaps(pair):
                one.start()

        @pl.when((pair == pairs - 2) & (step == tiles - 1))
        def _():
            cot_copy(0).wait_recv()
            cot_copy(2).start()

        @pl.when((pair == pairs - 1) & (step == tiles - 1))
        def _():
            cot_copy(0).wait_send()
            stay().wait()
            cot_copy(1).wait()
            cot_copy(2).wait()
            for one_pair in range(pairs):
                for one in swaps(one_pair):
                    one.wait()

    return pl.pallas_call(
        body,
        grid=(pairs, tiles),
        out_shape=(
            jax.ShapeDtypeStruct((length, width), BF16),
            jax.ShapeDtypeStruct((2 * pairs, length, LANES), BF16),
            jax.ShapeDtypeStruct((pairs, length, LANES), BF16),
            jax.ShapeDtypeStruct((length, width), BF16),
            jax.ShapeDtypeStruct((length, D), BF16),
        ),
        in_specs=[
            pl.BlockSpec((tile, LANES), lambda p, t: (t, p)),
            pl.BlockSpec((length, LANES), lambda p, t: (0, p)),
            pl.BlockSpec((length, LANES), lambda p, t: (0, p)),
            in_vmem(),
            pl.BlockSpec((1, blocks, 2 * RAND), lambda p, t: (p, 0, 0)),
            in_vmem(),
            anywhere(),
            anywhere(),
        ],
        out_specs=(
            pl.BlockSpec((tile, LANES), lambda p, t: (t, p)),
            pl.BlockSpec((2, tile, LANES), lambda p, t: (p, t, 0)),
            pl.BlockSpec((1, length, LANES), lambda p, t: (p, 0, 0)),
            anywhere(),
            anywhere(),
        ),
        scratch_shapes=[
            pltpu.VMEM((length, LANES), BF16),
            pltpu.VMEM((2, length, LANES), BF16),
            pltpu.VMEM((pairs, length, LANES), BF16),
            pltpu.VMEM((1, length), F32),
            pltpu.VMEM((1, length), F32),
            pltpu.SemaphoreType.DMA((2, pairs)),
            pltpu.SemaphoreType.DMA((2, pairs)),
            pltpu.SemaphoreType.DMA((4,)),
            pltpu.SemaphoreType.DMA((3,)),
        ],
        compiler_params=params(4),
        name="attend_forward",
    )(q, k, v, segments, random_blocks, global_blocks, cot_kept, cot_sent)


def feed_forward(context, context_other, tokens, w_out, vectors, cot, w_in, in_bias, w_down):
    rows = cot.shape[0]
    own = rows // 2
    width = context.shape[1]
    chunk = 4 * LANES
    steps = 4
    share = D // 16
    root = (2.0 / np.pi) ** 0.5
    cube = 0.044715

    def group(j):
        bits = my_bits()
        z_low = jnp.where(j < 2, 1 - bits[Z_LOW], bits[Z_LOW])
        return z_low, jnp.where(lax.rem(j, 2) == 0, 1 - bits[Y], bits[Y])

    def body(*refs):
        ctx_ref, other_ref, tok_ref, wo_ref, wo2_ref, vec_ref, c_ref = refs[:7]
        wi_refs, b_refs, wd_refs = refs[7:11], refs[11:15], refs[15:19]
        out_ref, out_got, dn_ref, dn_got, mid_ref, gb_ref = refs[19:25]
        keep, got = refs[25:31], refs[31:37]
        n_ref, nt_ref, out_acc, dn_acc, out_send, dn_send, gi_ref, gd_ref = refs[37:45]
        send_sem, recv_sem, keep_sem, swap_sem = refs[45:]
        step = pl.program_id(0)
        bits = my_bits()
        z_low, y = group(step)
        slot = 2 * z_low + y

        @pl.when(step == 0)
        def _():
            greet((Z_LOW, Y, X, MEMBER))
            mid = (
                tok_ref[...].astype(F32)
                + dot_nn(ctx_ref[...], wo_ref[...])
                + dot_nn(other_ref[...], wo2_ref[...])
                + vec_ref[0:1]
            )
            mid_ref[...] = mid
            unit, _ = normalise(mid)
            n2 = (unit * vec_ref[1:2] + vec_ref[2:3]).astype(BF16)
            n_ref[:own] = n2
            swap = remote(
                n_ref.at[pl.ds(0, own)], n_ref.at[pl.ds(own, own)], swap_sem.at[0, 0], swap_sem.at[1, 0], MEMBER
            )
            swap.start()
            nt_ref[:, :own] = turned(n2)
            swap.wait()
            nt_ref[:, own:] = turned(n_ref[own:])

        wi = jnp.concatenate([ref[...] for ref in wi_refs], axis=1)
        wd = jnp.concatenate([ref[...] for ref in wd_refs], axis=0)
        pre = dot_nn(n_ref[...], wi) + jnp.concatenate([ref[...] for ref in b_refs], axis=1)
        square = pre * pre
        th = jnp.tanh(root * pre * (1.0 + cube * square))
        half_up = 0.5 * (1.0 + th)
        hidden = (pre * half_up).astype(BF16)
        slope = half_up + 0.5 * pre * (1.0 - th * th) * (root * (1.0 + 3.0 * cube * square))

        def in_part(kind, at):
            bit = (X, Y, Z_LOW)[kind]
            rest = (ALL,) * (3 - bit) + (pl.ds(*IN_CUTS[kind]),)
            return lambda side: gi_ref.at[(at,) + (ALL,) * bit + (side,) + rest]

        def copies(kind, at, where, bit):
            return (
                lambda: remote(
                    where(1 - bits[bit]), got[kind].at[at], send_sem.at[kind, at], recv_sem.at[kind, at], bit
                ),
                lambda: pltpu.make_async_copy(where(bits[bit]), keep[kind].at[at], keep_sem.at[kind, at]),
            )

        def in_copies(kind, at):
            return copies(kind, at, in_part(kind, at), (X, Y, Z_LOW)[kind])

        def x_copies(at):
            return copies(3, at, lambda side: gd_ref.at[at, :, side, :, pl.ds(*DOWN_CUTS[0])], X)

        def y_copies(z):
            return copies(4, z, lambda side: gd_ref.at[2 * z + side, :, :, :, pl.ds(*DOWN_CUTS[1])], Y)

        def z_copies(at_y):
            return copies(
                5, at_y, lambda side: gd_ref.at[2 * side + at_y, :, :, :, pl.ds(*DOWN_CUTS[2])], Z_LOW
            )

        gd_ref[slot] = dot_tn(hidden, c_ref[...]).astype(BF16).reshape(2, 2, LANES, D)
        for one in x_copies(slot):
            one().start()

        @pl.when(lax.rem(step, 2) == 0)
        def _():
            y_copies(z_low)[0]().start()

        @pl.when(lax.rem(step, 2) == 1)
        def _():
            y_copies(z_low)[1]().start()

        @pl.when(step < 2)
        def _():
            z_copies(y)[0]().start()

        @pl.when(step >= 2)
        def _():
            z_copies(y)[1]().start()

        pre_grad = (dot_nt(c_ref[...], wd) * slope).astype(BF16)
        gb_ref[...] = jnp.sum(pre_grad.astype(F32), axis=0, keepdims=True)
        gi_ref[slot] = dot_nn(nt_ref[...], pre_grad).astype(BF16).reshape(2, 2, 2, 2, share, chunk)
        for kind in range(3):
            for one in in_copies(kind, slot):
                one().start()

        @pl.when(step == 0)
        def _():
            dn_acc[...] = dot_nt(pre_grad, wi)
            out_acc[...] = dot_nn(hidden, wd)

        @pl.when(step > 0)
        def _():
            dn_acc[...] += dot_nt(pre_grad, wi)
            out_acc[...] += dot_nn(hidden, wd)

        @pl.when(step == steps - 1)
        def _():
            dn_send[...] = dn_acc[own:].astype(BF16)
            out_send[...] = out_acc[own:].astype(BF16)
            swaps = [
                remote(dn_send, dn_got, swap_sem.at[0, 1], swap_sem.at[1, 1], MEMBER),
                remote(out_send, out_got, swap_sem.at[0, 2], swap_sem.at[1, 2], MEMBER),
            ]
            for one in swaps:
                one.start()
            dn_ref[...] = dn_acc[:own]
            out_ref[...] = mid_ref[...] + out_acc[:own] + vec_ref[3:4]
            for at in range(4):
                for kind in range(3):
                    for one in in_copies(kind, at):
                        one().wait()
                for one in x_copies(at):
                    one().wait()
            for at in range(2):
                for one in y_copies(at) + z_copies(at):
                    one().wait()
            for one in swaps:
                one.wait()

    def unit(z_high, x):
        def at(j):
            z_low, y = group(j)
            return 2 * (((2 * z_high + z_low) * 2 + y) * 2 + x) + lax.axis_index("member")

        return at

    units = [unit(z_high, x) for z_high in range(2) for x in range(2)]

    def column(u):
        return lambda j: (0, u(j))

    def row(u):
        return lambda j: (u(j), 0)

    def slot_of(j):
        z_low, y = group(j)
        return (0, 2 * z_low + y)

    whole = pl.BlockSpec((rows, D), lambda j: (0, 0))
    half = pl.BlockSpec((own, D), lambda j: (0, 0))
    half_ctx = pl.BlockSpec((own, width), lambda j: (0, 0))
    parts = [jax.ShapeDtypeStruct((4, 2, 2, 2, size, chunk), BF16) for _, size in IN_CUTS] + [
        jax.ShapeDtypeStruct((4, 2, LANES, DOWN_CUTS[0][1]), BF16),
        jax.ShapeDtypeStruct((2, 2, 2, LANES, DOWN_CUTS[1][1]), BF16),
        jax.ShapeDtypeStruct((2, 2, 2, LANES, DOWN_CUTS[2][1]), BF16),
    ]
    own_f32 = jax.ShapeDtypeStruct((own, D), F32)
    own_bf16 = jax.ShapeDtypeStruct((own, D), BF16)
    results = pl.pallas_call(
        body,
        grid=(steps,),
        out_shape=[
            own_f32,
            own_bf16,
            own_f32,
            own_bf16,
            own_f32,
            jax.ShapeDtypeStruct((1, steps * chunk), F32),
        ]
        + parts
        + parts,
        in_specs=[
            half_ctx,
            half_ctx,
            half,
            pl.BlockSpec((width, D), lambda j: (lax.axis_index("member"), 0)),
            pl.BlockSpec((width, D), lambda j: (1 - lax.axis_index("member"), 0)),
            pl.BlockSpec((8, D), lambda j: (0, 0)),
            whole,
        ]
        + [pl.BlockSpec((D, LANES), column(u)) for u in units]
        + [pl.BlockSpec((1, LANES), column(u)) for u in units]
        + [pl.BlockSpec((LANES, D), row(u)) for u in units],
        out_specs=[half, anywhere(), half, anywhere(), half, pl.BlockSpec((1, chunk), slot_of)]
        + [anywhere()] * 12,
        scratch_shapes=[
            pltpu.VMEM((rows, D), BF16),
            pltpu.VMEM((D, rows), BF16),
            pltpu.VMEM((rows, D), F32),
            pltpu.VMEM((rows, D), F32),
            pltpu.VMEM((own, D), BF16),
            pltpu.VMEM((own, D), BF16),
            pltpu.VMEM((4, 2, 2, 2, 2, share, chunk), BF16),
            pltpu.VMEM((4, 2, 2, LANES, D), BF16),
            pltpu.SemaphoreType.DMA((6, 4)),
            pltpu.SemaphoreType.DMA((6, 4)),
            pltpu.SemaphoreType.DMA((6, 4)),
            pltpu.SemaphoreType.DMA((2, 3)),
        ],
        compiler_params=params(1),
        name="feed_forward",
    )(context, context_other, tokens, w_out, w_out, vectors, cot, *[w_in] * 4, *[in_bias] * 4, *[w_down] * 4)
    return results[:6], results[6:12], results[12:]


def attend_backward(
    rows_aug, k, v, feat_k, ctx, ctx_other, mid, n2_grad, n2_grad_got, cot, vectors, w_out, normed_t, w_qkv, output_own,
    kept, got, tile=256,
):
    length, width = k.shape
    pairs = width // LANES
    early = 1
    tiles = length // tile
    own = length // 2
    chunk = kept[0].shape[-1]
    shapes = [a.shape for a in kept[:3]] + [(1, 2, 2, 2, LANES, a.shape[-1]) for a in kept[3:]]
    kept = [a.reshape(shape) for a, shape in zip(kept, shapes)]
    got = [a.reshape(shape) for a, shape in zip(got, shapes)]
    share = D // 16
    count = 9 + 3 * early

    def body(*refs):
        qa_ref, k_ref, v_ref, fk_ref, ctx_ref, other_ref, mid_ref, dn2_ref, dn2_got, c_ref, vec_ref, wo_ref = refs[:12]
        nt_ref, wq_ref, wk_ref, wv_ref, mine_ref = refs[12:17]
        keep_in, got_in = refs[17:23], refs[23:29]
        dn_ref, mg_ref, sum_ref, qb_ref, vb_ref, sum_in, sum_down, sum_out, sum_qkv, dn_got, theirs_ref = refs[29:40]
        keep_new, got_new = refs[40:43], refs[43:46]
        ga_ref, acc_ref, slab_ref, dn_acc, dn_send, gq_ref, br_ref, g_ref, go_ref = refs[46:55]
        begin, first = refs[55:61], refs[61:67]
        slots = refs[67 : 67 + 18 + 12 + 12 * early]
        send_sem, recv_sem, load_sem, new_send, new_recv, new_keep, swap_sem = refs[67 + 30 + 12 * early :]
        pair, step = pl.program_id(0), pl.program_id(1)
        now = pair * tiles + step
        member = lax.axis_index("member")

        sums = Sums(send_sem, recv_sem)
        for kind in range(6):
            sums.add(kind, begin[kind], LATER_DIMS[kind], ORDERS[kind % 3][1:], slots[3 * kind : 3 * kind + 3])
        for kind in range(3):
            sums.add(
                6 + kind,
                go_ref,
                CHIP,
                ORDERS[kind],
                slots[18 + 4 * kind : 22 + 4 * kind],
                (ALL, pl.ds(*OUT_CUTS[kind])),
            )
        for one_pair in range(early):
            for kind in range(3):
                number = 9 + 3 * one_pair + kind
                sums.add(
                    number,
                    gq_ref.at[one_pair, pl.ds(kind, 1)],
                    CHIP,
                    ORDERS[kind],
                    slots[30 + 4 * (number - 9) : 34 + 4 * (number - 9)],
                )

        def loads(kind):
            return (
                pltpu.make_async_copy(keep_in[kind], begin[kind], load_sem.at[0, kind]),
                pltpu.make_async_copy(got_in[kind], first[kind], load_sem.at[1, kind]),
            )

        def begin_sum(kind):
            for one in loads(kind):
                one.wait()
            begin[kind][...] = begin[kind][...] + first[kind][...]
            sums.send(kind, 0)

        def end_sum(number):
            total = sums.take(number, len(sums.pieces[number][2]) - 1)
            if number < 3:
                for z_low in range(2):
                    for y in range(2):
                        for z_high in range(2):
                            for x in range(2):
                                unit = ((2 * z_high + z_low) * 2 + y) * 2 + x
                                local = (2 * z_high + x) * LANES
                                sum_in[pl.ds(*IN_CUTS[number]), unit * LANES : (unit + 1) * LANES] = total[
                                    2 * z_low + y, :, local : local + LANES
                                ]
            elif number < 6:
                sum_down[:, pl.ds(*DOWN_CUTS[number - 3])] = total[0]
            elif number < 9:
                sum_out[:, pl.ds(*OUT_CUTS[number - 6])] = total[0]
            else:
                one_pair, kind = (number - 9) // 3, (number - 9) % 3
                place = (kind * early + one_pair) * LANES
                sum_qkv[:, place : place + LANES] = total[0]

        def do(number, depth):
            if depth == len(sums.pieces[number][2]) - 1:
                end_sum(number)
            else:
                sums.take(number, depth)

        def at(when, depth, *numbers):
            @pl.when(now == when)
            def _():
                for number in numbers:
                    do(number, depth)

        @pl.when(now == 0)
        def _():
            greet((Z_HIGH, Z_LOW, Y, X, MEMBER))
            for kind in range(6):
                for one in loads(kind):
                    one.start()
            for kind in (0, 1, 5, 2, 3, 4):
                begin_sum(kind)
            unit, scale = normalise(mid_ref[...])
            grad = dn2_ref[...] + dn2_got[...].astype(F32)
            cot_own = c_ref[...].astype(F32)
            mid_grad = cot_own + normalise_back(unit, scale, grad * vec_ref[1:2])
            mg_ref[...] = mid_grad
            branch = mid_grad.astype(BF16)
            br_ref[:own] = branch
            swap = remote(
                br_ref.at[pl.ds(0, own)], br_ref.at[pl.ds(own, own)], swap_sem.at[0, 0], swap_sem.at[1, 0], MEMBER
            )
            swap.start()
            sum_ref[0:1] = jnp.sum(branch.astype(F32), axis=0, keepdims=True)
            sum_ref[1:2] = jnp.sum(grad * unit, axis=0, keepdims=True)
            sum_ref[2:3] = jnp.sum(grad, axis=0, keepdims=True)
            sum_ref[3:4] = jnp.sum(cot_own, axis=0, keepdims=True)
            sum_ref[4:8] = jnp.zeros((4, D), F32)
            swap.wait()
            g_ref[...] = dot_nt(br_ref[...], wo_ref[...]).astype(BF16)
            columns = br_ref[:, pl.ds(pl.multiple_of(member * width, width), width)]
            go_ref[0, member] = dot_tn(ctx_ref[...], columns).astype(BF16).reshape(2, 2, 2, share, width)
            go_ref[0, 1 - member] = dot_tn(other_ref[...], columns).astype(BF16).reshape(2, 2, 2, share, width)
            for kind in range(6, 9):
                sums.send(kind, 0)

        output_swap = (mine_ref.at[pl.ds(own // 2, own // 2)], theirs_ref, swap_sem.at[0, 2], swap_sem.at[1, 2], X)

        @pl.when(now == 8)
        def _():
            remote(*output_swap).start()

        at(0, 0, 0, 1, 5)
        at(4, 0, 3, 4, 7, 2)
        at(5, 1, 5)
        at(5, 0, 8, 6)
        at(7, 1, 0, 1)
        at(7, 0, 10)
        at(8, 0, 11, 9)
        at(8, 1, 2, 3, 4)
        at(9, 1, 6, 7)
        at(10, 2, 5)
        at(10, 1, 8)
        at(10, 2, 0)
        at(11, 2, 1)
        at(12, 1, 10, 11, 9)
        at(12, 2, 8)
        at(13, 2, 2)
        at(14, 2, 3)

        slab_cols = pl.ds(pl.multiple_of(pair * LANES, LANES), LANES)

        @pl.when(step == 0)
        def _():
            lane = lax.broadcasted_iota(jnp.int32, (length, LANES), 1)
            low_half = lane < HD
            grads = g_ref[:, slab_cols]
            prod = grads.astype(F32) * ctx_ref[:, slab_cols].astype(F32)
            for parity in range(2):
                mine = low_half if parity == 0 else jnp.logical_not(low_half)
                lead = HD if parity == 0 else 0
                delta = -jnp.sum(jnp.where(mine, prod, 0.0), axis=-1, keepdims=True)
                hi, mid, low = three_parts(delta)
                rows = jnp.where(mine, grads, jnp.zeros_like(grads))
                rows = jnp.where(lane == lead, hi, rows)
                rows = jnp.where(lane == lead + 1, mid, rows)
                ga_ref[parity] = jnp.where(lane == lead + 2, low, rows)
            ga_ref[2] = grads
            acc_ref[...] = jnp.zeros_like(acc_ref)

        lane = lax.broadcasted_iota(jnp.int32, (tile, LANES), 1)
        low_half = lane < HD
        keys = k_ref[...]
        values = v_ref[...]
        feats = fk_ref[0]
        keys_t = turned(keys)
        dks, dvs = [], []
        for parity in range(2):
            lead = HD if parity == 0 else 0
            mine = low_half if parity == 0 else jnp.logical_not(low_half)
            key_rows = jnp.where(mine, keys, feats)
            ones = jnp.where((lane >= lead) & (lane < lead + 3), 1.0, 0.0).astype(BF16)
            value_rows = jnp.where(mine, values, ones)
            probs = jnp.exp(dot_nt(key_rows, qa_ref[parity]))
            diff = dot_nt(value_rows, ga_ref[parity])
            score_grad = (probs * diff).astype(BF16)
            dvs.append(dot_nn(probs.astype(BF16), ga_ref[2]))
            dks.append(dot_nn(score_grad, qa_ref[parity]))
            side = keys_t[parity * HD : (parity + 1) * HD]
            acc_ref[parity * HD : (parity + 1) * HD] += dot_nn(side, score_grad)
        place = pl.ds(pl.multiple_of(step * tile, tile), tile)
        slab_ref[place, LANES : 2 * LANES] = jnp.where(low_half, dks[0], dks[1]).astype(BF16)
        slab_ref[place, 2 * LANES :] = jnp.where(low_half, dvs[0], dvs[1]).astype(BF16)

        def new_copies(kind, late):
            bit = (X, Y, Z_LOW)[kind]
            whole = gq_ref.at[early + late, kind]
            return (
                pltpu.make_async_copy(
                    whole.at[(ALL,) * bit + (sums.bits[bit],)], keep_new[kind].at[late], new_keep.at[kind, late]
                ),
                remote(
                    whole.at[(ALL,) * bit + (1 - sums.bits[bit],)],
                    got_new[kind].at[late],
                    new_send.at[kind, late],
                    new_recv.at[kind, late],
                    bit,
                ),
            )

        @pl.when(step == tiles - 1)
        def _():
            slab_ref[:, :LANES] = (acc_ref[...].T * HD ** (-0.5)).astype(BF16)
            slabs = slab_ref[...]
            made = dot_nn(nt_ref[...], slabs).astype(BF16)
            for kind in range(3):
                gq_ref[pair, kind] = made[:, kind * LANES : (kind + 1) * LANES].reshape(
                    2, 2, 2, 2, share, LANES
                )
            for one_pair in range(pairs):

                @pl.when(pair == one_pair)
                def _(one_pair=one_pair):
                    for kind in range(3):
                        if one_pair < early:
                            sums.send(9 + 3 * one_pair + kind, 0)
                        else:
                            for one in new_copies(kind, one_pair - early):
                                one.start()

            qb_ref[...] = jnp.sum(slabs[:, :LANES].astype(F32), axis=0, keepdims=True)
            vb_ref[...] = jnp.sum(slabs[:, 2 * LANES :].astype(F32), axis=0, keepdims=True)

        dn_swap = (dn_send, dn_got, swap_sem.at[0, 1], swap_sem.at[1, 1], MEMBER)

        @pl.when(step == tiles - 1)
        def _():
            weights = jnp.concatenate([wq_ref[...], wk_ref[...], wv_ref[...]], axis=1)
            for rows in (slice(own, length), slice(0, own)):
                grown = dot_nt(slab_ref[rows], weights)

                @pl.when(pair == 0)
                def _(rows=rows, grown=grown):
                    dn_acc[rows] = grown

                @pl.when((pair > 0) & (pair < pairs - 1))
                def _(rows=rows, grown=grown):
                    dn_acc[rows] += grown

                @pl.when(pair == pairs - 1)
                def _(rows=rows, grown=grown):
                    total = dn_acc[rows] + grown
                    if rows.start:
                        dn_send[...] = total.astype(BF16)
                        remote(*dn_swap).start()
                    else:
                        dn_ref[...] = total

        @pl.when(now == pairs * tiles - 1)
        def _():
            do(6, 2)
            do(4, 2)
            do(11, 2)
            do(7, 2)
            do(9, 2)
            do(8, 3)
            do(10, 2)
            do(6, 3)
            do(11, 3)
            do(7, 3)
            do(9, 3)
            do(10, 3)
            for late in range(pairs - early):
                for kind in range(3):
                    for one in new_copies(kind, late):
                        one.wait()
            sums.finish()
            remote(*dn_swap).wait()
            remote(*output_swap).wait()

    part = pl.BlockSpec((tile, LANES), lambda p, t: (t, p))
    bias_part = pl.BlockSpec((1, LANES), lambda p, t: (0, p))

    def columns(which):
        return pl.BlockSpec(
            (D, LANES), lambda p, t: (0, (2 * which + lax.axis_index("member")) * pairs + p)
        )

    slots = []
    for shape in shapes:
        slots += slot_shapes(shape[0], 3, shape[4:])
    for _, size in OUT_CUTS:
        slots += slot_shapes(1, 4, (share, size))
    for _ in range(3 * early):
        slots += slot_shapes(1, 4, (share, LANES))
    new = [jax.ShapeDtypeStruct((pairs - early, 2, 2, 2, share, LANES), BF16)] * 3
    own_f32 = jax.ShapeDtypeStruct((own, D), F32)
    results = pl.pallas_call(
        body,
        grid=(pairs, tiles),
        out_shape=[
            own_f32,
            own_f32,
            jax.ShapeDtypeStruct((8, D), F32),
            jax.ShapeDtypeStruct((1, width), F32),
            jax.ShapeDtypeStruct((1, width), F32),
            jax.ShapeDtypeStruct((share, 4 * chunk), F32),
            jax.ShapeDtypeStruct((LANES, D), F32),
            jax.ShapeDtypeStruct((share, width), F32),
            jax.ShapeDtypeStruct((share, 3 * early * LANES), F32),
            jax.ShapeDtypeStruct((own, D), BF16),
            jax.ShapeDtypeStruct((own // 2, D), BF16),
        ]
        + new
        + new,
        in_specs=[
            pl.BlockSpec((2, length, LANES), lambda p, t: (p, 0, 0)),
            part,
            part,
            pl.BlockSpec((1, tile, LANES), lambda p, t: (p, t, 0)),
            in_vmem(),
            in_vmem(),
            in_vmem(),
            in_vmem(),
            in_vmem(),
            pl.BlockSpec((own, D), lambda p, t: (0, 0)),
            in_vmem(),
            pl.BlockSpec((width, D), lambda p, t: (lax.axis_index("member"), 0)),
            in_vmem(),
            columns(0),
            columns(1),
            columns(2),
        ]
        + [anywhere()] * 13,
        out_specs=[in_vmem(), in_vmem(), in_vmem(), bias_part, bias_part]
        + [in_vmem()] * 4
        + [anywhere()] * 8,
        scratch_shapes=[
            pltpu.VMEM((3, length, LANES), BF16),
            pltpu.VMEM((LANES, length), F32),
            pltpu.VMEM((length, 3 * LANES), BF16),
            pltpu.VMEM((length, D), F32),
            pltpu.VMEM((own, D), BF16),
            pltpu.VMEM((pairs, 3, 2, 2, 2, 2, share, LANES), BF16),
            pltpu.VMEM((length, D), BF16),
            pltpu.VMEM((length, width), BF16),
            pltpu.VMEM((1, 2, 2, 2, 2, share, width), BF16),
        ]
        + [pltpu.VMEM(shape, BF16) for shape in shapes]
        + [pltpu.VMEM(shape, BF16) for shape in shapes]
        + slots
        + [
            pltpu.SemaphoreType.DMA((count, 4)),
            pltpu.SemaphoreType.DMA((count, 4)),
            pltpu.SemaphoreType.DMA((2, 6)),
            pltpu.SemaphoreType.DMA((3, pairs - early)),
            pltpu.SemaphoreType.DMA((3, pairs - early)),
            pltpu.SemaphoreType.DMA((3, pairs - early)),
            pltpu.SemaphoreType.DMA((2, 3)),
        ],
        compiler_params=params(3),
        name="attend_backward",
    )(
        rows_aug, k, v, feat_k, ctx, ctx_other, mid, n2_grad, n2_grad_got, cot, vectors, w_out, normed_t,
        w_qkv, w_qkv, w_qkv, output_own, *kept, *got,
    )
    return results[:11], results[11:14], results[14:]


def finish(tokens, mid_grad, normed_grad, normed_grad_got, vectors, sums_in, in_bias_rows, q_sum, v_sum, ready, kept, got):
    own = mid_grad.shape[0]
    rows = own // 2
    width = q_sum.shape[1]
    late, share = kept[0].shape[0], kept[0].shape[-2]
    per = share // 2
    last = 3 * late * LANES + LANES

    def body(*refs):
        tok_ref, mg_ref, dn_ref, dn_got, vec_ref, sum_ref, inb_ref, qb_ref, vb_ref, ready_ref = refs[:10]
        keep, first = refs[10:13], refs[13:16]
        ig_ref, ig_got, ready_got, last_ref, last_got = refs[16:21]
        ig_send, source, last_all, flat, shares = refs[21:26]
        begin, slots = refs[26:29], refs[29:38]
        send_sem, recv_sem, swap_sem, share_sem = refs[38:]
        member = lax.axis_index("member")
        barrier = pltpu.get_barrier_semaphore()
        for mask in range(1, 16):
            pl.semaphore_signal(barrier, inc=1, device_id=chip_across(mask), device_id_type=MESH_IDS)
        pl.semaphore_signal(barrier, inc=1, device_id=device_across(MEMBER), device_id_type=MESH_IDS)
        pl.semaphore_wait(barrier, 16)
        theirs = pl.ds(pl.multiple_of((1 - member) * per, per), per)
        swaps = [
            remote(ready_ref.at[theirs], ready_got, swap_sem.at[0, 0], swap_sem.at[1, 0], MEMBER),
            remote(ig_send, ig_got, swap_sem.at[0, 1], swap_sem.at[1, 1], X),
            remote(last_all.at[theirs], last_got, swap_sem.at[0, 2], swap_sem.at[1, 2], MEMBER),
        ]
        sums = Sums(send_sem, recv_sem)
        for kind in range(3):
            dims = tuple(b for b in CHIP if b != ORDERS[kind][0])
            sums.add(kind, begin[kind], dims, ORDERS[kind][1:], slots[3 * kind : 3 * kind + 3])
            begin[kind][...] = keep[kind][...] + first[kind][...]
            sums.send(kind, 0)
        swaps[0].start()

        gain_sum, bias_sum = 0.0, 0.0
        for part in (slice(rows, own), slice(0, rows)):
            unit, scale = normalise(tok_ref[part].astype(F32))
            grad = dn_ref[part] + dn_got[part].astype(F32)
            input_grad = mg_ref[part] + normalise_back(unit, scale, grad * vec_ref[4:5])
            if part.start:
                ig_send[...] = input_grad.astype(BF16)
                swaps[1].start()
            else:
                ig_ref[...] = input_grad
            gain_sum = gain_sum + jnp.sum(grad * unit, axis=0, keepdims=True)
            bias_sum = bias_sum + jnp.sum(grad, axis=0, keepdims=True)
        flat[0:1] = gain_sum
        flat[1:2] = bias_sum
        flat[2:6] = sum_ref[0:4]
        blank = jnp.zeros((1, width), F32)
        for row, ref in ((6, qb_ref), (7, vb_ref)):
            value = ref[...]
            flat[row : row + 1, :width] = jnp.where(member == 0, value, blank)
            flat[row : row + 1, width:] = jnp.where(member == 1, value, blank)
        flat[8:16] = inb_ref[...]
        flat[16:] = jnp.zeros((LANES - 16, D), F32)
        source[...] = flat[...].T.astype(BF16).reshape(source.shape)

        def straight(mask):
            place = tuple(1 - bit if mask & flag else bit for bit, flag in zip(sums.bits, (8, 4, 2, 1)))
            return pltpu.make_async_remote_copy(
                src_ref=source.at[place],
                dst_ref=shares.at[mask],
                send_sem=share_sem.at[0, mask],
                recv_sem=share_sem.at[1, mask],
                device_id=chip_across(mask),
                device_id_type=MESH_IDS,
            )

        for mask in range(1, 16):
            straight(mask).start()
        for depth in range(3):
            for kind in range(3):
                total = sums.take(kind, depth)
                if depth == 2:
                    for pair in range(late):
                        place = (kind * late + pair) * LANES
                        last_all[:, place : place + LANES] = total[pair]
        total = source[sums.bits[:4]].astype(F32)
        for mask in range(1, 16):
            straight(mask).wait_recv()
            total = total + shares[mask].astype(F32)
        last_all[:, last - LANES :] = total
        swaps[2].start()
        last_ref[...] = last_all[...]
        sums.finish()
        for mask in range(1, 16):
            straight(mask).wait_send()
        for one in swaps:
            one.wait()

    slots = []
    for _ in range(3):
        slots += slot_shapes(late, 3, (share, LANES))
    return pl.pallas_call(
        body,
        out_shape=(
            jax.ShapeDtypeStruct((rows, D), F32),
            jax.ShapeDtypeStruct((rows, D), BF16),
            jax.ShapeDtypeStruct((per, ready.shape[1]), F32),
            jax.ShapeDtypeStruct((share, last), F32),
            jax.ShapeDtypeStruct((per, last), F32),
        ),
        in_specs=[in_vmem()] * 16,
        out_specs=(in_vmem(), anywhere(), anywhere(), in_vmem(), anywhere()),
        scratch_shapes=[
            pltpu.VMEM((rows, D), BF16),
            pltpu.VMEM((2, 2, 2, 2, share, LANES), BF16),
            pltpu.VMEM((share, last), F32),
            pltpu.VMEM((LANES, D), F32),
            pltpu.VMEM((16, share, LANES), BF16),
        ]
        + [pltpu.VMEM(kept[0].shape, BF16)] * 3
        + slots
        + [
            pltpu.SemaphoreType.DMA((3, 3)),
            pltpu.SemaphoreType.DMA((3, 3)),
            pltpu.SemaphoreType.DMA((2, 3)),
            pltpu.SemaphoreType.DMA((2, 16)),
        ],
        compiler_params=params(2),
        name="finish",
    )(
        tokens, mid_grad, normed_grad, normed_grad_got, vectors, sums_in, in_bias_rows, q_sum, v_sum, ready, *kept, *got
    )


def per_device_pair(
    tokens,
    ln1_gain,
    ln1_bias,
    w_qkv,
    q_bias,
    v_bias,
    w_out,
    out_bias,
    ln2_gain,
    ln2_bias,
    w_in,
    in_bias,
    w_down,
    down_bias,
    cotangent,
    segment_ids,
    random_blocks,
    global_blocks,
):
    rows = tokens.shape[0]
    blocks = segment_ids.shape[0] // BLK
    half = lax.axis_index("half")
    member = lax.axis_index("member")
    mine_d = D // 2
    heads = HEADS // 2
    chips = lax.axis_size("batch") * 2

    def sides(x):
        return (
            lax.dynamic_index_in_dim(x, half, 1, keepdims=False),
            lax.dynamic_index_in_dim(x, 1 - half, 1, keepdims=False),
        )

    def both_sequences(kept, other):
        return jnp.where(
            half == 0, jnp.stack([kept, other], axis=1), jnp.stack([other, kept], axis=1)
        )

    seq_random = lax.dynamic_index_in_dim(random_blocks, half, 1, keepdims=False)
    seq_random = lax.dynamic_slice_in_dim(seq_random, member * heads, heads, 1)
    pair_random = seq_random.reshape(blocks, heads // 2, 2 * RAND).transpose(1, 0, 2).astype(F32)
    blank = jnp.zeros((D,), BF16)
    vectors = jnp.stack(
        [out_bias, ln2_gain, ln2_bias, down_bias, ln1_gain, ln1_bias, blank, blank]
    ).astype(F32)

    own_tokens, normed_t, queries, keys, values = begin(
        *sides(tokens), vectors, w_qkv, q_bias.astype(F32).reshape(1, D), v_bias.astype(F32).reshape(1, D)
    )
    context, rows_aug, feat_k, context_other, cot = attend_forward(
        queries, keys, values, segment_ids.T, pair_random, global_blocks, *sides(cotangent)
    )
    (out_part, out_got, n2_grad, n2_grad_got, mid_stream, in_bias_grad), kept_parts, got_parts = feed_forward(
        context,
        context_other,
        own_tokens,
        w_out,
        vectors,
        cot,
        w_in,
        in_bias.astype(F32).reshape(1, -1),
        w_down,
    )
    output_own = (out_part + out_got.astype(F32)).astype(BF16)

    in_bias_rows = in_bias_grad.reshape(2, 2, 2, 2, 2, LANES // 2).transpose(4, 2, 0, 1, 3, 5).reshape(2, D)
    gone = jnp.zeros_like(in_bias_rows)
    in_bias_rows = jnp.concatenate(
        [
            jnp.where(member == 0, in_bias_rows, gone),
            jnp.where(member == 1, in_bias_rows, gone),
            jnp.zeros((4, D), F32),
        ]
    )

    (
        (
            normed_grad,
            mid_grad,
            sums_in,
            q_sum,
            v_sum,
            summed_in,
            summed_down,
            summed_out,
            summed_early,
            normed_grad_got,
            output_other,
        ),
        kept_qkv,
        got_qkv,
    ) = attend_backward(
        rows_aug,
        keys,
        values,
        feat_k,
        context,
        context_other,
        mid_stream,
        n2_grad,
        n2_grad_got,
        cot,
        vectors,
        w_out,
        normed_t,
        w_qkv,
        output_own,
        kept_parts,
        got_parts,
    )
    output = both_sequences(output_own[:rows], output_other)
    ready = jnp.concatenate([summed_in, summed_out, summed_early], axis=1)
    input_kept, input_other, ready_got, last_all, last_got = finish(
        own_tokens,
        mid_grad,
        normed_grad,
        normed_grad_got,
        vectors,
        sums_in,
        in_bias_rows,
        q_sum,
        v_sum,
        ready,
        kept_qkv,
        got_qkv,
    )
    input_grad = both_sequences(input_kept, input_other.astype(F32))

    per = ready.shape[0] // 2
    chip_rows = jnp.concatenate([ready, last_all], axis=1)
    mine_rows = lax.dynamic_slice_in_dim(chip_rows, member * per, per, 0)
    got_rows = jnp.concatenate([ready_got, last_got], axis=1)
    left = jnp.where(member == 0, mine_rows, got_rows)
    right = jnp.where(member == 0, got_rows, mine_rows)

    start_out = summed_in.shape[1]
    start_early = start_out + mine_d
    start_late = ready.shape[1]
    early = summed_early.shape[1] // 3
    late = mine_d - early
    pieces = []
    for part in range(3):
        for x in (left, right):
            pieces.append(x[:, start_early + part * early : start_early + (part + 1) * early])
            pieces.append(x[:, start_late + part * late : start_late + (part + 1) * late])
    w_qkv_grad = jnp.concatenate(pieces, axis=1)
    w_out_grad = jnp.concatenate([x[:, start_out : start_out + mine_d] for x in (left, right)], axis=1)
    w_in_grad = jnp.concatenate(
        [x[:, j * LANES : (j + 1) * LANES] for j in range(chips) for x in (left, right)], axis=1
    )
    start = start_late + 3 * late
    vector_sums = left[:, start : start + 8] + right[:, start : start + 8]
    in_mine = lax.dynamic_slice_in_dim(last_all, 3 * late + 8 + 2 * member, 2, 1)
    in_bias_out = in_mine.T.reshape(LANES)
    vec = [vector_sums[:, i] for i in range(8)]
    return (
        output,
        input_grad,
        vec[0],
        vec[1],
        w_qkv_grad,
        vec[6],
        vec[7],
        w_out_grad,
        vec[2],
        vec[3],
        vec[4],
        w_in_grad,
        in_bias_out,
        summed_down,
        vec[5],
    )


def solution(mesh):
    def program(*args):
        sequences = args[0].shape[1] // mesh.shape["batch"]
        seq = mesh.shape["seq"]
        fast = sequences == 2 and seq == 4 and mesh.shape["batch"] == 8
        if fast:
            use = jax.sharding.Mesh(
                mesh.devices.reshape(mesh.shape["batch"], 2, 2), ("batch", "half", "member")
            )
            seq_axes, all_axes, run = ("half", "member"), ("batch", "half", "member"), per_device_pair
        else:
            use, seq_axes, all_axes, run = mesh, "seq", ("batch", "seq"), per_device
        rows = P(seq_axes, "batch", None)
        in_specs = (rows,) + (P(),) * 13 + (
            rows,
            P(None, "batch"),
            P(None, "batch", None, None),
            P(None, "batch"),
        )
        vector, matrix = P(all_axes), P(all_axes, None)
        out_specs = (
            rows,
            rows,
            vector,
            vector,
            matrix,
            vector,
            vector,
            matrix,
            vector,
            vector,
            vector,
            matrix,
            vector,
            matrix,
            vector,
        )
        return jax.shard_map(
            run, mesh=use, in_specs=in_specs, out_specs=out_specs, check_vma=False
        )(*args)

    return program
```

```python
import jax
import jax.numpy as jnp
import numpy as np
from jax import lax
from jax.experimental import pallas as pl
from jax.experimental.pallas import tpu as pltpu
from jax.sharding import PartitionSpec as P

D = 1024
HEADS = 16
HD = 64
BLK = 64
RAND = 3
GLOB = 2


eps = 1e-05


def padded(x, sides, width):
    for axis, dim in sides:
        size, length = (lax.axis_size(axis), x.shape[dim])
        up = [(i, (i + 1) % size) for i in range(size - 1)]
        down = [(j, i) for i, j in up]
        last = lax.slice_in_dim(x, length - width, length, axis=dim)
        initial = lax.slice_in_dim(x, 0, width, axis=dim)
        before = lax.ppermute(last, axis, up)
        after = lax.ppermute(initial, axis, down)
        x = jnp.concatenate([before, x, after], axis=dim)
    return x


def layer_norm(values, gain_vec, shift_vec):
    row_mean = jnp.mean(values, axis=-1, keepdims=True)
    centred = values - row_mean
    spread = jnp.mean(centred * centred, axis=-1, keepdims=True)
    return centred * lax.rsqrt(spread + eps) * gain_vec + shift_vec


def gelu_tanh(values):
    return jax.nn.gelu(values, approximate=True)


def window_stack(extended, query_blocks):
    return jnp.stack(
        [extended[0:query_blocks], extended[1 : query_blocks + 1], extended[2 : query_blocks + 2]],
        axis=1,
    )


def pick_blocks(shard_rows, random_local, global_blocks):
    block_total = shard_rows.shape[0] // BLK
    seq_count = shard_rows.shape[1]
    numbers = jnp.arange(block_total, dtype=jnp.int32)
    random_hits = (random_local[..., None] == numbers).astype(jnp.bfloat16)
    global_hits = (global_blocks[..., None] == numbers).astype(jnp.bfloat16)
    blocks = shard_rows.reshape(block_total, BLK, seq_count, 2, HEADS, HD)
    picked_random = jnp.einsum(
        "ishjb,busxhd->ishjuxd", random_hits, blocks, preferred_element_type=jnp.float32
    )
    picked_global = jnp.einsum(
        "gsb,busc->gusc",
        global_hits,
        shard_rows.reshape(block_total, BLK, seq_count, 2 * D),
        preferred_element_type=jnp.float32,
    )
    return (picked_random, picked_global)


def key_products(left_side, window_kv, far_random, far_global, which_half):
    near_part = jnp.einsum(
        "itshd,iwushd->ishtwu",
        left_side,
        window_kv[:, :, :, :, which_half],
        preferred_element_type=jnp.float32,
    )
    far_part = jnp.einsum(
        "itshd,ishjud->ishtju",
        left_side,
        far_random[:, :, :, :, :, which_half],
        preferred_element_type=jnp.float32,
    )
    global_part = jnp.einsum(
        "itshd,gushd->ishtgu",
        left_side,
        far_global[:, :, :, which_half],
        preferred_element_type=jnp.float32,
    )
    lead_shape = near_part.shape[:4]
    return jnp.concatenate(
        [
            near_part.reshape(lead_shape + (-1,)),
            far_part.reshape(lead_shape + (-1,)),
            global_part.reshape(lead_shape + (-1,)),
        ],
        axis=-1,
    )


def split_slots(weights):
    lead_shape = weights.shape[:4]
    near_cut = 3 * BLK
    far_cut = (3 + RAND) * BLK
    near_part = weights[..., :near_cut].reshape(lead_shape + (3, BLK))
    far_part = weights[..., near_cut:far_cut].reshape(lead_shape + (RAND, BLK))
    global_part = weights[..., far_cut:].reshape(lead_shape + (GLOB, BLK))
    return (near_part, far_part, global_part)


def key_mix(weights, window_kv, far_random, far_global, which_half):
    near_part, far_part, global_part = split_slots(weights)
    mixed = jnp.einsum(
        "ishtwu,iwushd->itshd",
        near_part,
        window_kv[:, :, :, :, which_half],
        preferred_element_type=jnp.float32,
    )
    mixed = mixed + jnp.einsum(
        "ishtju,ishjud->itshd",
        far_part,
        far_random[:, :, :, :, :, which_half],
        preferred_element_type=jnp.float32,
    )
    mixed = mixed + jnp.einsum(
        "ishtgu,gushd->itshd",
        global_part,
        far_global[:, :, :, which_half],
        preferred_element_type=jnp.float32,
    )
    return mixed


def key_grads(weights, left_side):
    near_part, far_part, global_part = split_slots(weights)
    near_grad = jnp.einsum(
        "ishtwu,itshd->iwushd", near_part, left_side, preferred_element_type=jnp.float32
    )
    far_grad = jnp.einsum(
        "ishtju,itshd->ishjud", far_part, left_side, preferred_element_type=jnp.float32
    )
    global_grad = jnp.einsum(
        "ishtgu,itshd->gushd", global_part, left_side, preferred_element_type=jnp.float32
    )
    return (near_grad, far_grad, global_grad)


def per_device(
    tokens,
    ln1_gain,
    ln1_bias,
    w_qkv,
    q_bias,
    v_bias,
    w_out,
    out_bias,
    ln2_gain,
    ln2_bias,
    w_in,
    in_bias,
    w_down,
    down_bias,
    cotangent,
    segment_ids,
    random_blocks,
    global_blocks,
):
    row_count = tokens.shape[0]
    seq_count = tokens.shape[1]
    query_blocks = row_count // BLK
    seq_length = segment_ids.shape[0]
    device_now = lax.axis_index("seq")
    first_row = device_now * row_count
    score_scale = HD ** (-0.5)
    random_local = lax.dynamic_slice_in_dim(
        random_blocks, device_now * query_blocks, query_blocks, 0
    )
    inputs = tokens.astype(jnp.float32)
    normed_full, first_norm_back = jax.vjp(
        layer_norm, inputs, ln1_gain.astype(jnp.float32), ln1_bias.astype(jnp.float32)
    )
    normed = normed_full.astype(jnp.bfloat16)
    projected = jnp.einsum("rsd,de->rse", normed, w_qkv, preferred_element_type=jnp.float32)
    queries = (projected[:, :, :D] + q_bias.astype(jnp.float32)).astype(jnp.bfloat16)
    value_shift = jnp.concatenate([jnp.zeros((D,), jnp.float32), v_bias.astype(jnp.float32)])
    keyval = (projected[:, :, D:] + value_shift).astype(jnp.bfloat16)
    extended = padded(keyval, (("seq", 0),), BLK)
    window_kv = window_stack(
        extended.reshape(query_blocks + 2, BLK, seq_count, 2, HEADS, HD), query_blocks
    )
    picked = pick_blocks(
        lax.all_gather(keyval, "seq", axis=0, tiled=True), random_local, global_blocks
    )
    far_random = picked[0].astype(jnp.bfloat16)
    far_global = picked[1].astype(jnp.bfloat16).reshape(GLOB, BLK, seq_count, 2, HEADS, HD)
    query_segment = lax.dynamic_slice_in_dim(segment_ids, first_row, row_count, 0)
    query_segment = query_segment.reshape(query_blocks, BLK, seq_count).transpose(0, 2, 1)
    window_spots = first_row - BLK + jnp.arange(row_count + 2 * BLK, dtype=jnp.int32)
    inside_seq = (window_spots >= 0) & (window_spots < seq_length)
    near_segment = jnp.take(segment_ids, jnp.clip(window_spots, 0, seq_length - 1), axis=0)
    near_segment = jnp.where(inside_seq[:, None], near_segment, -1)
    near_segment = window_stack(
        near_segment.reshape(query_blocks + 2, BLK, seq_count), query_blocks
    )
    near_segment = near_segment.transpose(0, 3, 1, 2).reshape(query_blocks, seq_count, 1, 3 * BLK)
    segment_rows = segment_ids.T
    sequence_pick = jnp.arange(seq_count, dtype=jnp.int32)
    offsets = jnp.arange(BLK, dtype=jnp.int32)
    far_segment = segment_rows[
        sequence_pick[None, :, None, None, None], random_local[..., None] * BLK + offsets
    ]
    far_segment = far_segment.reshape(query_blocks, seq_count, HEADS, RAND * BLK)
    global_segment = segment_rows[
        sequence_pick[None, :, None], global_blocks[..., None] * BLK + offsets
    ]
    global_segment = global_segment.transpose(1, 0, 2).reshape(1, seq_count, 1, GLOB * BLK)
    key_segment = jnp.concatenate(
        [
            jnp.broadcast_to(near_segment, (query_blocks, seq_count, HEADS, 3 * BLK)),
            far_segment,
            jnp.broadcast_to(global_segment, (query_blocks, seq_count, HEADS, GLOB * BLK)),
        ],
        axis=-1,
    )
    allowed = key_segment[:, :, :, None, :] == query_segment[:, :, None, :, None]
    query_rows = queries.reshape(query_blocks, BLK, seq_count, HEADS, HD)
    scores = jnp.where(
        allowed, key_products(query_rows, window_kv, far_random, far_global, 0) * score_scale, -1e30
    )
    row_max = jnp.max(scores, axis=-1, keepdims=True)
    log_total = row_max + jnp.log(jnp.sum(jnp.exp(scores - row_max), axis=-1, keepdims=True))
    soft_full = jnp.exp(scores - log_total)
    attn_probs = soft_full.astype(jnp.bfloat16)
    context = (
        key_mix(attn_probs, window_kv, far_random, far_global, 1)
        .reshape(row_count, seq_count, D)
        .astype(jnp.bfloat16)
    )
    mid_stream = (
        inputs
        + jnp.einsum("rsd,de->rse", context, w_out, preferred_element_type=jnp.float32)
        + out_bias.astype(jnp.float32)
    )
    normed2_full, second_norm_back = jax.vjp(
        layer_norm, mid_stream, ln2_gain.astype(jnp.float32), ln2_bias.astype(jnp.float32)
    )
    normed2 = normed2_full.astype(jnp.bfloat16)
    pre_act = jnp.einsum(
        "rsd,df->rsf", normed2, w_in, preferred_element_type=jnp.float32
    ) + in_bias.astype(jnp.float32)
    hidden_full, gelu_back = jax.vjp(gelu_tanh, pre_act)
    hidden = hidden_full.astype(jnp.bfloat16)
    output = (
        mid_stream
        + jnp.einsum("rsf,fd->rsd", hidden, w_down, preferred_element_type=jnp.float32)
        + down_bias.astype(jnp.float32)
    ).astype(jnp.bfloat16)
    grad_out = cotangent.astype(jnp.float32)
    w_down_grad = jnp.einsum("rsf,rsd->fd", hidden, cotangent, preferred_element_type=jnp.float32)
    down_bias_grad = jnp.sum(grad_out, axis=(0, 1))
    pre_grad = gelu_back(
        jnp.einsum("rsd,fd->rsf", cotangent, w_down, preferred_element_type=jnp.float32)
    )[0].astype(jnp.bfloat16)
    w_in_grad = jnp.einsum("rsd,rsf->df", normed2, pre_grad, preferred_element_type=jnp.float32)
    in_bias_grad = jnp.sum(pre_grad.astype(jnp.float32), axis=(0, 1))
    mid_part, ln2_gain_grad, ln2_bias_grad = second_norm_back(
        jnp.einsum("rsf,df->rsd", pre_grad, w_in, preferred_element_type=jnp.float32)
    )
    mid_grad = grad_out + mid_part
    branch_grad = mid_grad.astype(jnp.bfloat16)
    w_out_grad = jnp.einsum("rsd,rse->de", context, branch_grad, preferred_element_type=jnp.float32)
    out_bias_grad = jnp.sum(branch_grad.astype(jnp.float32), axis=(0, 1))
    context_grad = jnp.einsum(
        "rse,de->rsd", branch_grad, w_out, preferred_element_type=jnp.float32
    ).astype(jnp.bfloat16)
    grad_rows = context_grad.reshape(query_blocks, BLK, seq_count, HEADS, HD)
    probs_grad = key_products(grad_rows, window_kv, far_random, far_global, 1)
    score_grad = (
        soft_full * (probs_grad - jnp.sum(soft_full * probs_grad, axis=-1, keepdims=True))
    ).astype(jnp.bfloat16)
    query_grad = (
        (key_mix(score_grad, window_kv, far_random, far_global, 0) * score_scale)
        .reshape(row_count, seq_count, D)
        .astype(jnp.bfloat16)
    )
    near_key, far_key, global_key = key_grads(score_grad, query_rows)
    near_value, far_value, global_value = key_grads(attn_probs, grad_rows)
    near_kv = jnp.stack([near_key * score_scale, near_value], axis=4)
    far_kv = jnp.stack([far_key * score_scale, far_value], axis=5)
    global_kv = jnp.stack([global_key * score_scale, global_value], axis=3).reshape(
        GLOB, BLK, seq_count, 2 * D
    )
    rest_pad = ((0, 0),) * 5
    extended_grad = (
        jnp.pad(near_kv[:, 0], ((0, 2),) + rest_pad)
        + jnp.pad(near_kv[:, 1], ((1, 1),) + rest_pad)
        + jnp.pad(near_kv[:, 2], ((2, 0),) + rest_pad)
    )
    extended_grad = extended_grad.reshape(row_count + 2 * BLK, seq_count, 2 * D)
    rim_grads = jnp.concatenate([extended_grad[:BLK], extended_grad[row_count + BLK :]], axis=0)
    returned = padded(rim_grads.astype(jnp.bfloat16), (("seq", 0),), BLK).astype(rim_grads.dtype)
    near_total = extended_grad[BLK : row_count + BLK]
    near_total = (
        near_total.at[:BLK].add(returned[:BLK]).at[row_count - BLK :].add(returned[3 * BLK :])
    )
    block_total = row_count * lax.axis_size("seq") // BLK
    numbers = jnp.arange(block_total, dtype=jnp.int32)
    random_hits = (random_local[..., None] == numbers).astype(jnp.float32)
    global_rows_hit = (global_blocks[..., None] == numbers).astype(jnp.float32)

    def far_sum(one_sequence):
        hits, kv, global_rows, global_sum = one_sequence
        random_term = jnp.einsum(
            "ihjb,ihjuxd->buxhd", hits, kv, precision=lax.Precision.HIGHEST
        )
        global_term = jnp.einsum(
            "gb,guc->buc", global_rows, global_sum, precision=lax.Precision.HIGHEST
        )
        flat = (block_total * BLK, 2 * D)
        return (random_term.reshape(flat) + global_term.reshape(flat)).astype(jnp.bfloat16)

    far_parts = lax.map(
        far_sum,
        (
            jnp.moveaxis(random_hits, 1, 0),
            jnp.moveaxis(far_kv, 1, 0),
            jnp.moveaxis(global_rows_hit, 1, 0),
            jnp.moveaxis(global_kv, 2, 0),
        ),
    )
    far_total = lax.psum_scatter(far_parts, "seq", scatter_dimension=1, tiled=True)
    far_total = jnp.moveaxis(far_total, 0, 1).astype(jnp.float32)
    keyval_grad = (near_total + far_total).astype(jnp.bfloat16)
    qkv_grad = jnp.concatenate([query_grad, keyval_grad], axis=-1)
    q_bias_grad = jnp.sum(query_grad.astype(jnp.float32), axis=(0, 1))
    v_bias_grad = jnp.sum(keyval_grad[:, :, D:].astype(jnp.float32), axis=(0, 1))
    w_qkv_grad = jnp.einsum("rsd,rse->de", normed, qkv_grad, preferred_element_type=jnp.float32)
    input_part, ln1_gain_grad, ln1_bias_grad = first_norm_back(
        jnp.einsum("rse,de->rsd", qkv_grad, w_qkv, preferred_element_type=jnp.float32)
    )
    input_grad = mid_grad + input_part
    summed = (
        lax.psum_scatter(ln1_gain_grad, ("batch", "seq"), scatter_dimension=0, tiled=True),
        lax.psum_scatter(ln1_bias_grad, ("batch", "seq"), scatter_dimension=0, tiled=True),
        lax.psum_scatter(w_qkv_grad, ("batch", "seq"), scatter_dimension=0, tiled=True),
        lax.psum_scatter(q_bias_grad, ("batch", "seq"), scatter_dimension=0, tiled=True),
        lax.psum_scatter(v_bias_grad, ("batch", "seq"), scatter_dimension=0, tiled=True),
        lax.psum_scatter(w_out_grad, ("batch", "seq"), scatter_dimension=0, tiled=True),
        lax.psum_scatter(out_bias_grad, ("batch", "seq"), scatter_dimension=0, tiled=True),
        lax.psum_scatter(ln2_gain_grad, ("batch", "seq"), scatter_dimension=0, tiled=True),
        lax.psum_scatter(ln2_bias_grad, ("batch", "seq"), scatter_dimension=0, tiled=True),
        lax.psum_scatter(w_in_grad, ("batch", "seq"), scatter_dimension=0, tiled=True),
        lax.psum_scatter(in_bias_grad, ("batch", "seq"), scatter_dimension=0, tiled=True),
        lax.psum_scatter(w_down_grad, ("batch", "seq"), scatter_dimension=0, tiled=True),
        lax.psum_scatter(down_bias_grad, ("batch", "seq"), scatter_dimension=0, tiled=True),
    )
    return (
        output,
        input_grad,
        summed[0],
        summed[1],
        summed[2],
        summed[3],
        summed[4],
        summed[5],
        summed[6],
        summed[7],
        summed[8],
        summed[9],
        summed[10],
        summed[11],
        summed[12],
    )


NEG = -1e30
LANES = 128
SEG_VALUES = 4
MESH_IDS = pl.DeviceIdType.MESH
VMEM_BYTES = 60 * 1024 * 1024
F32 = jnp.float32
BF16 = jnp.bfloat16
ALL = slice(None)
Z_HIGH, Z_LOW, Y, X, MEMBER = range(5)
CHIP = (Z_HIGH, Z_LOW, Y, X)


def three_parts(x):
    hi = x.astype(BF16)
    rest = x - hi.astype(F32)
    mid = rest.astype(BF16)
    low = (rest - mid.astype(F32)).astype(BF16)
    return hi, mid, low


def dot_nt(a, b):
    return lax.dot_general(a, b, (((1,), (1,)), ((), ())), preferred_element_type=F32)


def dot_nn(a, b):
    return lax.dot_general(a, b, (((1,), (0,)), ((), ())), preferred_element_type=F32)


def dot_tn(a, b):
    return lax.dot_general(a, b, (((0,), (0,)), ((), ())), preferred_element_type=F32)


def turned(x):
    return x.astype(F32).T.astype(BF16)


def normalise(values):
    mean = jnp.mean(values, axis=-1, keepdims=True)
    centred = values - mean
    scale = lax.rsqrt(jnp.mean(centred * centred, axis=-1, keepdims=True) + eps)
    return centred * scale, scale


def normalise_back(unit, scale, grad):
    first = jnp.mean(grad, axis=-1, keepdims=True)
    second = jnp.mean(grad * unit, axis=-1, keepdims=True)
    return (grad - first - unit * second) * scale


def my_bits():
    batch = lax.axis_index("batch")
    return (
        lax.div(batch, 4),
        lax.rem(lax.div(batch, 2), 2),
        lax.rem(batch, 2),
        lax.axis_index("half"),
        lax.axis_index("member"),
    )


def device_across(bit):
    batch = lax.axis_index("batch")
    half = lax.axis_index("half")
    member = lax.axis_index("member")
    if bit == MEMBER:
        return (batch, half, 1 - member)
    if bit == X:
        return (batch, 1 - half, member)
    stride = (4, 2, 1)[bit]
    return (batch + stride * (1 - 2 * my_bits()[bit]), half, member)


def chip_across(mask):
    z_high, z_low, y, x, member = my_bits()
    flipped = [1 - b if mask & flag else b for b, flag in zip((z_high, z_low, y, x), (8, 4, 2, 1))]
    return (4 * flipped[0] + 2 * flipped[1] + flipped[2], flipped[3], member)


def remote(src, dst, send, recv, bit):
    return pltpu.make_async_remote_copy(
        src_ref=src,
        dst_ref=dst,
        send_sem=send,
        recv_sem=recv,
        device_id=device_across(bit),
        device_id_type=MESH_IDS,
    )


def greet(bits):
    barrier = pltpu.get_barrier_semaphore()
    for bit in bits:
        pl.semaphore_signal(barrier, inc=1, device_id=device_across(bit), device_id_type=MESH_IDS)
    pl.semaphore_wait(barrier, len(bits))


class Sums:
    def __init__(self, send_sem, recv_sem):
        self.bits = my_bits()
        self.send_sem, self.recv_sem = send_sem, recv_sem
        self.pieces = {}

    def add(self, number, source, dims, order, slots, cut=()):
        self.pieces[number] = (source, dims, order, slots, cut)

    def side(self, number, depth, across):
        source, dims, order, slots, cut = self.pieces[number]
        bit = order[depth]
        value = 1 - self.bits[bit] if across else self.bits[bit]
        left = [b for b in dims if b not in order[:depth]]
        spot = left.index(bit)
        index = (ALL,) * (1 + spot) + (value,)
        if depth:
            return slots[depth - 1].at[index]
        return source.at[index + (ALL,) * (len(left) - 1 - spot) + cut]

    def copy(self, number, depth):
        _, _, order, slots, _ = self.pieces[number]
        return remote(
            self.side(number, depth, True),
            slots[depth],
            self.send_sem.at[number, depth],
            self.recv_sem.at[number, depth],
            order[depth],
        )

    def send(self, number, depth):
        self.copy(number, depth).start()

    def take(self, number, depth):
        _, _, order, slots, _ = self.pieces[number]
        self.copy(number, depth).wait_recv()
        mine = self.side(number, depth, False)[...]
        if depth == len(order) - 1:
            return mine.astype(F32) + slots[depth][...].astype(F32)
        slots[depth][...] = mine + slots[depth][...]
        self.send(number, depth + 1)
        return None

    def finish(self):
        for number, (_, _, order, _, _) in self.pieces.items():
            for depth in range(len(order)):
                self.copy(number, depth).wait_send()


def slot_shapes(lead, count, tail):
    return [pltpu.VMEM((lead,) + (2,) * (count - 1 - depth) + tail, BF16) for depth in range(count)]


ORDERS = ((X, Y, Z_LOW, Z_HIGH), (Y, Z_LOW, X, Z_HIGH), (Z_LOW, X, Y, Z_HIGH))
IN_CUTS = ((0, 16), (16, 16), (32, 32))
DOWN_CUTS = ((0, 384), (384, 384), (768, 256))
OUT_CUTS = ((0, 128), (128, 128), (256, 256))
LATER_DIMS = (
    (Z_HIGH, Z_LOW, Y),
    (Z_HIGH, Z_LOW, X),
    (Z_HIGH, Y, X),
    (Z_LOW, Y, Z_HIGH),
    (Z_LOW, Z_HIGH, X),
    (Y, Z_HIGH, X),
)


def in_vmem():
    return pl.BlockSpec(memory_space=pltpu.VMEM)


def anywhere():
    return pl.BlockSpec(memory_space=pl.ANY)


def params(collective):
    return pltpu.CompilerParams(
        collective_id=collective, has_side_effects=True, vmem_limit_bytes=VMEM_BYTES
    )


def take_rows(mixed, which):
    count = mixed.shape[0] // 2
    row = lax.broadcasted_iota(jnp.int32, (count, 2 * count), 0)
    column = lax.broadcasted_iota(jnp.int32, (count, 2 * count), 1)
    pick = jnp.where(column == 2 * row + which, 1.0, 0.0).astype(BF16)
    return dot_nn(pick, mixed).astype(BF16)


def begin(mixed, vectors, w_qkv, q_bias, v_bias):
    rows = mixed.shape[0] // 2
    length = 4 * rows
    width = D // 2
    cuts = 2
    size = rows // cuts

    def body(*refs):
        mixed_ref, vec_ref, wq_ref, wk_ref, wv_ref, qb_ref, vb_ref = refs[:7]
        tok_ref, nt_ref, q_ref, k_ref, v_ref = refs[7:12]
        all_ref, kept_ref, sent_ref, send_sem, recv_sem = refs[12:]
        half = lax.axis_index("half")
        sent_ref[...] = take_rows(mixed_ref[...], 1 - half)
        greet((X, MEMBER))

        def over_x(c):
            return remote(
                sent_ref.at[pl.ds(c * size, size)],
                all_ref.at[pl.ds(rows + c * size, size)],
                send_sem.at[c],
                recv_sem.at[c],
                X,
            )

        def on(c):
            return remote(
                all_ref.at[pl.ds(rows + c * size, size)],
                all_ref.at[pl.ds(3 * rows + c * size, size)],
                send_sem.at[cuts + c],
                recv_sem.at[cuts + c],
                MEMBER,
            )

        near = remote(
            kept_ref, all_ref.at[pl.ds(2 * rows, rows)], send_sem.at[2 * cuts], recv_sem.at[2 * cuts], MEMBER
        )
        for c in range(cuts):
            over_x(c).start()
        kept_ref[...] = take_rows(mixed_ref[...], half)
        near.start()

        def project(first, count):
            place = pl.ds(first, count)
            x = kept_ref[...] if first == 0 else all_ref[place, :]
            if first < 2 * rows:
                tok_ref[place, :] = x
            unit, _ = normalise(x.astype(F32))
            normed = (unit * vec_ref[4:5] + vec_ref[5:6]).astype(BF16)
            nt_ref[:, place] = turned(normed)
            q_ref[place, :] = (dot_nn(normed, wq_ref[...]) + qb_ref[...]).astype(BF16)
            k_ref[place, :] = dot_nn(normed, wk_ref[...]).astype(BF16)
            v_ref[place, :] = (dot_nn(normed, wv_ref[...]) + vb_ref[...]).astype(BF16)

        project(0, rows)
        near.wait_recv()
        project(2 * rows, rows)
        for c in range(cuts):
            over_x(c).wait_recv()
            on(c).start()
            project(rows + c * size, size)
        for c in range(cuts):
            on(c).wait_recv()
            project(3 * rows + c * size, size)
        near.wait_send()
        for c in range(cuts):
            over_x(c).wait_send()
            on(c).wait_send()

    def weight(which):
        return pl.BlockSpec((D, width), lambda i: (0, 2 * which + lax.axis_index("member")))

    def bias():
        return pl.BlockSpec((1, width), lambda i: (0, lax.axis_index("member")))

    def shape(count, columns):
        return jax.ShapeDtypeStruct((count, columns), BF16)

    return pl.pallas_call(
        body,
        grid=(1,),
        out_shape=(shape(2 * rows, D), shape(D, length)) + (shape(length, width),) * 3,
        in_specs=[in_vmem(), in_vmem(), weight(0), weight(1), weight(2), bias(), bias()],
        out_specs=(in_vmem(),) * 5,
        scratch_shapes=[
            pltpu.VMEM((length, D), BF16),
            pltpu.VMEM((rows, D), BF16),
            pltpu.VMEM((rows, D), BF16),
            pltpu.SemaphoreType.DMA((2 * cuts + 1,)),
            pltpu.SemaphoreType.DMA((2 * cuts + 1,)),
        ],
        compiler_params=params(5),
        name="begin",
    )(mixed, vectors, w_qkv, w_qkv, w_qkv, q_bias, v_bias)


def attend_forward(q, k, v, segments, random_blocks, global_blocks, cot_mixed, tile=512):
    length, width = q.shape
    pairs = width // LANES
    tiles = length // tile
    blocks = length // BLK
    own = length // 2
    rows = own // 2

    def body(*refs):
        q_ref, k_ref, v_ref, seg_ref, rand_ref, glob_ref, mixed_ref = refs[:7]
        ctx_ref, qa_ref, fk_ref, other_ref, cot_ref = refs[7:12]
        fq_ref, ka_ref, made_ref, seg_row, blk_row, kept_ref, sent_ref = refs[12:19]
        send_sem, recv_sem, cot_send, cot_recv = refs[19:]
        pair, step = pl.program_id(0), pl.program_id(1)
        half, member = lax.axis_index("half"), lax.axis_index("member")
        numbers = lax.broadcasted_iota(jnp.int32, (8, length), 0).astype(F32)

        def stay():
            return pltpu.make_async_copy(kept_ref, cot_ref.at[pl.ds(0, rows)], cot_send.at[3])

        def cot_copy(which):
            across = pl.ds(rows, rows)
            src, to, bit = (
                (sent_ref, across, X),
                (kept_ref, pl.ds(own, rows), MEMBER),
                (cot_ref.at[across], pl.ds(own + rows, rows), MEMBER),
            )[which]
            return remote(src, cot_ref.at[to], cot_send.at[which], cot_recv.at[which], bit)

        @pl.when((pair == 0) & (step == 0))
        def _():
            greet((X, MEMBER))
            sent_ref[...] = take_rows(mixed_ref[...], 1 - half)
            cot_copy(0).start()
            kept_ref[...] = take_rows(mixed_ref[...], half)
            cot_copy(1).start()
            stay().start()
            both = seg_ref[...].astype(F32)
            ids = jnp.where(half == 0, both[0:1], both[1:2])
            slots = []
            for j in range(2):
                for t in range(2):
                    want = lax.rem(half + t, 2) * 2 + lax.rem(member + j, 2)
                    piece = jnp.zeros((1, rows), F32)
                    for b in range(4):
                        piece = jnp.where(want == b, ids[:, b * rows : (b + 1) * rows], piece)
                    slots.append(piece)
            seg_row[...] = jnp.concatenate(slots, axis=1)
            spot = lax.broadcasted_iota(jnp.int32, (1, length), 1)
            side = lax.rem(half + lax.rem(spot // rows, 2), 2) * 2 + lax.rem(member + spot // own, 2)
            blk_row[...] = (side * (rows // BLK) + lax.rem(spot // BLK, rows // BLK)).astype(F32)
            count = lax.broadcasted_iota(jnp.int32, (blocks, length), 0).astype(F32)
            here = jnp.where(blk_row[...] == count, 1.0, 0.0)
            rest = jnp.zeros((HD - 8 - 2 * blocks, length), F32)
            apart = jnp.where((seg_row[...] == numbers) | (numbers >= SEG_VALUES), 0.0, NEG)
            feats = jnp.concatenate([apart, here, here, rest], axis=0)
            fq_ref[...] = jnp.concatenate([feats, feats], axis=0).T.astype(BF16)

        @pl.when(step == 0)
        def _():
            same = jnp.where(seg_row[...] == numbers, 1.0, 0.0)
            rest = jnp.zeros((HD - 16 - 2 * blocks, length), F32)
            ones = jnp.where(numbers < 3, 1.0, 0.0)
            here = blk_row[...]
            count = lax.broadcasted_iota(jnp.int32, (blocks, length), 0).astype(F32)
            common = jnp.where(jnp.abs(count - here) <= 1.0, 1.0, 0.0)
            for g in range(GLOB):
                named = jnp.where(half == 0, glob_ref[g : g + 1, 0:1], glob_ref[g : g + 1, 1:2])
                common = common + jnp.where(here == named.astype(F32), 1.0, 0.0)
            drawn = rand_ref[0]
            sides = []
            for parity in (1, 0):
                times = common
                for j in range(RAND):
                    column = parity * RAND + j
                    times = times + jnp.where(drawn[:, column : column + 1] == here, 1.0, 0.0)
                full = jnp.where(times > 0, jnp.log(jnp.maximum(times, 1.0)), NEG)
                high = full.astype(BF16).astype(F32)
                sides += [same, high, full - high, ones, rest]
            feats = jnp.concatenate(sides, axis=0).T.astype(BF16)
            fk_ref[0] = feats
            low_half = lax.broadcasted_iota(jnp.int32, (length, LANES), 1) < HD
            keys = k_ref[...]
            ka_ref[0] = jnp.where(low_half, keys, feats)
            ka_ref[1] = jnp.where(low_half, feats, keys)

        lane = lax.broadcasted_iota(jnp.int32, (tile, LANES), 1)
        low_half = lane < HD
        scaled = q_ref[...] * jnp.asarray(HD ** (-0.5), BF16)
        place = pl.ds(pl.multiple_of(step * tile, tile), tile)
        feats = fq_ref[place, :]
        results = []
        for parity in range(2):
            if parity == 0:
                aug = jnp.where(low_half, scaled, feats)
                first = HD + 8 + 2 * blocks
            else:
                aug = jnp.where(low_half, feats, scaled)
                first = 8 + 2 * blocks
            scores = dot_nt(aug, ka_ref[parity])
            top = jnp.max(scores, axis=-1, keepdims=True)
            weights = jnp.exp(scores - top)
            total = jnp.sum(weights, axis=-1, keepdims=True)
            mixed = dot_nn(weights.astype(BF16), v_ref[...])
            results.append(mixed / total)
            hi, mid, low = three_parts(-(top + jnp.log(total)))
            aug = jnp.where(lane == first, hi, aug)
            aug = jnp.where(lane == first + 1, mid, aug)
            aug = jnp.where(lane == first + 2, low, aug)
            qa_ref[parity] = aug
        context = jnp.where(low_half, results[0], results[1]).astype(BF16)
        ctx_ref[...] = context
        made_ref[pair, place, :] = context

        def swaps(one_pair):
            cols = pl.ds(pl.multiple_of(one_pair * LANES, LANES), LANES)
            return [
                remote(
                    made_ref.at[one_pair, pl.ds(from_row, own)],
                    other_ref.at[pl.ds(own - from_row, own), cols],
                    send_sem.at[side, one_pair],
                    recv_sem.at[side, one_pair],
                    MEMBER,
                )
                for side, from_row in enumerate((0, own))
            ]

        @pl.when(step == tiles - 1)
        def _():
            for one in swaps(pair):
                one.start()

        @pl.when((pair == pairs - 2) & (step == tiles - 1))
        def _():
            cot_copy(0).wait_recv()
            cot_copy(2).start()

        @pl.when((pair == pairs - 1) & (step == tiles - 1))
        def _():
            cot_copy(0).wait_send()
            stay().wait()
            cot_copy(1).wait()
            cot_copy(2).wait()
            for one_pair in range(pairs):
                for one in swaps(one_pair):
                    one.wait()

    return pl.pallas_call(
        body,
        grid=(pairs, tiles),
        out_shape=(
            jax.ShapeDtypeStruct((length, width), BF16),
            jax.ShapeDtypeStruct((2 * pairs, length, LANES), BF16),
            jax.ShapeDtypeStruct((pairs, length, LANES), BF16),
            jax.ShapeDtypeStruct((length, width), BF16),
            jax.ShapeDtypeStruct((length, D), BF16),
        ),
        in_specs=[
            pl.BlockSpec((tile, LANES), lambda p, t: (t, p)),
            pl.BlockSpec((length, LANES), lambda p, t: (0, p)),
            pl.BlockSpec((length, LANES), lambda p, t: (0, p)),
            in_vmem(),
            pl.BlockSpec((1, blocks, 2 * RAND), lambda p, t: (p, 0, 0)),
            in_vmem(),
            in_vmem(),
        ],
        out_specs=(
            pl.BlockSpec((tile, LANES), lambda p, t: (t, p)),
            pl.BlockSpec((2, tile, LANES), lambda p, t: (p, t, 0)),
            pl.BlockSpec((1, length, LANES), lambda p, t: (p, 0, 0)),
            anywhere(),
            anywhere(),
        ),
        scratch_shapes=[
            pltpu.VMEM((length, LANES), BF16),
            pltpu.VMEM((2, length, LANES), BF16),
            pltpu.VMEM((pairs, length, LANES), BF16),
            pltpu.VMEM((1, length), F32),
            pltpu.VMEM((1, length), F32),
            pltpu.VMEM((rows, D), BF16),
            pltpu.VMEM((rows, D), BF16),
            pltpu.SemaphoreType.DMA((2, pairs)),
            pltpu.SemaphoreType.DMA((2, pairs)),
            pltpu.SemaphoreType.DMA((4,)),
            pltpu.SemaphoreType.DMA((3,)),
        ],
        compiler_params=params(4),
        name="attend_forward",
    )(q, k, v, segments, random_blocks, global_blocks, cot_mixed)


def feed_forward(context, context_other, tokens, w_out, vectors, cot, w_in, in_bias, w_down):
    rows = cot.shape[0]
    own = rows // 2
    width = context.shape[1]
    chunk = 4 * LANES
    steps = 4
    share = D // 16
    root = (2.0 / np.pi) ** 0.5
    cube = 0.044715

    def group(j):
        bits = my_bits()
        z_low = jnp.where(j < 2, 1 - bits[Z_LOW], bits[Z_LOW])
        return z_low, jnp.where(lax.rem(j, 2) == 0, 1 - bits[Y], bits[Y])

    def body(*refs):
        ctx_ref, other_ref, tok_ref, wo_ref, wo2_ref, vec_ref, c_ref = refs[:7]
        wi_refs, b_refs, wd_refs = refs[7:11], refs[11:15], refs[15:19]
        out_ref, dn_ref, dn_got, mid_ref, gb_ref = refs[19:24]
        keep, got = refs[24:30], refs[30:36]
        n_ref, nt_ref, out_acc, dn_acc, out_send, out_got, dn_send, gi_ref, gd_ref = refs[36:45]
        send_sem, recv_sem, keep_sem, swap_sem = refs[45:]
        step = pl.program_id(0)
        bits = my_bits()
        z_low, y = group(step)
        slot = 2 * z_low + y

        @pl.when(step == 0)
        def _():
            greet((Z_LOW, Y, X, MEMBER))
            cut = own // 2
            swaps = []
            for at in range(2):
                part = slice(at * cut, (at + 1) * cut)
                mid = (
                    tok_ref[part].astype(F32)
                    + dot_nn(ctx_ref[part], wo_ref[...])
                    + dot_nn(other_ref[part], wo2_ref[...])
                    + vec_ref[0:1]
                )
                mid_ref[part] = mid
                unit, _ = normalise(mid)
                n_ref[part] = (unit * vec_ref[1:2] + vec_ref[2:3]).astype(BF16)
                swaps.append(
                    remote(
                        n_ref.at[pl.ds(at * cut, cut)],
                        n_ref.at[pl.ds(own + at * cut, cut)],
                        swap_sem.at[0, 3 * at],
                        swap_sem.at[1, 3 * at],
                        MEMBER,
                    )
                )
                swaps[at].start()
            nt_ref[:, :own] = turned(n_ref[:own])
            for at in range(2):
                swaps[at].wait()
                first = own + at * cut
                nt_ref[:, first : first + cut] = turned(n_ref[first : first + cut])

        wi = jnp.concatenate([ref[...] for ref in wi_refs], axis=1)
        wd = jnp.concatenate([ref[...] for ref in wd_refs], axis=0)
        pre = dot_nn(n_ref[...], wi) + jnp.concatenate([ref[...] for ref in b_refs], axis=1)
        square = pre * pre
        th = jnp.tanh(root * pre * (1.0 + cube * square))
        half_up = 0.5 * (1.0 + th)
        hidden = (pre * half_up).astype(BF16)
        slope = half_up + 0.5 * pre * (1.0 - th * th) * (root * (1.0 + 3.0 * cube * square))

        def in_part(kind, at):
            bit = (X, Y, Z_LOW)[kind]
            rest = (ALL,) * (3 - bit) + (pl.ds(*IN_CUTS[kind]),)
            return lambda side: gi_ref.at[(at,) + (ALL,) * bit + (side,) + rest]

        def copies(kind, at, where, bit):
            return (
                lambda: remote(
                    where(1 - bits[bit]), got[kind].at[at], send_sem.at[kind, at], recv_sem.at[kind, at], bit
                ),
                lambda: pltpu.make_async_copy(where(bits[bit]), keep[kind].at[at], keep_sem.at[kind, at]),
            )

        def in_copies(kind, at):
            return copies(kind, at, in_part(kind, at), (X, Y, Z_LOW)[kind])

        def x_copies(at):
            return copies(3, at, lambda side: gd_ref.at[at, :, side, :, pl.ds(*DOWN_CUTS[0])], X)

        def y_copies(z):
            return copies(4, z, lambda side: gd_ref.at[2 * z + side, :, :, :, pl.ds(*DOWN_CUTS[1])], Y)

        def z_copies(at_y):
            return copies(
                5, at_y, lambda side: gd_ref.at[2 * side + at_y, :, :, :, pl.ds(*DOWN_CUTS[2])], Z_LOW
            )

        gd_ref[slot] = dot_tn(hidden, c_ref[...]).astype(BF16).reshape(2, 2, LANES, D)
        for one in x_copies(slot):
            one().start()

        @pl.when(lax.rem(step, 2) == 0)
        def _():
            y_copies(z_low)[0]().start()

        @pl.when(lax.rem(step, 2) == 1)
        def _():
            y_copies(z_low)[1]().start()

        @pl.when(step < 2)
        def _():
            z_copies(y)[0]().start()

        @pl.when(step >= 2)
        def _():
            z_copies(y)[1]().start()

        pre_grad = (dot_nt(c_ref[...], wd) * slope).astype(BF16)
        gb_ref[...] = jnp.sum(pre_grad.astype(F32), axis=0, keepdims=True)
        gi_ref[slot] = dot_nn(nt_ref[...], pre_grad).astype(BF16).reshape(2, 2, 2, 2, share, chunk)
        for kind in range(3):
            for one in in_copies(kind, slot):
                one().start()

        dn_swap = (dn_send, dn_got, swap_sem.at[0, 1], swap_sem.at[1, 1], MEMBER)
        out_swap = (out_send, out_got, swap_sem.at[0, 2], swap_sem.at[1, 2], MEMBER)
        @pl.when(step == 0)
        def _():
            dn_acc[...] = dot_nt(pre_grad, wi)
            out_acc[...] = dot_nn(hidden, wd)

        @pl.when((step > 0) & (step < steps - 1))
        def _():
            dn_acc[...] += dot_nt(pre_grad, wi)
            out_acc[...] += dot_nn(hidden, wd)

        @pl.when(step == steps - 1)
        def _():
            theirs, ours = slice(own, rows), slice(0, own)
            dn_send[...] = (dn_acc[theirs] + dot_nt(pre_grad[theirs], wi)).astype(BF16)
            remote(*dn_swap).start()
            out_send[...] = (out_acc[theirs] + dot_nn(hidden[theirs], wd)).astype(BF16)
            remote(*out_swap).start()
            dn_ref[...] = dn_acc[ours] + dot_nt(pre_grad[ours], wi)
            out_acc[ours] += mid_ref[...] + vec_ref[3:4] + dot_nn(hidden[ours], wd)

        @pl.when(step == steps - 1)
        def _():
            for at in range(4):
                for kind in range(3):
                    for one in in_copies(kind, at):
                        one().wait()
                for one in x_copies(at):
                    one().wait()
            for at in range(2):
                for one in y_copies(at) + z_copies(at):
                    one().wait()
            remote(*dn_swap).wait()
            remote(*out_swap).wait()
            out_ref[...] = (out_acc[:own] + out_got[...].astype(F32)).astype(BF16)

    def unit(z_high, x):
        def at(j):
            z_low, y = group(j)
            return 2 * (((2 * z_high + z_low) * 2 + y) * 2 + x) + lax.axis_index("member")

        return at

    units = [unit(z_high, x) for z_high in range(2) for x in range(2)]

    def column(u):
        return lambda j: (0, u(j))

    def row(u):
        return lambda j: (u(j), 0)

    def slot_of(j):
        z_low, y = group(j)
        return (0, 2 * z_low + y)

    whole = pl.BlockSpec((rows, D), lambda j: (0, 0))
    half = pl.BlockSpec((own, D), lambda j: (0, 0))
    half_ctx = pl.BlockSpec((own, width), lambda j: (0, 0))
    parts = [jax.ShapeDtypeStruct((4, 2, 2, 2, size, chunk), BF16) for _, size in IN_CUTS] + [
        jax.ShapeDtypeStruct((4, 2, LANES, DOWN_CUTS[0][1]), BF16),
        jax.ShapeDtypeStruct((2, 2, 2, LANES, DOWN_CUTS[1][1]), BF16),
        jax.ShapeDtypeStruct((2, 2, 2, LANES, DOWN_CUTS[2][1]), BF16),
    ]
    own_f32 = jax.ShapeDtypeStruct((own, D), F32)
    own_bf16 = jax.ShapeDtypeStruct((own, D), BF16)
    results = pl.pallas_call(
        body,
        grid=(steps,),
        out_shape=[
            own_bf16,
            own_f32,
            own_bf16,
            own_f32,
            jax.ShapeDtypeStruct((1, steps * chunk), F32),
        ]
        + parts
        + parts,
        in_specs=[
            half_ctx,
            half_ctx,
            half,
            pl.BlockSpec((width, D), lambda j: (lax.axis_index("member"), 0)),
            pl.BlockSpec((width, D), lambda j: (1 - lax.axis_index("member"), 0)),
            pl.BlockSpec((8, D), lambda j: (0, 0)),
            whole,
        ]
        + [pl.BlockSpec((D, LANES), column(u)) for u in units]
        + [pl.BlockSpec((1, LANES), column(u)) for u in units]
        + [pl.BlockSpec((LANES, D), row(u)) for u in units],
        out_specs=[half, half, anywhere(), half, pl.BlockSpec((1, chunk), slot_of)]
        + [anywhere()] * 12,
        scratch_shapes=[
            pltpu.VMEM((rows, D), BF16),
            pltpu.VMEM((D, rows), BF16),
            pltpu.VMEM((rows, D), F32),
            pltpu.VMEM((rows, D), F32),
            pltpu.VMEM((own, D), BF16),
            pltpu.VMEM((own, D), BF16),
            pltpu.VMEM((own, D), BF16),
            pltpu.VMEM((4, 2, 2, 2, 2, share, chunk), BF16),
            pltpu.VMEM((4, 2, 2, LANES, D), BF16),
            pltpu.SemaphoreType.DMA((6, 4)),
            pltpu.SemaphoreType.DMA((6, 4)),
            pltpu.SemaphoreType.DMA((6, 4)),
            pltpu.SemaphoreType.DMA((2, 4)),
        ],
        compiler_params=params(1),
        name="feed_forward",
    )(context, context_other, tokens, w_out, w_out, vectors, cot, *[w_in] * 4, *[in_bias] * 4, *[w_down] * 4)
    return results[:5], results[5:11], results[11:]


def attend_backward(
    rows_aug, k, v, feat_k, ctx, ctx_other, mid, n2_grad, n2_grad_got, cot, vectors, w_out, normed_t, w_qkv, output_own,
    kept, got, tile=256,
):
    length, width = k.shape
    pairs = width // LANES
    early = 1
    tiles = length // tile
    own = length // 2
    chunk = kept[0].shape[-1]
    shapes = [a.shape for a in kept[:3]] + [(1, 2, 2, 2, LANES, a.shape[-1]) for a in kept[3:]]
    kept = [a.reshape(shape) for a, shape in zip(kept, shapes)]
    got = [a.reshape(shape) for a, shape in zip(got, shapes)]
    share = D // 16
    count = 9 + 3 * early

    def body(*refs):
        qa_ref, k_ref, v_ref, fk_ref, ctx_ref, other_ref, mid_ref, dn2_ref, dn2_got, c_ref, vec_ref, wo_ref = refs[:12]
        nt_ref, wq_ref, wk_ref, wv_ref, mine_ref = refs[12:17]
        keep_in, got_in = refs[17:23], refs[23:29]
        dn_ref, mg_ref, sum_ref, qb_ref, vb_ref, ready_ref, sum_down, dn_got, theirs_ref = refs[29:38]
        keep_new, got_new = refs[38:41], refs[41:44]
        ga_ref, acc_ref, slab_ref, dn_acc, dn_send, gq_ref, br_ref, g_ref, go_ref = refs[44:53]
        begin, first = refs[53:59], refs[59:65]
        slots = refs[65 : 65 + 18 + 12 + 12 * early]
        send_sem, recv_sem, load_sem, new_send, new_recv, new_keep, swap_sem = refs[65 + 30 + 12 * early :]
        pair, step = pl.program_id(0), pl.program_id(1)
        now = pair * tiles + step
        member = lax.axis_index("member")

        sums = Sums(send_sem, recv_sem)
        for kind in range(6):
            sums.add(kind, begin[kind], LATER_DIMS[kind], ORDERS[kind % 3][1:], slots[3 * kind : 3 * kind + 3])
        for kind in range(3):
            sums.add(
                6 + kind,
                go_ref,
                CHIP,
                ORDERS[kind],
                slots[18 + 4 * kind : 22 + 4 * kind],
                (ALL, pl.ds(*OUT_CUTS[kind])),
            )
        for one_pair in range(early):
            for kind in range(3):
                number = 9 + 3 * one_pair + kind
                sums.add(
                    number,
                    gq_ref.at[one_pair, pl.ds(kind, 1)],
                    CHIP,
                    ORDERS[kind],
                    slots[30 + 4 * (number - 9) : 34 + 4 * (number - 9)],
                )

        def loads(kind):
            return (
                pltpu.make_async_copy(keep_in[kind], begin[kind], load_sem.at[0, kind]),
                pltpu.make_async_copy(got_in[kind], first[kind], load_sem.at[1, kind]),
            )

        def begin_sum(kind):
            for one in loads(kind):
                one.wait()
            begin[kind][...] = begin[kind][...] + first[kind][...]
            sums.send(kind, 0)

        def end_sum(number):
            total = sums.take(number, len(sums.pieces[number][2]) - 1)
            if number < 3:
                for z_low in range(2):
                    for y in range(2):
                        for z_high in range(2):
                            for x in range(2):
                                unit = ((2 * z_high + z_low) * 2 + y) * 2 + x
                                local = (2 * z_high + x) * LANES
                                ready_ref[pl.ds(*IN_CUTS[number]), unit * LANES : (unit + 1) * LANES] = total[
                                    2 * z_low + y, :, local : local + LANES
                                ]
            elif number < 6:
                sum_down[:, pl.ds(*DOWN_CUTS[number - 3])] = total[0]
            elif number < 9:
                col, size = OUT_CUTS[number - 6]
                ready_ref[:, pl.ds(4 * chunk + col, size)] = total[0]
            else:
                one_pair, kind = (number - 9) // 3, (number - 9) % 3
                place = 4 * chunk + width + (kind * early + one_pair) * LANES
                ready_ref[:, place : place + LANES] = total[0]

        def do(number, depth):
            if depth == len(sums.pieces[number][2]) - 1:
                end_sum(number)
            else:
                sums.take(number, depth)

        def at(when, depth, *numbers):
            @pl.when(now == when)
            def _():
                for number in numbers:
                    do(number, depth)

        @pl.when(now == 0)
        def _():
            greet((Z_HIGH, Z_LOW, Y, X, MEMBER))
            for kind in range(6):
                for one in loads(kind):
                    one.start()
            for kind in (0, 1, 5, 2, 3, 4):
                begin_sum(kind)
            unit, scale = normalise(mid_ref[...])
            grad = dn2_ref[...] + dn2_got[...].astype(F32)
            cot_own = c_ref[...].astype(F32)
            mid_grad = cot_own + normalise_back(unit, scale, grad * vec_ref[1:2])
            mg_ref[...] = mid_grad
            branch = mid_grad.astype(BF16)
            br_ref[:own] = branch
            swap = remote(
                br_ref.at[pl.ds(0, own)], br_ref.at[pl.ds(own, own)], swap_sem.at[0, 0], swap_sem.at[1, 0], MEMBER
            )
            swap.start()
            sum_ref[0:1] = jnp.sum(branch.astype(F32), axis=0, keepdims=True)
            sum_ref[1:2] = jnp.sum(grad * unit, axis=0, keepdims=True)
            sum_ref[2:3] = jnp.sum(grad, axis=0, keepdims=True)
            sum_ref[3:4] = jnp.sum(cot_own, axis=0, keepdims=True)
            sum_ref[4:8] = jnp.zeros((4, D), F32)
            swap.wait()
            g_ref[...] = dot_nt(br_ref[...], wo_ref[...]).astype(BF16)
            columns = br_ref[:, pl.ds(pl.multiple_of(member * width, width), width)]
            go_ref[0, member] = dot_tn(ctx_ref[...], columns).astype(BF16).reshape(2, 2, 2, share, width)
            go_ref[0, 1 - member] = dot_tn(other_ref[...], columns).astype(BF16).reshape(2, 2, 2, share, width)
            for kind in range(6, 9):
                sums.send(kind, 0)

        output_swap = (mine_ref.at[pl.ds(own // 2, own // 2)], theirs_ref, swap_sem.at[0, 2], swap_sem.at[1, 2], X)

        @pl.when(now == 8)
        def _():
            remote(*output_swap).start()

        at(0, 0, 0, 1, 5)
        at(4, 0, 3, 4, 7, 2)
        at(5, 1, 5)
        at(5, 0, 8, 6)
        at(7, 1, 0, 1)
        at(7, 0, 10)
        at(8, 0, 11, 9)
        at(8, 1, 2, 3, 4)
        at(9, 1, 6, 7)
        at(10, 2, 5)
        at(10, 1, 8)
        at(10, 2, 0)
        at(11, 2, 1)
        at(12, 1, 10, 11, 9)
        at(12, 2, 8)
        at(13, 2, 2)
        at(14, 2, 3)

        slab_cols = pl.ds(pl.multiple_of(pair * LANES, LANES), LANES)

        @pl.when(step == 0)
        def _():
            lane = lax.broadcasted_iota(jnp.int32, (length, LANES), 1)
            low_half = lane < HD
            grads = g_ref[:, slab_cols]
            prod = grads.astype(F32) * ctx_ref[:, slab_cols].astype(F32)
            for parity in range(2):
                mine = low_half if parity == 0 else jnp.logical_not(low_half)
                lead = HD if parity == 0 else 0
                delta = -jnp.sum(jnp.where(mine, prod, 0.0), axis=-1, keepdims=True)
                hi, mid, low = three_parts(delta)
                rows = jnp.where(mine, grads, jnp.zeros_like(grads))
                rows = jnp.where(lane == lead, hi, rows)
                rows = jnp.where(lane == lead + 1, mid, rows)
                ga_ref[parity] = jnp.where(lane == lead + 2, low, rows)
            ga_ref[2] = grads
            acc_ref[...] = jnp.zeros_like(acc_ref)

        lane = lax.broadcasted_iota(jnp.int32, (tile, LANES), 1)
        low_half = lane < HD
        keys = k_ref[...]
        values = v_ref[...]
        feats = fk_ref[0]
        keys_t = turned(keys)
        dks, dvs = [], []
        for parity in range(2):
            lead = HD if parity == 0 else 0
            mine = low_half if parity == 0 else jnp.logical_not(low_half)
            key_rows = jnp.where(mine, keys, feats)
            ones = jnp.where((lane >= lead) & (lane < lead + 3), 1.0, 0.0).astype(BF16)
            value_rows = jnp.where(mine, values, ones)
            probs = jnp.exp(dot_nt(key_rows, qa_ref[parity]))
            diff = dot_nt(value_rows, ga_ref[parity])
            score_grad = (probs * diff).astype(BF16)
            dvs.append(dot_nn(probs.astype(BF16), ga_ref[2]))
            dks.append(dot_nn(score_grad, qa_ref[parity]))
            side = keys_t[parity * HD : (parity + 1) * HD]
            acc_ref[parity * HD : (parity + 1) * HD] += dot_nn(side, score_grad)
        place = pl.ds(pl.multiple_of(step * tile, tile), tile)
        slab_ref[place, LANES : 2 * LANES] = jnp.where(low_half, dks[0], dks[1]).astype(BF16)
        slab_ref[place, 2 * LANES :] = jnp.where(low_half, dvs[0], dvs[1]).astype(BF16)

        def new_copies(kind, late):
            bit = (X, Y, Z_LOW)[kind]
            whole = gq_ref.at[early + late, kind]
            return (
                pltpu.make_async_copy(
                    whole.at[(ALL,) * bit + (sums.bits[bit],)], keep_new[kind].at[late], new_keep.at[kind, late]
                ),
                remote(
                    whole.at[(ALL,) * bit + (1 - sums.bits[bit],)],
                    got_new[kind].at[late],
                    new_send.at[kind, late],
                    new_recv.at[kind, late],
                    bit,
                ),
            )

        @pl.when(step == tiles - 1)
        def _():
            slab_ref[:, :LANES] = (acc_ref[...].T * HD ** (-0.5)).astype(BF16)
            slabs = slab_ref[...]
            made = dot_nn(nt_ref[...], slabs).astype(BF16)
            for kind in range(3):
                gq_ref[pair, kind] = made[:, kind * LANES : (kind + 1) * LANES].reshape(
                    2, 2, 2, 2, share, LANES
                )
            for one_pair in range(pairs):

                @pl.when(pair == one_pair)
                def _(one_pair=one_pair):
                    for kind in range(3):
                        if one_pair < early:
                            sums.send(9 + 3 * one_pair + kind, 0)
                        else:
                            for one in new_copies(kind, one_pair - early):
                                one.start()

            qb_ref[...] = jnp.sum(slabs[:, :LANES].astype(F32), axis=0, keepdims=True)
            vb_ref[...] = jnp.sum(slabs[:, 2 * LANES :].astype(F32), axis=0, keepdims=True)

        dn_swap = (dn_send, dn_got, swap_sem.at[0, 1], swap_sem.at[1, 1], MEMBER)

        @pl.when(step == tiles - 1)
        def _():
            weights = jnp.concatenate([wq_ref[...], wk_ref[...], wv_ref[...]], axis=1)
            for rows in (slice(own, length), slice(0, own)):
                grown = dot_nt(slab_ref[rows], weights)

                @pl.when(pair == 0)
                def _(rows=rows, grown=grown):
                    dn_acc[rows] = grown

                @pl.when((pair > 0) & (pair < pairs - 1))
                def _(rows=rows, grown=grown):
                    dn_acc[rows] += grown

                @pl.when(pair == pairs - 1)
                def _(rows=rows, grown=grown):
                    total = dn_acc[rows] + grown
                    if rows.start:
                        dn_send[...] = total.astype(BF16)
                        remote(*dn_swap).start()
                    else:
                        dn_ref[...] = total

        @pl.when(now == pairs * tiles - 1)
        def _():
            do(6, 2)
            do(4, 2)
            do(11, 2)
            do(7, 2)
            do(9, 2)
            do(8, 3)
            do(10, 2)
            do(6, 3)
            do(11, 3)
            do(7, 3)
            do(9, 3)
            do(10, 3)
            for late in range(pairs - early):
                for kind in range(3):
                    for one in new_copies(kind, late):
                        one.wait()
            sums.finish()
            remote(*dn_swap).wait()
            remote(*output_swap).wait()

    part = pl.BlockSpec((tile, LANES), lambda p, t: (t, p))
    bias_part = pl.BlockSpec((1, LANES), lambda p, t: (0, p))

    def columns(which):
        return pl.BlockSpec(
            (D, LANES), lambda p, t: (0, (2 * which + lax.axis_index("member")) * pairs + p)
        )

    slots = []
    for shape in shapes:
        slots += slot_shapes(shape[0], 3, shape[4:])
    for _, size in OUT_CUTS:
        slots += slot_shapes(1, 4, (share, size))
    for _ in range(3 * early):
        slots += slot_shapes(1, 4, (share, LANES))
    new = [jax.ShapeDtypeStruct((pairs - early, 2, 2, 2, share, LANES), BF16)] * 3
    own_f32 = jax.ShapeDtypeStruct((own, D), F32)
    results = pl.pallas_call(
        body,
        grid=(pairs, tiles),
        out_shape=[
            own_f32,
            own_f32,
            jax.ShapeDtypeStruct((8, D), F32),
            jax.ShapeDtypeStruct((1, width), F32),
            jax.ShapeDtypeStruct((1, width), F32),
            jax.ShapeDtypeStruct((share, 4 * chunk + width + 3 * early * LANES), F32),
            jax.ShapeDtypeStruct((LANES, D), F32),
            jax.ShapeDtypeStruct((own, D), BF16),
            jax.ShapeDtypeStruct((own // 2, D), BF16),
        ]
        + new
        + new,
        in_specs=[
            pl.BlockSpec((2, length, LANES), lambda p, t: (p, 0, 0)),
            part,
            part,
            pl.BlockSpec((1, tile, LANES), lambda p, t: (p, t, 0)),
            in_vmem(),
            in_vmem(),
            in_vmem(),
            in_vmem(),
            in_vmem(),
            pl.BlockSpec((own, D), lambda p, t: (0, 0)),
            in_vmem(),
            pl.BlockSpec((width, D), lambda p, t: (lax.axis_index("member"), 0)),
            in_vmem(),
            columns(0),
            columns(1),
            columns(2),
        ]
        + [anywhere()] * 13,
        out_specs=[in_vmem(), in_vmem(), in_vmem(), bias_part, bias_part]
        + [in_vmem()] * 2
        + [anywhere()] * 8,
        scratch_shapes=[
            pltpu.VMEM((3, length, LANES), BF16),
            pltpu.VMEM((LANES, length), F32),
            pltpu.VMEM((length, 3 * LANES), BF16),
            pltpu.VMEM((length, D), F32),
            pltpu.VMEM((own, D), BF16),
            pltpu.VMEM((pairs, 3, 2, 2, 2, 2, share, LANES), BF16),
            pltpu.VMEM((length, D), BF16),
            pltpu.VMEM((length, width), BF16),
            pltpu.VMEM((1, 2, 2, 2, 2, share, width), BF16),
        ]
        + [pltpu.VMEM(shape, BF16) for shape in shapes]
        + [pltpu.VMEM(shape, BF16) for shape in shapes]
        + slots
        + [
            pltpu.SemaphoreType.DMA((count, 4)),
            pltpu.SemaphoreType.DMA((count, 4)),
            pltpu.SemaphoreType.DMA((2, 6)),
            pltpu.SemaphoreType.DMA((3, pairs - early)),
            pltpu.SemaphoreType.DMA((3, pairs - early)),
            pltpu.SemaphoreType.DMA((3, pairs - early)),
            pltpu.SemaphoreType.DMA((2, 3)),
        ],
        compiler_params=params(3),
        name="attend_backward",
    )(
        rows_aug, k, v, feat_k, ctx, ctx_other, mid, n2_grad, n2_grad_got, cot, vectors, w_out, normed_t,
        w_qkv, w_qkv, w_qkv, output_own, *kept, *got,
    )
    return results[:9], results[9:12], results[12:]


def finish(tokens, mid_grad, normed_grad, normed_grad_got, vectors, sums_in, in_bias_rows, q_sum, v_sum, ready, kept, got):
    own = mid_grad.shape[0]
    rows = own // 2
    width = q_sum.shape[1]
    late, share = kept[0].shape[0], kept[0].shape[-2]
    per = share // 2
    last = 3 * late * LANES + LANES

    def body(*refs):
        tok_ref, mg_ref, dn_ref, dn_got, vec_ref, sum_ref, inb_ref, qb_ref, vb_ref, ready_ref = refs[:10]
        keep, first = refs[10:13], refs[13:16]
        ig_ref, ig_got, ready_got, last_ref, last_got = refs[16:21]
        ig_send, source, last_all, flat, shares = refs[21:26]
        begin, slots = refs[26:29], refs[29:38]
        send_sem, recv_sem, swap_sem, share_sem = refs[38:]
        member = lax.axis_index("member")
        barrier = pltpu.get_barrier_semaphore()
        for mask in range(1, 16):
            pl.semaphore_signal(barrier, inc=1, device_id=chip_across(mask), device_id_type=MESH_IDS)
        pl.semaphore_signal(barrier, inc=1, device_id=device_across(MEMBER), device_id_type=MESH_IDS)
        pl.semaphore_wait(barrier, 16)
        theirs = pl.ds(pl.multiple_of((1 - member) * per, per), per)
        top, rest = pl.ds(0, rows // 2), pl.ds(rows // 2, rows // 2)
        swaps = [
            remote(ready_ref.at[theirs], ready_got, swap_sem.at[0, 0], swap_sem.at[1, 0], MEMBER),
            remote(ig_send.at[top], ig_got.at[top], swap_sem.at[0, 1], swap_sem.at[1, 1], X),
            remote(last_all.at[theirs], last_got, swap_sem.at[0, 2], swap_sem.at[1, 2], MEMBER),
            remote(ig_send.at[rest], ig_got.at[rest], swap_sem.at[0, 3], swap_sem.at[1, 3], X),
        ]
        sums = Sums(send_sem, recv_sem)
        for kind in range(3):
            dims = tuple(b for b in CHIP if b != ORDERS[kind][0])
            sums.add(kind, begin[kind], dims, ORDERS[kind][1:], slots[3 * kind : 3 * kind + 3])
            begin[kind][...] = keep[kind][...] + first[kind][...]
            sums.send(kind, 0)
        swaps[0].start()

        gain_sum, bias_sum = 0.0, 0.0
        for part in (slice(rows, rows + rows // 2), slice(rows + rows // 2, own), slice(0, rows)):
            unit, scale = normalise(tok_ref[part].astype(F32))
            grad = dn_ref[part] + dn_got[part].astype(F32)
            input_grad = mg_ref[part] + normalise_back(unit, scale, grad * vec_ref[4:5])
            if part.start == rows:
                ig_send[top] = input_grad.astype(BF16)
                swaps[1].start()
            elif part.start:
                ig_send[rest] = input_grad.astype(BF16)
            else:
                ig_ref[...] = input_grad
            gain_sum = gain_sum + jnp.sum(grad * unit, axis=0, keepdims=True)
            bias_sum = bias_sum + jnp.sum(grad, axis=0, keepdims=True)
        flat[0:1] = gain_sum
        flat[1:2] = bias_sum
        flat[2:6] = sum_ref[0:4]
        blank = jnp.zeros((1, width), F32)
        for row, ref in ((6, qb_ref), (7, vb_ref)):
            value = ref[...]
            flat[row : row + 1, :width] = jnp.where(member == 0, value, blank)
            flat[row : row + 1, width:] = jnp.where(member == 1, value, blank)
        flat[8:16] = inb_ref[...]
        flat[16:] = jnp.zeros((LANES - 16, D), F32)
        source[...] = flat[...].T.astype(BF16).reshape(source.shape)

        def straight(mask):
            place = tuple(1 - bit if mask & flag else bit for bit, flag in zip(sums.bits, (8, 4, 2, 1)))
            return pltpu.make_async_remote_copy(
                src_ref=source.at[place],
                dst_ref=shares.at[mask],
                send_sem=share_sem.at[0, mask],
                recv_sem=share_sem.at[1, mask],
                device_id=chip_across(mask),
                device_id_type=MESH_IDS,
            )

        for mask in range(1, 16):
            straight(mask).start()
        for depth in range(3):
            for kind in (1, 0, 2):
                total = sums.take(kind, depth)
                if depth == 0 and kind == 1:
                    swaps[3].start()
                if depth == 2:
                    for pair in range(late):
                        place = (kind * late + pair) * LANES
                        last_all[:, place : place + LANES] = total[pair]
        total = source[sums.bits[:4]].astype(F32)
        for mask in range(1, 16):
            straight(mask).wait_recv()
            total = total + shares[mask].astype(F32)
        last_all[:, last - LANES :] = total
        swaps[2].start()
        last_ref[...] = last_all[...]
        sums.finish()
        for mask in range(1, 16):
            straight(mask).wait_send()
        for one in swaps:
            one.wait()

    slots = []
    for _ in range(3):
        slots += slot_shapes(late, 3, (share, LANES))
    return pl.pallas_call(
        body,
        out_shape=(
            jax.ShapeDtypeStruct((rows, D), F32),
            jax.ShapeDtypeStruct((rows, D), BF16),
            jax.ShapeDtypeStruct((per, ready.shape[1]), F32),
            jax.ShapeDtypeStruct((share, last), F32),
            jax.ShapeDtypeStruct((per, last), F32),
        ),
        in_specs=[in_vmem()] * 16,
        out_specs=(in_vmem(), anywhere(), anywhere(), in_vmem(), anywhere()),
        scratch_shapes=[
            pltpu.VMEM((rows, D), BF16),
            pltpu.VMEM((2, 2, 2, 2, share, LANES), BF16),
            pltpu.VMEM((share, last), F32),
            pltpu.VMEM((LANES, D), F32),
            pltpu.VMEM((16, share, LANES), BF16),
        ]
        + [pltpu.VMEM(kept[0].shape, BF16)] * 3
        + slots
        + [
            pltpu.SemaphoreType.DMA((3, 3)),
            pltpu.SemaphoreType.DMA((3, 3)),
            pltpu.SemaphoreType.DMA((2, 4)),
            pltpu.SemaphoreType.DMA((2, 16)),
        ],
        compiler_params=params(2),
        name="finish",
    )(
        tokens, mid_grad, normed_grad, normed_grad_got, vectors, sums_in, in_bias_rows, q_sum, v_sum, ready, *kept, *got
    )


def per_device_pair(
    tokens,
    ln1_gain,
    ln1_bias,
    w_qkv,
    q_bias,
    v_bias,
    w_out,
    out_bias,
    ln2_gain,
    ln2_bias,
    w_in,
    in_bias,
    w_down,
    down_bias,
    cotangent,
    segment_ids,
    random_blocks,
    global_blocks,
):
    rows = tokens.shape[0]
    own = 2 * rows
    blocks = segment_ids.shape[0] // BLK
    half = lax.axis_index("half")
    member = lax.axis_index("member")
    mine_d = D // 2
    heads = HEADS // 2
    chips = lax.axis_size("batch") * 2

    def both_sequences(kept, other):
        return jnp.where(
            half == 0, jnp.stack([kept, other], axis=1), jnp.stack([other, kept], axis=1)
        )

    seq_random = lax.dynamic_index_in_dim(random_blocks, half, 1, keepdims=False)
    seq_random = lax.dynamic_slice_in_dim(seq_random, member * heads, heads, 1)
    pair_random = seq_random.reshape(blocks, heads // 2, 2 * RAND).transpose(1, 0, 2).astype(F32)
    blank = jnp.zeros((D,), BF16)
    vectors = jnp.stack(
        [out_bias, ln2_gain, ln2_bias, down_bias, ln1_gain, ln1_bias, blank, blank]
    ).astype(F32)

    own_tokens, normed_t, queries, keys, values = begin(
        tokens.reshape(own, D), vectors, w_qkv, q_bias.astype(F32).reshape(1, D), v_bias.astype(F32).reshape(1, D)
    )
    context, rows_aug, feat_k, context_other, cot = attend_forward(
        queries, keys, values, segment_ids.T, pair_random, global_blocks, cotangent.reshape(own, D)
    )
    (output_own, n2_grad, n2_grad_got, mid_stream, in_bias_grad), kept_parts, got_parts = feed_forward(
        context,
        context_other,
        own_tokens,
        w_out,
        vectors,
        cot,
        w_in,
        in_bias.astype(F32).reshape(1, -1),
        w_down,
    )

    in_bias_rows = in_bias_grad.reshape(2, 2, 2, 2, 2, LANES // 2).transpose(4, 2, 0, 1, 3, 5).reshape(2, D)
    gone = jnp.zeros_like(in_bias_rows)
    in_bias_rows = jnp.concatenate(
        [
            jnp.where(member == 0, in_bias_rows, gone),
            jnp.where(member == 1, in_bias_rows, gone),
            jnp.zeros((4, D), F32),
        ]
    )

    (
        (
            normed_grad,
            mid_grad,
            sums_in,
            q_sum,
            v_sum,
            ready,
            summed_down,
            normed_grad_got,
            output_other,
        ),
        kept_qkv,
        got_qkv,
    ) = attend_backward(
        rows_aug,
        keys,
        values,
        feat_k,
        context,
        context_other,
        mid_stream,
        n2_grad,
        n2_grad_got,
        cot,
        vectors,
        w_out,
        normed_t,
        w_qkv,
        output_own,
        kept_parts,
        got_parts,
    )
    output = both_sequences(output_own[:rows], output_other)
    input_kept, input_other, ready_got, last_all, last_got = finish(
        own_tokens,
        mid_grad,
        normed_grad,
        normed_grad_got,
        vectors,
        sums_in,
        in_bias_rows,
        q_sum,
        v_sum,
        ready,
        kept_qkv,
        got_qkv,
    )
    input_grad = both_sequences(input_kept, input_other.astype(F32))

    per = ready.shape[0] // 2
    chip_rows = jnp.concatenate([ready, last_all], axis=1)
    mine_rows = lax.dynamic_slice_in_dim(chip_rows, member * per, per, 0)
    got_rows = jnp.concatenate([ready_got, last_got], axis=1)
    left = jnp.where(member == 0, mine_rows, got_rows)
    right = jnp.where(member == 0, got_rows, mine_rows)

    start_out = w_in.shape[1] // 2
    start_early = start_out + mine_d
    start_late = ready.shape[1]
    early = (start_late - start_early) // 3
    late = mine_d - early
    pieces = []
    for part in range(3):
        for x in (left, right):
            pieces.append(x[:, start_early + part * early : start_early + (part + 1) * early])
            pieces.append(x[:, start_late + part * late : start_late + (part + 1) * late])
    w_qkv_grad = jnp.concatenate(pieces, axis=1)
    w_out_grad = jnp.concatenate([x[:, start_out : start_out + mine_d] for x in (left, right)], axis=1)
    w_in_grad = jnp.concatenate(
        [x[:, j * LANES : (j + 1) * LANES] for j in range(chips) for x in (left, right)], axis=1
    )
    start = start_late + 3 * late
    vector_sums = left[:, start : start + 8] + right[:, start : start + 8]
    in_mine = lax.dynamic_slice_in_dim(last_all, 3 * late + 8 + 2 * member, 2, 1)
    in_bias_out = in_mine.T.reshape(LANES)
    vec = [vector_sums[:, i] for i in range(8)]
    return (
        output,
        input_grad,
        vec[0],
        vec[1],
        w_qkv_grad,
        vec[6],
        vec[7],
        w_out_grad,
        vec[2],
        vec[3],
        vec[4],
        w_in_grad,
        in_bias_out,
        summed_down,
        vec[5],
    )


def solution(mesh):
    def program(*args):
        sequences = args[0].shape[1] // mesh.shape["batch"]
        seq = mesh.shape["seq"]
        fast = sequences == 2 and seq == 4 and mesh.shape["batch"] == 8
        if fast:
            use = jax.sharding.Mesh(
                mesh.devices.reshape(mesh.shape["batch"], 2, 2), ("batch", "half", "member")
            )
            seq_axes, all_axes, run = ("half", "member"), ("batch", "half", "member"), per_device_pair
        else:
            use, seq_axes, all_axes, run = mesh, "seq", ("batch", "seq"), per_device
        rows = P(seq_axes, "batch", None)
        in_specs = (rows,) + (P(),) * 13 + (
            rows,
            P(None, "batch"),
            P(None, "batch", None, None),
            P(None, "batch"),
        )
        vector, matrix = P(all_axes), P(all_axes, None)
        out_specs = (
            rows,
            rows,
            vector,
            vector,
            matrix,
            vector,
            vector,
            matrix,
            vector,
            vector,
            vector,
            matrix,
            vector,
            matrix,
            vector,
        )
        return jax.shard_map(
            run, mesh=use, in_specs=in_specs, out_specs=out_specs, check_vma=False
        )(*args)

    return program
```

```python
import jax
import jax.numpy as jnp
import numpy as np
from jax import lax
from jax.experimental import pallas as pl
from jax.experimental.pallas import tpu as pltpu
from jax.sharding import PartitionSpec as P

D = 1024
HEADS = 16
HD = 64
BLK = 64
RAND = 3
GLOB = 2


eps = 1e-05


def padded(x, sides, width):
    for axis, dim in sides:
        size, length = (lax.axis_size(axis), x.shape[dim])
        up = [(i, (i + 1) % size) for i in range(size - 1)]
        down = [(j, i) for i, j in up]
        last = lax.slice_in_dim(x, length - width, length, axis=dim)
        initial = lax.slice_in_dim(x, 0, width, axis=dim)
        before = lax.ppermute(last, axis, up)
        after = lax.ppermute(initial, axis, down)
        x = jnp.concatenate([before, x, after], axis=dim)
    return x


def layer_norm(values, gain_vec, shift_vec):
    row_mean = jnp.mean(values, axis=-1, keepdims=True)
    centred = values - row_mean
    spread = jnp.mean(centred * centred, axis=-1, keepdims=True)
    return centred * lax.rsqrt(spread + eps) * gain_vec + shift_vec


def gelu_tanh(values):
    return jax.nn.gelu(values, approximate=True)


def window_stack(extended, query_blocks):
    return jnp.stack(
        [extended[0:query_blocks], extended[1 : query_blocks + 1], extended[2 : query_blocks + 2]],
        axis=1,
    )


def pick_blocks(shard_rows, random_local, global_blocks):
    block_total = shard_rows.shape[0] // BLK
    seq_count = shard_rows.shape[1]
    numbers = jnp.arange(block_total, dtype=jnp.int32)
    random_hits = (random_local[..., None] == numbers).astype(jnp.bfloat16)
    global_hits = (global_blocks[..., None] == numbers).astype(jnp.bfloat16)
    blocks = shard_rows.reshape(block_total, BLK, seq_count, 2, HEADS, HD)
    picked_random = jnp.einsum(
        "ishjb,busxhd->ishjuxd", random_hits, blocks, preferred_element_type=jnp.float32
    )
    picked_global = jnp.einsum(
        "gsb,busc->gusc",
        global_hits,
        shard_rows.reshape(block_total, BLK, seq_count, 2 * D),
        preferred_element_type=jnp.float32,
    )
    return (picked_random, picked_global)


def key_products(left_side, window_kv, far_random, far_global, which_half):
    near_part = jnp.einsum(
        "itshd,iwushd->ishtwu",
        left_side,
        window_kv[:, :, :, :, which_half],
        preferred_element_type=jnp.float32,
    )
    far_part = jnp.einsum(
        "itshd,ishjud->ishtju",
        left_side,
        far_random[:, :, :, :, :, which_half],
        preferred_element_type=jnp.float32,
    )
    global_part = jnp.einsum(
        "itshd,gushd->ishtgu",
        left_side,
        far_global[:, :, :, which_half],
        preferred_element_type=jnp.float32,
    )
    lead_shape = near_part.shape[:4]
    return jnp.concatenate(
        [
            near_part.reshape(lead_shape + (-1,)),
            far_part.reshape(lead_shape + (-1,)),
            global_part.reshape(lead_shape + (-1,)),
        ],
        axis=-1,
    )


def split_slots(weights):
    lead_shape = weights.shape[:4]
    near_cut = 3 * BLK
    far_cut = (3 + RAND) * BLK
    near_part = weights[..., :near_cut].reshape(lead_shape + (3, BLK))
    far_part = weights[..., near_cut:far_cut].reshape(lead_shape + (RAND, BLK))
    global_part = weights[..., far_cut:].reshape(lead_shape + (GLOB, BLK))
    return (near_part, far_part, global_part)


def key_mix(weights, window_kv, far_random, far_global, which_half):
    near_part, far_part, global_part = split_slots(weights)
    mixed = jnp.einsum(
        "ishtwu,iwushd->itshd",
        near_part,
        window_kv[:, :, :, :, which_half],
        preferred_element_type=jnp.float32,
    )
    mixed = mixed + jnp.einsum(
        "ishtju,ishjud->itshd",
        far_part,
        far_random[:, :, :, :, :, which_half],
        preferred_element_type=jnp.float32,
    )
    mixed = mixed + jnp.einsum(
        "ishtgu,gushd->itshd",
        global_part,
        far_global[:, :, :, which_half],
        preferred_element_type=jnp.float32,
    )
    return mixed


def key_grads(weights, left_side):
    near_part, far_part, global_part = split_slots(weights)
    near_grad = jnp.einsum(
        "ishtwu,itshd->iwushd", near_part, left_side, preferred_element_type=jnp.float32
    )
    far_grad = jnp.einsum(
        "ishtju,itshd->ishjud", far_part, left_side, preferred_element_type=jnp.float32
    )
    global_grad = jnp.einsum(
        "ishtgu,itshd->gushd", global_part, left_side, preferred_element_type=jnp.float32
    )
    return (near_grad, far_grad, global_grad)


def per_device(
    tokens,
    ln1_gain,
    ln1_bias,
    w_qkv,
    q_bias,
    v_bias,
    w_out,
    out_bias,
    ln2_gain,
    ln2_bias,
    w_in,
    in_bias,
    w_down,
    down_bias,
    cotangent,
    segment_ids,
    random_blocks,
    global_blocks,
):
    row_count = tokens.shape[0]
    seq_count = tokens.shape[1]
    query_blocks = row_count // BLK
    seq_length = segment_ids.shape[0]
    device_now = lax.axis_index("seq")
    first_row = device_now * row_count
    score_scale = HD ** (-0.5)
    random_local = lax.dynamic_slice_in_dim(
        random_blocks, device_now * query_blocks, query_blocks, 0
    )
    inputs = tokens.astype(jnp.float32)
    normed_full, first_norm_back = jax.vjp(
        layer_norm, inputs, ln1_gain.astype(jnp.float32), ln1_bias.astype(jnp.float32)
    )
    normed = normed_full.astype(jnp.bfloat16)
    projected = jnp.einsum("rsd,de->rse", normed, w_qkv, preferred_element_type=jnp.float32)
    queries = (projected[:, :, :D] + q_bias.astype(jnp.float32)).astype(jnp.bfloat16)
    value_shift = jnp.concatenate([jnp.zeros((D,), jnp.float32), v_bias.astype(jnp.float32)])
    keyval = (projected[:, :, D:] + value_shift).astype(jnp.bfloat16)
    extended = padded(keyval, (("seq", 0),), BLK)
    window_kv = window_stack(
        extended.reshape(query_blocks + 2, BLK, seq_count, 2, HEADS, HD), query_blocks
    )
    picked = pick_blocks(
        lax.all_gather(keyval, "seq", axis=0, tiled=True), random_local, global_blocks
    )
    far_random = picked[0].astype(jnp.bfloat16)
    far_global = picked[1].astype(jnp.bfloat16).reshape(GLOB, BLK, seq_count, 2, HEADS, HD)
    query_segment = lax.dynamic_slice_in_dim(segment_ids, first_row, row_count, 0)
    query_segment = query_segment.reshape(query_blocks, BLK, seq_count).transpose(0, 2, 1)
    window_spots = first_row - BLK + jnp.arange(row_count + 2 * BLK, dtype=jnp.int32)
    inside_seq = (window_spots >= 0) & (window_spots < seq_length)
    near_segment = jnp.take(segment_ids, jnp.clip(window_spots, 0, seq_length - 1), axis=0)
    near_segment = jnp.where(inside_seq[:, None], near_segment, -1)
    near_segment = window_stack(
        near_segment.reshape(query_blocks + 2, BLK, seq_count), query_blocks
    )
    near_segment = near_segment.transpose(0, 3, 1, 2).reshape(query_blocks, seq_count, 1, 3 * BLK)
    segment_rows = segment_ids.T
    sequence_pick = jnp.arange(seq_count, dtype=jnp.int32)
    offsets = jnp.arange(BLK, dtype=jnp.int32)
    far_segment = segment_rows[
        sequence_pick[None, :, None, None, None], random_local[..., None] * BLK + offsets
    ]
    far_segment = far_segment.reshape(query_blocks, seq_count, HEADS, RAND * BLK)
    global_segment = segment_rows[
        sequence_pick[None, :, None], global_blocks[..., None] * BLK + offsets
    ]
    global_segment = global_segment.transpose(1, 0, 2).reshape(1, seq_count, 1, GLOB * BLK)
    key_segment = jnp.concatenate(
        [
            jnp.broadcast_to(near_segment, (query_blocks, seq_count, HEADS, 3 * BLK)),
            far_segment,
            jnp.broadcast_to(global_segment, (query_blocks, seq_count, HEADS, GLOB * BLK)),
        ],
        axis=-1,
    )
    allowed = key_segment[:, :, :, None, :] == query_segment[:, :, None, :, None]
    query_rows = queries.reshape(query_blocks, BLK, seq_count, HEADS, HD)
    scores = jnp.where(
        allowed, key_products(query_rows, window_kv, far_random, far_global, 0) * score_scale, -1e30
    )
    row_max = jnp.max(scores, axis=-1, keepdims=True)
    log_total = row_max + jnp.log(jnp.sum(jnp.exp(scores - row_max), axis=-1, keepdims=True))
    soft_full = jnp.exp(scores - log_total)
    attn_probs = soft_full.astype(jnp.bfloat16)
    context = (
        key_mix(attn_probs, window_kv, far_random, far_global, 1)
        .reshape(row_count, seq_count, D)
        .astype(jnp.bfloat16)
    )
    mid_stream = (
        inputs
        + jnp.einsum("rsd,de->rse", context, w_out, preferred_element_type=jnp.float32)
        + out_bias.astype(jnp.float32)
    )
    normed2_full, second_norm_back = jax.vjp(
        layer_norm, mid_stream, ln2_gain.astype(jnp.float32), ln2_bias.astype(jnp.float32)
    )
    normed2 = normed2_full.astype(jnp.bfloat16)
    pre_act = jnp.einsum(
        "rsd,df->rsf", normed2, w_in, preferred_element_type=jnp.float32
    ) + in_bias.astype(jnp.float32)
    hidden_full, gelu_back = jax.vjp(gelu_tanh, pre_act)
    hidden = hidden_full.astype(jnp.bfloat16)
    output = (
        mid_stream
        + jnp.einsum("rsf,fd->rsd", hidden, w_down, preferred_element_type=jnp.float32)
        + down_bias.astype(jnp.float32)
    ).astype(jnp.bfloat16)
    grad_out = cotangent.astype(jnp.float32)
    w_down_grad = jnp.einsum("rsf,rsd->fd", hidden, cotangent, preferred_element_type=jnp.float32)
    down_bias_grad = jnp.sum(grad_out, axis=(0, 1))
    pre_grad = gelu_back(
        jnp.einsum("rsd,fd->rsf", cotangent, w_down, preferred_element_type=jnp.float32)
    )[0].astype(jnp.bfloat16)
    w_in_grad = jnp.einsum("rsd,rsf->df", normed2, pre_grad, preferred_element_type=jnp.float32)
    in_bias_grad = jnp.sum(pre_grad.astype(jnp.float32), axis=(0, 1))
    mid_part, ln2_gain_grad, ln2_bias_grad = second_norm_back(
        jnp.einsum("rsf,df->rsd", pre_grad, w_in, preferred_element_type=jnp.float32)
    )
    mid_grad = grad_out + mid_part
    branch_grad = mid_grad.astype(jnp.bfloat16)
    w_out_grad = jnp.einsum("rsd,rse->de", context, branch_grad, preferred_element_type=jnp.float32)
    out_bias_grad = jnp.sum(branch_grad.astype(jnp.float32), axis=(0, 1))
    context_grad = jnp.einsum(
        "rse,de->rsd", branch_grad, w_out, preferred_element_type=jnp.float32
    ).astype(jnp.bfloat16)
    grad_rows = context_grad.reshape(query_blocks, BLK, seq_count, HEADS, HD)
    probs_grad = key_products(grad_rows, window_kv, far_random, far_global, 1)
    score_grad = (
        soft_full * (probs_grad - jnp.sum(soft_full * probs_grad, axis=-1, keepdims=True))
    ).astype(jnp.bfloat16)
    query_grad = (
        (key_mix(score_grad, window_kv, far_random, far_global, 0) * score_scale)
        .reshape(row_count, seq_count, D)
        .astype(jnp.bfloat16)
    )
    near_key, far_key, global_key = key_grads(score_grad, query_rows)
    near_value, far_value, global_value = key_grads(attn_probs, grad_rows)
    near_kv = jnp.stack([near_key * score_scale, near_value], axis=4)
    far_kv = jnp.stack([far_key * score_scale, far_value], axis=5)
    global_kv = jnp.stack([global_key * score_scale, global_value], axis=3).reshape(
        GLOB, BLK, seq_count, 2 * D
    )
    rest_pad = ((0, 0),) * 5
    extended_grad = (
        jnp.pad(near_kv[:, 0], ((0, 2),) + rest_pad)
        + jnp.pad(near_kv[:, 1], ((1, 1),) + rest_pad)
        + jnp.pad(near_kv[:, 2], ((2, 0),) + rest_pad)
    )
    extended_grad = extended_grad.reshape(row_count + 2 * BLK, seq_count, 2 * D)
    rim_grads = jnp.concatenate([extended_grad[:BLK], extended_grad[row_count + BLK :]], axis=0)
    returned = padded(rim_grads.astype(jnp.bfloat16), (("seq", 0),), BLK).astype(rim_grads.dtype)
    near_total = extended_grad[BLK : row_count + BLK]
    near_total = (
        near_total.at[:BLK].add(returned[:BLK]).at[row_count - BLK :].add(returned[3 * BLK :])
    )
    block_total = row_count * lax.axis_size("seq") // BLK
    numbers = jnp.arange(block_total, dtype=jnp.int32)
    random_hits = (random_local[..., None] == numbers).astype(jnp.float32)
    global_rows_hit = (global_blocks[..., None] == numbers).astype(jnp.float32)

    def far_sum(one_sequence):
        hits, kv, global_rows, global_sum = one_sequence
        random_term = jnp.einsum(
            "ihjb,ihjuxd->buxhd", hits, kv, precision=lax.Precision.HIGHEST
        )
        global_term = jnp.einsum(
            "gb,guc->buc", global_rows, global_sum, precision=lax.Precision.HIGHEST
        )
        flat = (block_total * BLK, 2 * D)
        return (random_term.reshape(flat) + global_term.reshape(flat)).astype(jnp.bfloat16)

    far_parts = lax.map(
        far_sum,
        (
            jnp.moveaxis(random_hits, 1, 0),
            jnp.moveaxis(far_kv, 1, 0),
            jnp.moveaxis(global_rows_hit, 1, 0),
            jnp.moveaxis(global_kv, 2, 0),
        ),
    )
    far_total = lax.psum_scatter(far_parts, "seq", scatter_dimension=1, tiled=True)
    far_total = jnp.moveaxis(far_total, 0, 1).astype(jnp.float32)
    keyval_grad = (near_total + far_total).astype(jnp.bfloat16)
    qkv_grad = jnp.concatenate([query_grad, keyval_grad], axis=-1)
    q_bias_grad = jnp.sum(query_grad.astype(jnp.float32), axis=(0, 1))
    v_bias_grad = jnp.sum(keyval_grad[:, :, D:].astype(jnp.float32), axis=(0, 1))
    w_qkv_grad = jnp.einsum("rsd,rse->de", normed, qkv_grad, preferred_element_type=jnp.float32)
    input_part, ln1_gain_grad, ln1_bias_grad = first_norm_back(
        jnp.einsum("rse,de->rsd", qkv_grad, w_qkv, preferred_element_type=jnp.float32)
    )
    input_grad = mid_grad + input_part
    summed = (
        lax.psum_scatter(ln1_gain_grad, ("batch", "seq"), scatter_dimension=0, tiled=True),
        lax.psum_scatter(ln1_bias_grad, ("batch", "seq"), scatter_dimension=0, tiled=True),
        lax.psum_scatter(w_qkv_grad, ("batch", "seq"), scatter_dimension=0, tiled=True),
        lax.psum_scatter(q_bias_grad, ("batch", "seq"), scatter_dimension=0, tiled=True),
        lax.psum_scatter(v_bias_grad, ("batch", "seq"), scatter_dimension=0, tiled=True),
        lax.psum_scatter(w_out_grad, ("batch", "seq"), scatter_dimension=0, tiled=True),
        lax.psum_scatter(out_bias_grad, ("batch", "seq"), scatter_dimension=0, tiled=True),
        lax.psum_scatter(ln2_gain_grad, ("batch", "seq"), scatter_dimension=0, tiled=True),
        lax.psum_scatter(ln2_bias_grad, ("batch", "seq"), scatter_dimension=0, tiled=True),
        lax.psum_scatter(w_in_grad, ("batch", "seq"), scatter_dimension=0, tiled=True),
        lax.psum_scatter(in_bias_grad, ("batch", "seq"), scatter_dimension=0, tiled=True),
        lax.psum_scatter(w_down_grad, ("batch", "seq"), scatter_dimension=0, tiled=True),
        lax.psum_scatter(down_bias_grad, ("batch", "seq"), scatter_dimension=0, tiled=True),
    )
    return (
        output,
        input_grad,
        summed[0],
        summed[1],
        summed[2],
        summed[3],
        summed[4],
        summed[5],
        summed[6],
        summed[7],
        summed[8],
        summed[9],
        summed[10],
        summed[11],
        summed[12],
    )


NEG = -1e30
LANES = 128
SEG_VALUES = 4
MESH_IDS = pl.DeviceIdType.MESH
VMEM_BYTES = 60 * 1024 * 1024
F32 = jnp.float32
BF16 = jnp.bfloat16
ALL = slice(None)
Z_HIGH, Z_LOW, Y, X, MEMBER = range(5)
CHIP = (Z_HIGH, Z_LOW, Y, X)


def three_parts(x):
    hi = x.astype(BF16)
    rest = x - hi.astype(F32)
    mid = rest.astype(BF16)
    low = (rest - mid.astype(F32)).astype(BF16)
    return hi, mid, low


def dot_nt(a, b):
    return lax.dot_general(a, b, (((1,), (1,)), ((), ())), preferred_element_type=F32)


def dot_nn(a, b):
    return lax.dot_general(a, b, (((1,), (0,)), ((), ())), preferred_element_type=F32)


def dot_tn(a, b):
    return lax.dot_general(a, b, (((0,), (0,)), ((), ())), preferred_element_type=F32)


def turned(x):
    return x.astype(F32).T.astype(BF16)


def normalise(values):
    mean = jnp.mean(values, axis=-1, keepdims=True)
    centred = values - mean
    scale = lax.rsqrt(jnp.mean(centred * centred, axis=-1, keepdims=True) + eps)
    return centred * scale, scale


def normalise_back(unit, scale, grad):
    first = jnp.mean(grad, axis=-1, keepdims=True)
    second = jnp.mean(grad * unit, axis=-1, keepdims=True)
    return (grad - first - unit * second) * scale


def my_bits():
    batch = lax.axis_index("batch")
    return (
        lax.div(batch, 4),
        lax.rem(lax.div(batch, 2), 2),
        lax.rem(batch, 2),
        lax.axis_index("half"),
        lax.axis_index("member"),
    )


def device_across(bit):
    batch = lax.axis_index("batch")
    half = lax.axis_index("half")
    member = lax.axis_index("member")
    if bit == MEMBER:
        return (batch, half, 1 - member)
    if bit == X:
        return (batch, 1 - half, member)
    stride = (4, 2, 1)[bit]
    return (batch + stride * (1 - 2 * my_bits()[bit]), half, member)


def place_across(mask):
    z_high, z_low, y, x, member = (
        1 - bit if mask & flag else bit for bit, flag in zip(my_bits(), (16, 8, 4, 2, 1))
    )
    return (4 * z_high + 2 * z_low + y, x, member)


def remote(src, dst, send, recv, bit):
    return pltpu.make_async_remote_copy(
        src_ref=src,
        dst_ref=dst,
        send_sem=send,
        recv_sem=recv,
        device_id=device_across(bit),
        device_id_type=MESH_IDS,
    )


def greet(bits):
    barrier = pltpu.get_barrier_semaphore()
    for bit in bits:
        pl.semaphore_signal(barrier, inc=1, device_id=device_across(bit), device_id_type=MESH_IDS)
    pl.semaphore_wait(barrier, len(bits))


class Sums:
    def __init__(self, send_sem, recv_sem):
        self.bits = my_bits()
        self.send_sem, self.recv_sem = send_sem, recv_sem
        self.pieces = {}

    def add(self, number, source, dims, order, slots, cut=()):
        self.pieces[number] = (source, dims, order, slots, cut)

    def side(self, number, depth, across):
        source, dims, order, slots, cut = self.pieces[number]
        bit = order[depth]
        value = 1 - self.bits[bit] if across else self.bits[bit]
        left = [b for b in dims if b not in order[:depth]]
        spot = left.index(bit)
        index = (ALL,) * (1 + spot) + (value,)
        if depth:
            return slots[depth - 1].at[index]
        return source.at[index + (ALL,) * (len(left) - 1 - spot) + cut]

    def copy(self, number, depth):
        _, _, order, slots, _ = self.pieces[number]
        return remote(
            self.side(number, depth, True),
            slots[depth],
            self.send_sem.at[number, depth],
            self.recv_sem.at[number, depth],
            order[depth],
        )

    def send(self, number, depth):
        self.copy(number, depth).start()

    def take(self, number, depth):
        _, _, order, slots, _ = self.pieces[number]
        self.copy(number, depth).wait_recv()
        mine = self.side(number, depth, False)[...]
        if depth == len(order) - 1:
            return mine.astype(F32) + slots[depth][...].astype(F32)
        slots[depth][...] = mine + slots[depth][...]
        self.send(number, depth + 1)
        return None

    def finish(self):
        for number, (_, _, order, _, _) in self.pieces.items():
            for depth in range(len(order)):
                self.copy(number, depth).wait_send()


def slot_shapes(lead, count, tail):
    return [pltpu.VMEM((lead,) + (2,) * (count - 1 - depth) + tail, BF16) for depth in range(count)]


ORDERS = ((X, Y, Z_LOW, Z_HIGH), (Y, Z_LOW, X, Z_HIGH), (Z_LOW, X, Y, Z_HIGH))
IN_CUTS = ((0, 16), (16, 16), (32, 32))
DOWN_CUTS = ((0, 384), (384, 384), (768, 256))
OUT_CUTS = ((0, 128), (128, 128), (256, 256))
LATER_DIMS = (
    (Z_HIGH, Z_LOW, Y),
    (Z_HIGH, Z_LOW, X),
    (Z_HIGH, Y, X),
    (Z_LOW, Y, Z_HIGH),
    (Z_LOW, Z_HIGH, X),
    (Y, Z_HIGH, X),
)


def in_vmem():
    return pl.BlockSpec(memory_space=pltpu.VMEM)


def anywhere():
    return pl.BlockSpec(memory_space=pl.ANY)


def params(collective):
    return pltpu.CompilerParams(
        collective_id=collective, has_side_effects=True, vmem_limit_bytes=VMEM_BYTES
    )


def take_rows(mixed, which):
    count = mixed.shape[0] // 2
    row = lax.broadcasted_iota(jnp.int32, (count, 2 * count), 0)
    column = lax.broadcasted_iota(jnp.int32, (count, 2 * count), 1)
    pick = jnp.where(column == 2 * row + which, 1.0, 0.0).astype(BF16)
    return dot_nn(pick, mixed).astype(BF16)


def sequence_rows(seg_ref, rows, length):
    half, member = lax.axis_index("half"), lax.axis_index("member")
    own = length // 2
    both = seg_ref[...].astype(F32)
    ids = jnp.where(half == 0, both[0:1], both[1:2])
    slots = []
    for j in range(2):
        for t in range(2):
            want = lax.rem(half + t, 2) * 2 + lax.rem(member + j, 2)
            piece = jnp.zeros((1, rows), F32)
            for b in range(4):
                piece = jnp.where(want == b, ids[:, b * rows : (b + 1) * rows], piece)
            slots.append(piece)
    spot = lax.broadcasted_iota(jnp.int32, (1, length), 1)
    side = lax.rem(half + lax.rem(spot // rows, 2), 2) * 2 + lax.rem(member + spot // own, 2)
    block = side * (rows // BLK) + lax.rem(spot // BLK, rows // BLK)
    return jnp.concatenate(slots, axis=1), block.astype(F32)


def make_features(segment, block, rand_ref, glob_ref, fq_ref, fk_ref):
    length = segment.shape[1]
    blocks = length // BLK
    half = lax.axis_index("half")
    numbers = lax.broadcasted_iota(jnp.int32, (8, length), 0).astype(F32)
    count = lax.broadcasted_iota(jnp.int32, (blocks, length), 0).astype(F32)
    here = jnp.where(block == count, 1.0, 0.0)
    apart = jnp.where((segment == numbers) | (numbers >= SEG_VALUES), 0.0, NEG)
    feats = jnp.concatenate([apart, here, here, jnp.zeros((HD - 8 - 2 * blocks, length), F32)], axis=0)
    fq_ref[...] = jnp.concatenate([feats, feats], axis=0).T.astype(BF16)

    same = jnp.where(segment == numbers, 1.0, 0.0)
    rest = jnp.zeros((HD - 16 - 2 * blocks, length), F32)
    ones = jnp.where(numbers < 3, 1.0, 0.0)
    common = jnp.where(jnp.abs(count - block) <= 1.0, 1.0, 0.0)
    for g in range(GLOB):
        named = jnp.where(half == 0, glob_ref[g : g + 1, 0:1], glob_ref[g : g + 1, 1:2])
        common = common + jnp.where(block == named.astype(F32), 1.0, 0.0)
    for pair in range(fk_ref.shape[0]):
        drawn = rand_ref[pair]
        sides = []
        for parity in (1, 0):
            times = common
            for j in range(RAND):
                column = parity * RAND + j
                times = times + jnp.where(drawn[:, column : column + 1] == block, 1.0, 0.0)
            full = jnp.where(times > 0, jnp.log(jnp.maximum(times, 1.0)), NEG)
            high = full.astype(BF16).astype(F32)
            sides += [same, high, full - high, ones, rest]
        fk_ref[pair] = jnp.concatenate(sides, axis=0).T.astype(BF16)


def begin(mixed, small, w_qkv, segments, random_blocks, global_blocks):
    rows = mixed.shape[0] // 2
    length = 4 * rows
    width = D // 2
    pairs = width // LANES
    cuts = 2
    size = rows // cuts

    def body(*refs):
        mixed_ref, wq_ref, wk_ref, wv_ref, seg_ref, rand_ref, glob_ref = refs[:7]
        small_refs, in_ref = refs[7:15], refs[15]
        tok_ref, nt_ref, q_ref, k_ref, v_ref, fq_ref, fk_ref, vec_ref, in_row = refs[16:25]
        all_ref, kept_ref, sent_ref, norm_ref, send_sem, recv_sem = refs[25:]
        half = lax.axis_index("half")
        sent_ref[...] = take_rows(mixed_ref[...], 1 - half)
        greet((X, MEMBER))

        def over_x(c):
            return remote(
                sent_ref.at[pl.ds(c * size, size)],
                all_ref.at[pl.ds(rows + c * size, size)],
                send_sem.at[c],
                recv_sem.at[c],
                X,
            )

        def on(c):
            return remote(
                all_ref.at[pl.ds(rows + c * size, size)],
                all_ref.at[pl.ds(3 * rows + c * size, size)],
                send_sem.at[cuts + c],
                recv_sem.at[cuts + c],
                MEMBER,
            )

        near = remote(
            kept_ref, all_ref.at[pl.ds(2 * rows, rows)], send_sem.at[2 * cuts], recv_sem.at[2 * cuts], MEMBER
        )
        for c in range(cuts):
            over_x(c).start()
        kept_ref[...] = take_rows(mixed_ref[...], half)
        near.start()

        for at, ref in enumerate(small_refs):
            vec_ref[at : at + 1] = ref[...].astype(F32).reshape(1, D)
        in_row[...] = in_ref[...].astype(F32).reshape(in_row.shape)
        first_half = lax.axis_index("member") == 0
        q_shift, v_shift = (
            jnp.where(first_half, vec_ref[row : row + 1, :width], vec_ref[row : row + 1, width:]) for row in (6, 7)
        )

        def project(first, count):
            place = pl.ds(first, count)
            x = kept_ref[...] if first == 0 else all_ref[place, :]
            if first < 2 * rows:
                tok_ref[place, :] = x
            unit, _ = normalise(x.astype(F32))
            normed = (unit * vec_ref[4:5] + vec_ref[5:6]).astype(BF16)
            if count % LANES == 0:
                nt_ref[:, place] = turned(normed)
            else:
                norm_ref[pl.ds(first % (2 * count), count), :] = normed
                if first % (2 * count):
                    nt_ref[:, first - count : first + count] = turned(norm_ref[...])
            q_ref[place, :] = (dot_nn(normed, wq_ref[...]) + q_shift).astype(BF16)
            k_ref[place, :] = dot_nn(normed, wk_ref[...]).astype(BF16)
            v_ref[place, :] = (dot_nn(normed, wv_ref[...]) + v_shift).astype(BF16)

        project(0, rows)
        near.wait_recv()
        project(2 * rows, rows)
        make_features(*sequence_rows(seg_ref, rows, length), rand_ref, glob_ref, fq_ref, fk_ref)
        for c in range(cuts):
            over_x(c).wait_recv()
            on(c).start()
            project(rows + c * size, size)
        for c in range(cuts):
            on(c).wait_recv()
            project(3 * rows + c * size, size)
        near.wait_send()
        for c in range(cuts):
            over_x(c).wait_send()
            on(c).wait_send()

    def weight(which):
        return pl.BlockSpec((D, width), lambda i: (0, 2 * which + lax.axis_index("member")))

    def shape(count, columns):
        return jax.ShapeDtypeStruct((count, columns), BF16)

    return pl.pallas_call(
        body,
        grid=(1,),
        out_shape=(shape(2 * rows, D), shape(D, length))
        + (shape(length, width),) * 3
        + (shape(length, LANES), jax.ShapeDtypeStruct((pairs, length, LANES), BF16))
        + (jax.ShapeDtypeStruct((8, D), F32), jax.ShapeDtypeStruct((1,) + small[8].shape, F32)),
        in_specs=[in_vmem(), weight(0), weight(1), weight(2)] + [in_vmem()] * 12,
        out_specs=(in_vmem(),) * 9,
        scratch_shapes=[
            pltpu.VMEM((length, D), BF16),
            pltpu.VMEM((rows, D), BF16),
            pltpu.VMEM((rows, D), BF16),
            pltpu.VMEM((2 * size, D), BF16),
            pltpu.SemaphoreType.DMA((2 * cuts + 1,)),
            pltpu.SemaphoreType.DMA((2 * cuts + 1,)),
        ],
        compiler_params=params(5),
        name="begin",
    )(mixed, w_qkv, w_qkv, w_qkv, segments, random_blocks, global_blocks, *small)


def attend_forward(q, k, v, feat_q, feat_k, cot_mixed, tile=512):
    length, width = q.shape
    pairs = width // LANES
    tiles = length // tile
    blocks = length // BLK
    own = length // 2
    rows = own // 2

    def body(*refs):
        q_ref, k_ref, v_ref, fq_ref, fk_ref, mixed_ref = refs[:6]
        ctx_ref, qa_ref, other_ref, cot_ref = refs[6:10]
        ka_ref, made_ref, kept_ref, sent_ref, send_sem, recv_sem, cot_send, cot_recv = refs[10:]
        pair, step = pl.program_id(0), pl.program_id(1)
        half = lax.axis_index("half")

        def stay():
            return pltpu.make_async_copy(kept_ref, cot_ref.at[pl.ds(0, rows)], cot_send.at[3])

        def cot_copy(which):
            across = pl.ds(rows, rows)
            src, to, bit = (
                (sent_ref, across, X),
                (kept_ref, pl.ds(own, rows), MEMBER),
                (cot_ref.at[across], pl.ds(own + rows, rows), MEMBER),
            )[which]
            return remote(src, cot_ref.at[to], cot_send.at[which], cot_recv.at[which], bit)

        @pl.when((pair == 0) & (step == 0))
        def _():
            greet((X, MEMBER))
            sent_ref[...] = take_rows(mixed_ref[...], 1 - half)
            cot_copy(0).start()
            kept_ref[...] = take_rows(mixed_ref[...], half)
            cot_copy(1).start()
            stay().start()

        @pl.when(step == 0)
        def _():
            feats = fk_ref[0]
            low_half = lax.broadcasted_iota(jnp.int32, (length, LANES), 1) < HD
            keys = k_ref[...]
            ka_ref[0] = jnp.where(low_half, keys, feats)
            ka_ref[1] = jnp.where(low_half, feats, keys)

        lane = lax.broadcasted_iota(jnp.int32, (tile, LANES), 1)
        low_half = lane < HD
        scaled = q_ref[...] * jnp.asarray(HD ** (-0.5), BF16)
        place = pl.ds(pl.multiple_of(step * tile, tile), tile)
        feats = fq_ref[...]
        results = []
        for parity in range(2):
            if parity == 0:
                aug = jnp.where(low_half, scaled, feats)
                first = HD + 8 + 2 * blocks
            else:
                aug = jnp.where(low_half, feats, scaled)
                first = 8 + 2 * blocks
            scores = dot_nt(aug, ka_ref[parity])
            top = jnp.max(scores, axis=-1, keepdims=True)
            weights = jnp.exp(scores - top)
            total = jnp.sum(weights, axis=-1, keepdims=True)
            mixed = dot_nn(weights.astype(BF16), v_ref[...])
            results.append(mixed / total)
            hi, mid, low = three_parts(-(top + jnp.log(total)))
            aug = jnp.where(lane == first, hi, aug)
            aug = jnp.where(lane == first + 1, mid, aug)
            aug = jnp.where(lane == first + 2, low, aug)
            qa_ref[parity] = aug
        context = jnp.where(low_half, results[0], results[1]).astype(BF16)
        ctx_ref[...] = context
        made_ref[pair, place, :] = context

        def swaps(one_pair):
            cols = pl.ds(pl.multiple_of(one_pair * LANES, LANES), LANES)
            return [
                remote(
                    made_ref.at[one_pair, pl.ds(from_row, own)],
                    other_ref.at[pl.ds(own - from_row, own), cols],
                    send_sem.at[side, one_pair],
                    recv_sem.at[side, one_pair],
                    MEMBER,
                )
                for side, from_row in enumerate((0, own))
            ]

        @pl.when(step == tiles - 1)
        def _():
            for one in swaps(pair):
                one.start()

        @pl.when((pair == pairs - 2) & (step == tiles - 1))
        def _():
            cot_copy(0).wait_recv()
            cot_copy(2).start()

        @pl.when((pair == pairs - 1) & (step == tiles - 1))
        def _():
            cot_copy(0).wait_send()
            stay().wait()
            cot_copy(1).wait()
            cot_copy(2).wait()
            for one_pair in range(pairs):
                for one in swaps(one_pair):
                    one.wait()

    return pl.pallas_call(
        body,
        grid=(pairs, tiles),
        out_shape=(
            jax.ShapeDtypeStruct((length, width), BF16),
            jax.ShapeDtypeStruct((2 * pairs, length, LANES), BF16),
            jax.ShapeDtypeStruct((length, width), BF16),
            jax.ShapeDtypeStruct((length, D), BF16),
        ),
        in_specs=[
            pl.BlockSpec((tile, LANES), lambda p, t: (t, p)),
            pl.BlockSpec((length, LANES), lambda p, t: (0, p)),
            pl.BlockSpec((length, LANES), lambda p, t: (0, p)),
            pl.BlockSpec((tile, LANES), lambda p, t: (t, 0)),
            pl.BlockSpec((1, length, LANES), lambda p, t: (p, 0, 0)),
            in_vmem(),
        ],
        out_specs=(
            pl.BlockSpec((tile, LANES), lambda p, t: (t, p)),
            pl.BlockSpec((2, tile, LANES), lambda p, t: (p, t, 0)),
            anywhere(),
            anywhere(),
        ),
        scratch_shapes=[
            pltpu.VMEM((2, length, LANES), BF16),
            pltpu.VMEM((pairs, length, LANES), BF16),
            pltpu.VMEM((rows, D), BF16),
            pltpu.VMEM((rows, D), BF16),
            pltpu.SemaphoreType.DMA((2, pairs)),
            pltpu.SemaphoreType.DMA((2, pairs)),
            pltpu.SemaphoreType.DMA((4,)),
            pltpu.SemaphoreType.DMA((3,)),
        ],
        compiler_params=params(4),
        name="attend_forward",
    )(q, k, v, feat_q, feat_k, cot_mixed)


def feed_forward(context, context_other, tokens, w_out, vectors, cot, w_in, in_bias, w_down):
    rows = cot.shape[0]
    own = rows // 2
    width = context.shape[1]
    chunk = 4 * LANES
    steps = 4
    share = D // 16
    root = (2.0 / np.pi) ** 0.5
    cube = 0.044715

    def group(j):
        bits = my_bits()
        z_low = jnp.where(j < 2, 1 - bits[Z_LOW], bits[Z_LOW])
        return z_low, jnp.where(lax.rem(j, 2) == 0, 1 - bits[Y], bits[Y])

    def body(*refs):
        ctx_ref, other_ref, tok_ref, wo_ref, wo2_ref, vec_ref, c_ref = refs[:7]
        wi_refs, inb_ref, wd_refs = refs[7:11], refs[11], refs[12:16]
        out_ref, dn_ref, dn_got, mid_ref, gb_ref = refs[16:21]
        keep, got = refs[21:27], refs[27:33]
        n_ref, nt_ref, out_acc, dn_acc, out_send, out_got, dn_send, gi_ref, gd_ref = refs[33:42]
        send_sem, recv_sem, keep_sem, swap_sem = refs[42:]
        step = pl.program_id(0)
        bits = my_bits()
        z_low, y = group(step)
        slot = 2 * z_low + y

        @pl.when(step == 0)
        def _():
            greet((Z_LOW, Y, X, MEMBER))
            cut = own // 2
            swaps = []
            for at in range(2):
                part = slice(at * cut, (at + 1) * cut)
                mid = (
                    tok_ref[part].astype(F32)
                    + dot_nn(ctx_ref[part], wo_ref[...])
                    + dot_nn(other_ref[part], wo2_ref[...])
                    + vec_ref[0:1]
                )
                mid_ref[part] = mid
                unit, _ = normalise(mid)
                n_ref[part] = (unit * vec_ref[1:2] + vec_ref[2:3]).astype(BF16)
                swaps.append(
                    remote(
                        n_ref.at[pl.ds(at * cut, cut)],
                        n_ref.at[pl.ds(own + at * cut, cut)],
                        swap_sem.at[0, 3 * at],
                        swap_sem.at[1, 3 * at],
                        MEMBER,
                    )
                )
                swaps[at].start()
            nt_ref[:, :own] = turned(n_ref[:own])
            for at in range(2):
                swaps[at].wait()
                first = own + at * cut
                nt_ref[:, first : first + cut] = turned(n_ref[first : first + cut])

        wi = jnp.concatenate([ref[...] for ref in wi_refs], axis=1)
        wd = jnp.concatenate([ref[...] for ref in wd_refs], axis=0)
        def shift(u):
            return inb_ref[:, pl.ds(pl.multiple_of(u(step) * LANES, LANES), LANES)]

        in_shift = jnp.concatenate([shift(u) for u in units], axis=1)
        pre = dot_nn(n_ref[...], wi) + in_shift
        square = pre * pre
        th = jnp.tanh(root * pre * (1.0 + cube * square))
        half_up = 0.5 * (1.0 + th)
        hidden = (pre * half_up).astype(BF16)
        slope = half_up + 0.5 * pre * (1.0 - th * th) * (root * (1.0 + 3.0 * cube * square))

        def in_part(kind, at):
            bit = (X, Y, Z_LOW)[kind]
            rest = (ALL,) * (3 - bit) + (pl.ds(*IN_CUTS[kind]),)
            return lambda side: gi_ref.at[(at,) + (ALL,) * bit + (side,) + rest]

        def copies(kind, at, where, bit):
            return (
                lambda: remote(
                    where(1 - bits[bit]), got[kind].at[at], send_sem.at[kind, at], recv_sem.at[kind, at], bit
                ),
                lambda: pltpu.make_async_copy(where(bits[bit]), keep[kind].at[at], keep_sem.at[kind, at]),
            )

        def in_copies(kind, at):
            return copies(kind, at, in_part(kind, at), (X, Y, Z_LOW)[kind])

        def x_copies(at):
            return copies(3, at, lambda side: gd_ref.at[at, :, side, :, pl.ds(*DOWN_CUTS[0])], X)

        def y_copies(z):
            return copies(4, z, lambda side: gd_ref.at[2 * z + side, :, :, :, pl.ds(*DOWN_CUTS[1])], Y)

        def z_copies(at_y):
            return copies(
                5, at_y, lambda side: gd_ref.at[2 * side + at_y, :, :, :, pl.ds(*DOWN_CUTS[2])], Z_LOW
            )

        gd_ref[slot] = dot_tn(hidden, c_ref[...]).astype(BF16).reshape(2, 2, LANES, D)
        for one in x_copies(slot):
            one().start()

        @pl.when(lax.rem(step, 2) == 0)
        def _():
            y_copies(z_low)[0]().start()

        @pl.when(lax.rem(step, 2) == 1)
        def _():
            y_copies(z_low)[1]().start()

        @pl.when(step < 2)
        def _():
            z_copies(y)[0]().start()

        @pl.when(step >= 2)
        def _():
            z_copies(y)[1]().start()

        pre_grad = (dot_nt(c_ref[...], wd) * slope).astype(BF16)
        gb_ref[...] = jnp.sum(pre_grad.astype(F32), axis=0, keepdims=True)
        gi_ref[slot] = dot_nn(nt_ref[...], pre_grad).astype(BF16).reshape(2, 2, 2, 2, share, chunk)
        for kind in range(3):
            for one in in_copies(kind, slot):
                one().start()

        dn_swap = (dn_send, dn_got, swap_sem.at[0, 1], swap_sem.at[1, 1], MEMBER)
        out_swap = (out_send, out_got, swap_sem.at[0, 2], swap_sem.at[1, 2], MEMBER)
        @pl.when(step == 0)
        def _():
            dn_acc[...] = dot_nt(pre_grad, wi)
            out_acc[...] = dot_nn(hidden, wd)

        @pl.when((step > 0) & (step < steps - 1))
        def _():
            dn_acc[...] += dot_nt(pre_grad, wi)
            out_acc[...] += dot_nn(hidden, wd)

        @pl.when(step == steps - 1)
        def _():
            theirs, ours = slice(own, rows), slice(0, own)
            dn_send[...] = (dn_acc[theirs] + dot_nt(pre_grad[theirs], wi)).astype(BF16)
            remote(*dn_swap).start()
            out_send[...] = (out_acc[theirs] + dot_nn(hidden[theirs], wd)).astype(BF16)
            remote(*out_swap).start()
            dn_ref[...] = dn_acc[ours] + dot_nt(pre_grad[ours], wi)
            out_acc[ours] += mid_ref[...] + vec_ref[3:4] + dot_nn(hidden[ours], wd)

        @pl.when(step == steps - 1)
        def _():
            for at in range(4):
                for kind in range(3):
                    for one in in_copies(kind, at):
                        one().wait()
                for one in x_copies(at):
                    one().wait()
            for at in range(2):
                for one in y_copies(at) + z_copies(at):
                    one().wait()
            remote(*dn_swap).wait()
            remote(*out_swap).wait()
            out_ref[...] = (out_acc[:own] + out_got[...].astype(F32)).astype(BF16)

    def unit(z_high, x):
        def at(j):
            z_low, y = group(j)
            return 2 * (((2 * z_high + z_low) * 2 + y) * 2 + x) + lax.axis_index("member")

        return at

    units = [unit(z_high, x) for z_high in range(2) for x in range(2)]

    def column(u):
        return lambda j: (0, u(j))

    def row(u):
        return lambda j: (u(j), 0)

    def slot_of(j):
        z_low, y = group(j)
        return (0, 2 * z_low + y)

    whole = pl.BlockSpec((rows, D), lambda j: (0, 0))
    half = pl.BlockSpec((own, D), lambda j: (0, 0))
    half_ctx = pl.BlockSpec((own, width), lambda j: (0, 0))
    parts = [jax.ShapeDtypeStruct((4, 2, 2, 2, size, chunk), BF16) for _, size in IN_CUTS] + [
        jax.ShapeDtypeStruct((4, 2, LANES, DOWN_CUTS[0][1]), BF16),
        jax.ShapeDtypeStruct((2, 2, 2, LANES, DOWN_CUTS[1][1]), BF16),
        jax.ShapeDtypeStruct((2, 2, 2, LANES, DOWN_CUTS[2][1]), BF16),
    ]
    own_f32 = jax.ShapeDtypeStruct((own, D), F32)
    own_bf16 = jax.ShapeDtypeStruct((own, D), BF16)
    results = pl.pallas_call(
        body,
        grid=(steps,),
        out_shape=[
            own_bf16,
            own_f32,
            own_bf16,
            own_f32,
            jax.ShapeDtypeStruct((1, steps * chunk), F32),
        ]
        + parts
        + parts,
        in_specs=[
            half_ctx,
            half_ctx,
            half,
            pl.BlockSpec((width, D), lambda j: (lax.axis_index("member"), 0)),
            pl.BlockSpec((width, D), lambda j: (1 - lax.axis_index("member"), 0)),
            pl.BlockSpec((8, D), lambda j: (0, 0)),
            whole,
        ]
        + [pl.BlockSpec((D, LANES), column(u)) for u in units]
        + [in_vmem()]
        + [pl.BlockSpec((LANES, D), row(u)) for u in units],
        out_specs=[half, half, anywhere(), half, pl.BlockSpec((1, chunk), slot_of)]
        + [anywhere()] * 12,
        scratch_shapes=[
            pltpu.VMEM((rows, D), BF16),
            pltpu.VMEM((D, rows), BF16),
            pltpu.VMEM((rows, D), F32),
            pltpu.VMEM((rows, D), F32),
            pltpu.VMEM((own, D), BF16),
            pltpu.VMEM((own, D), BF16),
            pltpu.VMEM((own, D), BF16),
            pltpu.VMEM((4, 2, 2, 2, 2, share, chunk), BF16),
            pltpu.VMEM((4, 2, 2, LANES, D), BF16),
            pltpu.SemaphoreType.DMA((6, 4)),
            pltpu.SemaphoreType.DMA((6, 4)),
            pltpu.SemaphoreType.DMA((6, 4)),
            pltpu.SemaphoreType.DMA((2, 4)),
        ],
        compiler_params=params(1),
        name="feed_forward",
    )(context, context_other, tokens, w_out, w_out, vectors, cot, *[w_in] * 4, in_bias, *[w_down] * 4)
    return results[:5], results[5:11], results[11:]


def attend_backward(
    rows_aug, k, v, feat_k, ctx, ctx_other, mid, n2_grad, n2_grad_got, cot, vectors, w_out, normed_t, w_qkv, output_own,
    kept, got, tile=256,
):
    length, width = k.shape
    pairs = width // LANES
    early = 1
    tiles = length // tile
    own = length // 2
    chunk = kept[0].shape[-1]
    shapes = [a.shape for a in kept[:3]] + [(1, 2, 2, 2, LANES, a.shape[-1]) for a in kept[3:]]
    kept = [a.reshape(shape) for a, shape in zip(kept, shapes)]
    got = [a.reshape(shape) for a, shape in zip(got, shapes)]
    share = D // 16
    count = 9 + 3 * early

    def body(*refs):
        qa_ref, k_ref, v_ref, fk_ref, ctx_ref, other_ref, mid_ref, dn2_ref, dn2_got, c_ref, vec_ref, wo_ref = refs[:12]
        nt_ref, wq_ref, wk_ref, wv_ref, mine_ref = refs[12:17]
        keep_in, got_in = refs[17:23], refs[23:29]
        dn_ref, mg_ref, sum_ref, qb_ref, vb_ref, ready_ref, sum_down, dn_got, theirs_ref = refs[29:38]
        keep_new, got_new = refs[38:41], refs[41:44]
        ga_ref, acc_ref, slab_ref, dn_acc, dn_send, gq_ref, br_ref, g_ref, go_ref = refs[44:53]
        begin, first = refs[53:59], refs[59:65]
        slots = refs[65 : 65 + 18 + 12 + 12 * early]
        send_sem, recv_sem, load_sem, new_send, new_recv, new_keep, swap_sem = refs[65 + 30 + 12 * early :]
        pair, step = pl.program_id(0), pl.program_id(1)
        now = pair * tiles + step
        member = lax.axis_index("member")

        sums = Sums(send_sem, recv_sem)
        for kind in range(6):
            sums.add(kind, begin[kind], LATER_DIMS[kind], ORDERS[kind % 3][1:], slots[3 * kind : 3 * kind + 3])
        for kind in range(3):
            sums.add(
                6 + kind,
                go_ref,
                CHIP,
                ORDERS[kind],
                slots[18 + 4 * kind : 22 + 4 * kind],
                (ALL, pl.ds(*OUT_CUTS[kind])),
            )
        for one_pair in range(early):
            for kind in range(3):
                number = 9 + 3 * one_pair + kind
                sums.add(
                    number,
                    gq_ref.at[one_pair, pl.ds(kind, 1)],
                    CHIP,
                    ORDERS[kind],
                    slots[30 + 4 * (number - 9) : 34 + 4 * (number - 9)],
                )

        def loads(kind):
            return (
                pltpu.make_async_copy(keep_in[kind], begin[kind], load_sem.at[0, kind]),
                pltpu.make_async_copy(got_in[kind], first[kind], load_sem.at[1, kind]),
            )

        def begin_sum(kind):
            for one in loads(kind):
                one.wait()
            begin[kind][...] = begin[kind][...] + first[kind][...]
            sums.send(kind, 0)

        def end_sum(number):
            total = sums.take(number, len(sums.pieces[number][2]) - 1)
            if number < 3:
                for z_low in range(2):
                    for y in range(2):
                        for z_high in range(2):
                            for x in range(2):
                                unit = ((2 * z_high + z_low) * 2 + y) * 2 + x
                                local = (2 * z_high + x) * LANES
                                ready_ref[pl.ds(*IN_CUTS[number]), unit * LANES : (unit + 1) * LANES] = total[
                                    2 * z_low + y, :, local : local + LANES
                                ]
            elif number < 6:
                sum_down[:, pl.ds(*DOWN_CUTS[number - 3])] = total[0]
            elif number < 9:
                col, size = OUT_CUTS[number - 6]
                ready_ref[:, pl.ds(4 * chunk + col, size)] = total[0]
            else:
                one_pair, kind = (number - 9) // 3, (number - 9) % 3
                place = 4 * chunk + width + (kind * early + one_pair) * LANES
                ready_ref[:, place : place + LANES] = total[0]

        def do(number, depth):
            if depth == len(sums.pieces[number][2]) - 1:
                end_sum(number)
            else:
                sums.take(number, depth)

        def at(when, depth, *numbers):
            @pl.when(now == when)
            def _():
                for number in numbers:
                    do(number, depth)

        @pl.when(now == 0)
        def _():
            greet((Z_HIGH, Z_LOW, Y, X, MEMBER))
            for kind in range(6):
                for one in loads(kind):
                    one.start()
            for kind in (0, 1, 5, 2, 3, 4):
                begin_sum(kind)
            unit, scale = normalise(mid_ref[...])
            grad = dn2_ref[...] + dn2_got[...].astype(F32)
            cot_own = c_ref[...].astype(F32)
            mid_grad = cot_own + normalise_back(unit, scale, grad * vec_ref[1:2])
            mg_ref[...] = mid_grad
            branch = mid_grad.astype(BF16)
            br_ref[:own] = branch
            swap = remote(
                br_ref.at[pl.ds(0, own)], br_ref.at[pl.ds(own, own)], swap_sem.at[0, 0], swap_sem.at[1, 0], MEMBER
            )
            swap.start()
            sum_ref[0:1] = jnp.sum(branch.astype(F32), axis=0, keepdims=True)
            sum_ref[1:2] = jnp.sum(grad * unit, axis=0, keepdims=True)
            sum_ref[2:3] = jnp.sum(grad, axis=0, keepdims=True)
            sum_ref[3:4] = jnp.sum(cot_own, axis=0, keepdims=True)
            sum_ref[4:8] = jnp.zeros((4, D), F32)
            swap.wait()
            g_ref[...] = dot_nt(br_ref[...], wo_ref[...]).astype(BF16)
            columns = br_ref[:, pl.ds(pl.multiple_of(member * width, width), width)]
            go_ref[0, member] = dot_tn(ctx_ref[...], columns).astype(BF16).reshape(2, 2, 2, share, width)
            go_ref[0, 1 - member] = dot_tn(other_ref[...], columns).astype(BF16).reshape(2, 2, 2, share, width)
            for kind in range(6, 9):
                sums.send(kind, 0)

        output_swap = (mine_ref.at[pl.ds(own // 2, own // 2)], theirs_ref, swap_sem.at[0, 2], swap_sem.at[1, 2], X)

        @pl.when(now == 11)
        def _():
            remote(*output_swap).start()

        at(1, 0, 0, 1, 5)
        at(4, 0, 3, 4)
        at(5, 0, 7, 2)
        at(6, 1, 5)
        at(6, 0, 8)
        at(7, 0, 6)
        at(8, 1, 0, 1)
        at(8, 0, 10, 11, 9)
        at(9, 1, 2)
        at(10, 1, 3, 4, 6, 7)
        at(11, 2, 5)
        at(11, 1, 8)
        at(12, 1, 9)
        at(12, 2, 0)
        at(12, 1, 11)
        at(12, 2, 7, 1)
        at(13, 1, 10)
        at(13, 2, 8)
        at(15, 2, 2)

        slab_cols = pl.ds(pl.multiple_of(pair * LANES, LANES), LANES)

        @pl.when(step == 0)
        def _():
            lane = lax.broadcasted_iota(jnp.int32, (length, LANES), 1)
            low_half = lane < HD
            grads = g_ref[:, slab_cols]
            prod = grads.astype(F32) * ctx_ref[:, slab_cols].astype(F32)
            for parity in range(2):
                mine = low_half if parity == 0 else jnp.logical_not(low_half)
                lead = HD if parity == 0 else 0
                delta = -jnp.sum(jnp.where(mine, prod, 0.0), axis=-1, keepdims=True)
                hi, mid, low = three_parts(delta)
                rows = jnp.where(mine, grads, jnp.zeros_like(grads))
                rows = jnp.where(lane == lead, hi, rows)
                rows = jnp.where(lane == lead + 1, mid, rows)
                ga_ref[parity] = jnp.where(lane == lead + 2, low, rows)
            ga_ref[2] = grads
            acc_ref[...] = jnp.zeros_like(acc_ref)

        lane = lax.broadcasted_iota(jnp.int32, (tile, LANES), 1)
        low_half = lane < HD
        keys = k_ref[...]
        values = v_ref[...]
        feats = fk_ref[0]
        keys_t = turned(keys)
        dks, dvs = [], []
        for parity in range(2):
            lead = HD if parity == 0 else 0
            mine = low_half if parity == 0 else jnp.logical_not(low_half)
            key_rows = jnp.where(mine, keys, feats)
            ones = jnp.where((lane >= lead) & (lane < lead + 3), 1.0, 0.0).astype(BF16)
            value_rows = jnp.where(mine, values, ones)
            probs = jnp.exp(dot_nt(key_rows, qa_ref[parity]))
            diff = dot_nt(value_rows, ga_ref[parity])
            score_grad = (probs * diff).astype(BF16)
            dvs.append(dot_nn(probs.astype(BF16), ga_ref[2]))
            dks.append(dot_nn(score_grad, qa_ref[parity]))
            side = keys_t[parity * HD : (parity + 1) * HD]
            acc_ref[parity * HD : (parity + 1) * HD] += dot_nn(side, score_grad)
        place = pl.ds(pl.multiple_of(step * tile, tile), tile)
        slab_ref[place, LANES : 2 * LANES] = jnp.where(low_half, dks[0], dks[1]).astype(BF16)
        slab_ref[place, 2 * LANES :] = jnp.where(low_half, dvs[0], dvs[1]).astype(BF16)

        def new_copies(kind, late):
            bit = (X, Y, Z_LOW)[kind]
            whole = gq_ref.at[early + late, kind]
            return (
                pltpu.make_async_copy(
                    whole.at[(ALL,) * bit + (sums.bits[bit],)], keep_new[kind].at[late], new_keep.at[kind, late]
                ),
                remote(
                    whole.at[(ALL,) * bit + (1 - sums.bits[bit],)],
                    got_new[kind].at[late],
                    new_send.at[kind, late],
                    new_recv.at[kind, late],
                    bit,
                ),
            )

        @pl.when(step == tiles - 1)
        def _():
            slab_ref[:, :LANES] = (acc_ref[...].T * HD ** (-0.5)).astype(BF16)
            slabs = slab_ref[...]
            made = dot_nn(nt_ref[...], slabs).astype(BF16)
            for kind in range(3):
                gq_ref[pair, kind] = made[:, kind * LANES : (kind + 1) * LANES].reshape(
                    2, 2, 2, 2, share, LANES
                )
            for one_pair in range(pairs):

                @pl.when(pair == one_pair)
                def _(one_pair=one_pair):
                    for kind in range(3):
                        if one_pair < early:
                            sums.send(9 + 3 * one_pair + kind, 0)
                        else:
                            for one in new_copies(kind, one_pair - early):
                                one.start()

            qb_ref[...] = jnp.sum(slabs[:, :LANES].astype(F32), axis=0, keepdims=True)
            vb_ref[...] = jnp.sum(slabs[:, 2 * LANES :].astype(F32), axis=0, keepdims=True)

        dn_swap = (dn_send, dn_got, swap_sem.at[0, 1], swap_sem.at[1, 1], MEMBER)

        @pl.when(step == tiles - 1)
        def _():
            weights = jnp.concatenate([wq_ref[...], wk_ref[...], wv_ref[...]], axis=1)
            for rows in (slice(own, length), slice(0, own)):
                grown = dot_nt(slab_ref[rows], weights)

                @pl.when(pair == 0)
                def _(rows=rows, grown=grown):
                    dn_acc[rows] = grown

                @pl.when((pair > 0) & (pair < pairs - 1))
                def _(rows=rows, grown=grown):
                    dn_acc[rows] += grown

                @pl.when(pair == pairs - 1)
                def _(rows=rows, grown=grown):
                    total = dn_acc[rows] + grown
                    if rows.start:
                        dn_send[...] = total.astype(BF16)
                        remote(*dn_swap).start()
                    else:
                        dn_ref[...] = total

        @pl.when(now == pairs * tiles - 1)
        def _():
            do(11, 2)
            do(6, 2)
            do(3, 2)
            do(9, 2)
            do(4, 2)
            do(7, 3)
            do(10, 2)
            do(8, 3)
            do(11, 3)
            do(6, 3)
            do(9, 3)
            do(10, 3)
            for late in range(pairs - early):
                for kind in range(3):
                    for one in new_copies(kind, late):
                        one.wait()
            sums.finish()
            remote(*dn_swap).wait()
            remote(*output_swap).wait()

    part = pl.BlockSpec((tile, LANES), lambda p, t: (t, p))
    bias_part = pl.BlockSpec((1, LANES), lambda p, t: (0, p))

    def columns(which):
        return pl.BlockSpec(
            (D, LANES), lambda p, t: (0, (2 * which + lax.axis_index("member")) * pairs + p)
        )

    slots = []
    for shape in shapes:
        slots += slot_shapes(shape[0], 3, shape[4:])
    for _, size in OUT_CUTS:
        slots += slot_shapes(1, 4, (share, size))
    for _ in range(3 * early):
        slots += slot_shapes(1, 4, (share, LANES))
    new = [jax.ShapeDtypeStruct((pairs - early, 2, 2, 2, share, LANES), BF16)] * 3
    own_f32 = jax.ShapeDtypeStruct((own, D), F32)
    results = pl.pallas_call(
        body,
        grid=(pairs, tiles),
        out_shape=[
            own_f32,
            own_f32,
            jax.ShapeDtypeStruct((8, D), F32),
            jax.ShapeDtypeStruct((1, width), F32),
            jax.ShapeDtypeStruct((1, width), F32),
            jax.ShapeDtypeStruct((share, 4 * chunk + width + 3 * early * LANES), F32),
            jax.ShapeDtypeStruct((LANES, D), F32),
            jax.ShapeDtypeStruct((own, D), BF16),
            jax.ShapeDtypeStruct((own // 2, D), BF16),
        ]
        + new
        + new,
        in_specs=[
            pl.BlockSpec((2, length, LANES), lambda p, t: (p, 0, 0)),
            part,
            part,
            pl.BlockSpec((1, tile, LANES), lambda p, t: (p, t, 0)),
            in_vmem(),
            in_vmem(),
            in_vmem(),
            in_vmem(),
            in_vmem(),
            pl.BlockSpec((own, D), lambda p, t: (0, 0)),
            in_vmem(),
            pl.BlockSpec((width, D), lambda p, t: (lax.axis_index("member"), 0)),
            in_vmem(),
            columns(0),
            columns(1),
            columns(2),
        ]
        + [anywhere()] * 13,
        out_specs=[in_vmem(), in_vmem(), in_vmem(), bias_part, bias_part]
        + [in_vmem()] * 2
        + [anywhere()] * 8,
        scratch_shapes=[
            pltpu.VMEM((3, length, LANES), BF16),
            pltpu.VMEM((LANES, length), F32),
            pltpu.VMEM((length, 3 * LANES), BF16),
            pltpu.VMEM((length, D), F32),
            pltpu.VMEM((own, D), BF16),
            pltpu.VMEM((pairs, 3, 2, 2, 2, 2, share, LANES), BF16),
            pltpu.VMEM((length, D), BF16),
            pltpu.VMEM((length, width), BF16),
            pltpu.VMEM((1, 2, 2, 2, 2, share, width), BF16),
        ]
        + [pltpu.VMEM(shape, BF16) for shape in shapes]
        + [pltpu.VMEM(shape, BF16) for shape in shapes]
        + slots
        + [
            pltpu.SemaphoreType.DMA((count, 4)),
            pltpu.SemaphoreType.DMA((count, 4)),
            pltpu.SemaphoreType.DMA((2, 6)),
            pltpu.SemaphoreType.DMA((3, pairs - early)),
            pltpu.SemaphoreType.DMA((3, pairs - early)),
            pltpu.SemaphoreType.DMA((3, pairs - early)),
            pltpu.SemaphoreType.DMA((2, 3)),
        ],
        compiler_params=params(3),
        name="attend_backward",
    )(
        rows_aug, k, v, feat_k, ctx, ctx_other, mid, n2_grad, n2_grad_got, cot, vectors, w_out, normed_t,
        w_qkv, w_qkv, w_qkv, output_own, *kept, *got,
    )
    return results[:9], results[9:12], results[12:]


def in_turn(first, second):
    count = first.shape[0]
    row = lax.broadcasted_iota(jnp.int32, (2 * count, count), 0)
    column = lax.broadcasted_iota(jnp.int32, (2 * count, count), 1)
    even = jnp.where(row == 2 * column, 1.0, 0.0).astype(BF16)
    odd = jnp.where(row == 2 * column + 1, 1.0, 0.0).astype(BF16)
    return (dot_nn(even, first) + dot_nn(odd, second)).astype(BF16)


def finish(
    tokens, mid_grad, normed_grad, normed_grad_got, vectors, sums_in, in_bias_grad, q_sum, v_sum, ready, out_mine,
    out_other, kept, got,
):
    own = mid_grad.shape[0]
    rows = own // 2
    width = q_sum.shape[1]
    late, share = kept[0].shape[0], kept[0].shape[-2]
    per = share // 2
    size = late * LANES

    def body(*refs):
        vec_ref, sum_ref, inb_ref, qb_ref, vb_ref = refs[:5]
        keep, first = refs[5:8], refs[8:11]
        big_in = refs[11:18]
        ig_ref, ig_got, ready_got, qkv_ref, vec_sum, out_ref = refs[18:24]
        big = refs[24:31]
        ig_send, source, flat, shares, near_got, far_got = refs[31:37]
        begin, slots = refs[37:40], refs[40:46]
        send_sem, recv_sem, swap_sem, share_sem, near_sem, far_sem, load_sem = refs[46:]
        tok_ref, mg_ref, dn_ref, dn_got, mine_ref, other_ref, ready_ref = big
        member = lax.axis_index("member")

        def load(which):
            return pltpu.make_async_copy(big_in[which], big[which], load_sem.at[which])

        for which in range(7):
            load(which).start()
        barrier = pltpu.get_barrier_semaphore()
        for mask in range(1, 32):
            pl.semaphore_signal(barrier, inc=1, device_id=place_across(mask), device_id_type=MESH_IDS)
        pl.semaphore_wait(barrier, 31)
        sums = Sums(send_sem, recv_sem)
        for kind in range(3):
            dims = tuple(b for b in CHIP if b != ORDERS[kind][0])
            sums.add(kind, begin[kind], dims, ORDERS[kind][1:3], slots[2 * kind : 2 * kind + 2])
            begin[kind][...] = keep[kind][...] + first[kind][...]
            sums.send(kind, 0)
        theirs = pl.ds(pl.multiple_of((1 - member) * per, per), per)
        ours = pl.ds(pl.multiple_of(member * per, per), per)
        top, rest = pl.ds(0, rows // 2), pl.ds(rows // 2, rows // 2)
        swaps = [
            remote(ready_ref.at[theirs], ready_got, swap_sem.at[0, 0], swap_sem.at[1, 0], MEMBER),
            remote(ig_send.at[top], ig_got.at[top], swap_sem.at[0, 1], swap_sem.at[1, 1], X),
            remote(ig_send.at[rest], ig_got.at[rest], swap_sem.at[0, 2], swap_sem.at[1, 2], X),
        ]

        for which in range(4):
            load(which).wait()
        gain_sum, bias_sum = 0.0, 0.0
        for part in (slice(rows, rows + rows // 2), slice(rows + rows // 2, own), slice(0, rows)):
            unit, scale = normalise(tok_ref[part].astype(F32))
            grad = dn_ref[part] + dn_got[part].astype(F32)
            input_grad = mg_ref[part] + normalise_back(unit, scale, grad * vec_ref[4:5])
            if part.start == rows:
                ig_send[top] = input_grad.astype(BF16)
                swaps[1].start()
            elif part.start:
                ig_send[rest] = input_grad.astype(BF16)
            else:
                ig_ref[...] = input_grad
            gain_sum = gain_sum + jnp.sum(grad * unit, axis=0, keepdims=True)
            bias_sum = bias_sum + jnp.sum(grad, axis=0, keepdims=True)
        flat[0:1] = gain_sum
        flat[1:2] = bias_sum
        flat[2:6] = sum_ref[0:4]
        blank = jnp.zeros((1, width), F32)
        for row, ref in ((6, qb_ref), (7, vb_ref)):
            value = ref[...]
            flat[row : row + 1, :width] = jnp.where(member == 0, value, blank)
            flat[row : row + 1, width:] = jnp.where(member == 1, value, blank)
        flat[8:] = jnp.zeros((LANES - 8, D), F32)
        source[:, :, :, :, :, :per] = flat[...].T.astype(BF16).reshape(2, 2, 2, 2, 2, per, LANES)
        source[:, :, :, :, :, per:] = jnp.zeros((2, 2, 2, 2, 2, 16, LANES), BF16)
        for z_high, z_low, y, x in np.ndindex(2, 2, 2, 2):
            unit = (((z_low * 2 + y) * 2 + z_high) * 2 + x) * LANES
            source[z_high, z_low, y, x, member, per:] = jnp.broadcast_to(
                inb_ref[:, unit : unit + LANES], (16, LANES)
            ).astype(BF16)

        def straight(mask):
            place = tuple(
                1 - bit if mask & flag else bit for bit, flag in zip(sums.bits, (16, 8, 4, 2, 1))
            )
            return pltpu.make_async_remote_copy(
                src_ref=source.at[place],
                dst_ref=shares.at[mask],
                send_sem=share_sem.at[0, mask],
                recv_sem=share_sem.at[1, mask],
                device_id=place_across(mask),
                device_id_type=MESH_IDS,
            )

        for mask in range(1, 32):
            straight(mask).start()

        def near(kind):
            return remote(
                slots[2 * kind + 1].at[:, sums.bits[0], theirs],
                near_got.at[kind],
                near_sem.at[0, kind],
                near_sem.at[1, kind],
                MEMBER,
            )

        def far(kind, flipped):
            return pltpu.make_async_remote_copy(
                src_ref=slots[2 * kind + 1].at[:, 1 - sums.bits[0], theirs if flipped else ours],
                dst_ref=far_got.at[flipped, kind],
                send_sem=far_sem.at[0, 2 * kind + flipped],
                recv_sem=far_sem.at[1, 2 * kind + flipped],
                device_id=place_across(16 + flipped),
                device_id_type=MESH_IDS,
            )

        for depth in range(2):
            for kind in (1, 0, 2):
                sums.copy(kind, depth).wait_recv()
                slots[2 * kind + depth][...] = sums.side(kind, depth, False)[...] + slots[2 * kind + depth][...]
                if depth == 0:
                    sums.send(kind, 1)
                else:
                    far(kind, 1).start()
                    far(kind, 0).start()
                    near(kind).start()
                if depth == 0 and kind == 1:
                    swaps[2].start()
                    for which in range(4, 7):
                        load(which).wait()
                    swaps[0].start()
                    mine, other = mine_ref[...], other_ref[...]
                    here = lax.axis_index("half") == 0
                    out_ref[...] = in_turn(jnp.where(here, mine, other), jnp.where(here, other, mine))
        total = source[sums.bits].astype(F32)
        for mask in range(1, 32):
            straight(mask).wait_recv()
            total = total + shares[mask].astype(F32)
        vec_sum[...] = total
        for kind in (1, 0, 2):
            far(kind, 0).wait_recv()
            ours_sum = slots[2 * kind + 1][:, sums.bits[0], ours].astype(F32) + far_got[0, kind].astype(F32)
            near(kind).wait_recv()
            far(kind, 1).wait_recv()
            theirs_sum = near_got[kind].astype(F32) + far_got[1, kind].astype(F32)
            for pair in range(late):
                place = kind * size + pair * LANES
                qkv_ref[member, :, place : place + LANES] = ours_sum[pair]
                qkv_ref[1 - member, :, place : place + LANES] = theirs_sum[pair]
        sums.finish()
        for kind in range(3):
            near(kind).wait_send()
            far(kind, 0).wait_send()
            far(kind, 1).wait_send()
        for mask in range(1, 32):
            straight(mask).wait_send()
        for one in swaps:
            one.wait()

    slots = []
    for _ in range(3):
        slots += slot_shapes(late, 3, (share, LANES))[:2]
    return pl.pallas_call(
        body,
        out_shape=(
            jax.ShapeDtypeStruct((rows, D), F32),
            jax.ShapeDtypeStruct((rows, D), BF16),
            jax.ShapeDtypeStruct((per, ready.shape[1]), F32),
            jax.ShapeDtypeStruct((2, per, 3 * size), F32),
            jax.ShapeDtypeStruct((per + 16, LANES), F32),
            jax.ShapeDtypeStruct((own, D), BF16),
        ),
        grid=(1,),
        in_specs=[in_vmem()] * 11 + [anywhere()] * 7,
        out_specs=(in_vmem(), anywhere(), anywhere(), in_vmem(), in_vmem(), in_vmem()),
        scratch_shapes=[
            pltpu.VMEM((own, D), BF16),
            pltpu.VMEM((own, D), F32),
            pltpu.VMEM((own, D), F32),
            pltpu.VMEM((own, D), BF16),
            pltpu.VMEM((rows, D), BF16),
            pltpu.VMEM((rows, D), BF16),
            pltpu.VMEM(ready.shape, F32),
            pltpu.VMEM((rows, D), BF16),
            pltpu.VMEM((2, 2, 2, 2, 2, per + 16, LANES), BF16),
            pltpu.VMEM((LANES, D), F32),
            pltpu.VMEM((32, per + 16, LANES), BF16),
            pltpu.VMEM((3, late, per, LANES), BF16),
            pltpu.VMEM((2, 3, late, per, LANES), BF16),
        ]
        + [pltpu.VMEM(kept[0].shape, BF16)] * 3
        + slots
        + [
            pltpu.SemaphoreType.DMA((3, 2)),
            pltpu.SemaphoreType.DMA((3, 2)),
            pltpu.SemaphoreType.DMA((2, 3)),
            pltpu.SemaphoreType.DMA((2, 32)),
            pltpu.SemaphoreType.DMA((2, 3)),
            pltpu.SemaphoreType.DMA((2, 6)),
            pltpu.SemaphoreType.DMA((7,)),
        ],
        compiler_params=params(2),
        name="finish",
    )(
        vectors, sums_in, in_bias_grad, q_sum, v_sum, *kept, *got, tokens, mid_grad, normed_grad, normed_grad_got,
        out_mine, out_other, ready,
    )


def per_device_pair(
    tokens,
    ln1_gain,
    ln1_bias,
    w_qkv,
    q_bias,
    v_bias,
    w_out,
    out_bias,
    ln2_gain,
    ln2_bias,
    w_in,
    in_bias,
    w_down,
    down_bias,
    cotangent,
    segment_ids,
    random_blocks,
    global_blocks,
):
    rows = tokens.shape[0]
    own = 2 * rows
    blocks = segment_ids.shape[0] // BLK
    half = lax.axis_index("half")
    member = lax.axis_index("member")
    mine_d = D // 2
    heads = HEADS // 2
    chips = lax.axis_size("batch") * 2

    def both_sequences(kept, other):
        return jnp.where(
            half == 0, jnp.stack([kept, other], axis=1), jnp.stack([other, kept], axis=1)
        )

    seq_random = lax.dynamic_index_in_dim(random_blocks, half, 1, keepdims=False)
    seq_random = lax.dynamic_slice_in_dim(seq_random, member * heads, heads, 1)
    pair_random = seq_random.reshape(blocks, heads // 2, 2 * RAND).transpose(1, 0, 2).astype(F32)
    own_tokens, normed_t, queries, keys, values, feat_q, feat_k, vectors, in_shift = begin(
        tokens.reshape(own, D),
        (out_bias, ln2_gain, ln2_bias, down_bias, ln1_gain, ln1_bias, q_bias, v_bias, in_bias),
        w_qkv,
        segment_ids.T,
        pair_random,
        global_blocks,
    )
    context, rows_aug, context_other, cot = attend_forward(
        queries, keys, values, feat_q, feat_k, cotangent.reshape(own, D)
    )
    (output_own, n2_grad, n2_grad_got, mid_stream, in_bias_grad), kept_parts, got_parts = feed_forward(
        context,
        context_other,
        own_tokens,
        w_out,
        vectors,
        cot,
        w_in,
        in_shift,
        w_down,
    )

    (
        (
            normed_grad,
            mid_grad,
            sums_in,
            q_sum,
            v_sum,
            ready,
            summed_down,
            normed_grad_got,
            output_other,
        ),
        kept_qkv,
        got_qkv,
    ) = attend_backward(
        rows_aug,
        keys,
        values,
        feat_k,
        context,
        context_other,
        mid_stream,
        n2_grad,
        n2_grad_got,
        cot,
        vectors,
        w_out,
        normed_t,
        w_qkv,
        output_own,
        kept_parts,
        got_parts,
    )
    input_kept, input_other, ready_got, qkv_late, vector_rows, output = finish(
        own_tokens,
        mid_grad,
        normed_grad,
        normed_grad_got,
        vectors,
        sums_in,
        in_bias_grad,
        q_sum,
        v_sum,
        ready,
        output_own[:rows],
        output_other,
        kept_qkv,
        got_qkv,
    )
    input_grad = both_sequences(input_kept, input_other.astype(F32))

    per = ready.shape[0] // 2
    mine_rows = lax.dynamic_slice_in_dim(ready, member * per, per, 0)
    left = jnp.where(member == 0, mine_rows, ready_got)
    right = jnp.where(member == 0, ready_got, mine_rows)

    start_out = w_in.shape[1] // 2
    start_early = start_out + mine_d
    early = (ready.shape[1] - start_early) // 3
    late = mine_d - early
    pieces = []
    for part in range(3):
        for x, later in ((left, qkv_late[0]), (right, qkv_late[1])):
            pieces.append(x[:, start_early + part * early : start_early + (part + 1) * early])
            pieces.append(later[:, part * late : (part + 1) * late])
    w_qkv_grad = jnp.concatenate(pieces, axis=1)
    w_out_grad = jnp.concatenate([x[:, start_out : start_out + mine_d] for x in (left, right)], axis=1)
    w_in_grad = jnp.concatenate(
        [x[:, j * LANES : (j + 1) * LANES] for j in range(chips) for x in (left, right)], axis=1
    )
    in_bias_out = vector_rows[per]
    vec = [vector_rows[:per, i] for i in range(8)]
    return (
        output.reshape(rows, 2, D),
        input_grad,
        vec[0],
        vec[1],
        w_qkv_grad,
        vec[6],
        vec[7],
        w_out_grad,
        vec[2],
        vec[3],
        vec[4],
        w_in_grad,
        in_bias_out,
        summed_down,
        vec[5],
    )


def solution(mesh):
    def program(*args):
        sequences = args[0].shape[1] // mesh.shape["batch"]
        seq = mesh.shape["seq"]
        fast = sequences == 2 and seq == 4 and mesh.shape["batch"] == 8
        if fast:
            use = jax.sharding.Mesh(
                mesh.devices.reshape(mesh.shape["batch"], 2, 2), ("batch", "half", "member")
            )
            seq_axes, all_axes, run = ("half", "member"), ("batch", "half", "member"), per_device_pair
        else:
            use, seq_axes, all_axes, run = mesh, "seq", ("batch", "seq"), per_device
        rows = P(seq_axes, "batch", None)
        in_specs = (rows,) + (P(),) * 13 + (
            rows,
            P(None, "batch"),
            P(None, "batch", None, None),
            P(None, "batch"),
        )
        vector, matrix = P(all_axes), P(all_axes, None)
        out_specs = (
            rows,
            rows,
            vector,
            vector,
            matrix,
            vector,
            vector,
            matrix,
            vector,
            vector,
            vector,
            matrix,
            vector,
            matrix,
            vector,
        )
        return jax.shard_map(
            run, mesh=use, in_specs=in_specs, out_specs=out_specs, check_vma=False
        )(*args)

    return program
```

```python
import jax
import jax.numpy as jnp
import numpy as np
from jax import lax
from jax.experimental import pallas as pl
from jax.experimental.pallas import tpu as pltpu
from jax.sharding import PartitionSpec as P

D = 1024
HEADS = 16
HD = 64
BLK = 64
RAND = 3
GLOB = 2


eps = 1e-05


def padded(x, sides, width):
    for axis, dim in sides:
        size, length = (lax.axis_size(axis), x.shape[dim])
        up = [(i, (i + 1) % size) for i in range(size - 1)]
        down = [(j, i) for i, j in up]
        last = lax.slice_in_dim(x, length - width, length, axis=dim)
        initial = lax.slice_in_dim(x, 0, width, axis=dim)
        before = lax.ppermute(last, axis, up)
        after = lax.ppermute(initial, axis, down)
        x = jnp.concatenate([before, x, after], axis=dim)
    return x


def layer_norm(values, gain_vec, shift_vec):
    row_mean = jnp.mean(values, axis=-1, keepdims=True)
    centred = values - row_mean
    spread = jnp.mean(centred * centred, axis=-1, keepdims=True)
    return centred * lax.rsqrt(spread + eps) * gain_vec + shift_vec


def gelu_tanh(values):
    return jax.nn.gelu(values, approximate=True)


def window_stack(extended, query_blocks):
    return jnp.stack(
        [extended[0:query_blocks], extended[1 : query_blocks + 1], extended[2 : query_blocks + 2]],
        axis=1,
    )


def pick_blocks(shard_rows, random_local, global_blocks):
    block_total = shard_rows.shape[0] // BLK
    seq_count = shard_rows.shape[1]
    numbers = jnp.arange(block_total, dtype=jnp.int32)
    random_hits = (random_local[..., None] == numbers).astype(jnp.bfloat16)
    global_hits = (global_blocks[..., None] == numbers).astype(jnp.bfloat16)
    blocks = shard_rows.reshape(block_total, BLK, seq_count, 2, HEADS, HD)
    picked_random = jnp.einsum(
        "ishjb,busxhd->ishjuxd", random_hits, blocks, preferred_element_type=jnp.float32
    )
    picked_global = jnp.einsum(
        "gsb,busc->gusc",
        global_hits,
        shard_rows.reshape(block_total, BLK, seq_count, 2 * D),
        preferred_element_type=jnp.float32,
    )
    return (picked_random, picked_global)


def key_products(left_side, window_kv, far_random, far_global, which_half):
    near_part = jnp.einsum(
        "itshd,iwushd->ishtwu",
        left_side,
        window_kv[:, :, :, :, which_half],
        preferred_element_type=jnp.float32,
    )
    far_part = jnp.einsum(
        "itshd,ishjud->ishtju",
        left_side,
        far_random[:, :, :, :, :, which_half],
        preferred_element_type=jnp.float32,
    )
    global_part = jnp.einsum(
        "itshd,gushd->ishtgu",
        left_side,
        far_global[:, :, :, which_half],
        preferred_element_type=jnp.float32,
    )
    lead_shape = near_part.shape[:4]
    return jnp.concatenate(
        [
            near_part.reshape(lead_shape + (-1,)),
            far_part.reshape(lead_shape + (-1,)),
            global_part.reshape(lead_shape + (-1,)),
        ],
        axis=-1,
    )


def split_slots(weights):
    lead_shape = weights.shape[:4]
    near_cut = 3 * BLK
    far_cut = (3 + RAND) * BLK
    near_part = weights[..., :near_cut].reshape(lead_shape + (3, BLK))
    far_part = weights[..., near_cut:far_cut].reshape(lead_shape + (RAND, BLK))
    global_part = weights[..., far_cut:].reshape(lead_shape + (GLOB, BLK))
    return (near_part, far_part, global_part)


def key_mix(weights, window_kv, far_random, far_global, which_half):
    near_part, far_part, global_part = split_slots(weights)
    mixed = jnp.einsum(
        "ishtwu,iwushd->itshd",
        near_part,
        window_kv[:, :, :, :, which_half],
        preferred_element_type=jnp.float32,
    )
    mixed = mixed + jnp.einsum(
        "ishtju,ishjud->itshd",
        far_part,
        far_random[:, :, :, :, :, which_half],
        preferred_element_type=jnp.float32,
    )
    mixed = mixed + jnp.einsum(
        "ishtgu,gushd->itshd",
        global_part,
        far_global[:, :, :, which_half],
        preferred_element_type=jnp.float32,
    )
    return mixed


def key_grads(weights, left_side):
    near_part, far_part, global_part = split_slots(weights)
    near_grad = jnp.einsum(
        "ishtwu,itshd->iwushd", near_part, left_side, preferred_element_type=jnp.float32
    )
    far_grad = jnp.einsum(
        "ishtju,itshd->ishjud", far_part, left_side, preferred_element_type=jnp.float32
    )
    global_grad = jnp.einsum(
        "ishtgu,itshd->gushd", global_part, left_side, preferred_element_type=jnp.float32
    )
    return (near_grad, far_grad, global_grad)


def per_device(
    tokens,
    ln1_gain,
    ln1_bias,
    w_qkv,
    q_bias,
    v_bias,
    w_out,
    out_bias,
    ln2_gain,
    ln2_bias,
    w_in,
    in_bias,
    w_down,
    down_bias,
    cotangent,
    segment_ids,
    random_blocks,
    global_blocks,
):
    row_count = tokens.shape[0]
    seq_count = tokens.shape[1]
    query_blocks = row_count // BLK
    seq_length = segment_ids.shape[0]
    device_now = lax.axis_index("seq")
    first_row = device_now * row_count
    score_scale = HD ** (-0.5)
    random_local = lax.dynamic_slice_in_dim(
        random_blocks, device_now * query_blocks, query_blocks, 0
    )
    inputs = tokens.astype(jnp.float32)
    normed_full, first_norm_back = jax.vjp(
        layer_norm, inputs, ln1_gain.astype(jnp.float32), ln1_bias.astype(jnp.float32)
    )
    normed = normed_full.astype(jnp.bfloat16)
    projected = jnp.einsum("rsd,de->rse", normed, w_qkv, preferred_element_type=jnp.float32)
    queries = (projected[:, :, :D] + q_bias.astype(jnp.float32)).astype(jnp.bfloat16)
    value_shift = jnp.concatenate([jnp.zeros((D,), jnp.float32), v_bias.astype(jnp.float32)])
    keyval = (projected[:, :, D:] + value_shift).astype(jnp.bfloat16)
    extended = padded(keyval, (("seq", 0),), BLK)
    window_kv = window_stack(
        extended.reshape(query_blocks + 2, BLK, seq_count, 2, HEADS, HD), query_blocks
    )
    picked = pick_blocks(
        lax.all_gather(keyval, "seq", axis=0, tiled=True), random_local, global_blocks
    )
    far_random = picked[0].astype(jnp.bfloat16)
    far_global = picked[1].astype(jnp.bfloat16).reshape(GLOB, BLK, seq_count, 2, HEADS, HD)
    query_segment = lax.dynamic_slice_in_dim(segment_ids, first_row, row_count, 0)
    query_segment = query_segment.reshape(query_blocks, BLK, seq_count).transpose(0, 2, 1)
    window_spots = first_row - BLK + jnp.arange(row_count + 2 * BLK, dtype=jnp.int32)
    inside_seq = (window_spots >= 0) & (window_spots < seq_length)
    near_segment = jnp.take(segment_ids, jnp.clip(window_spots, 0, seq_length - 1), axis=0)
    near_segment = jnp.where(inside_seq[:, None], near_segment, -1)
    near_segment = window_stack(
        near_segment.reshape(query_blocks + 2, BLK, seq_count), query_blocks
    )
    near_segment = near_segment.transpose(0, 3, 1, 2).reshape(query_blocks, seq_count, 1, 3 * BLK)
    segment_rows = segment_ids.T
    sequence_pick = jnp.arange(seq_count, dtype=jnp.int32)
    offsets = jnp.arange(BLK, dtype=jnp.int32)
    far_segment = segment_rows[
        sequence_pick[None, :, None, None, None], random_local[..., None] * BLK + offsets
    ]
    far_segment = far_segment.reshape(query_blocks, seq_count, HEADS, RAND * BLK)
    global_segment = segment_rows[
        sequence_pick[None, :, None], global_blocks[..., None] * BLK + offsets
    ]
    global_segment = global_segment.transpose(1, 0, 2).reshape(1, seq_count, 1, GLOB * BLK)
    key_segment = jnp.concatenate(
        [
            jnp.broadcast_to(near_segment, (query_blocks, seq_count, HEADS, 3 * BLK)),
            far_segment,
            jnp.broadcast_to(global_segment, (query_blocks, seq_count, HEADS, GLOB * BLK)),
        ],
        axis=-1,
    )
    allowed = key_segment[:, :, :, None, :] == query_segment[:, :, None, :, None]
    query_rows = queries.reshape(query_blocks, BLK, seq_count, HEADS, HD)
    scores = jnp.where(
        allowed, key_products(query_rows, window_kv, far_random, far_global, 0) * score_scale, -1e30
    )
    row_max = jnp.max(scores, axis=-1, keepdims=True)
    log_total = row_max + jnp.log(jnp.sum(jnp.exp(scores - row_max), axis=-1, keepdims=True))
    soft_full = jnp.exp(scores - log_total)
    attn_probs = soft_full.astype(jnp.bfloat16)
    context = (
        key_mix(attn_probs, window_kv, far_random, far_global, 1)
        .reshape(row_count, seq_count, D)
        .astype(jnp.bfloat16)
    )
    mid_stream = (
        inputs
        + jnp.einsum("rsd,de->rse", context, w_out, preferred_element_type=jnp.float32)
        + out_bias.astype(jnp.float32)
    )
    normed2_full, second_norm_back = jax.vjp(
        layer_norm, mid_stream, ln2_gain.astype(jnp.float32), ln2_bias.astype(jnp.float32)
    )
    normed2 = normed2_full.astype(jnp.bfloat16)
    pre_act = jnp.einsum(
        "rsd,df->rsf", normed2, w_in, preferred_element_type=jnp.float32
    ) + in_bias.astype(jnp.float32)
    hidden_full, gelu_back = jax.vjp(gelu_tanh, pre_act)
    hidden = hidden_full.astype(jnp.bfloat16)
    output = (
        mid_stream
        + jnp.einsum("rsf,fd->rsd", hidden, w_down, preferred_element_type=jnp.float32)
        + down_bias.astype(jnp.float32)
    ).astype(jnp.bfloat16)
    grad_out = cotangent.astype(jnp.float32)
    w_down_grad = jnp.einsum("rsf,rsd->fd", hidden, cotangent, preferred_element_type=jnp.float32)
    down_bias_grad = jnp.sum(grad_out, axis=(0, 1))
    pre_grad = gelu_back(
        jnp.einsum("rsd,fd->rsf", cotangent, w_down, preferred_element_type=jnp.float32)
    )[0].astype(jnp.bfloat16)
    w_in_grad = jnp.einsum("rsd,rsf->df", normed2, pre_grad, preferred_element_type=jnp.float32)
    in_bias_grad = jnp.sum(pre_grad.astype(jnp.float32), axis=(0, 1))
    mid_part, ln2_gain_grad, ln2_bias_grad = second_norm_back(
        jnp.einsum("rsf,df->rsd", pre_grad, w_in, preferred_element_type=jnp.float32)
    )
    mid_grad = grad_out + mid_part
    branch_grad = mid_grad.astype(jnp.bfloat16)
    w_out_grad = jnp.einsum("rsd,rse->de", context, branch_grad, preferred_element_type=jnp.float32)
    out_bias_grad = jnp.sum(branch_grad.astype(jnp.float32), axis=(0, 1))
    context_grad = jnp.einsum(
        "rse,de->rsd", branch_grad, w_out, preferred_element_type=jnp.float32
    ).astype(jnp.bfloat16)
    grad_rows = context_grad.reshape(query_blocks, BLK, seq_count, HEADS, HD)
    probs_grad = key_products(grad_rows, window_kv, far_random, far_global, 1)
    score_grad = (
        soft_full * (probs_grad - jnp.sum(soft_full * probs_grad, axis=-1, keepdims=True))
    ).astype(jnp.bfloat16)
    query_grad = (
        (key_mix(score_grad, window_kv, far_random, far_global, 0) * score_scale)
        .reshape(row_count, seq_count, D)
        .astype(jnp.bfloat16)
    )
    near_key, far_key, global_key = key_grads(score_grad, query_rows)
    near_value, far_value, global_value = key_grads(attn_probs, grad_rows)
    near_kv = jnp.stack([near_key * score_scale, near_value], axis=4)
    far_kv = jnp.stack([far_key * score_scale, far_value], axis=5)
    global_kv = jnp.stack([global_key * score_scale, global_value], axis=3).reshape(
        GLOB, BLK, seq_count, 2 * D
    )
    rest_pad = ((0, 0),) * 5
    extended_grad = (
        jnp.pad(near_kv[:, 0], ((0, 2),) + rest_pad)
        + jnp.pad(near_kv[:, 1], ((1, 1),) + rest_pad)
        + jnp.pad(near_kv[:, 2], ((2, 0),) + rest_pad)
    )
    extended_grad = extended_grad.reshape(row_count + 2 * BLK, seq_count, 2 * D)
    rim_grads = jnp.concatenate([extended_grad[:BLK], extended_grad[row_count + BLK :]], axis=0)
    returned = padded(rim_grads.astype(jnp.bfloat16), (("seq", 0),), BLK).astype(rim_grads.dtype)
    near_total = extended_grad[BLK : row_count + BLK]
    near_total = (
        near_total.at[:BLK].add(returned[:BLK]).at[row_count - BLK :].add(returned[3 * BLK :])
    )
    block_total = row_count * lax.axis_size("seq") // BLK
    numbers = jnp.arange(block_total, dtype=jnp.int32)
    random_hits = (random_local[..., None] == numbers).astype(jnp.float32)
    global_rows_hit = (global_blocks[..., None] == numbers).astype(jnp.float32)

    def far_sum(one_sequence):
        hits, kv, global_rows, global_sum = one_sequence
        random_term = jnp.einsum(
            "ihjb,ihjuxd->buxhd", hits, kv, precision=lax.Precision.HIGHEST
        )
        global_term = jnp.einsum(
            "gb,guc->buc", global_rows, global_sum, precision=lax.Precision.HIGHEST
        )
        flat = (block_total * BLK, 2 * D)
        return (random_term.reshape(flat) + global_term.reshape(flat)).astype(jnp.bfloat16)

    far_parts = lax.map(
        far_sum,
        (
            jnp.moveaxis(random_hits, 1, 0),
            jnp.moveaxis(far_kv, 1, 0),
            jnp.moveaxis(global_rows_hit, 1, 0),
            jnp.moveaxis(global_kv, 2, 0),
        ),
    )
    far_total = lax.psum_scatter(far_parts, "seq", scatter_dimension=1, tiled=True)
    far_total = jnp.moveaxis(far_total, 0, 1).astype(jnp.float32)
    keyval_grad = (near_total + far_total).astype(jnp.bfloat16)
    qkv_grad = jnp.concatenate([query_grad, keyval_grad], axis=-1)
    q_bias_grad = jnp.sum(query_grad.astype(jnp.float32), axis=(0, 1))
    v_bias_grad = jnp.sum(keyval_grad[:, :, D:].astype(jnp.float32), axis=(0, 1))
    w_qkv_grad = jnp.einsum("rsd,rse->de", normed, qkv_grad, preferred_element_type=jnp.float32)
    input_part, ln1_gain_grad, ln1_bias_grad = first_norm_back(
        jnp.einsum("rse,de->rsd", qkv_grad, w_qkv, preferred_element_type=jnp.float32)
    )
    input_grad = mid_grad + input_part
    summed = (
        lax.psum_scatter(ln1_gain_grad, ("batch", "seq"), scatter_dimension=0, tiled=True),
        lax.psum_scatter(ln1_bias_grad, ("batch", "seq"), scatter_dimension=0, tiled=True),
        lax.psum_scatter(w_qkv_grad, ("batch", "seq"), scatter_dimension=0, tiled=True),
        lax.psum_scatter(q_bias_grad, ("batch", "seq"), scatter_dimension=0, tiled=True),
        lax.psum_scatter(v_bias_grad, ("batch", "seq"), scatter_dimension=0, tiled=True),
        lax.psum_scatter(w_out_grad, ("batch", "seq"), scatter_dimension=0, tiled=True),
        lax.psum_scatter(out_bias_grad, ("batch", "seq"), scatter_dimension=0, tiled=True),
        lax.psum_scatter(ln2_gain_grad, ("batch", "seq"), scatter_dimension=0, tiled=True),
        lax.psum_scatter(ln2_bias_grad, ("batch", "seq"), scatter_dimension=0, tiled=True),
        lax.psum_scatter(w_in_grad, ("batch", "seq"), scatter_dimension=0, tiled=True),
        lax.psum_scatter(in_bias_grad, ("batch", "seq"), scatter_dimension=0, tiled=True),
        lax.psum_scatter(w_down_grad, ("batch", "seq"), scatter_dimension=0, tiled=True),
        lax.psum_scatter(down_bias_grad, ("batch", "seq"), scatter_dimension=0, tiled=True),
    )
    return (
        output,
        input_grad,
        summed[0],
        summed[1],
        summed[2],
        summed[3],
        summed[4],
        summed[5],
        summed[6],
        summed[7],
        summed[8],
        summed[9],
        summed[10],
        summed[11],
        summed[12],
    )


NEG = -1e30
LANES = 128
SEG_VALUES = 4
MESH_IDS = pl.DeviceIdType.MESH
VMEM_BYTES = 60 * 1024 * 1024
F32 = jnp.float32
BF16 = jnp.bfloat16
ALL = slice(None)
Z_HIGH, Z_LOW, Y, X, MEMBER = range(5)
CHIP = (Z_HIGH, Z_LOW, Y, X)


def three_parts(x):
    hi = x.astype(BF16)
    rest = x - hi.astype(F32)
    mid = rest.astype(BF16)
    low = (rest - mid.astype(F32)).astype(BF16)
    return hi, mid, low


def dot_nt(a, b):
    return lax.dot_general(a, b, (((1,), (1,)), ((), ())), preferred_element_type=F32)


def dot_nn(a, b):
    return lax.dot_general(a, b, (((1,), (0,)), ((), ())), preferred_element_type=F32)


def dot_tn(a, b):
    return lax.dot_general(a, b, (((0,), (0,)), ((), ())), preferred_element_type=F32)


def turned(x):
    return x.astype(F32).T.astype(BF16)


def normalise(values):
    mean = jnp.mean(values, axis=-1, keepdims=True)
    centred = values - mean
    scale = lax.rsqrt(jnp.mean(centred * centred, axis=-1, keepdims=True) + eps)
    return centred * scale, scale


def normalise_back(unit, scale, grad):
    first = jnp.mean(grad, axis=-1, keepdims=True)
    second = jnp.mean(grad * unit, axis=-1, keepdims=True)
    return (grad - first - unit * second) * scale


def my_bits():
    batch = lax.axis_index("batch")
    return (
        lax.div(batch, 4),
        lax.rem(lax.div(batch, 2), 2),
        lax.rem(batch, 2),
        lax.axis_index("half"),
        lax.axis_index("member"),
    )


def device_across(bit):
    batch = lax.axis_index("batch")
    half = lax.axis_index("half")
    member = lax.axis_index("member")
    if bit == MEMBER:
        return (batch, half, 1 - member)
    if bit == X:
        return (batch, 1 - half, member)
    stride = (4, 2, 1)[bit]
    return (batch + stride * (1 - 2 * my_bits()[bit]), half, member)


def place_across(mask):
    z_high, z_low, y, x, member = (
        1 - bit if mask & flag else bit for bit, flag in zip(my_bits(), (16, 8, 4, 2, 1))
    )
    return (4 * z_high + 2 * z_low + y, x, member)


def remote(src, dst, send, recv, bit):
    return pltpu.make_async_remote_copy(
        src_ref=src,
        dst_ref=dst,
        send_sem=send,
        recv_sem=recv,
        device_id=device_across(bit),
        device_id_type=MESH_IDS,
    )


def greet(bits):
    barrier = pltpu.get_barrier_semaphore()
    for bit in bits:
        pl.semaphore_signal(barrier, inc=1, device_id=device_across(bit), device_id_type=MESH_IDS)
    pl.semaphore_wait(barrier, len(bits))


class Sums:
    def __init__(self, send_sem, recv_sem):
        self.bits = my_bits()
        self.send_sem, self.recv_sem = send_sem, recv_sem
        self.pieces = {}

    def add(self, number, source, dims, order, slots, cut=()):
        self.pieces[number] = (source, dims, order, slots, cut)

    def side(self, number, depth, across):
        source, dims, order, slots, cut = self.pieces[number]
        bit = order[depth]
        value = 1 - self.bits[bit] if across else self.bits[bit]
        left = [b for b in dims if b not in order[:depth]]
        spot = left.index(bit)
        index = (ALL,) * (1 + spot) + (value,)
        if depth:
            return slots[depth - 1].at[index]
        return source.at[index + (ALL,) * (len(left) - 1 - spot) + cut]

    def copy(self, number, depth):
        _, _, order, slots, _ = self.pieces[number]
        return remote(
            self.side(number, depth, True),
            slots[depth],
            self.send_sem.at[number, depth],
            self.recv_sem.at[number, depth],
            order[depth],
        )

    def send(self, number, depth):
        self.copy(number, depth).start()

    def take(self, number, depth):
        _, _, order, slots, _ = self.pieces[number]
        self.copy(number, depth).wait_recv()
        mine = self.side(number, depth, False)[...]
        if depth == len(order) - 1:
            return mine.astype(F32) + slots[depth][...].astype(F32)
        slots[depth][...] = mine + slots[depth][...]
        self.send(number, depth + 1)
        return None

    def finish(self):
        for number, (_, _, order, _, _) in self.pieces.items():
            for depth in range(len(order)):
                self.copy(number, depth).wait_send()


def slot_shapes(lead, count, tail):
    return [pltpu.VMEM((lead,) + (2,) * (count - 1 - depth) + tail, BF16) for depth in range(count)]


ORDERS = ((X, Y, Z_LOW, Z_HIGH), (Y, Z_LOW, X, Z_HIGH), (Z_LOW, X, Y, Z_HIGH))
IN_CUTS = ((0, 16), (16, 16), (32, 32))
DOWN_CUTS = ((0, 384), (384, 384), (768, 256))
OUT_CUTS = ((0, 128), (128, 128), (256, 256))
LATER_DIMS = (
    (Z_HIGH, Z_LOW, Y),
    (Z_HIGH, Z_LOW, X),
    (Z_HIGH, Y, X),
    (Z_LOW, Y, Z_HIGH),
    (Z_LOW, Z_HIGH, X),
    (Y, Z_HIGH, X),
)


def in_vmem():
    return pl.BlockSpec(memory_space=pltpu.VMEM)


def anywhere():
    return pl.BlockSpec(memory_space=pl.ANY)


def params(collective):
    return pltpu.CompilerParams(
        collective_id=collective, has_side_effects=True, vmem_limit_bytes=VMEM_BYTES
    )


def take_rows(mixed, which):
    count = mixed.shape[0] // 2
    row = lax.broadcasted_iota(jnp.int32, (count, 2 * count), 0)
    column = lax.broadcasted_iota(jnp.int32, (count, 2 * count), 1)
    pick = jnp.where(column == 2 * row + which, 1.0, 0.0).astype(BF16)
    return dot_nn(pick, mixed).astype(BF16)


def sequence_rows(seg_ref, rows, length):
    half, member = lax.axis_index("half"), lax.axis_index("member")
    own = length // 2
    both = seg_ref[...].astype(F32)
    ids = jnp.where(half == 0, both[0:1], both[1:2])
    slots = []
    for j in range(2):
        for t in range(2):
            want = lax.rem(half + t, 2) * 2 + lax.rem(member + j, 2)
            piece = jnp.zeros((1, rows), F32)
            for b in range(4):
                piece = jnp.where(want == b, ids[:, b * rows : (b + 1) * rows], piece)
            slots.append(piece)
    spot = lax.broadcasted_iota(jnp.int32, (1, length), 1)
    side = lax.rem(half + lax.rem(spot // rows, 2), 2) * 2 + lax.rem(member + spot // own, 2)
    block = side * (rows // BLK) + lax.rem(spot // BLK, rows // BLK)
    return jnp.concatenate(slots, axis=1), block.astype(F32)


def make_features(segment, block, rand_ref, glob_ref, fq_ref, fk_ref):
    length = segment.shape[1]
    blocks = length // BLK
    half = lax.axis_index("half")
    numbers = lax.broadcasted_iota(jnp.int32, (8, length), 0).astype(F32)
    count = lax.broadcasted_iota(jnp.int32, (blocks, length), 0).astype(F32)
    here = jnp.where(block == count, 1.0, 0.0)
    apart = jnp.where((segment == numbers) | (numbers >= SEG_VALUES), 0.0, NEG)
    feats = jnp.concatenate([apart, here, here, jnp.zeros((HD - 8 - 2 * blocks, length), F32)], axis=0)
    fq_ref[...] = jnp.concatenate([feats, feats], axis=0).T.astype(BF16)

    same = jnp.where(segment == numbers, 1.0, 0.0)
    rest = jnp.zeros((HD - 16 - 2 * blocks, length), F32)
    ones = jnp.where(numbers < 3, 1.0, 0.0)
    common = jnp.where(jnp.abs(count - block) <= 1.0, 1.0, 0.0)
    for g in range(GLOB):
        named = jnp.where(half == 0, glob_ref[g : g + 1, 0:1], glob_ref[g : g + 1, 1:2])
        common = common + jnp.where(block == named.astype(F32), 1.0, 0.0)
    for pair in range(fk_ref.shape[0]):
        drawn = rand_ref[pair]
        sides = []
        for parity in (1, 0):
            times = common
            for j in range(RAND):
                column = parity * RAND + j
                times = times + jnp.where(drawn[:, column : column + 1] == block, 1.0, 0.0)
            full = jnp.where(times > 0, jnp.log(jnp.maximum(times, 1.0)), NEG)
            high = full.astype(BF16).astype(F32)
            sides += [same, high, full - high, ones, rest]
        fk_ref[pair] = jnp.concatenate(sides, axis=0).T.astype(BF16)


def begin(mixed, small, w_qkv, segments, random_blocks, global_blocks):
    rows = mixed.shape[0] // 2
    length = 4 * rows
    width = D // 2
    pairs = width // LANES
    cuts = 2
    size = rows // cuts

    def body(*refs):
        mixed_ref, wq_ref, wk_ref, wv_ref, seg_ref, rand_ref, glob_ref = refs[:7]
        small_refs, in_ref = refs[7:15], refs[15]
        tok_ref, nt_ref, q_ref, k_ref, v_ref, fq_ref, fk_ref, vec_ref, in_row = refs[16:25]
        all_ref, kept_ref, sent_ref, norm_ref, send_sem, recv_sem = refs[25:]
        half = lax.axis_index("half")
        sent_ref[...] = take_rows(mixed_ref[...], 1 - half)
        greet((X, MEMBER))

        def over_x(c):
            return remote(
                sent_ref.at[pl.ds(c * size, size)],
                all_ref.at[pl.ds(rows + c * size, size)],
                send_sem.at[c],
                recv_sem.at[c],
                X,
            )

        def on(c):
            return remote(
                all_ref.at[pl.ds(rows + c * size, size)],
                all_ref.at[pl.ds(3 * rows + c * size, size)],
                send_sem.at[cuts + c],
                recv_sem.at[cuts + c],
                MEMBER,
            )

        near = remote(
            kept_ref, all_ref.at[pl.ds(2 * rows, rows)], send_sem.at[2 * cuts], recv_sem.at[2 * cuts], MEMBER
        )
        for c in range(cuts):
            over_x(c).start()
        kept_ref[...] = take_rows(mixed_ref[...], half)
        near.start()

        for at, ref in enumerate(small_refs):
            vec_ref[at : at + 1] = ref[...].astype(F32).reshape(1, D)
        in_row[...] = in_ref[...].astype(F32).reshape(in_row.shape)
        first_half = lax.axis_index("member") == 0
        q_shift, v_shift = (
            jnp.where(first_half, vec_ref[row : row + 1, :width], vec_ref[row : row + 1, width:]) for row in (6, 7)
        )

        def project(first, count):
            place = pl.ds(first, count)
            x = kept_ref[...] if first == 0 else all_ref[place, :]
            if first < 2 * rows:
                tok_ref[place, :] = x
            unit, _ = normalise(x.astype(F32))
            normed = (unit * vec_ref[4:5] + vec_ref[5:6]).astype(BF16)
            if count % LANES == 0:
                nt_ref[:, place] = turned(normed)
            else:
                norm_ref[pl.ds(first % (2 * count), count), :] = normed
                if first % (2 * count):
                    nt_ref[:, first - count : first + count] = turned(norm_ref[...])
            q_ref[place, :] = (dot_nn(normed, wq_ref[...]) + q_shift).astype(BF16)
            k_ref[place, :] = dot_nn(normed, wk_ref[...]).astype(BF16)
            v_ref[place, :] = (dot_nn(normed, wv_ref[...]) + v_shift).astype(BF16)

        project(0, rows)
        near.wait_recv()
        project(2 * rows, rows)
        make_features(*sequence_rows(seg_ref, rows, length), rand_ref, glob_ref, fq_ref, fk_ref)
        for c in range(cuts):
            over_x(c).wait_recv()
            on(c).start()
            project(rows + c * size, size)
        for c in range(cuts):
            on(c).wait_recv()
            project(3 * rows + c * size, size)
        near.wait_send()
        for c in range(cuts):
            over_x(c).wait_send()
            on(c).wait_send()

    def weight(which):
        return pl.BlockSpec((D, width), lambda i: (0, 2 * which + lax.axis_index("member")))

    def shape(count, columns):
        return jax.ShapeDtypeStruct((count, columns), BF16)

    return pl.pallas_call(
        body,
        grid=(1,),
        out_shape=(shape(2 * rows, D), shape(D, length))
        + (shape(length, width),) * 3
        + (shape(length, LANES), jax.ShapeDtypeStruct((pairs, length, LANES), BF16))
        + (jax.ShapeDtypeStruct((8, D), F32), jax.ShapeDtypeStruct((1,) + small[8].shape, F32)),
        in_specs=[in_vmem(), weight(0), weight(1), weight(2)] + [in_vmem()] * 12,
        out_specs=(in_vmem(),) * 9,
        scratch_shapes=[
            pltpu.VMEM((length, D), BF16),
            pltpu.VMEM((rows, D), BF16),
            pltpu.VMEM((rows, D), BF16),
            pltpu.VMEM((2 * size, D), BF16),
            pltpu.SemaphoreType.DMA((2 * cuts + 1,)),
            pltpu.SemaphoreType.DMA((2 * cuts + 1,)),
        ],
        compiler_params=params(5),
        name="begin",
    )(mixed, w_qkv, w_qkv, w_qkv, segments, random_blocks, global_blocks, *small)


def attend_forward(q, k, v, feat_q, feat_k, cot_mixed, tile=1024):
    length, width = q.shape
    pairs = width // LANES
    tiles = length // tile
    blocks = length // BLK
    own = length // 2
    rows = own // 2

    def body(*refs):
        q_ref, k_ref, v_ref, fq_ref, fk_ref, mixed_ref = refs[:6]
        ctx_ref, qa_ref, other_ref, cot_ref = refs[6:10]
        ka_ref, made_ref, kept_ref, sent_ref, send_sem, recv_sem, cot_send, cot_recv = refs[10:]
        pair, step = pl.program_id(0), pl.program_id(1)
        half = lax.axis_index("half")

        def stay():
            return pltpu.make_async_copy(kept_ref, cot_ref.at[pl.ds(0, rows)], cot_send.at[3])

        def cot_copy(which):
            across = pl.ds(rows, rows)
            src, to, bit = (
                (sent_ref, across, X),
                (kept_ref, pl.ds(own, rows), MEMBER),
                (cot_ref.at[across], pl.ds(own + rows, rows), MEMBER),
            )[which]
            return remote(src, cot_ref.at[to], cot_send.at[which], cot_recv.at[which], bit)

        @pl.when((pair == 0) & (step == 0))
        def _():
            greet((X, MEMBER))
            sent_ref[...] = take_rows(mixed_ref[...], 1 - half)
            cot_copy(0).start()
            kept_ref[...] = take_rows(mixed_ref[...], half)
            cot_copy(1).start()
            stay().start()

        @pl.when(step == 0)
        def _():
            feats = fk_ref[0]
            low_half = lax.broadcasted_iota(jnp.int32, (length, LANES), 1) < HD
            keys = k_ref[...]
            ka_ref[0] = jnp.where(low_half, keys, feats)
            ka_ref[1] = jnp.where(low_half, feats, keys)

        lane = lax.broadcasted_iota(jnp.int32, (tile, LANES), 1)
        low_half = lane < HD
        scaled = q_ref[...] * jnp.asarray(HD ** (-0.5), BF16)
        place = pl.ds(pl.multiple_of(step * tile, tile), tile)
        feats = fq_ref[...]
        results = []
        for parity in range(2):
            if parity == 0:
                aug = jnp.where(low_half, scaled, feats)
                first = HD + 8 + 2 * blocks
            else:
                aug = jnp.where(low_half, feats, scaled)
                first = 8 + 2 * blocks
            scores = dot_nt(aug, ka_ref[parity])
            top = jnp.max(scores, axis=-1, keepdims=True)
            weights = jnp.exp(scores - top)
            total = jnp.sum(weights, axis=-1, keepdims=True)
            mixed = dot_nn(weights.astype(BF16), v_ref[...])
            results.append(mixed / total)
            hi, mid, low = three_parts(-(top + jnp.log(total)))
            aug = jnp.where(lane == first, hi, aug)
            aug = jnp.where(lane == first + 1, mid, aug)
            aug = jnp.where(lane == first + 2, low, aug)
            qa_ref[parity] = aug
        context = jnp.where(low_half, results[0], results[1]).astype(BF16)
        ctx_ref[...] = context
        made_ref[pair, place, :] = context

        def swaps(one_pair):
            cols = pl.ds(pl.multiple_of(one_pair * LANES, LANES), LANES)
            return [
                remote(
                    made_ref.at[one_pair, pl.ds(from_row, own)],
                    other_ref.at[pl.ds(own - from_row, own), cols],
                    send_sem.at[side, one_pair],
                    recv_sem.at[side, one_pair],
                    MEMBER,
                )
                for side, from_row in enumerate((0, own))
            ]

        @pl.when(step == tiles - 1)
        def _():
            for one in swaps(pair):
                one.start()

        @pl.when((pair == pairs - 2) & (step == tiles - 1))
        def _():
            cot_copy(0).wait_recv()
            cot_copy(2).start()

        @pl.when((pair == pairs - 1) & (step == tiles - 1))
        def _():
            cot_copy(0).wait_send()
            stay().wait()
            cot_copy(1).wait()
            cot_copy(2).wait()
            for one_pair in range(pairs):
                for one in swaps(one_pair):
                    one.wait()

    return pl.pallas_call(
        body,
        grid=(pairs, tiles),
        out_shape=(
            jax.ShapeDtypeStruct((length, width), BF16),
            jax.ShapeDtypeStruct((2 * pairs, length, LANES), BF16),
            jax.ShapeDtypeStruct((length, width), BF16),
            jax.ShapeDtypeStruct((length, D), BF16),
        ),
        in_specs=[
            pl.BlockSpec((tile, LANES), lambda p, t: (t, p)),
            pl.BlockSpec((length, LANES), lambda p, t: (0, p)),
            pl.BlockSpec((length, LANES), lambda p, t: (0, p)),
            pl.BlockSpec((tile, LANES), lambda p, t: (t, 0)),
            pl.BlockSpec((1, length, LANES), lambda p, t: (p, 0, 0)),
            in_vmem(),
        ],
        out_specs=(
            pl.BlockSpec((tile, LANES), lambda p, t: (t, p)),
            pl.BlockSpec((2, tile, LANES), lambda p, t: (p, t, 0)),
            anywhere(),
            anywhere(),
        ),
        scratch_shapes=[
            pltpu.VMEM((2, length, LANES), BF16),
            pltpu.VMEM((pairs, length, LANES), BF16),
            pltpu.VMEM((rows, D), BF16),
            pltpu.VMEM((rows, D), BF16),
            pltpu.SemaphoreType.DMA((2, pairs)),
            pltpu.SemaphoreType.DMA((2, pairs)),
            pltpu.SemaphoreType.DMA((4,)),
            pltpu.SemaphoreType.DMA((3,)),
        ],
        compiler_params=params(4),
        name="attend_forward",
    )(q, k, v, feat_q, feat_k, cot_mixed)


def feed_forward(context, context_other, tokens, w_out, vectors, cot, w_in, in_bias, w_down):
    rows = cot.shape[0]
    own = rows // 2
    width = context.shape[1]
    chunk = 4 * LANES
    steps = 4
    share = D // 16
    root = (2.0 / np.pi) ** 0.5
    cube = 0.044715

    def group(j):
        bits = my_bits()
        z_low = jnp.where(j < 2, 1 - bits[Z_LOW], bits[Z_LOW])
        return z_low, jnp.where(lax.rem(j, 2) == 0, 1 - bits[Y], bits[Y])

    def body(*refs):
        ctx_ref, other_ref, tok_ref, wo_ref, wo2_ref, vec_ref, c_ref = refs[:7]
        wi_refs, inb_ref, wd_refs = refs[7:11], refs[11], refs[12:16]
        out_ref, dn_ref, dn_got, mid_ref, gb_ref = refs[16:21]
        keep, got = refs[21:27], refs[27:33]
        n_ref, nt_ref, out_acc, dn_acc, out_send, out_got, dn_send, gi_ref, gd_ref = refs[33:42]
        send_sem, recv_sem, keep_sem, swap_sem = refs[42:]
        step = pl.program_id(0)
        bits = my_bits()
        z_low, y = group(step)
        slot = 2 * z_low + y

        @pl.when(step == 0)
        def _():
            greet((Z_LOW, Y, X, MEMBER))
            cut = own // 2
            swaps = []
            for at in range(2):
                part = slice(at * cut, (at + 1) * cut)
                mid = (
                    tok_ref[part].astype(F32)
                    + dot_nn(ctx_ref[part], wo_ref[...])
                    + dot_nn(other_ref[part], wo2_ref[...])
                    + vec_ref[0:1]
                )
                mid_ref[part] = mid
                unit, _ = normalise(mid)
                n_ref[part] = (unit * vec_ref[1:2] + vec_ref[2:3]).astype(BF16)
                swaps.append(
                    remote(
                        n_ref.at[pl.ds(at * cut, cut)],
                        n_ref.at[pl.ds(own + at * cut, cut)],
                        swap_sem.at[0, 3 * at],
                        swap_sem.at[1, 3 * at],
                        MEMBER,
                    )
                )
                swaps[at].start()
            nt_ref[:, :own] = turned(n_ref[:own])
            for at in range(2):
                swaps[at].wait()
                first = own + at * cut
                nt_ref[:, first : first + cut] = turned(n_ref[first : first + cut])

        wi = jnp.concatenate([ref[...] for ref in wi_refs], axis=1)
        wd = jnp.concatenate([ref[...] for ref in wd_refs], axis=0)
        def shift(u):
            return inb_ref[:, pl.ds(pl.multiple_of(u(step) * LANES, LANES), LANES)]

        in_shift = jnp.concatenate([shift(u) for u in units], axis=1)
        pre = dot_nn(n_ref[...], wi) + in_shift
        square = pre * pre
        th = jnp.tanh(root * pre * (1.0 + cube * square))
        half_up = 0.5 * (1.0 + th)
        hidden = (pre * half_up).astype(BF16)
        slope = half_up + 0.5 * pre * (1.0 - th * th) * (root * (1.0 + 3.0 * cube * square))

        def in_part(kind, at):
            bit = (X, Y, Z_LOW)[kind]
            rest = (ALL,) * (3 - bit) + (pl.ds(*IN_CUTS[kind]),)
            return lambda side: gi_ref.at[(at,) + (ALL,) * bit + (side,) + rest]

        def copies(kind, at, where, bit):
            return (
                lambda: remote(
                    where(1 - bits[bit]), got[kind].at[at], send_sem.at[kind, at], recv_sem.at[kind, at], bit
                ),
                lambda: pltpu.make_async_copy(where(bits[bit]), keep[kind].at[at], keep_sem.at[kind, at]),
            )

        def in_copies(kind, at):
            return copies(kind, at, in_part(kind, at), (X, Y, Z_LOW)[kind])

        def x_copies(at):
            return copies(3, at, lambda side: gd_ref.at[at, :, side, :, pl.ds(*DOWN_CUTS[0])], X)

        def y_copies(z):
            return copies(4, z, lambda side: gd_ref.at[2 * z + side, :, :, :, pl.ds(*DOWN_CUTS[1])], Y)

        def z_copies(at_y):
            return copies(
                5, at_y, lambda side: gd_ref.at[2 * side + at_y, :, :, :, pl.ds(*DOWN_CUTS[2])], Z_LOW
            )

        gd_ref[slot] = dot_tn(hidden, c_ref[...]).astype(BF16).reshape(2, 2, LANES, D)
        for one in x_copies(slot):
            one().start()

        @pl.when(lax.rem(step, 2) == 0)
        def _():
            y_copies(z_low)[0]().start()

        @pl.when(lax.rem(step, 2) == 1)
        def _():
            y_copies(z_low)[1]().start()

        @pl.when(step < 2)
        def _():
            z_copies(y)[0]().start()

        @pl.when(step >= 2)
        def _():
            z_copies(y)[1]().start()

        pre_grad = (dot_nt(c_ref[...], wd) * slope).astype(BF16)
        gb_ref[...] = jnp.sum(pre_grad.astype(F32), axis=0, keepdims=True)
        gi_ref[slot] = dot_nn(nt_ref[...], pre_grad).astype(BF16).reshape(2, 2, 2, 2, share, chunk)
        for kind in range(3):
            for one in in_copies(kind, slot):
                one().start()

        dn_swap = (dn_send, dn_got, swap_sem.at[0, 1], swap_sem.at[1, 1], MEMBER)
        out_swap = (out_send, out_got, swap_sem.at[0, 2], swap_sem.at[1, 2], MEMBER)
        @pl.when(step == 0)
        def _():
            dn_acc[...] = dot_nt(pre_grad, wi)
            out_acc[...] = dot_nn(hidden, wd)

        @pl.when((step > 0) & (step < steps - 1))
        def _():
            dn_acc[...] += dot_nt(pre_grad, wi)
            out_acc[...] += dot_nn(hidden, wd)

        @pl.when(step == steps - 1)
        def _():
            theirs, ours = slice(own, rows), slice(0, own)
            dn_send[...] = (dn_acc[theirs] + dot_nt(pre_grad[theirs], wi)).astype(BF16)
            remote(*dn_swap).start()
            out_send[...] = (out_acc[theirs] + dot_nn(hidden[theirs], wd)).astype(BF16)
            remote(*out_swap).start()
            dn_ref[...] = dn_acc[ours] + dot_nt(pre_grad[ours], wi)
            out_acc[ours] += mid_ref[...] + vec_ref[3:4] + dot_nn(hidden[ours], wd)

        @pl.when(step == steps - 1)
        def _():
            for at in range(4):
                for kind in range(3):
                    for one in in_copies(kind, at):
                        one().wait()
                for one in x_copies(at):
                    one().wait()
            for at in range(2):
                for one in y_copies(at) + z_copies(at):
                    one().wait()
            remote(*dn_swap).wait()
            remote(*out_swap).wait()
            out_ref[...] = (out_acc[:own] + out_got[...].astype(F32)).astype(BF16)

    def unit(z_high, x):
        def at(j):
            z_low, y = group(j)
            return 2 * (((2 * z_high + z_low) * 2 + y) * 2 + x) + lax.axis_index("member")

        return at

    units = [unit(z_high, x) for z_high in range(2) for x in range(2)]

    def column(u):
        return lambda j: (0, u(j))

    def row(u):
        return lambda j: (u(j), 0)

    def slot_of(j):
        z_low, y = group(j)
        return (0, 2 * z_low + y)

    whole = pl.BlockSpec((rows, D), lambda j: (0, 0))
    half = pl.BlockSpec((own, D), lambda j: (0, 0))
    half_ctx = pl.BlockSpec((own, width), lambda j: (0, 0))
    parts = [jax.ShapeDtypeStruct((4, 2, 2, 2, size, chunk), BF16) for _, size in IN_CUTS] + [
        jax.ShapeDtypeStruct((4, 2, LANES, DOWN_CUTS[0][1]), BF16),
        jax.ShapeDtypeStruct((2, 2, 2, LANES, DOWN_CUTS[1][1]), BF16),
        jax.ShapeDtypeStruct((2, 2, 2, LANES, DOWN_CUTS[2][1]), BF16),
    ]
    own_f32 = jax.ShapeDtypeStruct((own, D), F32)
    own_bf16 = jax.ShapeDtypeStruct((own, D), BF16)
    results = pl.pallas_call(
        body,
        grid=(steps,),
        out_shape=[
            own_bf16,
            own_f32,
            own_bf16,
            own_f32,
            jax.ShapeDtypeStruct((1, steps * chunk), F32),
        ]
        + parts
        + parts,
        in_specs=[
            half_ctx,
            half_ctx,
            half,
            pl.BlockSpec((width, D), lambda j: (lax.axis_index("member"), 0)),
            pl.BlockSpec((width, D), lambda j: (1 - lax.axis_index("member"), 0)),
            pl.BlockSpec((8, D), lambda j: (0, 0)),
            whole,
        ]
        + [pl.BlockSpec((D, LANES), column(u)) for u in units]
        + [in_vmem()]
        + [pl.BlockSpec((LANES, D), row(u)) for u in units],
        out_specs=[half, half, anywhere(), half, pl.BlockSpec((1, chunk), slot_of)]
        + [anywhere()] * 12,
        scratch_shapes=[
            pltpu.VMEM((rows, D), BF16),
            pltpu.VMEM((D, rows), BF16),
            pltpu.VMEM((rows, D), F32),
            pltpu.VMEM((rows, D), F32),
            pltpu.VMEM((own, D), BF16),
            pltpu.VMEM((own, D), BF16),
            pltpu.VMEM((own, D), BF16),
            pltpu.VMEM((4, 2, 2, 2, 2, share, chunk), BF16),
            pltpu.VMEM((4, 2, 2, LANES, D), BF16),
            pltpu.SemaphoreType.DMA((6, 4)),
            pltpu.SemaphoreType.DMA((6, 4)),
            pltpu.SemaphoreType.DMA((6, 4)),
            pltpu.SemaphoreType.DMA((2, 4)),
        ],
        compiler_params=params(1),
        name="feed_forward",
    )(context, context_other, tokens, w_out, w_out, vectors, cot, *[w_in] * 4, in_bias, *[w_down] * 4)
    return results[:5], results[5:11], results[11:]


def attend_backward(
    rows_aug, k, v, feat_k, ctx, ctx_other, mid, n2_grad, n2_grad_got, cot, vectors, w_out, normed_t, w_qkv, output_own,
    kept, got, tile=256,
):
    length, width = k.shape
    pairs = width // LANES
    early = 1
    tiles = length // tile
    own = length // 2
    chunk = kept[0].shape[-1]
    shapes = [a.shape for a in kept[:3]] + [(1, 2, 2, 2, LANES, a.shape[-1]) for a in kept[3:]]
    kept = [a.reshape(shape) for a, shape in zip(kept, shapes)]
    got = [a.reshape(shape) for a, shape in zip(got, shapes)]
    share = D // 16
    count = 9 + 3 * early

    def body(*refs):
        qa_ref, k_ref, v_ref, fk_ref, ctx_ref, other_ref, mid_ref, dn2_ref, dn2_got, c_ref, vec_ref, wo_ref = refs[:12]
        nt_ref, wq_ref, wk_ref, wv_ref, mine_ref = refs[12:17]
        keep_in, got_in = refs[17:23], refs[23:29]
        dn_ref, mg_ref, sum_ref, qb_ref, vb_ref, ready_ref, sum_down, dn_got, theirs_ref = refs[29:38]
        keep_new, got_new = refs[38:41], refs[41:44]
        ga_ref, acc_ref, slab_ref, dn_acc, dn_send, gq_ref, br_ref, g_ref, go_ref = refs[44:53]
        begin, first = refs[53:59], refs[59:65]
        slots = refs[65 : 65 + 18 + 12 + 12 * early]
        send_sem, recv_sem, load_sem, new_send, new_recv, new_keep, swap_sem = refs[65 + 30 + 12 * early :]
        pair, step = pl.program_id(0), pl.program_id(1)
        now = pair * tiles + step
        member = lax.axis_index("member")

        sums = Sums(send_sem, recv_sem)
        for kind in range(6):
            sums.add(kind, begin[kind], LATER_DIMS[kind], ORDERS[kind % 3][1:], slots[3 * kind : 3 * kind + 3])
        for kind in range(3):
            sums.add(
                6 + kind,
                go_ref,
                CHIP,
                ORDERS[kind],
                slots[18 + 4 * kind : 22 + 4 * kind],
                (ALL, pl.ds(*OUT_CUTS[kind])),
            )
        for one_pair in range(early):
            for kind in range(3):
                number = 9 + 3 * one_pair + kind
                sums.add(
                    number,
                    gq_ref.at[one_pair, pl.ds(kind, 1)],
                    CHIP,
                    ORDERS[kind],
                    slots[30 + 4 * (number - 9) : 34 + 4 * (number - 9)],
                )

        def loads(kind):
            return (
                pltpu.make_async_copy(keep_in[kind], begin[kind], load_sem.at[0, kind]),
                pltpu.make_async_copy(got_in[kind], first[kind], load_sem.at[1, kind]),
            )

        def begin_sum(kind):
            for one in loads(kind):
                one.wait()
            begin[kind][...] = begin[kind][...] + first[kind][...]
            sums.send(kind, 0)

        def end_sum(number):
            total = sums.take(number, len(sums.pieces[number][2]) - 1)
            if number < 3:
                for z_low in range(2):
                    for y in range(2):
                        for z_high in range(2):
                            for x in range(2):
                                unit = ((2 * z_high + z_low) * 2 + y) * 2 + x
                                local = (2 * z_high + x) * LANES
                                ready_ref[pl.ds(*IN_CUTS[number]), unit * LANES : (unit + 1) * LANES] = total[
                                    2 * z_low + y, :, local : local + LANES
                                ]
            elif number < 6:
                sum_down[:, pl.ds(*DOWN_CUTS[number - 3])] = total[0]
            elif number < 9:
                col, size = OUT_CUTS[number - 6]
                ready_ref[:, pl.ds(4 * chunk + col, size)] = total[0]
            else:
                one_pair, kind = (number - 9) // 3, (number - 9) % 3
                place = 4 * chunk + width + (kind * early + one_pair) * LANES
                ready_ref[:, place : place + LANES] = total[0]

        def do(number, depth):
            if depth == len(sums.pieces[number][2]) - 1:
                end_sum(number)
            else:
                sums.take(number, depth)

        def at(when, depth, *numbers):
            @pl.when(now == when)
            def _():
                for number in numbers:
                    do(number, depth)

        @pl.when(now == 0)
        def _():
            greet((Z_HIGH, Z_LOW, Y, X, MEMBER))
            for kind in range(6):
                for one in loads(kind):
                    one.start()
            for kind in (0, 1, 5, 2, 3, 4):
                begin_sum(kind)
            unit, scale = normalise(mid_ref[...])
            grad = dn2_ref[...] + dn2_got[...].astype(F32)
            cot_own = c_ref[...].astype(F32)
            mid_grad = cot_own + normalise_back(unit, scale, grad * vec_ref[1:2])
            mg_ref[...] = mid_grad
            branch = mid_grad.astype(BF16)
            br_ref[:own] = branch
            swap = remote(
                br_ref.at[pl.ds(0, own)], br_ref.at[pl.ds(own, own)], swap_sem.at[0, 0], swap_sem.at[1, 0], MEMBER
            )
            swap.start()
            sum_ref[0:1] = jnp.sum(branch.astype(F32), axis=0, keepdims=True)
            sum_ref[1:2] = jnp.sum(grad * unit, axis=0, keepdims=True)
            sum_ref[2:3] = jnp.sum(grad, axis=0, keepdims=True)
            sum_ref[3:4] = jnp.sum(cot_own, axis=0, keepdims=True)
            sum_ref[4:8] = jnp.zeros((4, D), F32)
            swap.wait()
            g_ref[...] = dot_nt(br_ref[...], wo_ref[...]).astype(BF16)
            columns = br_ref[:, pl.ds(pl.multiple_of(member * width, width), width)]
            go_ref[0, member] = dot_tn(ctx_ref[...], columns).astype(BF16).reshape(2, 2, 2, share, width)
            go_ref[0, 1 - member] = dot_tn(other_ref[...], columns).astype(BF16).reshape(2, 2, 2, share, width)
            for kind in range(6, 9):
                sums.send(kind, 0)

        output_swap = (mine_ref.at[pl.ds(own // 2, own // 2)], theirs_ref, swap_sem.at[0, 2], swap_sem.at[1, 2], X)

        @pl.when(now == 11)
        def _():
            remote(*output_swap).start()

        at(1, 0, 0, 1, 5)
        at(4, 0, 3, 4)
        at(5, 0, 7, 2)
        at(6, 1, 5)
        at(6, 0, 8)
        at(7, 0, 6)
        at(8, 1, 0, 1)
        at(8, 0, 10, 11, 9)
        at(9, 1, 2)
        at(10, 1, 3, 4, 6, 7)
        at(11, 2, 5)
        at(11, 1, 8)
        at(12, 1, 9)
        at(12, 2, 0)
        at(12, 1, 11)
        at(12, 2, 7, 1)
        at(13, 1, 10)
        at(13, 2, 8)
        at(15, 2, 2)

        slab_cols = pl.ds(pl.multiple_of(pair * LANES, LANES), LANES)

        @pl.when(step == 0)
        def _():
            lane = lax.broadcasted_iota(jnp.int32, (length, LANES), 1)
            low_half = lane < HD
            grads = g_ref[:, slab_cols]
            prod = grads.astype(F32) * ctx_ref[:, slab_cols].astype(F32)
            for parity in range(2):
                mine = low_half if parity == 0 else jnp.logical_not(low_half)
                lead = HD if parity == 0 else 0
                delta = -jnp.sum(jnp.where(mine, prod, 0.0), axis=-1, keepdims=True)
                hi, mid, low = three_parts(delta)
                rows = jnp.where(mine, grads, jnp.zeros_like(grads))
                rows = jnp.where(lane == lead, hi, rows)
                rows = jnp.where(lane == lead + 1, mid, rows)
                ga_ref[parity] = jnp.where(lane == lead + 2, low, rows)
            ga_ref[2] = grads
            acc_ref[...] = jnp.zeros_like(acc_ref)

        lane = lax.broadcasted_iota(jnp.int32, (tile, LANES), 1)
        low_half = lane < HD
        keys = k_ref[...]
        values = v_ref[...]
        feats = fk_ref[0]
        keys_t = turned(keys)
        dks, dvs = [], []
        for parity in range(2):
            lead = HD if parity == 0 else 0
            mine = low_half if parity == 0 else jnp.logical_not(low_half)
            key_rows = jnp.where(mine, keys, feats)
            ones = jnp.where((lane >= lead) & (lane < lead + 3), 1.0, 0.0).astype(BF16)
            value_rows = jnp.where(mine, values, ones)
            probs = jnp.exp(dot_nt(key_rows, qa_ref[parity]))
            diff = dot_nt(value_rows, ga_ref[parity])
            score_grad = (probs * diff).astype(BF16)
            dvs.append(dot_nn(probs.astype(BF16), ga_ref[2]))
            dks.append(dot_nn(score_grad, qa_ref[parity]))
            side = keys_t[parity * HD : (parity + 1) * HD]
            acc_ref[parity * HD : (parity + 1) * HD] += dot_nn(side, score_grad)
        place = pl.ds(pl.multiple_of(step * tile, tile), tile)
        slab_ref[place, LANES : 2 * LANES] = jnp.where(low_half, dks[0], dks[1]).astype(BF16)
        slab_ref[place, 2 * LANES :] = jnp.where(low_half, dvs[0], dvs[1]).astype(BF16)

        def new_copies(kind, late):
            bit = (X, Y, Z_LOW)[kind]
            whole = gq_ref.at[early + late, kind]
            return (
                pltpu.make_async_copy(
                    whole.at[(ALL,) * bit + (sums.bits[bit],)], keep_new[kind].at[late], new_keep.at[kind, late]
                ),
                remote(
                    whole.at[(ALL,) * bit + (1 - sums.bits[bit],)],
                    got_new[kind].at[late],
                    new_send.at[kind, late],
                    new_recv.at[kind, late],
                    bit,
                ),
            )

        @pl.when(step == tiles - 1)
        def _():
            slab_ref[:, :LANES] = (acc_ref[...].T * HD ** (-0.5)).astype(BF16)
            slabs = slab_ref[...]
            made = dot_nn(nt_ref[...], slabs).astype(BF16)
            for kind in range(3):
                gq_ref[pair, kind] = made[:, kind * LANES : (kind + 1) * LANES].reshape(
                    2, 2, 2, 2, share, LANES
                )
            for one_pair in range(pairs):

                @pl.when(pair == one_pair)
                def _(one_pair=one_pair):
                    for kind in range(3):
                        if one_pair < early:
                            sums.send(9 + 3 * one_pair + kind, 0)
                        else:
                            for one in new_copies(kind, one_pair - early):
                                one.start()

            qb_ref[...] = jnp.sum(slabs[:, :LANES].astype(F32), axis=0, keepdims=True)
            vb_ref[...] = jnp.sum(slabs[:, 2 * LANES :].astype(F32), axis=0, keepdims=True)

        dn_swap = (dn_send, dn_got, swap_sem.at[0, 1], swap_sem.at[1, 1], MEMBER)

        @pl.when(step == tiles - 1)
        def _():
            weights = jnp.concatenate([wq_ref[...], wk_ref[...], wv_ref[...]], axis=1)
            for rows in (slice(own, length), slice(0, own)):
                grown = dot_nt(slab_ref[rows], weights)

                @pl.when(pair == 0)
                def _(rows=rows, grown=grown):
                    dn_acc[rows] = grown

                @pl.when((pair > 0) & (pair < pairs - 1))
                def _(rows=rows, grown=grown):
                    dn_acc[rows] += grown

                @pl.when(pair == pairs - 1)
                def _(rows=rows, grown=grown):
                    total = dn_acc[rows] + grown
                    if rows.start:
                        dn_send[...] = total.astype(BF16)
                        remote(*dn_swap).start()
                    else:
                        dn_ref[...] = total

        @pl.when(now == pairs * tiles - 1)
        def _():
            do(11, 2)
            do(6, 2)
            do(3, 2)
            do(9, 2)
            do(4, 2)
            do(7, 3)
            do(10, 2)
            do(8, 3)
            do(11, 3)
            do(6, 3)
            do(9, 3)
            do(10, 3)
            for late in range(pairs - early):
                for kind in range(3):
                    for one in new_copies(kind, late):
                        one.wait()
            sums.finish()
            remote(*dn_swap).wait()
            remote(*output_swap).wait()

    part = pl.BlockSpec((tile, LANES), lambda p, t: (t, p))
    bias_part = pl.BlockSpec((1, LANES), lambda p, t: (0, p))

    def columns(which):
        return pl.BlockSpec(
            (D, LANES), lambda p, t: (0, (2 * which + lax.axis_index("member")) * pairs + p)
        )

    slots = []
    for shape in shapes:
        slots += slot_shapes(shape[0], 3, shape[4:])
    for _, size in OUT_CUTS:
        slots += slot_shapes(1, 4, (share, size))
    for _ in range(3 * early):
        slots += slot_shapes(1, 4, (share, LANES))
    new = [jax.ShapeDtypeStruct((pairs - early, 2, 2, 2, share, LANES), BF16)] * 3
    own_f32 = jax.ShapeDtypeStruct((own, D), F32)
    results = pl.pallas_call(
        body,
        grid=(pairs, tiles),
        out_shape=[
            own_f32,
            own_f32,
            jax.ShapeDtypeStruct((8, D), F32),
            jax.ShapeDtypeStruct((1, width), F32),
            jax.ShapeDtypeStruct((1, width), F32),
            jax.ShapeDtypeStruct((share, 4 * chunk + width + 3 * early * LANES), F32),
            jax.ShapeDtypeStruct((LANES, D), F32),
            jax.ShapeDtypeStruct((own, D), BF16),
            jax.ShapeDtypeStruct((own // 2, D), BF16),
        ]
        + new
        + new,
        in_specs=[
            pl.BlockSpec((2, length, LANES), lambda p, t: (p, 0, 0)),
            part,
            part,
            pl.BlockSpec((1, tile, LANES), lambda p, t: (p, t, 0)),
            in_vmem(),
            in_vmem(),
            in_vmem(),
            in_vmem(),
            in_vmem(),
            pl.BlockSpec((own, D), lambda p, t: (0, 0)),
            in_vmem(),
            pl.BlockSpec((width, D), lambda p, t: (lax.axis_index("member"), 0)),
            in_vmem(),
            columns(0),
            columns(1),
            columns(2),
        ]
        + [anywhere()] * 13,
        out_specs=[in_vmem(), in_vmem(), in_vmem(), bias_part, bias_part]
        + [in_vmem()] * 2
        + [anywhere()] * 8,
        scratch_shapes=[
            pltpu.VMEM((3, length, LANES), BF16),
            pltpu.VMEM((LANES, length), F32),
            pltpu.VMEM((length, 3 * LANES), BF16),
            pltpu.VMEM((length, D), F32),
            pltpu.VMEM((own, D), BF16),
            pltpu.VMEM((pairs, 3, 2, 2, 2, 2, share, LANES), BF16),
            pltpu.VMEM((length, D), BF16),
            pltpu.VMEM((length, width), BF16),
            pltpu.VMEM((1, 2, 2, 2, 2, share, width), BF16),
        ]
        + [pltpu.VMEM(shape, BF16) for shape in shapes]
        + [pltpu.VMEM(shape, BF16) for shape in shapes]
        + slots
        + [
            pltpu.SemaphoreType.DMA((count, 4)),
            pltpu.SemaphoreType.DMA((count, 4)),
            pltpu.SemaphoreType.DMA((2, 6)),
            pltpu.SemaphoreType.DMA((3, pairs - early)),
            pltpu.SemaphoreType.DMA((3, pairs - early)),
            pltpu.SemaphoreType.DMA((3, pairs - early)),
            pltpu.SemaphoreType.DMA((2, 3)),
        ],
        compiler_params=params(3),
        name="attend_backward",
    )(
        rows_aug, k, v, feat_k, ctx, ctx_other, mid, n2_grad, n2_grad_got, cot, vectors, w_out, normed_t,
        w_qkv, w_qkv, w_qkv, output_own, *kept, *got,
    )
    return results[:9], results[9:12], results[12:]


def in_turn(first, second):
    count = first.shape[0]
    row = lax.broadcasted_iota(jnp.int32, (2 * count, count), 0)
    column = lax.broadcasted_iota(jnp.int32, (2 * count, count), 1)
    even = jnp.where(row == 2 * column, 1.0, 0.0).astype(BF16)
    odd = jnp.where(row == 2 * column + 1, 1.0, 0.0).astype(BF16)
    return (dot_nn(even, first) + dot_nn(odd, second)).astype(BF16)


def finish(
    tokens, mid_grad, normed_grad, normed_grad_got, vectors, sums_in, in_bias_grad, q_sum, v_sum, ready, out_mine,
    out_other, kept, got,
):
    own = mid_grad.shape[0]
    rows = own // 2
    width = q_sum.shape[1]
    late, share = kept[0].shape[0], kept[0].shape[-2]
    per = share // 2
    size = late * LANES

    def body(*refs):
        vec_ref, sum_ref, inb_ref, qb_ref, vb_ref = refs[:5]
        keep, first = refs[5:8], refs[8:11]
        big_in = refs[11:18]
        ig_ref, ig_got, ready_got, qkv_ref, vec_sum, out_ref = refs[18:24]
        big = refs[24:31]
        ig_send, source, flat, shares, near_got, far_got = refs[31:37]
        begin, slots = refs[37:40], refs[40:46]
        send_sem, recv_sem, swap_sem, share_sem, near_sem, far_sem, load_sem = refs[46:]
        tok_ref, mg_ref, dn_ref, dn_got, mine_ref, other_ref, ready_ref = big
        member = lax.axis_index("member")

        def load(which):
            src = big_in[which].at[pl.ds(0, rows)] if which == 4 else big_in[which]
            return pltpu.make_async_copy(src, big[which], load_sem.at[which])

        for which in range(7):
            load(which).start()
        barrier = pltpu.get_barrier_semaphore()
        for mask in range(1, 32):
            pl.semaphore_signal(barrier, inc=1, device_id=place_across(mask), device_id_type=MESH_IDS)
        pl.semaphore_wait(barrier, 31)
        sums = Sums(send_sem, recv_sem)
        for kind in range(3):
            dims = tuple(b for b in CHIP if b != ORDERS[kind][0])
            sums.add(kind, begin[kind], dims, ORDERS[kind][1:3], slots[2 * kind : 2 * kind + 2])
            begin[kind][...] = keep[kind][...] + first[kind][...]
            sums.send(kind, 0)
        theirs = pl.ds(pl.multiple_of((1 - member) * per, per), per)
        ours = pl.ds(pl.multiple_of(member * per, per), per)
        top, rest = pl.ds(0, rows // 2), pl.ds(rows // 2, rows // 2)
        swaps = [
            remote(ready_ref.at[theirs], ready_got, swap_sem.at[0, 0], swap_sem.at[1, 0], MEMBER),
            remote(ig_send.at[top], ig_got.at[top], swap_sem.at[0, 1], swap_sem.at[1, 1], X),
            remote(ig_send.at[rest], ig_got.at[rest], swap_sem.at[0, 2], swap_sem.at[1, 2], X),
        ]

        for which in range(4):
            load(which).wait()
        gain_sum, bias_sum = 0.0, 0.0
        for part in (slice(rows, rows + rows // 2), slice(rows + rows // 2, own), slice(0, rows)):
            unit, scale = normalise(tok_ref[part].astype(F32))
            grad = dn_ref[part] + dn_got[part].astype(F32)
            input_grad = mg_ref[part] + normalise_back(unit, scale, grad * vec_ref[4:5])
            if part.start == rows:
                ig_send[top] = input_grad.astype(BF16)
                swaps[1].start()
            elif part.start:
                ig_send[rest] = input_grad.astype(BF16)
            else:
                ig_ref[...] = input_grad
            gain_sum = gain_sum + jnp.sum(grad * unit, axis=0, keepdims=True)
            bias_sum = bias_sum + jnp.sum(grad, axis=0, keepdims=True)
        flat[0:1] = gain_sum
        flat[1:2] = bias_sum
        flat[2:6] = sum_ref[0:4]
        blank = jnp.zeros((1, width), F32)
        for row, ref in ((6, qb_ref), (7, vb_ref)):
            value = ref[...]
            flat[row : row + 1, :width] = jnp.where(member == 0, value, blank)
            flat[row : row + 1, width:] = jnp.where(member == 1, value, blank)
        flat[8:] = jnp.zeros((LANES - 8, D), F32)
        source[:, :, :, :, :, :per] = flat[...].T.astype(BF16).reshape(2, 2, 2, 2, 2, per, LANES)
        source[:, :, :, :, :, per:] = jnp.zeros((2, 2, 2, 2, 2, 16, LANES), BF16)
        for z_high, z_low, y, x in np.ndindex(2, 2, 2, 2):
            unit = (((z_low * 2 + y) * 2 + z_high) * 2 + x) * LANES
            source[z_high, z_low, y, x, member, per:] = jnp.broadcast_to(
                inb_ref[:, unit : unit + LANES], (16, LANES)
            ).astype(BF16)

        def straight(mask):
            place = tuple(
                1 - bit if mask & flag else bit for bit, flag in zip(sums.bits, (16, 8, 4, 2, 1))
            )
            return pltpu.make_async_remote_copy(
                src_ref=source.at[place],
                dst_ref=shares.at[mask],
                send_sem=share_sem.at[0, mask],
                recv_sem=share_sem.at[1, mask],
                device_id=place_across(mask),
                device_id_type=MESH_IDS,
            )

        for mask in range(1, 32):
            straight(mask).start()

        def near(kind):
            return remote(
                slots[2 * kind + 1].at[:, sums.bits[0], theirs],
                near_got.at[kind],
                near_sem.at[0, kind],
                near_sem.at[1, kind],
                MEMBER,
            )

        def far(kind, flipped):
            return pltpu.make_async_remote_copy(
                src_ref=slots[2 * kind + 1].at[:, 1 - sums.bits[0], theirs if flipped else ours],
                dst_ref=far_got.at[flipped, kind],
                send_sem=far_sem.at[0, 2 * kind + flipped],
                recv_sem=far_sem.at[1, 2 * kind + flipped],
                device_id=place_across(16 + flipped),
                device_id_type=MESH_IDS,
            )

        for depth in range(2):
            for kind in (1, 0, 2):
                sums.copy(kind, depth).wait_recv()
                slots[2 * kind + depth][...] = sums.side(kind, depth, False)[...] + slots[2 * kind + depth][...]
                if depth == 0:
                    sums.send(kind, 1)
                else:
                    far(kind, 1).start()
                    far(kind, 0).start()
                    near(kind).start()
                if depth == 0 and kind == 1:
                    swaps[2].start()
                    for which in range(4, 7):
                        load(which).wait()
                    swaps[0].start()
                    mine, other = mine_ref[...], other_ref[...]
                    here = lax.axis_index("half") == 0
                    out_ref[...] = in_turn(jnp.where(here, mine, other), jnp.where(here, other, mine))
        total = source[sums.bits].astype(F32)
        for mask in range(1, 32):
            straight(mask).wait_recv()
            total = total + shares[mask].astype(F32)
        vec_sum[...] = total
        for kind in (1, 0, 2):
            far(kind, 0).wait_recv()
            ours_sum = slots[2 * kind + 1][:, sums.bits[0], ours].astype(F32) + far_got[0, kind].astype(F32)
            near(kind).wait_recv()
            far(kind, 1).wait_recv()
            theirs_sum = near_got[kind].astype(F32) + far_got[1, kind].astype(F32)
            for pair in range(late):
                place = kind * size + pair * LANES
                qkv_ref[member, :, place : place + LANES] = ours_sum[pair]
                qkv_ref[1 - member, :, place : place + LANES] = theirs_sum[pair]
        sums.finish()
        for kind in range(3):
            near(kind).wait_send()
            far(kind, 0).wait_send()
            far(kind, 1).wait_send()
        for mask in range(1, 32):
            straight(mask).wait_send()
        for one in swaps:
            one.wait()

    slots = []
    for _ in range(3):
        slots += slot_shapes(late, 3, (share, LANES))[:2]
    return pl.pallas_call(
        body,
        out_shape=(
            jax.ShapeDtypeStruct((rows, D), F32),
            jax.ShapeDtypeStruct((rows, D), BF16),
            jax.ShapeDtypeStruct((per, ready.shape[1]), F32),
            jax.ShapeDtypeStruct((2, per, 3 * size), F32),
            jax.ShapeDtypeStruct((per + 16, LANES), F32),
            jax.ShapeDtypeStruct((own, D), BF16),
        ),
        grid=(1,),
        in_specs=[in_vmem()] * 11 + [anywhere()] * 7,
        out_specs=(in_vmem(), anywhere(), anywhere(), in_vmem(), in_vmem(), in_vmem()),
        scratch_shapes=[
            pltpu.VMEM((own, D), BF16),
            pltpu.VMEM((own, D), F32),
            pltpu.VMEM((own, D), F32),
            pltpu.VMEM((own, D), BF16),
            pltpu.VMEM((rows, D), BF16),
            pltpu.VMEM((rows, D), BF16),
            pltpu.VMEM(ready.shape, F32),
            pltpu.VMEM((rows, D), BF16),
            pltpu.VMEM((2, 2, 2, 2, 2, per + 16, LANES), BF16),
            pltpu.VMEM((LANES, D), F32),
            pltpu.VMEM((32, per + 16, LANES), BF16),
            pltpu.VMEM((3, late, per, LANES), BF16),
            pltpu.VMEM((2, 3, late, per, LANES), BF16),
        ]
        + [pltpu.VMEM(kept[0].shape, BF16)] * 3
        + slots
        + [
            pltpu.SemaphoreType.DMA((3, 2)),
            pltpu.SemaphoreType.DMA((3, 2)),
            pltpu.SemaphoreType.DMA((2, 3)),
            pltpu.SemaphoreType.DMA((2, 32)),
            pltpu.SemaphoreType.DMA((2, 3)),
            pltpu.SemaphoreType.DMA((2, 6)),
            pltpu.SemaphoreType.DMA((7,)),
        ],
        compiler_params=params(2),
        name="finish",
    )(
        vectors, sums_in, in_bias_grad, q_sum, v_sum, *kept, *got, tokens, mid_grad, normed_grad, normed_grad_got,
        out_mine, out_other, ready,
    )


def per_device_pair(
    tokens,
    ln1_gain,
    ln1_bias,
    w_qkv,
    q_bias,
    v_bias,
    w_out,
    out_bias,
    ln2_gain,
    ln2_bias,
    w_in,
    in_bias,
    w_down,
    down_bias,
    cotangent,
    segment_ids,
    random_blocks,
    global_blocks,
):
    rows = tokens.shape[0]
    own = 2 * rows
    blocks = segment_ids.shape[0] // BLK
    half = lax.axis_index("half")
    member = lax.axis_index("member")
    mine_d = D // 2
    heads = HEADS // 2
    chips = lax.axis_size("batch") * 2

    def both_sequences(kept, other):
        return jnp.where(
            half == 0, jnp.stack([kept, other], axis=1), jnp.stack([other, kept], axis=1)
        )

    seq_random = lax.dynamic_index_in_dim(random_blocks, half, 1, keepdims=False)
    seq_random = lax.dynamic_slice_in_dim(seq_random, member * heads, heads, 1)
    pair_random = seq_random.reshape(blocks, heads // 2, 2 * RAND).transpose(1, 0, 2).astype(F32)
    own_tokens, normed_t, queries, keys, values, feat_q, feat_k, vectors, in_shift = begin(
        tokens.reshape(own, D),
        (out_bias, ln2_gain, ln2_bias, down_bias, ln1_gain, ln1_bias, q_bias, v_bias, in_bias),
        w_qkv,
        segment_ids.T,
        pair_random,
        global_blocks,
    )
    context, rows_aug, context_other, cot = attend_forward(
        queries, keys, values, feat_q, feat_k, cotangent.reshape(own, D)
    )
    (output_own, n2_grad, n2_grad_got, mid_stream, in_bias_grad), kept_parts, got_parts = feed_forward(
        context,
        context_other,
        own_tokens,
        w_out,
        vectors,
        cot,
        w_in,
        in_shift,
        w_down,
    )

    (
        (
            normed_grad,
            mid_grad,
            sums_in,
            q_sum,
            v_sum,
            ready,
            summed_down,
            normed_grad_got,
            output_other,
        ),
        kept_qkv,
        got_qkv,
    ) = attend_backward(
        rows_aug,
        keys,
        values,
        feat_k,
        context,
        context_other,
        mid_stream,
        n2_grad,
        n2_grad_got,
        cot,
        vectors,
        w_out,
        normed_t,
        w_qkv,
        output_own,
        kept_parts,
        got_parts,
    )
    input_kept, input_other, ready_got, qkv_late, vector_rows, output = finish(
        own_tokens,
        mid_grad,
        normed_grad,
        normed_grad_got,
        vectors,
        sums_in,
        in_bias_grad,
        q_sum,
        v_sum,
        ready,
        output_own,
        output_other,
        kept_qkv,
        got_qkv,
    )
    input_grad = both_sequences(input_kept, input_other.astype(F32))

    per = ready.shape[0] // 2
    mine_rows = lax.dynamic_slice_in_dim(ready, member * per, per, 0)
    left = jnp.where(member == 0, mine_rows, ready_got)
    right = jnp.where(member == 0, ready_got, mine_rows)

    start_out = w_in.shape[1] // 2
    start_early = start_out + mine_d
    early = (ready.shape[1] - start_early) // 3
    late = mine_d - early
    pieces = []
    for part in range(3):
        for x, later in ((left, qkv_late[0]), (right, qkv_late[1])):
            pieces.append(x[:, start_early + part * early : start_early + (part + 1) * early])
            pieces.append(later[:, part * late : (part + 1) * late])
    w_qkv_grad = jnp.concatenate(pieces, axis=1)
    w_out_grad = jnp.concatenate([x[:, start_out : start_out + mine_d] for x in (left, right)], axis=1)
    w_in_grad = jnp.concatenate(
        [x[:, j * LANES : (j + 1) * LANES] for j in range(chips) for x in (left, right)], axis=1
    )
    in_bias_out = vector_rows[per]
    vec = [vector_rows[:per, i] for i in range(8)]
    return (
        output.reshape(rows, 2, D),
        input_grad,
        vec[0],
        vec[1],
        w_qkv_grad,
        vec[6],
        vec[7],
        w_out_grad,
        vec[2],
        vec[3],
        vec[4],
        w_in_grad,
        in_bias_out,
        summed_down,
        vec[5],
    )


def solution(mesh):
    def program(*args):
        sequences = args[0].shape[1] // mesh.shape["batch"]
        seq = mesh.shape["seq"]
        fast = sequences == 2 and seq == 4 and mesh.shape["batch"] == 8
        if fast:
            use = jax.sharding.Mesh(
                mesh.devices.reshape(mesh.shape["batch"], 2, 2), ("batch", "half", "member")
            )
            seq_axes, all_axes, run = ("half", "member"), ("batch", "half", "member"), per_device_pair
        else:
            use, seq_axes, all_axes, run = mesh, "seq", ("batch", "seq"), per_device
        rows = P(seq_axes, "batch", None)
        in_specs = (rows,) + (P(),) * 13 + (
            rows,
            P(None, "batch"),
            P(None, "batch", None, None),
            P(None, "batch"),
        )
        vector, matrix = P(all_axes), P(all_axes, None)
        out_specs = (
            rows,
            rows,
            vector,
            vector,
            matrix,
            vector,
            vector,
            matrix,
            vector,
            vector,
            vector,
            matrix,
            vector,
            matrix,
            vector,
        )
        return jax.shard_map(
            run, mesh=use, in_specs=in_specs, out_specs=out_specs, check_vma=False
        )(*args)

    return program
```

```python
import jax
import jax.numpy as jnp
import numpy as np
from jax import lax
from jax.experimental import pallas as pl
from jax.experimental.pallas import tpu as pltpu
from jax.sharding import PartitionSpec as P

D = 1024
HEADS = 16
HD = 64
BLK = 64
RAND = 3
GLOB = 2


eps = 1e-05


def padded(x, sides, width):
    for axis, dim in sides:
        size, length = (lax.axis_size(axis), x.shape[dim])
        up = [(i, (i + 1) % size) for i in range(size - 1)]
        down = [(j, i) for i, j in up]
        last = lax.slice_in_dim(x, length - width, length, axis=dim)
        initial = lax.slice_in_dim(x, 0, width, axis=dim)
        before = lax.ppermute(last, axis, up)
        after = lax.ppermute(initial, axis, down)
        x = jnp.concatenate([before, x, after], axis=dim)
    return x


def layer_norm(values, gain_vec, shift_vec):
    row_mean = jnp.mean(values, axis=-1, keepdims=True)
    centred = values - row_mean
    spread = jnp.mean(centred * centred, axis=-1, keepdims=True)
    return centred * lax.rsqrt(spread + eps) * gain_vec + shift_vec


def gelu_tanh(values):
    return jax.nn.gelu(values, approximate=True)


def window_stack(extended, query_blocks):
    return jnp.stack(
        [extended[0:query_blocks], extended[1 : query_blocks + 1], extended[2 : query_blocks + 2]],
        axis=1,
    )


def pick_blocks(shard_rows, random_local, global_blocks):
    block_total = shard_rows.shape[0] // BLK
    seq_count = shard_rows.shape[1]
    numbers = jnp.arange(block_total, dtype=jnp.int32)
    random_hits = (random_local[..., None] == numbers).astype(jnp.bfloat16)
    global_hits = (global_blocks[..., None] == numbers).astype(jnp.bfloat16)
    blocks = shard_rows.reshape(block_total, BLK, seq_count, 2, HEADS, HD)
    picked_random = jnp.einsum(
        "ishjb,busxhd->ishjuxd", random_hits, blocks, preferred_element_type=jnp.float32
    )
    picked_global = jnp.einsum(
        "gsb,busc->gusc",
        global_hits,
        shard_rows.reshape(block_total, BLK, seq_count, 2 * D),
        preferred_element_type=jnp.float32,
    )
    return (picked_random, picked_global)


def key_products(left_side, window_kv, far_random, far_global, which_half):
    near_part = jnp.einsum(
        "itshd,iwushd->ishtwu",
        left_side,
        window_kv[:, :, :, :, which_half],
        preferred_element_type=jnp.float32,
    )
    far_part = jnp.einsum(
        "itshd,ishjud->ishtju",
        left_side,
        far_random[:, :, :, :, :, which_half],
        preferred_element_type=jnp.float32,
    )
    global_part = jnp.einsum(
        "itshd,gushd->ishtgu",
        left_side,
        far_global[:, :, :, which_half],
        preferred_element_type=jnp.float32,
    )
    lead_shape = near_part.shape[:4]
    return jnp.concatenate(
        [
            near_part.reshape(lead_shape + (-1,)),
            far_part.reshape(lead_shape + (-1,)),
            global_part.reshape(lead_shape + (-1,)),
        ],
        axis=-1,
    )


def split_slots(weights):
    lead_shape = weights.shape[:4]
    near_cut = 3 * BLK
    far_cut = (3 + RAND) * BLK
    near_part = weights[..., :near_cut].reshape(lead_shape + (3, BLK))
    far_part = weights[..., near_cut:far_cut].reshape(lead_shape + (RAND, BLK))
    global_part = weights[..., far_cut:].reshape(lead_shape + (GLOB, BLK))
    return (near_part, far_part, global_part)


def key_mix(weights, window_kv, far_random, far_global, which_half):
    near_part, far_part, global_part = split_slots(weights)
    mixed = jnp.einsum(
        "ishtwu,iwushd->itshd",
        near_part,
        window_kv[:, :, :, :, which_half],
        preferred_element_type=jnp.float32,
    )
    mixed = mixed + jnp.einsum(
        "ishtju,ishjud->itshd",
        far_part,
        far_random[:, :, :, :, :, which_half],
        preferred_element_type=jnp.float32,
    )
    mixed = mixed + jnp.einsum(
        "ishtgu,gushd->itshd",
        global_part,
        far_global[:, :, :, which_half],
        preferred_element_type=jnp.float32,
    )
    return mixed


def key_grads(weights, left_side):
    near_part, far_part, global_part = split_slots(weights)
    near_grad = jnp.einsum(
        "ishtwu,itshd->iwushd", near_part, left_side, preferred_element_type=jnp.float32
    )
    far_grad = jnp.einsum(
        "ishtju,itshd->ishjud", far_part, left_side, preferred_element_type=jnp.float32
    )
    global_grad = jnp.einsum(
        "ishtgu,itshd->gushd", global_part, left_side, preferred_element_type=jnp.float32
    )
    return (near_grad, far_grad, global_grad)


def per_device(
    tokens,
    ln1_gain,
    ln1_bias,
    w_qkv,
    q_bias,
    v_bias,
    w_out,
    out_bias,
    ln2_gain,
    ln2_bias,
    w_in,
    in_bias,
    w_down,
    down_bias,
    cotangent,
    segment_ids,
    random_blocks,
    global_blocks,
):
    row_count = tokens.shape[0]
    seq_count = tokens.shape[1]
    query_blocks = row_count // BLK
    seq_length = segment_ids.shape[0]
    device_now = lax.axis_index("seq")
    first_row = device_now * row_count
    score_scale = HD ** (-0.5)
    random_local = lax.dynamic_slice_in_dim(
        random_blocks, device_now * query_blocks, query_blocks, 0
    )
    inputs = tokens.astype(jnp.float32)
    normed_full, first_norm_back = jax.vjp(
        layer_norm, inputs, ln1_gain.astype(jnp.float32), ln1_bias.astype(jnp.float32)
    )
    normed = normed_full.astype(jnp.bfloat16)
    projected = jnp.einsum("rsd,de->rse", normed, w_qkv, preferred_element_type=jnp.float32)
    queries = (projected[:, :, :D] + q_bias.astype(jnp.float32)).astype(jnp.bfloat16)
    value_shift = jnp.concatenate([jnp.zeros((D,), jnp.float32), v_bias.astype(jnp.float32)])
    keyval = (projected[:, :, D:] + value_shift).astype(jnp.bfloat16)
    extended = padded(keyval, (("seq", 0),), BLK)
    window_kv = window_stack(
        extended.reshape(query_blocks + 2, BLK, seq_count, 2, HEADS, HD), query_blocks
    )
    picked = pick_blocks(
        lax.all_gather(keyval, "seq", axis=0, tiled=True), random_local, global_blocks
    )
    far_random = picked[0].astype(jnp.bfloat16)
    far_global = picked[1].astype(jnp.bfloat16).reshape(GLOB, BLK, seq_count, 2, HEADS, HD)
    query_segment = lax.dynamic_slice_in_dim(segment_ids, first_row, row_count, 0)
    query_segment = query_segment.reshape(query_blocks, BLK, seq_count).transpose(0, 2, 1)
    window_spots = first_row - BLK + jnp.arange(row_count + 2 * BLK, dtype=jnp.int32)
    inside_seq = (window_spots >= 0) & (window_spots < seq_length)
    near_segment = jnp.take(segment_ids, jnp.clip(window_spots, 0, seq_length - 1), axis=0)
    near_segment = jnp.where(inside_seq[:, None], near_segment, -1)
    near_segment = window_stack(
        near_segment.reshape(query_blocks + 2, BLK, seq_count), query_blocks
    )
    near_segment = near_segment.transpose(0, 3, 1, 2).reshape(query_blocks, seq_count, 1, 3 * BLK)
    segment_rows = segment_ids.T
    sequence_pick = jnp.arange(seq_count, dtype=jnp.int32)
    offsets = jnp.arange(BLK, dtype=jnp.int32)
    far_segment = segment_rows[
        sequence_pick[None, :, None, None, None], random_local[..., None] * BLK + offsets
    ]
    far_segment = far_segment.reshape(query_blocks, seq_count, HEADS, RAND * BLK)
    global_segment = segment_rows[
        sequence_pick[None, :, None], global_blocks[..., None] * BLK + offsets
    ]
    global_segment = global_segment.transpose(1, 0, 2).reshape(1, seq_count, 1, GLOB * BLK)
    key_segment = jnp.concatenate(
        [
            jnp.broadcast_to(near_segment, (query_blocks, seq_count, HEADS, 3 * BLK)),
            far_segment,
            jnp.broadcast_to(global_segment, (query_blocks, seq_count, HEADS, GLOB * BLK)),
        ],
        axis=-1,
    )
    allowed = key_segment[:, :, :, None, :] == query_segment[:, :, None, :, None]
    query_rows = queries.reshape(query_blocks, BLK, seq_count, HEADS, HD)
    scores = jnp.where(
        allowed, key_products(query_rows, window_kv, far_random, far_global, 0) * score_scale, -1e30
    )
    row_max = jnp.max(scores, axis=-1, keepdims=True)
    log_total = row_max + jnp.log(jnp.sum(jnp.exp(scores - row_max), axis=-1, keepdims=True))
    soft_full = jnp.exp(scores - log_total)
    attn_probs = soft_full.astype(jnp.bfloat16)
    context = (
        key_mix(attn_probs, window_kv, far_random, far_global, 1)
        .reshape(row_count, seq_count, D)
        .astype(jnp.bfloat16)
    )
    mid_stream = (
        inputs
        + jnp.einsum("rsd,de->rse", context, w_out, preferred_element_type=jnp.float32)
        + out_bias.astype(jnp.float32)
    )
    normed2_full, second_norm_back = jax.vjp(
        layer_norm, mid_stream, ln2_gain.astype(jnp.float32), ln2_bias.astype(jnp.float32)
    )
    normed2 = normed2_full.astype(jnp.bfloat16)
    pre_act = jnp.einsum(
        "rsd,df->rsf", normed2, w_in, preferred_element_type=jnp.float32
    ) + in_bias.astype(jnp.float32)
    hidden_full, gelu_back = jax.vjp(gelu_tanh, pre_act)
    hidden = hidden_full.astype(jnp.bfloat16)
    output = (
        mid_stream
        + jnp.einsum("rsf,fd->rsd", hidden, w_down, preferred_element_type=jnp.float32)
        + down_bias.astype(jnp.float32)
    ).astype(jnp.bfloat16)
    grad_out = cotangent.astype(jnp.float32)
    w_down_grad = jnp.einsum("rsf,rsd->fd", hidden, cotangent, preferred_element_type=jnp.float32)
    down_bias_grad = jnp.sum(grad_out, axis=(0, 1))
    pre_grad = gelu_back(
        jnp.einsum("rsd,fd->rsf", cotangent, w_down, preferred_element_type=jnp.float32)
    )[0].astype(jnp.bfloat16)
    w_in_grad = jnp.einsum("rsd,rsf->df", normed2, pre_grad, preferred_element_type=jnp.float32)
    in_bias_grad = jnp.sum(pre_grad.astype(jnp.float32), axis=(0, 1))
    mid_part, ln2_gain_grad, ln2_bias_grad = second_norm_back(
        jnp.einsum("rsf,df->rsd", pre_grad, w_in, preferred_element_type=jnp.float32)
    )
    mid_grad = grad_out + mid_part
    branch_grad = mid_grad.astype(jnp.bfloat16)
    w_out_grad = jnp.einsum("rsd,rse->de", context, branch_grad, preferred_element_type=jnp.float32)
    out_bias_grad = jnp.sum(branch_grad.astype(jnp.float32), axis=(0, 1))
    context_grad = jnp.einsum(
        "rse,de->rsd", branch_grad, w_out, preferred_element_type=jnp.float32
    ).astype(jnp.bfloat16)
    grad_rows = context_grad.reshape(query_blocks, BLK, seq_count, HEADS, HD)
    probs_grad = key_products(grad_rows, window_kv, far_random, far_global, 1)
    score_grad = (
        soft_full * (probs_grad - jnp.sum(soft_full * probs_grad, axis=-1, keepdims=True))
    ).astype(jnp.bfloat16)
    query_grad = (
        (key_mix(score_grad, window_kv, far_random, far_global, 0) * score_scale)
        .reshape(row_count, seq_count, D)
        .astype(jnp.bfloat16)
    )
    near_key, far_key, global_key = key_grads(score_grad, query_rows)
    near_value, far_value, global_value = key_grads(attn_probs, grad_rows)
    near_kv = jnp.stack([near_key * score_scale, near_value], axis=4)
    far_kv = jnp.stack([far_key * score_scale, far_value], axis=5)
    global_kv = jnp.stack([global_key * score_scale, global_value], axis=3).reshape(
        GLOB, BLK, seq_count, 2 * D
    )
    rest_pad = ((0, 0),) * 5
    extended_grad = (
        jnp.pad(near_kv[:, 0], ((0, 2),) + rest_pad)
        + jnp.pad(near_kv[:, 1], ((1, 1),) + rest_pad)
        + jnp.pad(near_kv[:, 2], ((2, 0),) + rest_pad)
    )
    extended_grad = extended_grad.reshape(row_count + 2 * BLK, seq_count, 2 * D)
    rim_grads = jnp.concatenate([extended_grad[:BLK], extended_grad[row_count + BLK :]], axis=0)
    returned = padded(rim_grads.astype(jnp.bfloat16), (("seq", 0),), BLK).astype(rim_grads.dtype)
    near_total = extended_grad[BLK : row_count + BLK]
    near_total = (
        near_total.at[:BLK].add(returned[:BLK]).at[row_count - BLK :].add(returned[3 * BLK :])
    )
    block_total = row_count * lax.axis_size("seq") // BLK
    numbers = jnp.arange(block_total, dtype=jnp.int32)
    random_hits = (random_local[..., None] == numbers).astype(jnp.float32)
    global_rows_hit = (global_blocks[..., None] == numbers).astype(jnp.float32)

    def far_sum(one_sequence):
        hits, kv, global_rows, global_sum = one_sequence
        random_term = jnp.einsum(
            "ihjb,ihjuxd->buxhd", hits, kv, precision=lax.Precision.HIGHEST
        )
        global_term = jnp.einsum(
            "gb,guc->buc", global_rows, global_sum, precision=lax.Precision.HIGHEST
        )
        flat = (block_total * BLK, 2 * D)
        return (random_term.reshape(flat) + global_term.reshape(flat)).astype(jnp.bfloat16)

    far_parts = lax.map(
        far_sum,
        (
            jnp.moveaxis(random_hits, 1, 0),
            jnp.moveaxis(far_kv, 1, 0),
            jnp.moveaxis(global_rows_hit, 1, 0),
            jnp.moveaxis(global_kv, 2, 0),
        ),
    )
    far_total = lax.psum_scatter(far_parts, "seq", scatter_dimension=1, tiled=True)
    far_total = jnp.moveaxis(far_total, 0, 1).astype(jnp.float32)
    keyval_grad = (near_total + far_total).astype(jnp.bfloat16)
    qkv_grad = jnp.concatenate([query_grad, keyval_grad], axis=-1)
    q_bias_grad = jnp.sum(query_grad.astype(jnp.float32), axis=(0, 1))
    v_bias_grad = jnp.sum(keyval_grad[:, :, D:].astype(jnp.float32), axis=(0, 1))
    w_qkv_grad = jnp.einsum("rsd,rse->de", normed, qkv_grad, preferred_element_type=jnp.float32)
    input_part, ln1_gain_grad, ln1_bias_grad = first_norm_back(
        jnp.einsum("rse,de->rsd", qkv_grad, w_qkv, preferred_element_type=jnp.float32)
    )
    input_grad = mid_grad + input_part
    summed = (
        lax.psum_scatter(ln1_gain_grad, ("batch", "seq"), scatter_dimension=0, tiled=True),
        lax.psum_scatter(ln1_bias_grad, ("batch", "seq"), scatter_dimension=0, tiled=True),
        lax.psum_scatter(w_qkv_grad, ("batch", "seq"), scatter_dimension=0, tiled=True),
        lax.psum_scatter(q_bias_grad, ("batch", "seq"), scatter_dimension=0, tiled=True),
        lax.psum_scatter(v_bias_grad, ("batch", "seq"), scatter_dimension=0, tiled=True),
        lax.psum_scatter(w_out_grad, ("batch", "seq"), scatter_dimension=0, tiled=True),
        lax.psum_scatter(out_bias_grad, ("batch", "seq"), scatter_dimension=0, tiled=True),
        lax.psum_scatter(ln2_gain_grad, ("batch", "seq"), scatter_dimension=0, tiled=True),
        lax.psum_scatter(ln2_bias_grad, ("batch", "seq"), scatter_dimension=0, tiled=True),
        lax.psum_scatter(w_in_grad, ("batch", "seq"), scatter_dimension=0, tiled=True),
        lax.psum_scatter(in_bias_grad, ("batch", "seq"), scatter_dimension=0, tiled=True),
        lax.psum_scatter(w_down_grad, ("batch", "seq"), scatter_dimension=0, tiled=True),
        lax.psum_scatter(down_bias_grad, ("batch", "seq"), scatter_dimension=0, tiled=True),
    )
    return (
        output,
        input_grad,
        summed[0],
        summed[1],
        summed[2],
        summed[3],
        summed[4],
        summed[5],
        summed[6],
        summed[7],
        summed[8],
        summed[9],
        summed[10],
        summed[11],
        summed[12],
    )


NEG = -1e30
LANES = 128
SEG_VALUES = 4
MESH_IDS = pl.DeviceIdType.MESH
VMEM_BYTES = 60 * 1024 * 1024
F32 = jnp.float32
BF16 = jnp.bfloat16
ALL = slice(None)
Z_HIGH, Z_LOW, Y, X, MEMBER = range(5)
CHIP = (Z_HIGH, Z_LOW, Y, X)


def three_parts(x):
    hi = x.astype(BF16)
    rest = x - hi.astype(F32)
    mid = rest.astype(BF16)
    low = (rest - mid.astype(F32)).astype(BF16)
    return hi, mid, low


def dot_nt(a, b):
    return lax.dot_general(a, b, (((1,), (1,)), ((), ())), preferred_element_type=F32)


def dot_nn(a, b):
    return lax.dot_general(a, b, (((1,), (0,)), ((), ())), preferred_element_type=F32)


def dot_tn(a, b):
    return lax.dot_general(a, b, (((0,), (0,)), ((), ())), preferred_element_type=F32)


def turned(x):
    return x.astype(F32).T.astype(BF16)


def normalise(values):
    mean = jnp.mean(values, axis=-1, keepdims=True)
    centred = values - mean
    scale = lax.rsqrt(jnp.mean(centred * centred, axis=-1, keepdims=True) + eps)
    return centred * scale, scale


def normalise_back(unit, scale, grad):
    first = jnp.mean(grad, axis=-1, keepdims=True)
    second = jnp.mean(grad * unit, axis=-1, keepdims=True)
    return (grad - first - unit * second) * scale


def my_bits():
    batch = lax.axis_index("batch")
    return (
        lax.div(batch, 4),
        lax.rem(lax.div(batch, 2), 2),
        lax.rem(batch, 2),
        lax.axis_index("half"),
        lax.axis_index("member"),
    )


def device_across(bit):
    batch = lax.axis_index("batch")
    half = lax.axis_index("half")
    member = lax.axis_index("member")
    if bit == MEMBER:
        return (batch, half, 1 - member)
    if bit == X:
        return (batch, 1 - half, member)
    stride = (4, 2, 1)[bit]
    return (batch + stride * (1 - 2 * my_bits()[bit]), half, member)


def place_across(mask):
    z_high, z_low, y, x, member = (
        1 - bit if mask & flag else bit for bit, flag in zip(my_bits(), (16, 8, 4, 2, 1))
    )
    return (4 * z_high + 2 * z_low + y, x, member)


def remote(src, dst, send, recv, bit):
    return pltpu.make_async_remote_copy(
        src_ref=src,
        dst_ref=dst,
        send_sem=send,
        recv_sem=recv,
        device_id=device_across(bit),
        device_id_type=MESH_IDS,
    )


def greet(bits):
    barrier = pltpu.get_barrier_semaphore()
    for bit in bits:
        pl.semaphore_signal(barrier, inc=1, device_id=device_across(bit), device_id_type=MESH_IDS)
    pl.semaphore_wait(barrier, len(bits))


class Sums:
    def __init__(self, send_sem, recv_sem):
        self.bits = my_bits()
        self.send_sem, self.recv_sem = send_sem, recv_sem
        self.pieces = {}

    def add(self, number, source, dims, order, slots, cut=()):
        self.pieces[number] = (source, dims, order, slots, cut)

    def side(self, number, depth, across):
        source, dims, order, slots, cut = self.pieces[number]
        bit = order[depth]
        value = 1 - self.bits[bit] if across else self.bits[bit]
        left = [b for b in dims if b not in order[:depth]]
        spot = left.index(bit)
        index = (ALL,) * (1 + spot) + (value,)
        if depth:
            return slots[depth - 1].at[index]
        return source.at[index + (ALL,) * (len(left) - 1 - spot) + cut]

    def copy(self, number, depth):
        _, _, order, slots, _ = self.pieces[number]
        return remote(
            self.side(number, depth, True),
            slots[depth],
            self.send_sem.at[number, depth],
            self.recv_sem.at[number, depth],
            order[depth],
        )

    def send(self, number, depth):
        self.copy(number, depth).start()

    def take(self, number, depth):
        _, _, order, slots, _ = self.pieces[number]
        self.copy(number, depth).wait_recv()
        mine = self.side(number, depth, False)[...]
        if depth == len(order) - 1:
            return mine.astype(F32) + slots[depth][...].astype(F32)
        slots[depth][...] = mine + slots[depth][...]
        self.send(number, depth + 1)
        return None

    def finish(self):
        for number, (_, _, order, _, _) in self.pieces.items():
            for depth in range(len(order)):
                self.copy(number, depth).wait_send()


def slot_shapes(lead, count, tail):
    return [pltpu.VMEM((lead,) + (2,) * (count - 1 - depth) + tail, BF16) for depth in range(count)]


ORDERS = ((X, Y, Z_LOW, Z_HIGH), (Y, Z_LOW, X, Z_HIGH), (Z_LOW, X, Y, Z_HIGH))
IN_CUTS = ((0, 16), (16, 16), (32, 32))
DOWN_CUTS = ((0, 384), (384, 384), (768, 256))
OUT_CUTS = ((0, 128), (128, 128), (256, 256))
LATER_DIMS = (
    (Z_HIGH, Z_LOW, Y),
    (Z_HIGH, Z_LOW, X),
    (Z_HIGH, Y, X),
    (Z_LOW, Y, Z_HIGH),
    (Z_LOW, Z_HIGH, X),
    (Y, Z_HIGH, X),
)


def in_vmem():
    return pl.BlockSpec(memory_space=pltpu.VMEM)


def anywhere():
    return pl.BlockSpec(memory_space=pl.ANY)


def params(collective):
    return pltpu.CompilerParams(
        collective_id=collective, has_side_effects=True, vmem_limit_bytes=VMEM_BYTES
    )


def take_rows(mixed, which):
    count = mixed.shape[0] // 2
    row = lax.broadcasted_iota(jnp.int32, (count, 2 * count), 0)
    column = lax.broadcasted_iota(jnp.int32, (count, 2 * count), 1)
    pick = jnp.where(column == 2 * row + which, 1.0, 0.0).astype(BF16)
    return dot_nn(pick, mixed).astype(BF16)


def sequence_rows(seg_ref, rows, length):
    half, member = lax.axis_index("half"), lax.axis_index("member")
    own = length // 2
    both = seg_ref[...].astype(F32)
    ids = jnp.where(half == 0, both[0:1], both[1:2])
    slots = []
    for j in range(2):
        for t in range(2):
            want = lax.rem(half + t, 2) * 2 + lax.rem(member + j, 2)
            piece = jnp.zeros((1, rows), F32)
            for b in range(4):
                piece = jnp.where(want == b, ids[:, b * rows : (b + 1) * rows], piece)
            slots.append(piece)
    spot = lax.broadcasted_iota(jnp.int32, (1, length), 1)
    side = lax.rem(half + lax.rem(spot // rows, 2), 2) * 2 + lax.rem(member + spot // own, 2)
    block = side * (rows // BLK) + lax.rem(spot // BLK, rows // BLK)
    return jnp.concatenate(slots, axis=1), block.astype(F32)


def make_features(segment, block, rand_ref, glob_ref, fq_ref, fk_ref):
    length = segment.shape[1]
    blocks = length // BLK
    half = lax.axis_index("half")
    numbers = lax.broadcasted_iota(jnp.int32, (8, length), 0).astype(F32)
    count = lax.broadcasted_iota(jnp.int32, (blocks, length), 0).astype(F32)
    here = jnp.where(block == count, 1.0, 0.0)
    apart = jnp.where((segment == numbers) | (numbers >= SEG_VALUES), 0.0, NEG)
    feats = jnp.concatenate([apart, here, here, jnp.zeros((HD - 8 - 2 * blocks, length), F32)], axis=0)
    fq_ref[...] = jnp.concatenate([feats, feats], axis=0).T.astype(BF16)

    same = jnp.where(segment == numbers, 1.0, 0.0)
    rest = jnp.zeros((HD - 16 - 2 * blocks, length), F32)
    ones = jnp.where(numbers < 3, 1.0, 0.0)
    common = jnp.where(jnp.abs(count - block) <= 1.0, 1.0, 0.0)
    for g in range(GLOB):
        named = jnp.where(half == 0, glob_ref[g : g + 1, 0:1], glob_ref[g : g + 1, 1:2])
        common = common + jnp.where(block == named.astype(F32), 1.0, 0.0)
    for pair in range(fk_ref.shape[0]):
        drawn = rand_ref[pair]
        sides = []
        for parity in (1, 0):
            times = common
            for j in range(RAND):
                column = parity * RAND + j
                times = times + jnp.where(drawn[:, column : column + 1] == block, 1.0, 0.0)
            full = jnp.where(times > 0, jnp.log(jnp.maximum(times, 1.0)), NEG)
            high = full.astype(BF16).astype(F32)
            sides += [same, high, full - high, ones, rest]
        fk_ref[pair] = jnp.concatenate(sides, axis=0).T.astype(BF16)


def begin(mixed, small, w_qkv, segments, random_blocks, global_blocks):
    rows = mixed.shape[0] // 2
    length = 4 * rows
    width = D // 2
    pairs = width // LANES
    cuts = 2
    size = rows // cuts

    def body(*refs):
        mixed_ref, w_ref, seg_ref, rand_ref, glob_ref = refs[:5]
        small_refs, in_ref = refs[5:13], refs[13]
        tok_ref, nt_ref, q_ref, k_ref, v_ref, fq_ref, fk_ref, vec_ref, in_row = refs[14:23]
        all_ref, kept_ref, sent_ref, norm_ref, wq_ref, wk_ref, wv_ref, send_sem, recv_sem, load_sem = refs[23:]

        def load(which):
            first = (2 * which + lax.axis_index("member")) * width
            place = pl.ds(pl.multiple_of(first, LANES), width)
            return pltpu.make_async_copy(w_ref.at[:, place], (wq_ref, wk_ref, wv_ref)[which], load_sem.at[which])

        for which in range(3):
            load(which).start()
        half = lax.axis_index("half")
        sent_ref[...] = take_rows(mixed_ref[...], 1 - half)
        greet((X, MEMBER))

        def over_x(c):
            return remote(
                sent_ref.at[pl.ds(c * size, size)],
                all_ref.at[pl.ds(rows + c * size, size)],
                send_sem.at[c],
                recv_sem.at[c],
                X,
            )

        def on(c):
            return remote(
                all_ref.at[pl.ds(rows + c * size, size)],
                all_ref.at[pl.ds(3 * rows + c * size, size)],
                send_sem.at[cuts + c],
                recv_sem.at[cuts + c],
                MEMBER,
            )

        near = remote(
            kept_ref, all_ref.at[pl.ds(2 * rows, rows)], send_sem.at[2 * cuts], recv_sem.at[2 * cuts], MEMBER
        )
        for c in range(cuts):
            over_x(c).start()
        kept_ref[...] = take_rows(mixed_ref[...], half)
        near.start()

        for at, ref in enumerate(small_refs):
            vec_ref[at : at + 1] = ref[...].astype(F32).reshape(1, D)
        in_row[...] = in_ref[...].astype(F32).reshape(in_row.shape)
        first_half = lax.axis_index("member") == 0
        q_shift, v_shift = (
            jnp.where(first_half, vec_ref[row : row + 1, :width], vec_ref[row : row + 1, width:]) for row in (6, 7)
        )

        for which in range(3):
            load(which).wait()

        def project(first, count):
            place = pl.ds(first, count)
            x = kept_ref[...] if first == 0 else all_ref[place, :]
            if first < 2 * rows:
                tok_ref[place, :] = x
            unit, _ = normalise(x.astype(F32))
            normed = (unit * vec_ref[4:5] + vec_ref[5:6]).astype(BF16)
            if count % LANES == 0:
                nt_ref[:, place] = turned(normed)
            else:
                norm_ref[pl.ds(first % (2 * count), count), :] = normed
                if first % (2 * count):
                    nt_ref[:, first - count : first + count] = turned(norm_ref[...])
            q_ref[place, :] = (dot_nn(normed, wq_ref[...]) + q_shift).astype(BF16)
            k_ref[place, :] = dot_nn(normed, wk_ref[...]).astype(BF16)
            v_ref[place, :] = (dot_nn(normed, wv_ref[...]) + v_shift).astype(BF16)

        project(0, rows)
        near.wait_recv()
        project(2 * rows, rows)
        make_features(*sequence_rows(seg_ref, rows, length), rand_ref, glob_ref, fq_ref, fk_ref)
        for c in range(cuts):
            over_x(c).wait_recv()
            on(c).start()
            project(rows + c * size, size)
        for c in range(cuts):
            on(c).wait_recv()
            project(3 * rows + c * size, size)
        near.wait_send()
        for c in range(cuts):
            over_x(c).wait_send()
            on(c).wait_send()

    def shape(count, columns):
        return jax.ShapeDtypeStruct((count, columns), BF16)

    return pl.pallas_call(
        body,
        grid=(1,),
        out_shape=(shape(2 * rows, D), shape(D, length))
        + (shape(length, width),) * 3
        + (shape(length, LANES), jax.ShapeDtypeStruct((pairs, length, LANES), BF16))
        + (jax.ShapeDtypeStruct((8, D), F32), jax.ShapeDtypeStruct((1,) + small[8].shape, F32)),
        in_specs=[in_vmem(), anywhere()] + [in_vmem()] * 12,
        out_specs=(in_vmem(),) * 9,
        scratch_shapes=[
            pltpu.VMEM((length, D), BF16),
            pltpu.VMEM((rows, D), BF16),
            pltpu.VMEM((rows, D), BF16),
            pltpu.VMEM((2 * size, D), BF16),
            pltpu.VMEM((D, width), BF16),
            pltpu.VMEM((D, width), BF16),
            pltpu.VMEM((D, width), BF16),
            pltpu.SemaphoreType.DMA((2 * cuts + 1,)),
            pltpu.SemaphoreType.DMA((2 * cuts + 1,)),
            pltpu.SemaphoreType.DMA((3,)),
        ],
        compiler_params=params(5),
        name="begin",
    )(mixed, w_qkv, segments, random_blocks, global_blocks, *small)


def attend_forward(q, k, v, feat_q, feat_k, cot_mixed, tile=1024):
    length, width = q.shape
    pairs = width // LANES
    tiles = length // tile
    blocks = length // BLK
    own = length // 2
    rows = own // 2

    def body(*refs):
        q_ref, k_ref, v_ref, fq_ref, fk_ref, mixed_ref = refs[:6]
        ctx_ref, qa_ref, other_ref, cot_ref = refs[6:10]
        ka_ref, made_ref, kept_ref, sent_ref, send_sem, recv_sem, cot_send, cot_recv = refs[10:]
        pair, step = pl.program_id(0), pl.program_id(1)
        half = lax.axis_index("half")

        def stay():
            return pltpu.make_async_copy(kept_ref, cot_ref.at[pl.ds(0, rows)], cot_send.at[3])

        def cot_copy(which):
            across = pl.ds(rows, rows)
            src, to, bit = (
                (sent_ref, across, X),
                (kept_ref, pl.ds(own, rows), MEMBER),
                (cot_ref.at[across], pl.ds(own + rows, rows), MEMBER),
            )[which]
            return remote(src, cot_ref.at[to], cot_send.at[which], cot_recv.at[which], bit)

        @pl.when((pair == 0) & (step == 0))
        def _():
            greet((X, MEMBER))
            sent_ref[...] = take_rows(mixed_ref[...], 1 - half)
            cot_copy(0).start()
            kept_ref[...] = take_rows(mixed_ref[...], half)
            cot_copy(1).start()
            stay().start()

        @pl.when(step == 0)
        def _():
            feats = fk_ref[0]
            low_half = lax.broadcasted_iota(jnp.int32, (length, LANES), 1) < HD
            keys = k_ref[...]
            ka_ref[0] = jnp.where(low_half, keys, feats)
            ka_ref[1] = jnp.where(low_half, feats, keys)

        lane = lax.broadcasted_iota(jnp.int32, (tile, LANES), 1)
        low_half = lane < HD
        scaled = q_ref[...] * jnp.asarray(HD ** (-0.5), BF16)
        place = pl.ds(pl.multiple_of(step * tile, tile), tile)
        feats = fq_ref[...]
        results = []
        for parity in range(2):
            if parity == 0:
                aug = jnp.where(low_half, scaled, feats)
                first = HD + 8 + 2 * blocks
            else:
                aug = jnp.where(low_half, feats, scaled)
                first = 8 + 2 * blocks
            scores = dot_nt(aug, ka_ref[parity])
            top = jnp.max(scores, axis=-1, keepdims=True)
            weights = jnp.exp(scores - top)
            total = jnp.sum(weights, axis=-1, keepdims=True)
            mixed = dot_nn(weights.astype(BF16), v_ref[...])
            results.append(mixed / total)
            hi, mid, low = three_parts(-(top + jnp.log(total)))
            aug = jnp.where(lane == first, hi, aug)
            aug = jnp.where(lane == first + 1, mid, aug)
            aug = jnp.where(lane == first + 2, low, aug)
            qa_ref[parity] = aug
        context = jnp.where(low_half, results[0], results[1]).astype(BF16)
        ctx_ref[...] = context
        made_ref[pair, place, :] = context

        def swaps(one_pair):
            cols = pl.ds(pl.multiple_of(one_pair * LANES, LANES), LANES)
            return [
                remote(
                    made_ref.at[one_pair, pl.ds(from_row, own)],
                    other_ref.at[pl.ds(own - from_row, own), cols],
                    send_sem.at[side, one_pair],
                    recv_sem.at[side, one_pair],
                    MEMBER,
                )
                for side, from_row in enumerate((0, own))
            ]

        @pl.when(step == tiles - 1)
        def _():
            for one in swaps(pair):
                one.start()

        @pl.when((pair == pairs - 2) & (step == tiles - 1))
        def _():
            cot_copy(0).wait_recv()
            cot_copy(2).start()

        @pl.when((pair == pairs - 1) & (step == tiles - 1))
        def _():
            cot_copy(0).wait_send()
            stay().wait()
            cot_copy(1).wait()
            cot_copy(2).wait()
            for one_pair in range(pairs):
                for one in swaps(one_pair):
                    one.wait()

    return pl.pallas_call(
        body,
        grid=(pairs, tiles),
        out_shape=(
            jax.ShapeDtypeStruct((length, width), BF16),
            jax.ShapeDtypeStruct((2 * pairs, length, LANES), BF16),
            jax.ShapeDtypeStruct((length, width), BF16),
            jax.ShapeDtypeStruct((length, D), BF16),
        ),
        in_specs=[
            pl.BlockSpec((tile, LANES), lambda p, t: (t, p)),
            pl.BlockSpec((length, LANES), lambda p, t: (0, p)),
            pl.BlockSpec((length, LANES), lambda p, t: (0, p)),
            pl.BlockSpec((tile, LANES), lambda p, t: (t, 0)),
            pl.BlockSpec((1, length, LANES), lambda p, t: (p, 0, 0)),
            in_vmem(),
        ],
        out_specs=(
            pl.BlockSpec((tile, LANES), lambda p, t: (t, p)),
            pl.BlockSpec((2, tile, LANES), lambda p, t: (p, t, 0)),
            anywhere(),
            anywhere(),
        ),
        scratch_shapes=[
            pltpu.VMEM((2, length, LANES), BF16),
            pltpu.VMEM((pairs, length, LANES), BF16),
            pltpu.VMEM((rows, D), BF16),
            pltpu.VMEM((rows, D), BF16),
            pltpu.SemaphoreType.DMA((2, pairs)),
            pltpu.SemaphoreType.DMA((2, pairs)),
            pltpu.SemaphoreType.DMA((4,)),
            pltpu.SemaphoreType.DMA((3,)),
        ],
        compiler_params=params(4),
        name="attend_forward",
    )(q, k, v, feat_q, feat_k, cot_mixed)


def feed_forward(context, context_other, tokens, w_out, vectors, cot, w_in, in_bias, w_down):
    rows = cot.shape[0]
    own = rows // 2
    width = context.shape[1]
    chunk = 4 * LANES
    steps = 4
    share = D // 16
    root = (2.0 / np.pi) ** 0.5
    cube = 0.044715

    def group(j):
        bits = my_bits()
        z_low = jnp.where(j < 2, 1 - bits[Z_LOW], bits[Z_LOW])
        return z_low, jnp.where(lax.rem(j, 2) == 0, 1 - bits[Y], bits[Y])

    def body(*refs):
        ctx_ref, other_ref, tok_ref, wo_ref, wo2_ref, vec_ref, c_ref = refs[:7]
        wi_refs, inb_ref, wd_refs = refs[7:11], refs[11], refs[12:16]
        out_ref, dn_ref, dn_got, mid_ref, gb_ref = refs[16:21]
        keep, got = refs[21:27], refs[27:33]
        n_ref, nt_ref, out_acc, dn_acc, out_send, out_got, dn_send, gi_ref, gd_ref = refs[33:42]
        send_sem, recv_sem, keep_sem, swap_sem = refs[42:]
        step = pl.program_id(0)
        bits = my_bits()
        z_low, y = group(step)
        slot = 2 * z_low + y

        @pl.when(step == 0)
        def _():
            greet((Z_LOW, Y, X, MEMBER))
            cut = own // 2
            swaps = []
            for at in range(2):
                part = slice(at * cut, (at + 1) * cut)
                mid = (
                    tok_ref[part].astype(F32)
                    + dot_nn(ctx_ref[part], wo_ref[...])
                    + dot_nn(other_ref[part], wo2_ref[...])
                    + vec_ref[0:1]
                )
                mid_ref[part] = mid
                unit, _ = normalise(mid)
                n_ref[part] = (unit * vec_ref[1:2] + vec_ref[2:3]).astype(BF16)
                swaps.append(
                    remote(
                        n_ref.at[pl.ds(at * cut, cut)],
                        n_ref.at[pl.ds(own + at * cut, cut)],
                        swap_sem.at[0, 3 * at],
                        swap_sem.at[1, 3 * at],
                        MEMBER,
                    )
                )
                swaps[at].start()
            nt_ref[:, :own] = turned(n_ref[:own])
            for at in range(2):
                swaps[at].wait()
                first = own + at * cut
                nt_ref[:, first : first + cut] = turned(n_ref[first : first + cut])

        wi = jnp.concatenate([ref[...] for ref in wi_refs], axis=1)
        wd = jnp.concatenate([ref[...] for ref in wd_refs], axis=0)
        def shift(u):
            return inb_ref[:, pl.ds(pl.multiple_of(u(step) * LANES, LANES), LANES)]

        in_shift = jnp.concatenate([shift(u) for u in units], axis=1)
        pre = dot_nn(n_ref[...], wi) + in_shift
        square = pre * pre
        share_up = 0.5 * jnp.tanh(pre * (root + (root * cube) * square)) + 0.5
        active = pre * share_up
        hidden = active.astype(BF16)
        slope = share_up + active * (1.0 - share_up) * (2.0 * root + (6.0 * root * cube) * square)

        def in_part(kind, at):
            bit = (X, Y, Z_LOW)[kind]
            rest = (ALL,) * (3 - bit) + (pl.ds(*IN_CUTS[kind]),)
            return lambda side: gi_ref.at[(at,) + (ALL,) * bit + (side,) + rest]

        def copies(kind, at, where, bit):
            return (
                lambda: remote(
                    where(1 - bits[bit]), got[kind].at[at], send_sem.at[kind, at], recv_sem.at[kind, at], bit
                ),
                lambda: pltpu.make_async_copy(where(bits[bit]), keep[kind].at[at], keep_sem.at[kind, at]),
            )

        def in_copies(kind, at):
            return copies(kind, at, in_part(kind, at), (X, Y, Z_LOW)[kind])

        def x_copies(at):
            return copies(3, at, lambda side: gd_ref.at[at, :, side, :, pl.ds(*DOWN_CUTS[0])], X)

        def y_copies(z):
            return copies(4, z, lambda side: gd_ref.at[2 * z + side, :, :, :, pl.ds(*DOWN_CUTS[1])], Y)

        def z_copies(at_y):
            return copies(
                5, at_y, lambda side: gd_ref.at[2 * side + at_y, :, :, :, pl.ds(*DOWN_CUTS[2])], Z_LOW
            )

        gd_ref[slot] = dot_tn(hidden, c_ref[...]).astype(BF16).reshape(2, 2, LANES, D)
        for one in x_copies(slot):
            one().start()

        @pl.when(lax.rem(step, 2) == 0)
        def _():
            y_copies(z_low)[0]().start()

        @pl.when(lax.rem(step, 2) == 1)
        def _():
            y_copies(z_low)[1]().start()

        @pl.when(step < 2)
        def _():
            z_copies(y)[0]().start()

        @pl.when(step >= 2)
        def _():
            z_copies(y)[1]().start()

        pre_grad = (dot_nt(c_ref[...], wd) * slope).astype(BF16)
        gb_ref[...] = jnp.sum(pre_grad.astype(F32), axis=0, keepdims=True)
        gi_ref[slot] = dot_nn(nt_ref[...], pre_grad).astype(BF16).reshape(2, 2, 2, 2, share, chunk)
        for kind in range(3):
            for one in in_copies(kind, slot):
                one().start()

        dn_swap = (dn_send, dn_got, swap_sem.at[0, 1], swap_sem.at[1, 1], MEMBER)
        out_swap = (out_send, out_got, swap_sem.at[0, 2], swap_sem.at[1, 2], MEMBER)
        @pl.when(step == 0)
        def _():
            dn_acc[...] = dot_nt(pre_grad, wi)
            out_acc[...] = dot_nn(hidden, wd)

        @pl.when((step > 0) & (step < steps - 1))
        def _():
            dn_acc[...] += dot_nt(pre_grad, wi)
            out_acc[...] += dot_nn(hidden, wd)

        @pl.when(step == steps - 1)
        def _():
            theirs, ours = slice(own, rows), slice(0, own)
            dn_send[...] = (dn_acc[theirs] + dot_nt(pre_grad[theirs], wi)).astype(BF16)
            remote(*dn_swap).start()
            out_send[...] = (out_acc[theirs] + dot_nn(hidden[theirs], wd)).astype(BF16)
            remote(*out_swap).start()
            dn_ref[...] = dn_acc[ours] + dot_nt(pre_grad[ours], wi)
            out_acc[ours] += mid_ref[...] + vec_ref[3:4] + dot_nn(hidden[ours], wd)

        @pl.when(step == steps - 1)
        def _():
            for at in range(4):
                for kind in range(3):
                    for one in in_copies(kind, at):
                        one().wait()
                for one in x_copies(at):
                    one().wait()
            for at in range(2):
                for one in y_copies(at) + z_copies(at):
                    one().wait()
            remote(*dn_swap).wait()
            remote(*out_swap).wait()
            out_ref[...] = (out_acc[:own] + out_got[...].astype(F32)).astype(BF16)

    def unit(z_high, x):
        def at(j):
            z_low, y = group(j)
            return 2 * (((2 * z_high + z_low) * 2 + y) * 2 + x) + lax.axis_index("member")

        return at

    units = [unit(z_high, x) for z_high in range(2) for x in range(2)]

    def column(u):
        return lambda j: (0, u(j))

    def row(u):
        return lambda j: (u(j), 0)

    def slot_of(j):
        z_low, y = group(j)
        return (0, 2 * z_low + y)

    whole = pl.BlockSpec((rows, D), lambda j: (0, 0))
    half = pl.BlockSpec((own, D), lambda j: (0, 0))
    half_ctx = pl.BlockSpec((own, width), lambda j: (0, 0))
    parts = [jax.ShapeDtypeStruct((4, 2, 2, 2, size, chunk), BF16) for _, size in IN_CUTS] + [
        jax.ShapeDtypeStruct((4, 2, LANES, DOWN_CUTS[0][1]), BF16),
        jax.ShapeDtypeStruct((2, 2, 2, LANES, DOWN_CUTS[1][1]), BF16),
        jax.ShapeDtypeStruct((2, 2, 2, LANES, DOWN_CUTS[2][1]), BF16),
    ]
    own_f32 = jax.ShapeDtypeStruct((own, D), F32)
    own_bf16 = jax.ShapeDtypeStruct((own, D), BF16)
    results = pl.pallas_call(
        body,
        grid=(steps,),
        out_shape=[
            own_bf16,
            own_f32,
            own_bf16,
            own_f32,
            jax.ShapeDtypeStruct((1, steps * chunk), F32),
        ]
        + parts
        + parts,
        in_specs=[
            half_ctx,
            half_ctx,
            half,
            pl.BlockSpec((width, D), lambda j: (lax.axis_index("member"), 0)),
            pl.BlockSpec((width, D), lambda j: (1 - lax.axis_index("member"), 0)),
            pl.BlockSpec((8, D), lambda j: (0, 0)),
            whole,
        ]
        + [pl.BlockSpec((D, LANES), column(u)) for u in units]
        + [in_vmem()]
        + [pl.BlockSpec((LANES, D), row(u)) for u in units],
        out_specs=[half, half, anywhere(), half, pl.BlockSpec((1, chunk), slot_of)]
        + [anywhere()] * 12,
        scratch_shapes=[
            pltpu.VMEM((rows, D), BF16),
            pltpu.VMEM((D, rows), BF16),
            pltpu.VMEM((rows, D), F32),
            pltpu.VMEM((rows, D), F32),
            pltpu.VMEM((own, D), BF16),
            pltpu.VMEM((own, D), BF16),
            pltpu.VMEM((own, D), BF16),
            pltpu.VMEM((4, 2, 2, 2, 2, share, chunk), BF16),
            pltpu.VMEM((4, 2, 2, LANES, D), BF16),
            pltpu.SemaphoreType.DMA((6, 4)),
            pltpu.SemaphoreType.DMA((6, 4)),
            pltpu.SemaphoreType.DMA((6, 4)),
            pltpu.SemaphoreType.DMA((2, 4)),
        ],
        compiler_params=params(1),
        name="feed_forward",
    )(context, context_other, tokens, w_out, w_out, vectors, cot, *[w_in] * 4, in_bias, *[w_down] * 4)
    return results[:5], results[5:11], results[11:]


def attend_backward(
    rows_aug, k, v, feat_k, ctx, ctx_other, mid, n2_grad, n2_grad_got, cot, vectors, w_out, normed_t, w_qkv, output_own,
    kept, got, tile=256,
):
    length, width = k.shape
    pairs = width // LANES
    early = 1
    tiles = length // tile
    own = length // 2
    chunk = kept[0].shape[-1]
    shapes = [a.shape for a in kept[:3]] + [(1, 2, 2, 2, LANES, a.shape[-1]) for a in kept[3:]]
    kept = [a.reshape(shape) for a, shape in zip(kept, shapes)]
    got = [a.reshape(shape) for a, shape in zip(got, shapes)]
    share = D // 16
    count = 9 + 3 * early

    def body(*refs):
        qa_ref, k_ref, v_ref, fk_ref, ctx_ref, other_ref, mid_ref, dn2_ref, dn2_got, c_ref, vec_ref, wo_ref = refs[:12]
        nt_ref, wq_ref, wk_ref, wv_ref, mine_ref = refs[12:17]
        keep_in, got_in = refs[17:23], refs[23:29]
        dn_ref, mg_ref, sum_ref, qb_ref, vb_ref, ready_ref, sum_down, dn_got, theirs_ref = refs[29:38]
        keep_new, got_new = refs[38:41], refs[41:44]
        ga_ref, acc_ref, slab_ref, dn_acc, dn_send, gq_ref, br_ref, g_ref, go_ref = refs[44:53]
        begin, first = refs[53:59], refs[59:65]
        slots = refs[65 : 65 + 18 + 12 + 12 * early]
        send_sem, recv_sem, load_sem, new_send, new_recv, new_keep, swap_sem = refs[65 + 30 + 12 * early :]
        pair, step = pl.program_id(0), pl.program_id(1)
        now = pair * tiles + step
        member = lax.axis_index("member")

        sums = Sums(send_sem, recv_sem)
        for kind in range(6):
            sums.add(kind, begin[kind], LATER_DIMS[kind], ORDERS[kind % 3][1:], slots[3 * kind : 3 * kind + 3])
        for kind in range(3):
            sums.add(
                6 + kind,
                go_ref,
                CHIP,
                ORDERS[kind],
                slots[18 + 4 * kind : 22 + 4 * kind],
                (ALL, pl.ds(*OUT_CUTS[kind])),
            )
        for one_pair in range(early):
            for kind in range(3):
                number = 9 + 3 * one_pair + kind
                sums.add(
                    number,
                    gq_ref.at[one_pair, pl.ds(kind, 1)],
                    CHIP,
                    ORDERS[kind],
                    slots[30 + 4 * (number - 9) : 34 + 4 * (number - 9)],
                )

        def loads(kind):
            return (
                pltpu.make_async_copy(keep_in[kind], begin[kind], load_sem.at[0, kind]),
                pltpu.make_async_copy(got_in[kind], first[kind], load_sem.at[1, kind]),
            )

        def begin_sum(kind):
            for one in loads(kind):
                one.wait()
            begin[kind][...] = begin[kind][...] + first[kind][...]
            sums.send(kind, 0)

        def end_sum(number):
            total = sums.take(number, len(sums.pieces[number][2]) - 1)
            if number < 3:
                for z_low in range(2):
                    for y in range(2):
                        for z_high in range(2):
                            for x in range(2):
                                unit = ((2 * z_high + z_low) * 2 + y) * 2 + x
                                local = (2 * z_high + x) * LANES
                                ready_ref[pl.ds(*IN_CUTS[number]), unit * LANES : (unit + 1) * LANES] = total[
                                    2 * z_low + y, :, local : local + LANES
                                ]
            elif number < 6:
                sum_down[:, pl.ds(*DOWN_CUTS[number - 3])] = total[0]
            elif number < 9:
                col, size = OUT_CUTS[number - 6]
                ready_ref[:, pl.ds(4 * chunk + col, size)] = total[0]
            else:
                one_pair, kind = (number - 9) // 3, (number - 9) % 3
                place = 4 * chunk + width + (kind * early + one_pair) * LANES
                ready_ref[:, place : place + LANES] = total[0]

        def do(number, depth):
            if depth == len(sums.pieces[number][2]) - 1:
                end_sum(number)
            else:
                sums.take(number, depth)

        def at(when, depth, *numbers):
            @pl.when(now == when)
            def _():
                for number in numbers:
                    do(number, depth)

        @pl.when(now == 0)
        def _():
            greet((Z_HIGH, Z_LOW, Y, X, MEMBER))
            for kind in range(6):
                for one in loads(kind):
                    one.start()
            for kind in (0, 1, 5, 2, 3, 4):
                begin_sum(kind)
            unit, scale = normalise(mid_ref[...])
            grad = dn2_ref[...] + dn2_got[...].astype(F32)
            cot_own = c_ref[...].astype(F32)
            mid_grad = cot_own + normalise_back(unit, scale, grad * vec_ref[1:2])
            mg_ref[...] = mid_grad
            branch = mid_grad.astype(BF16)
            br_ref[:own] = branch
            swap = remote(
                br_ref.at[pl.ds(0, own)], br_ref.at[pl.ds(own, own)], swap_sem.at[0, 0], swap_sem.at[1, 0], MEMBER
            )
            swap.start()
            sum_ref[0:1] = jnp.sum(branch.astype(F32), axis=0, keepdims=True)
            sum_ref[1:2] = jnp.sum(grad * unit, axis=0, keepdims=True)
            sum_ref[2:3] = jnp.sum(grad, axis=0, keepdims=True)
            sum_ref[3:4] = jnp.sum(cot_own, axis=0, keepdims=True)
            sum_ref[4:8] = jnp.zeros((4, D), F32)
            swap.wait()
            g_ref[...] = dot_nt(br_ref[...], wo_ref[...]).astype(BF16)
            columns = br_ref[:, pl.ds(pl.multiple_of(member * width, width), width)]
            go_ref[0, member] = dot_tn(ctx_ref[...], columns).astype(BF16).reshape(2, 2, 2, share, width)
            go_ref[0, 1 - member] = dot_tn(other_ref[...], columns).astype(BF16).reshape(2, 2, 2, share, width)
            for kind in range(6, 9):
                sums.send(kind, 0)

        output_swap = (mine_ref.at[pl.ds(own // 2, own // 2)], theirs_ref, swap_sem.at[0, 2], swap_sem.at[1, 2], X)

        @pl.when(now == 11)
        def _():
            remote(*output_swap).start()

        at(1, 0, 0, 1, 5)
        at(4, 0, 3, 4)
        at(5, 0, 7, 2)
        at(6, 1, 5)
        at(6, 0, 8)
        at(7, 0, 6)
        at(8, 1, 0, 1)
        at(8, 0, 10, 11, 9)
        at(9, 1, 2)
        at(10, 1, 3, 4, 6, 7)
        at(11, 2, 5)
        at(11, 1, 8)
        at(12, 1, 9)
        at(12, 2, 0)
        at(12, 1, 11)
        at(12, 2, 7, 1)
        at(13, 1, 10)
        at(13, 2, 8)
        at(15, 2, 2)

        slab_cols = pl.ds(pl.multiple_of(pair * LANES, LANES), LANES)

        @pl.when(step == 0)
        def _():
            lane = lax.broadcasted_iota(jnp.int32, (length, LANES), 1)
            low_half = lane < HD
            grads = g_ref[:, slab_cols]
            prod = grads.astype(F32) * ctx_ref[:, slab_cols].astype(F32)
            for parity in range(2):
                mine = low_half if parity == 0 else jnp.logical_not(low_half)
                lead = HD if parity == 0 else 0
                delta = -jnp.sum(jnp.where(mine, prod, 0.0), axis=-1, keepdims=True)
                hi, mid, low = three_parts(delta)
                rows = jnp.where(mine, grads, jnp.zeros_like(grads))
                rows = jnp.where(lane == lead, hi, rows)
                rows = jnp.where(lane == lead + 1, mid, rows)
                ga_ref[parity] = jnp.where(lane == lead + 2, low, rows)
            ga_ref[2] = grads
            acc_ref[...] = jnp.zeros_like(acc_ref)

        lane = lax.broadcasted_iota(jnp.int32, (tile, LANES), 1)
        low_half = lane < HD
        keys = k_ref[...]
        values = v_ref[...]
        feats = fk_ref[0]
        keys_t = turned(keys)
        dks, dvs = [], []
        for parity in range(2):
            lead = HD if parity == 0 else 0
            mine = low_half if parity == 0 else jnp.logical_not(low_half)
            key_rows = jnp.where(mine, keys, feats)
            ones = jnp.where((lane >= lead) & (lane < lead + 3), 1.0, 0.0).astype(BF16)
            value_rows = jnp.where(mine, values, ones)
            probs = jnp.exp(dot_nt(key_rows, qa_ref[parity]))
            diff = dot_nt(value_rows, ga_ref[parity])
            score_grad = (probs * diff).astype(BF16)
            dvs.append(dot_nn(probs.astype(BF16), ga_ref[2]))
            dks.append(dot_nn(score_grad, qa_ref[parity]))
            side = keys_t[parity * HD : (parity + 1) * HD]
            acc_ref[parity * HD : (parity + 1) * HD] += dot_nn(side, score_grad)
        place = pl.ds(pl.multiple_of(step * tile, tile), tile)
        slab_ref[place, LANES : 2 * LANES] = jnp.where(low_half, dks[0], dks[1]).astype(BF16)
        slab_ref[place, 2 * LANES :] = jnp.where(low_half, dvs[0], dvs[1]).astype(BF16)

        def new_copies(kind, late):
            bit = (X, Y, Z_LOW)[kind]
            whole = gq_ref.at[early + late, kind]
            return (
                pltpu.make_async_copy(
                    whole.at[(ALL,) * bit + (sums.bits[bit],)], keep_new[kind].at[late], new_keep.at[kind, late]
                ),
                remote(
                    whole.at[(ALL,) * bit + (1 - sums.bits[bit],)],
                    got_new[kind].at[late],
                    new_send.at[kind, late],
                    new_recv.at[kind, late],
                    bit,
                ),
            )

        @pl.when(step == tiles - 1)
        def _():
            slab_ref[:, :LANES] = (acc_ref[...].T * HD ** (-0.5)).astype(BF16)
            slabs = slab_ref[...]
            made = dot_nn(nt_ref[...], slabs).astype(BF16)
            for kind in range(3):
                gq_ref[pair, kind] = made[:, kind * LANES : (kind + 1) * LANES].reshape(
                    2, 2, 2, 2, share, LANES
                )
            for one_pair in range(pairs):

                @pl.when(pair == one_pair)
                def _(one_pair=one_pair):
                    for kind in range(3):
                        if one_pair < early:
                            sums.send(9 + 3 * one_pair + kind, 0)
                        else:
                            for one in new_copies(kind, one_pair - early):
                                one.start()

            qb_ref[...] = jnp.sum(slabs[:, :LANES].astype(F32), axis=0, keepdims=True)
            vb_ref[...] = jnp.sum(slabs[:, 2 * LANES :].astype(F32), axis=0, keepdims=True)

        dn_swap = (dn_send, dn_got, swap_sem.at[0, 1], swap_sem.at[1, 1], MEMBER)

        @pl.when(step == tiles - 1)
        def _():
            weights = jnp.concatenate([wq_ref[...], wk_ref[...], wv_ref[...]], axis=1)
            for rows in (slice(own, length), slice(0, own)):
                grown = dot_nt(slab_ref[rows], weights)

                @pl.when(pair == 0)
                def _(rows=rows, grown=grown):
                    dn_acc[rows] = grown

                @pl.when((pair > 0) & (pair < pairs - 1))
                def _(rows=rows, grown=grown):
                    dn_acc[rows] += grown

                @pl.when(pair == pairs - 1)
                def _(rows=rows, grown=grown):
                    total = dn_acc[rows] + grown
                    if rows.start:
                        dn_send[...] = total.astype(BF16)
                        remote(*dn_swap).start()
                    else:
                        dn_ref[...] = total

        @pl.when(now == pairs * tiles - 1)
        def _():
            do(11, 2)
            do(6, 2)
            do(3, 2)
            do(9, 2)
            do(4, 2)
            do(7, 3)
            do(10, 2)
            do(8, 3)
            do(11, 3)
            do(6, 3)
            do(9, 3)
            do(10, 3)
            for late in range(pairs - early):
                for kind in range(3):
                    for one in new_copies(kind, late):
                        one.wait()
            sums.finish()
            remote(*dn_swap).wait()
            remote(*output_swap).wait()

    part = pl.BlockSpec((tile, LANES), lambda p, t: (t, p))
    bias_part = pl.BlockSpec((1, LANES), lambda p, t: (0, p))

    def columns(which):
        return pl.BlockSpec(
            (D, LANES), lambda p, t: (0, (2 * which + lax.axis_index("member")) * pairs + p)
        )

    slots = []
    for shape in shapes:
        slots += slot_shapes(shape[0], 3, shape[4:])
    for _, size in OUT_CUTS:
        slots += slot_shapes(1, 4, (share, size))
    for _ in range(3 * early):
        slots += slot_shapes(1, 4, (share, LANES))
    new = [jax.ShapeDtypeStruct((pairs - early, 2, 2, 2, share, LANES), BF16)] * 3
    own_f32 = jax.ShapeDtypeStruct((own, D), F32)
    results = pl.pallas_call(
        body,
        grid=(pairs, tiles),
        out_shape=[
            own_f32,
            own_f32,
            jax.ShapeDtypeStruct((8, D), F32),
            jax.ShapeDtypeStruct((1, width), F32),
            jax.ShapeDtypeStruct((1, width), F32),
            jax.ShapeDtypeStruct((share, 4 * chunk + width + 3 * early * LANES), F32),
            jax.ShapeDtypeStruct((LANES, D), F32),
            jax.ShapeDtypeStruct((own, D), BF16),
            jax.ShapeDtypeStruct((own // 2, D), BF16),
        ]
        + new
        + new,
        in_specs=[
            pl.BlockSpec((2, length, LANES), lambda p, t: (p, 0, 0)),
            part,
            part,
            pl.BlockSpec((1, tile, LANES), lambda p, t: (p, t, 0)),
            in_vmem(),
            in_vmem(),
            in_vmem(),
            in_vmem(),
            in_vmem(),
            pl.BlockSpec((own, D), lambda p, t: (0, 0)),
            in_vmem(),
            pl.BlockSpec((width, D), lambda p, t: (lax.axis_index("member"), 0)),
            in_vmem(),
            columns(0),
            columns(1),
            columns(2),
        ]
        + [anywhere()] * 13,
        out_specs=[in_vmem(), in_vmem(), in_vmem(), bias_part, bias_part]
        + [in_vmem()] * 2
        + [anywhere()] * 8,
        scratch_shapes=[
            pltpu.VMEM((3, length, LANES), BF16),
            pltpu.VMEM((LANES, length), F32),
            pltpu.VMEM((length, 3 * LANES), BF16),
            pltpu.VMEM((length, D), F32),
            pltpu.VMEM((own, D), BF16),
            pltpu.VMEM((pairs, 3, 2, 2, 2, 2, share, LANES), BF16),
            pltpu.VMEM((length, D), BF16),
            pltpu.VMEM((length, width), BF16),
            pltpu.VMEM((1, 2, 2, 2, 2, share, width), BF16),
        ]
        + [pltpu.VMEM(shape, BF16) for shape in shapes]
        + [pltpu.VMEM(shape, BF16) for shape in shapes]
        + slots
        + [
            pltpu.SemaphoreType.DMA((count, 4)),
            pltpu.SemaphoreType.DMA((count, 4)),
            pltpu.SemaphoreType.DMA((2, 6)),
            pltpu.SemaphoreType.DMA((3, pairs - early)),
            pltpu.SemaphoreType.DMA((3, pairs - early)),
            pltpu.SemaphoreType.DMA((3, pairs - early)),
            pltpu.SemaphoreType.DMA((2, 3)),
        ],
        compiler_params=params(3),
        name="attend_backward",
    )(
        rows_aug, k, v, feat_k, ctx, ctx_other, mid, n2_grad, n2_grad_got, cot, vectors, w_out, normed_t,
        w_qkv, w_qkv, w_qkv, output_own, *kept, *got,
    )
    return results[:9], results[9:12], results[12:]


def in_turn(first, second):
    count = first.shape[0]
    row = lax.broadcasted_iota(jnp.int32, (2 * count, count), 0)
    column = lax.broadcasted_iota(jnp.int32, (2 * count, count), 1)
    even = jnp.where(row == 2 * column, 1.0, 0.0).astype(BF16)
    odd = jnp.where(row == 2 * column + 1, 1.0, 0.0).astype(BF16)
    return (dot_nn(even, first) + dot_nn(odd, second)).astype(BF16)


def finish(
    tokens, mid_grad, normed_grad, normed_grad_got, vectors, sums_in, in_bias_grad, q_sum, v_sum, ready, out_mine,
    out_other, kept, got,
):
    own = mid_grad.shape[0]
    rows = own // 2
    width = q_sum.shape[1]
    late, share = kept[0].shape[0], kept[0].shape[-2]
    per = share // 2
    size = late * LANES

    def body(*refs):
        vec_ref, sum_ref, inb_ref, qb_ref, vb_ref = refs[:5]
        keep, first = refs[5:8], refs[8:11]
        big_in = refs[11:18]
        ig_ref, ig_got, ready_got, qkv_ref, vec_sum, out_ref = refs[18:24]
        big = refs[24:31]
        ig_send, source, flat, shares, near_got, far_got = refs[31:37]
        begin, slots = refs[37:40], refs[40:46]
        send_sem, recv_sem, swap_sem, share_sem, near_sem, far_sem, load_sem = refs[46:]
        tok_ref, mg_ref, dn_ref, dn_got, mine_ref, other_ref, ready_ref = big
        member = lax.axis_index("member")

        def load(which):
            src = big_in[which].at[pl.ds(0, rows)] if which == 4 else big_in[which]
            return pltpu.make_async_copy(src, big[which], load_sem.at[which])

        for which in range(7):
            load(which).start()
        barrier = pltpu.get_barrier_semaphore()
        for mask in range(1, 32):
            pl.semaphore_signal(barrier, inc=1, device_id=place_across(mask), device_id_type=MESH_IDS)
        pl.semaphore_wait(barrier, 31)
        sums = Sums(send_sem, recv_sem)
        for kind in range(3):
            dims = tuple(b for b in CHIP if b != ORDERS[kind][0])
            sums.add(kind, begin[kind], dims, ORDERS[kind][1:3], slots[2 * kind : 2 * kind + 2])
            begin[kind][...] = keep[kind][...] + first[kind][...]
            sums.send(kind, 0)
        theirs = pl.ds(pl.multiple_of((1 - member) * per, per), per)
        ours = pl.ds(pl.multiple_of(member * per, per), per)
        top, rest = pl.ds(0, rows // 2), pl.ds(rows // 2, rows // 2)
        swaps = [
            remote(ready_ref.at[theirs], ready_got, swap_sem.at[0, 0], swap_sem.at[1, 0], MEMBER),
            remote(ig_send.at[top], ig_got.at[top], swap_sem.at[0, 1], swap_sem.at[1, 1], X),
            remote(ig_send.at[rest], ig_got.at[rest], swap_sem.at[0, 2], swap_sem.at[1, 2], X),
        ]

        for which in range(4):
            load(which).wait()
        gain_sum, bias_sum = 0.0, 0.0
        for part in (slice(rows, rows + rows // 2), slice(rows + rows // 2, own), slice(0, rows)):
            unit, scale = normalise(tok_ref[part].astype(F32))
            grad = dn_ref[part] + dn_got[part].astype(F32)
            input_grad = mg_ref[part] + normalise_back(unit, scale, grad * vec_ref[4:5])
            if part.start == rows:
                ig_send[top] = input_grad.astype(BF16)
                swaps[1].start()
            elif part.start:
                ig_send[rest] = input_grad.astype(BF16)
            else:
                ig_ref[...] = input_grad
            gain_sum = gain_sum + jnp.sum(grad * unit, axis=0, keepdims=True)
            bias_sum = bias_sum + jnp.sum(grad, axis=0, keepdims=True)
        flat[0:1] = gain_sum
        flat[1:2] = bias_sum
        flat[2:6] = sum_ref[0:4]
        blank = jnp.zeros((1, width), F32)
        for row, ref in ((6, qb_ref), (7, vb_ref)):
            value = ref[...]
            flat[row : row + 1, :width] = jnp.where(member == 0, value, blank)
            flat[row : row + 1, width:] = jnp.where(member == 1, value, blank)
        flat[8:] = jnp.zeros((LANES - 8, D), F32)
        source[:, :, :, :, :, :per] = flat[...].T.astype(BF16).reshape(2, 2, 2, 2, 2, per, LANES)
        source[:, :, :, :, :, per:] = jnp.zeros((2, 2, 2, 2, 2, 16, LANES), BF16)
        for z_high, z_low, y, x in np.ndindex(2, 2, 2, 2):
            unit = (((z_low * 2 + y) * 2 + z_high) * 2 + x) * LANES
            source[z_high, z_low, y, x, member, per:] = jnp.broadcast_to(
                inb_ref[:, unit : unit + LANES], (16, LANES)
            ).astype(BF16)

        def straight(mask):
            place = tuple(
                1 - bit if mask & flag else bit for bit, flag in zip(sums.bits, (16, 8, 4, 2, 1))
            )
            return pltpu.make_async_remote_copy(
                src_ref=source.at[place],
                dst_ref=shares.at[mask],
                send_sem=share_sem.at[0, mask],
                recv_sem=share_sem.at[1, mask],
                device_id=place_across(mask),
                device_id_type=MESH_IDS,
            )

        for mask in range(1, 32):
            straight(mask).start()

        def near(kind):
            return remote(
                slots[2 * kind + 1].at[:, sums.bits[0], theirs],
                near_got.at[kind],
                near_sem.at[0, kind],
                near_sem.at[1, kind],
                MEMBER,
            )

        def far(kind, flipped):
            return pltpu.make_async_remote_copy(
                src_ref=slots[2 * kind + 1].at[:, 1 - sums.bits[0], theirs if flipped else ours],
                dst_ref=far_got.at[flipped, kind],
                send_sem=far_sem.at[0, 2 * kind + flipped],
                recv_sem=far_sem.at[1, 2 * kind + flipped],
                device_id=place_across(16 + flipped),
                device_id_type=MESH_IDS,
            )

        for depth in range(2):
            for kind in (1, 0, 2):
                sums.copy(kind, depth).wait_recv()
                slots[2 * kind + depth][...] = sums.side(kind, depth, False)[...] + slots[2 * kind + depth][...]
                if depth == 0:
                    sums.send(kind, 1)
                else:
                    far(kind, 1).start()
                    far(kind, 0).start()
                    near(kind).start()
                if depth == 0 and kind == 1:
                    swaps[2].start()
                    for which in range(4, 7):
                        load(which).wait()
                    swaps[0].start()
                    mine, other = mine_ref[...], other_ref[...]
                    here = lax.axis_index("half") == 0
                    out_ref[...] = in_turn(jnp.where(here, mine, other), jnp.where(here, other, mine))
        total = source[sums.bits].astype(F32)
        for mask in range(1, 32):
            straight(mask).wait_recv()
            total = total + shares[mask].astype(F32)
        vec_sum[...] = total
        for kind in (1, 0, 2):
            far(kind, 0).wait_recv()
            ours_sum = slots[2 * kind + 1][:, sums.bits[0], ours].astype(F32) + far_got[0, kind].astype(F32)
            near(kind).wait_recv()
            far(kind, 1).wait_recv()
            theirs_sum = near_got[kind].astype(F32) + far_got[1, kind].astype(F32)
            for pair in range(late):
                place = kind * size + pair * LANES
                qkv_ref[member, :, place : place + LANES] = ours_sum[pair]
                qkv_ref[1 - member, :, place : place + LANES] = theirs_sum[pair]
        sums.finish()
        for kind in range(3):
            near(kind).wait_send()
            far(kind, 0).wait_send()
            far(kind, 1).wait_send()
        for mask in range(1, 32):
            straight(mask).wait_send()
        for one in swaps:
            one.wait()

    slots = []
    for _ in range(3):
        slots += slot_shapes(late, 3, (share, LANES))[:2]
    return pl.pallas_call(
        body,
        out_shape=(
            jax.ShapeDtypeStruct((rows, D), F32),
            jax.ShapeDtypeStruct((rows, D), BF16),
            jax.ShapeDtypeStruct((per, ready.shape[1]), F32),
            jax.ShapeDtypeStruct((2, per, 3 * size), F32),
            jax.ShapeDtypeStruct((per + 16, LANES), F32),
            jax.ShapeDtypeStruct((own, D), BF16),
        ),
        grid=(1,),
        in_specs=[in_vmem()] * 11 + [anywhere()] * 7,
        out_specs=(in_vmem(), anywhere(), anywhere(), in_vmem(), in_vmem(), in_vmem()),
        scratch_shapes=[
            pltpu.VMEM((own, D), BF16),
            pltpu.VMEM((own, D), F32),
            pltpu.VMEM((own, D), F32),
            pltpu.VMEM((own, D), BF16),
            pltpu.VMEM((rows, D), BF16),
            pltpu.VMEM((rows, D), BF16),
            pltpu.VMEM(ready.shape, F32),
            pltpu.VMEM((rows, D), BF16),
            pltpu.VMEM((2, 2, 2, 2, 2, per + 16, LANES), BF16),
            pltpu.VMEM((LANES, D), F32),
            pltpu.VMEM((32, per + 16, LANES), BF16),
            pltpu.VMEM((3, late, per, LANES), BF16),
            pltpu.VMEM((2, 3, late, per, LANES), BF16),
        ]
        + [pltpu.VMEM(kept[0].shape, BF16)] * 3
        + slots
        + [
            pltpu.SemaphoreType.DMA((3, 2)),
            pltpu.SemaphoreType.DMA((3, 2)),
            pltpu.SemaphoreType.DMA((2, 3)),
            pltpu.SemaphoreType.DMA((2, 32)),
            pltpu.SemaphoreType.DMA((2, 3)),
            pltpu.SemaphoreType.DMA((2, 6)),
            pltpu.SemaphoreType.DMA((7,)),
        ],
        compiler_params=params(2),
        name="finish",
    )(
        vectors, sums_in, in_bias_grad, q_sum, v_sum, *kept, *got, tokens, mid_grad, normed_grad, normed_grad_got,
        out_mine, out_other, ready,
    )


def per_device_pair(
    tokens,
    ln1_gain,
    ln1_bias,
    w_qkv,
    q_bias,
    v_bias,
    w_out,
    out_bias,
    ln2_gain,
    ln2_bias,
    w_in,
    in_bias,
    w_down,
    down_bias,
    cotangent,
    segment_ids,
    random_blocks,
    global_blocks,
):
    rows = tokens.shape[0]
    own = 2 * rows
    blocks = segment_ids.shape[0] // BLK
    half = lax.axis_index("half")
    member = lax.axis_index("member")
    mine_d = D // 2
    heads = HEADS // 2
    chips = lax.axis_size("batch") * 2

    def both_sequences(kept, other):
        return jnp.where(
            half == 0, jnp.stack([kept, other], axis=1), jnp.stack([other, kept], axis=1)
        )

    seq_random = lax.dynamic_index_in_dim(random_blocks, half, 1, keepdims=False)
    seq_random = lax.dynamic_slice_in_dim(seq_random, member * heads, heads, 1)
    pair_random = seq_random.reshape(blocks, heads // 2, 2 * RAND).transpose(1, 0, 2).astype(F32)
    own_tokens, normed_t, queries, keys, values, feat_q, feat_k, vectors, in_shift = begin(
        tokens.reshape(own, D),
        (out_bias, ln2_gain, ln2_bias, down_bias, ln1_gain, ln1_bias, q_bias, v_bias, in_bias),
        w_qkv,
        segment_ids.T,
        pair_random,
        global_blocks,
    )
    context, rows_aug, context_other, cot = attend_forward(
        queries, keys, values, feat_q, feat_k, cotangent.reshape(own, D)
    )
    (output_own, n2_grad, n2_grad_got, mid_stream, in_bias_grad), kept_parts, got_parts = feed_forward(
        context,
        context_other,
        own_tokens,
        w_out,
        vectors,
        cot,
        w_in,
        in_shift,
        w_down,
    )

    (
        (
            normed_grad,
            mid_grad,
            sums_in,
            q_sum,
            v_sum,
            ready,
            summed_down,
            normed_grad_got,
            output_other,
        ),
        kept_qkv,
        got_qkv,
    ) = attend_backward(
        rows_aug,
        keys,
        values,
        feat_k,
        context,
        context_other,
        mid_stream,
        n2_grad,
        n2_grad_got,
        cot,
        vectors,
        w_out,
        normed_t,
        w_qkv,
        output_own,
        kept_parts,
        got_parts,
    )
    input_kept, input_other, ready_got, qkv_late, vector_rows, output = finish(
        own_tokens,
        mid_grad,
        normed_grad,
        normed_grad_got,
        vectors,
        sums_in,
        in_bias_grad,
        q_sum,
        v_sum,
        ready,
        output_own,
        output_other,
        kept_qkv,
        got_qkv,
    )
    input_grad = both_sequences(input_kept, input_other.astype(F32))

    per = ready.shape[0] // 2
    mine_rows = lax.dynamic_slice_in_dim(ready, member * per, per, 0)
    left = jnp.where(member == 0, mine_rows, ready_got)
    right = jnp.where(member == 0, ready_got, mine_rows)

    start_out = w_in.shape[1] // 2
    start_early = start_out + mine_d
    early = (ready.shape[1] - start_early) // 3
    late = mine_d - early
    pieces = []
    for part in range(3):
        for x, later in ((left, qkv_late[0]), (right, qkv_late[1])):
            pieces.append(x[:, start_early + part * early : start_early + (part + 1) * early])
            pieces.append(later[:, part * late : (part + 1) * late])
    w_qkv_grad = jnp.concatenate(pieces, axis=1)
    w_out_grad = jnp.concatenate([x[:, start_out : start_out + mine_d] for x in (left, right)], axis=1)
    w_in_grad = jnp.concatenate(
        [x[:, j * LANES : (j + 1) * LANES] for j in range(chips) for x in (left, right)], axis=1
    )
    in_bias_out = vector_rows[per]
    vec = [vector_rows[:per, i] for i in range(8)]
    return (
        output.reshape(rows, 2, D),
        input_grad,
        vec[0],
        vec[1],
        w_qkv_grad,
        vec[6],
        vec[7],
        w_out_grad,
        vec[2],
        vec[3],
        vec[4],
        w_in_grad,
        in_bias_out,
        summed_down,
        vec[5],
    )


def solution(mesh):
    def program(*args):
        sequences = args[0].shape[1] // mesh.shape["batch"]
        seq = mesh.shape["seq"]
        fast = sequences == 2 and seq == 4 and mesh.shape["batch"] == 8
        if fast:
            use = jax.sharding.Mesh(
                mesh.devices.reshape(mesh.shape["batch"], 2, 2), ("batch", "half", "member")
            )
            seq_axes, all_axes, run = ("half", "member"), ("batch", "half", "member"), per_device_pair
        else:
            use, seq_axes, all_axes, run = mesh, "seq", ("batch", "seq"), per_device
        rows = P(seq_axes, "batch", None)
        in_specs = (rows,) + (P(),) * 13 + (
            rows,
            P(None, "batch"),
            P(None, "batch", None, None),
            P(None, "batch"),
        )
        vector, matrix = P(all_axes), P(all_axes, None)
        out_specs = (
            rows,
            rows,
            vector,
            vector,
            matrix,
            vector,
            vector,
            matrix,
            vector,
            vector,
            vector,
            matrix,
            vector,
            matrix,
            vector,
        )
        return jax.shard_map(
            run, mesh=use, in_specs=in_specs, out_specs=out_specs, check_vma=False
        )(*args)

    return program
```
